32 devices in a mesh: grp: 4 (over y, x), seq: 8 (over z, core).
Axes of the slice: x: 2, y: 2, z: 4, core: 2. Of those that a mesh axis runs over, the one named last changes fastest.
Arguments:
- frames: bfloat16 [8, 1536, 1024], P('grp', 'seq'), may hold values from -6 to 6
- shortcut: bfloat16 [8, 1536, 1024], P('grp', 'seq'), may hold values from -6 to 6
- time_embed: float32 [8, 2, 1024], P('grp'), may hold values from -6 to 6
- lengths: int32 [8, 2], P('grp'), may hold values from 1 to 1024, 1536 in all within a row
- kept_mask: int32 [8, 1536], P('grp', 'seq'), may hold values from 0 to 1, as said below
- target: bfloat16 [8, 1536, 1024], P('grp', 'seq'), may hold values from -6 to 6
- combine: bfloat16 [2048, 1024], P('seq'), may hold values from -0.125 to 0.125
- modulation: bfloat16 [1024, 6144], P('seq'), may hold values from -0.1875 to 0.1875
- projection: bfloat16 [1024, 3072], P('seq'), may hold values from -0.1875 to 0.1875
- readout: bfloat16 [1024, 1024], P('seq'), may hold values from -2.5 to 2.5
- expand: bfloat16 [1024, 4096], P('seq'), may hold values from -0.1875 to 0.1875
- contract: bfloat16 [4096, 1024], P('seq'), may hold values from -0.09375 to 0.09375
Outputs:
- result: bfloat16 [8, 1536, 1024], P('grp', 'seq')
- frames_grad: float32 [8, 1536, 1024], P('grp', 'seq')
- shortcut_grad: float32 [8, 1536, 1024], P('grp', 'seq')
- time_grad: float32 [8, 2, 1024], P('grp')
- combine_grad: float32 [2048, 1024], P('seq')
- modulation_grad: float32 [1024, 6144], P('seq')
- projection_grad: float32 [1024, 3072], P('seq')
- readout_grad: float32 [1024, 1024], P('seq')
- expand_grad: float32 [1024, 4096], P('seq')
- contract_grad: float32 [4096, 1024], P('seq')
The draws below stay inside these ranges and needn't reach their ends.
Inputs may be any that keep to these rules, and one draw needn't show every extreme that they name: Each group's 2 utterance lengths sum to 1536; utterances lie end to end in the order given. `kept_mask`: the last frame of every group is kept.
All inputs are finite; a program needn't handle non-finite values.
Results may differ from the reference program's by a relative error of at most 0.018.
The reference program's roundings to bfloat16 on the way count: a program that leaves them out, or rounds other values in their place, can miss the bound.
Values may be sent and summed in bfloat16 or wider, within the bound.
A program may use at most 320 MiB of HBM per device.

```python
import math
import jax
import jax.numpy as jnp
import numpy as np
from jax import lax

HEADS = 16
HEAD_DIM = 64
D = 1024
FF = 4096
GROUP_FRAMES = 1536
GROUPS = 8
UTTS = 2
MOST_LEN = 1024


def draw_kept_mask(key, part):
    key = jax.random.fold_in(key, 7)
    group_index = jnp.arange(GROUPS, dtype=jnp.int32)[:, None]
    frame_index = jnp.arange(GROUP_FRAMES, dtype=jnp.int32)[None, :]
    threshold = 150 + 400 * group_index // max(GROUPS - 1, 1) + 400 * frame_index // (GROUP_FRAMES - 1)
    lottery = jax.random.randint(key, (GROUPS, GROUP_FRAMES), 0, 1000, dtype=jnp.int32)
    chosen = (lottery < threshold).astype(jnp.int32)
    return jnp.where(frame_index == GROUP_FRAMES - 1, 1, chosen).astype(jnp.int32)


def levels(key, extent, shards, low, top_value):
    factor_of = 1.0
    for dim, parts in shards:
        draws = jax.random.uniform(jax.random.fold_in(jax.random.fold_in(key, 6), dim), (parts,), jnp.float32, low / len(shards), top_value / len(shards))
        factor_of = factor_of * jnp.repeat(jnp.exp(draws), extent[dim] // parts).reshape((-1,) + (1,) * (len(extent) - 1 - dim))
    return factor_of


def profile(amount, total, limit, lean):
    loads = [(1 << 20) // math.isqrt(rank ** lean) + 1 for rank in range(2, amount + 1)]
    spare, counts = total - limit - (amount - 1), [1] * (amount - 1)
    while spare > 0:
        movable = [i for i in range(amount - 1) if counts[i] < limit]
        mass, budget = sum([loads[i] for i in movable]), spare
        for i in movable:
            extra = min(limit - counts[i], max(1, budget * loads[i] // mass), spare)
            counts[i] = counts[i] + extra
            spare = spare - extra
    return np.array([limit] + counts)


def uneven_parts(stream_key, number_of, total, bound, skew):
    if number_of == 2:
        one = jax.random.randint(stream_key, (), max(1, total - bound), min(bound, total - 1) + 1)
        return jnp.stack([one, total - one])
    tallies = jnp.asarray(profile(number_of, total, bound, skew), jnp.int32)
    twos = (number_of - 1) // 2
    donor, taker = tallies[1:1 + 2 * twos:2], tallies[2:2 + 2 * twos:2]
    margin = jnp.minimum(donor - 1, bound - taker)
    moved = jax.random.randint(jax.random.fold_in(stream_key, 1), (twos,), 0, 1 << 20) % (margin + 1)
    tallies = tallies.at[1:1 + 2 * twos:2].set(donor - moved).at[2:2 + 2 * twos:2].set(taker + moved)
    return tallies[jax.random.permutation(jax.random.fold_in(stream_key, 2), number_of)]


def noise(key, shape, scale, reach, cuts=(), kind=jnp.bfloat16):
    factor_of = levels(key, shape, cuts, -0.22, 0.18) if cuts else 1.0
    entries = jax.random.normal(key, shape, jnp.float32) * scale * factor_of
    return jnp.minimum(jnp.maximum(entries, -reach), reach).astype(kind)


def setup_inputs(seed: int = 0) -> dict:
    keys = jax.random.split(jax.random.key(seed), 13)
    frames = noise(keys[0], (GROUPS, GROUP_FRAMES, D), 1.0, 6.0, ((0, 4), (1, 8)))
    shortcut = noise(keys[1], (GROUPS, GROUP_FRAMES, D), 1.0, 6.0, ((0, 4), (1, 8)))
    time_embed = noise(keys[2], (GROUPS, UTTS, D), 1.0, 6.0, ((0, 4),), jnp.float32)
    lengths = jax.vmap(lambda own: uneven_parts(own, UTTS, GROUP_FRAMES, MOST_LEN, 1))(jax.random.split(keys[3], GROUPS)).reshape((GROUPS, UTTS)).astype(jnp.int32)
    kept_mask = draw_kept_mask(jax.random.fold_in(keys[12], 71), 0)
    target = noise(keys[5], (GROUPS, GROUP_FRAMES, D), 1.0, 6.0, ((0, 4), (1, 8)))
    combine = noise(keys[6], (2 * D, D), (2 * D) ** -0.5, 0.125, ((0, 8),))
    modulation = noise(keys[7], (D, 6 * D), D ** -0.5, 0.1875, ((0, 8),))
    projection = noise(keys[8], (D, 3 * D), D ** -0.5, 0.1875, ((0, 8),))
    readout = noise(keys[9], (D, D), (max(1, 8 * D // GROUP_FRAMES)) ** -0.5, 2.5, ((0, 8),))
    expand = noise(keys[10], (D, FF), D ** -0.5, 0.1875, ((0, 8),))
    contract = noise(keys[11], (FF, D), FF ** -0.5, 0.09375, ((0, 8),))
    return dict(frames=frames, shortcut=shortcut, time_embed=time_embed, lengths=lengths, kept_mask=kept_mask, target=target, combine=combine, modulation=modulation, projection=projection, readout=readout, expand=expand, contract=contract)


precise = lax.Precision.HIGHEST
epsilon = 1e-06
rope_base = 10000.0

@jax.custom_vjp
def low(v):
    return lax.optimization_barrier(v.astype(jnp.bfloat16)).astype(jnp.float32)

@jax.custom_vjp
def low_back(v):
    return v

def low_keep(v):
    return (low(v), None)

def low_pass(kept, grad):
    return (grad,)

def back_keep(v):
    return (v, None)

def back_low(kept, grad):
    return (low(grad),)
low.defvjp(low_keep, low_pass)
low_back.defvjp(back_keep, back_low)

def matmul(first_op, second_op):
    return jnp.dot(first_op, second_op, precision=precise, preferred_element_type=jnp.float32)

def modulate(hidden, shift_part, scale_part):
    center = hidden - lax.optimization_barrier(jnp.mean(hidden, axis=-1, keepdims=True))
    variance = lax.optimization_barrier(jnp.mean(center * center, axis=-1, keepdims=True))
    return center * lax.rsqrt(variance + epsilon) * (1.0 + scale_part) + shift_part

def segment_info(lengths, frame_index):
    utter_count = lengths.shape[0]
    utter_ends = jnp.cumsum(lengths).astype(jnp.int32)
    starts = (utter_ends - lengths).astype(jnp.int32)
    segment = lax.optimization_barrier(jnp.sum((frame_index[:, None] >= utter_ends[None, :]).astype(jnp.int32), axis=1)).astype(jnp.int32)
    member = segment[:, None] == jnp.arange(utter_count, dtype=jnp.int32)[None, :]
    offset = lax.optimization_barrier(jnp.sum(jnp.where(member, starts[None, :], 0), axis=1)).astype(jnp.int32)
    return (segment, member, (frame_index - offset).astype(jnp.int32))

def rotary_tables(position):
    half_dim = HEAD_DIM // 2
    ladder = jnp.arange(half_dim, dtype=jnp.float32) / half_dim
    inverse = jnp.exp(-jnp.log(rope_base) * ladder)
    angles = position.astype(jnp.float32)[:, None] * inverse[None, :]
    return (jnp.cos(angles)[:, None, :], jnp.sin(angles)[:, None, :])

def rotate(vectors, cos_table, sin_table):
    half_dim = vectors.shape[-1] // 2
    front_half = vectors[..., :half_dim]
    back_half = vectors[..., half_dim:]
    return jnp.concatenate([front_half * cos_table - back_half * sin_table, back_half * cos_table + front_half * sin_table], axis=-1)

def attend_block(query_block, segment_block, key_all, value_all, segment_all):
    raw_scores = jnp.einsum('qhd,khd->hqk', query_block, key_all, precision=precise)
    scores = low_back(raw_scores) * HEAD_DIM ** (-0.5)
    same_utter = segment_block[:, None] == segment_all[None, :]
    scores = jnp.where(same_utter[None, :, :], scores, -1e+30)
    row_peak = lax.optimization_barrier(jnp.max(scores, axis=-1, keepdims=True))
    lifted = jnp.exp(scores - row_peak)
    attn_weight = low(lifted / lax.optimization_barrier(jnp.sum(lifted, axis=-1, keepdims=True)))
    return jnp.einsum('hqk,khd->qhd', attn_weight, value_all, precision=precise)

def attention(queries, key_all, value_all, segment):
    total_rows = queries.shape[0]
    block_rows = min(512, total_rows)
    blocks = total_rows // block_rows
    query_blocks = queries.reshape(blocks, block_rows, HEADS, HEAD_DIM)
    segment_blocks = segment.reshape(blocks, block_rows)

    def one_block(pieces):
        return attend_block(pieces[0], pieces[1], key_all, value_all, segment)
    mixture = lax.map(jax.checkpoint(one_block), (query_blocks, segment_blocks))
    return mixture.reshape(total_rows, HEADS * HEAD_DIM)

def reference(frames, shortcut, time_embed, lengths, kept_mask, target, combine, modulation, projection, readout, expand, contract):
    weights = tuple((matrix.astype(jnp.float32) for matrix in (combine, modulation, projection, readout, expand, contract)))
    kept_total = jnp.sum(kept_mask.astype(jnp.float32))
    loss_scale = GROUPS * GROUP_FRAMES / kept_total
    frame_index = jnp.arange(GROUP_FRAMES, dtype=jnp.int32)
    head_shape = (GROUP_FRAMES, HEADS, HEAD_DIM)

    def group_step(running, group_items):
        frame_rows, shortcut_rows, embed_rows, length_row, kept_row, target_rows = group_items
        segment, member, position = segment_info(length_row, frame_index)
        member_float = member.astype(jnp.float32)
        cos_table, sin_table = rotary_tables(position)
        kept_float = kept_row.astype(jnp.float32)[:, None]
        target_float = target_rows.astype(jnp.float32)

        def whole_layer(frame_in, shortcut_in, embed_in, combine_w, modulation_w, projection_w, readout_w, expand_w, contract_w):
            joined = jnp.concatenate([frame_in, shortcut_in], axis=1)
            hidden = low_back(matmul(joined, combine_w))
            condition = low(jax.nn.silu(embed_in))
            modulation_utter = low_back(matmul(condition, modulation_w))
            modulation_frame = matmul(member_float, modulation_utter)
            shift_first, scale_first, gate_first, shift_second, scale_second, gate_second = jnp.split(modulation_frame, 6, axis=1)
            normed = low(modulate(hidden, shift_first, scale_first))
            packed = low_back(matmul(normed, projection_w))
            query_raw, key_raw, value_raw = jnp.split(packed, 3, axis=1)
            queries = low(low_back(rotate(query_raw.reshape(head_shape), cos_table, sin_table)))
            key_all = low(low_back(rotate(key_raw.reshape(head_shape), cos_table, sin_table)))
            value_all = low(low_back(value_raw.reshape(head_shape)))
            mixture = low(low_back(attention(queries, key_all, value_all, segment)))
            branch = low_back(matmul(mixture, readout_w))
            middle = hidden + gate_first * branch
            normed_second = low(modulate(middle, shift_second, scale_second))
            expanded = low_back(matmul(normed_second, expand_w))
            active = low(jax.nn.gelu(expanded, approximate=True))
            contracted = low_back(matmul(active, contract_w))
            output = middle + gate_second * contracted
            missing = output - target_float
            loss_value = 0.5 * loss_scale * jnp.sum(kept_float * missing * missing)
            return (output, loss_value)
        (output, loss_value), pullback = jax.vjp(whole_layer, frame_rows.astype(jnp.float32), shortcut_rows.astype(jnp.float32), embed_rows, *weights)
        gradients = pullback((jnp.zeros_like(output), jnp.ones_like(loss_value)))
        updated = tuple((total_now + gradient for total_now, gradient in zip(running, gradients[3:])))
        return (updated, (output.astype(jnp.bfloat16), gradients[0], gradients[1], gradients[2]))
    zero_totals = tuple((jnp.zeros(matrix.shape, jnp.float32) for matrix in weights))
    totals, per_group = lax.scan(group_step, zero_totals, (frames, shortcut, time_embed, lengths, kept_mask, target))
    return (per_group[0], per_group[1], per_group[2], per_group[3], totals[0], totals[1], totals[2], totals[3], totals[4], totals[5])
```

```python
import functools

import jax
import jax.numpy as jnp
from jax import lax
from jax.experimental import pallas as pl
from jax.experimental.pallas import tpu as pltpu
from jax.sharding import PartitionSpec as P

HEADS = 16
HEAD_DIM = 64


precise = lax.Precision.HIGHEST
epsilon = 1e-06
rope_base = 10000.0


def product(first_op, second_op):
    return jnp.dot(first_op, second_op, preferred_element_type=jnp.float32)


def product_left(first_op, second_op):
    return lax.dot_general(
        first_op, second_op, (((0,), (0,)), ((), ())), preferred_element_type=jnp.float32
    )


def product_right(first_op, second_op):
    return lax.dot_general(
        first_op, second_op, (((1,), (1,)), ((), ())), preferred_element_type=jnp.float32
    )


def gelu_tanh(values):
    return jax.nn.gelu(values, approximate=True)


def modulate(hidden, shift_part, scale_part):
    center = hidden - jnp.mean(hidden, axis=-1, keepdims=True)
    variance = jnp.mean(center * center, axis=-1, keepdims=True)
    return center * lax.rsqrt(variance + epsilon) * (1.0 + scale_part) + shift_part


def segment_info(lengths, frame_index):
    utter_count = lengths.shape[0]
    utter_ends = jnp.cumsum(lengths)
    starts = utter_ends - lengths
    segment = jnp.sum((frame_index[:, None] >= utter_ends[None, :]).astype(jnp.int32), axis=1)
    member = segment[:, None] == jnp.arange(utter_count, dtype=jnp.int32)[None, :]
    offset = jnp.sum(jnp.where(member, starts[None, :], 0), axis=1)
    return (segment, member, frame_index - offset)


def rotary_tables(position):
    half_dim = HEAD_DIM // 2
    ladder = jnp.arange(half_dim, dtype=jnp.float32) / half_dim
    inverse = jnp.exp(-jnp.log(rope_base) * ladder)
    angles = position.astype(jnp.float32)[:, None] * inverse[None, :]
    return (jnp.cos(angles)[:, None, :], jnp.sin(angles)[:, None, :])


def rotate(vectors, cos_table, sin_table):
    half_dim = vectors.shape[-1] // 2
    front_half = vectors[..., :half_dim]
    back_half = vectors[..., half_dim:]
    return jnp.concatenate(
        [
            front_half * cos_table - back_half * sin_table,
            back_half * cos_table + front_half * sin_table,
        ],
        axis=-1,
    )


MESH = pl.DeviceIdType.MESH
NEG = -1e30


def utter_features(boundary, total_rows, for_keys):
    row = lax.broadcasted_iota(jnp.int32, (total_rows, 128), 0)
    lane = lax.broadcasted_iota(jnp.int32, (total_rows, 128), 1)
    second = (row >= boundary).astype(jnp.float32)
    ahead = (lane == 0).astype(jnp.float32)
    after = (lane == 1).astype(jnp.float32)
    if for_keys:
        return (NEG * (second * ahead + (1.0 - second) * after)).astype(jnp.bfloat16)
    return (second * after + (1.0 - second) * ahead).astype(jnp.bfloat16)


def head_lanes(values, head):
    lane = lax.broadcasted_iota(jnp.int32, values.shape, 1)
    own = (lane >= head * HEAD_DIM) & (lane < (head + 1) * HEAD_DIM)
    return jnp.where(own, values.astype(jnp.float32), 0.0).astype(jnp.bfloat16)


def dot_nn(first_op, second_op):
    return jnp.dot(first_op, second_op, preferred_element_type=jnp.float32)


def dot_nt(first_op, second_op):
    return lax.dot_general(
        first_op, second_op, (((1,), (1,)), ((), ())), preferred_element_type=jnp.float32
    )


def fold_rows(values, combine):
    return combine(values.reshape(values.shape[0] // 8, 8, values.shape[1]), axis=0)


def enter(partners):
    barrier = pltpu.get_barrier_semaphore()
    for partner in partners:
        pl.semaphore_signal(barrier, inc=1, device_id=partner, device_id_type=MESH)
    pl.semaphore_wait(barrier, len(partners))


def key_span(third, total_rows):
    size = total_rows // 3
    return (max(third - 1, 0) * size, min(third + 2, 3) * size)


def forward_kernel(
    seq_count, bound_ref, qkv_ref, kept_ref, mixture_ref, log_ref,
    key_scr, query_scr, value_t_scr, score_scr, mix_t_scr, mix_scr,
    send_sem, recv_sem, back_send_sem, back_recv_sem, local_sem,
):
    group_count, local_rows, local_width = qkv_ref.shape[1], qkv_ref.shape[3], qkv_ref.shape[4]
    total_rows = seq_count * local_rows
    heads = local_width // HEAD_DIM
    me = lax.axis_index("seq")
    grp = lax.axis_index("grp")
    others = [lax.rem(me + step, seq_count) for step in range(1, seq_count)]
    origins = [lax.rem(me + seq_count - step, seq_count) for step in range(1, seq_count)]
    block = min(256, total_rows // 3)
    enter([(grp, other) for other in others])
    copies = []
    for group in range(group_count):
        own = pltpu.make_async_copy(qkv_ref.at[me, group], kept_ref.at[me, group], local_sem.at[group])
        own.start()
        row = [own]
        for step, other in enumerate(others):
            copy = pltpu.make_async_remote_copy(
                qkv_ref.at[other, group], kept_ref.at[me, group],
                send_sem.at[group, step], recv_sem.at[group, step],
                device_id=(grp, other), device_id_type=MESH,
            )
            copy.start()
            row.append(copy)
        copies.append(row)
    back = []
    for group in range(group_count):
        for copy in copies[group]:
            copy.wait()
        boundary = bound_ref[group]
        keys = kept_ref[:, group, 1].reshape(total_rows, local_width)
        values = kept_ref[:, group, 2].reshape(total_rows, local_width)
        key_scr[:, :local_width] = keys
        key_scr[:, local_width:] = utter_features(boundary, total_rows, True)
        query_scr[:, local_width:] = utter_features(boundary, total_rows, False)
        value_t_scr[...] = values.astype(jnp.float32).T.astype(jnp.bfloat16)

        def one_head(head, carry):
            queries = kept_ref[:, group, 0].reshape(total_rows, local_width)
            query_scr[:, :local_width] = head_lanes(queries, head) * jnp.bfloat16(HEAD_DIM ** (-0.5))
            for third in range(3):
                first_key, last_key = key_span(third, total_rows)
                chunks = range(first_key, last_key, block)

                def one_block(index, carry):
                    first_row = pl.multiple_of(third * (total_rows // 3) + index * block, block)
                    query_block = query_scr[pl.ds(first_row, block), :]
                    peak = jnp.full((8, block), -jnp.inf, jnp.float32)
                    for first in chunks:
                        scores = dot_nt(key_scr[first:first + block, :], query_block)
                        score_scr[first:first + block, :] = scores
                        peak = jnp.maximum(peak, fold_rows(scores, jnp.max))
                    peak = jnp.max(peak, axis=0, keepdims=True)
                    total = jnp.zeros((8, block), jnp.float32)
                    for first in chunks:
                        lifted = jnp.exp(score_scr[first:first + block, :] - peak)
                        score_scr[first:first + block, :] = lifted
                        total = total + fold_rows(lifted, jnp.sum)
                    total = jnp.sum(total, axis=0, keepdims=True)
                    inverse = 1.0 / total
                    mixed = jnp.zeros((HEAD_DIM, block), jnp.float32)
                    rows = pl.ds(pl.multiple_of(head * HEAD_DIM, HEAD_DIM), HEAD_DIM)
                    for first in chunks:
                        weight = (score_scr[first:first + block, :] * inverse).astype(jnp.bfloat16)
                        mixed = mixed + dot_nn(value_t_scr[rows, first:first + block], weight)
                    mix_t_scr[rows, pl.ds(first_row, block)] = mixed
                    log_ref[group, head, :, pl.ds(first_row, block)] = peak + jnp.log(total)
                    return carry

                lax.fori_loop(0, total_rows // 3 // block, one_block, 0)
            return carry

        lax.fori_loop(0, heads, one_head, 0)
        mix_scr[group] = mix_t_scr[...].T.astype(jnp.bfloat16).reshape(seq_count, local_rows, local_width)
        own = pltpu.make_async_copy(
            mix_scr.at[group, me], mixture_ref.at[me, group], local_sem.at[group_count + group]
        )
        own.start()
        back.append(own)
        for step, other in enumerate(others):
            copy = pltpu.make_async_remote_copy(
                mix_scr.at[group, other], mixture_ref.at[me, group],
                back_send_sem.at[group, step], back_recv_sem.at[group, step],
                device_id=(grp, other), device_id_type=MESH,
            )
            copy.start()
            back.append(copy)
    for copy in back:
        copy.wait()


def attend_forward(bounds, qkv):
    seq_count, group_count, _, local_rows, local_width = qkv.shape
    total_rows = seq_count * local_rows
    heads = local_width // HEAD_DIM
    block = min(256, total_rows // 3)
    vmem = pl.BlockSpec(memory_space=pltpu.VMEM)
    return pl.pallas_call(
        functools.partial(forward_kernel, seq_count),
        out_shape=(
            jax.ShapeDtypeStruct(qkv.shape, jnp.bfloat16),
            jax.ShapeDtypeStruct((seq_count, group_count, local_rows, local_width), jnp.bfloat16),
            jax.ShapeDtypeStruct((group_count, heads, 1, total_rows), jnp.float32),
        ),
        in_specs=[pl.BlockSpec(memory_space=pltpu.SMEM), pl.BlockSpec(memory_space=pl.ANY)],
        out_specs=(vmem, vmem, vmem),
        scratch_shapes=[
            pltpu.VMEM((total_rows, local_width + 128), jnp.bfloat16),
            pltpu.VMEM((total_rows, local_width + 128), jnp.bfloat16),
            pltpu.VMEM((local_width, total_rows), jnp.bfloat16),
            pltpu.VMEM((total_rows, block), jnp.float32),
            pltpu.VMEM((local_width, total_rows), jnp.float32),
            pltpu.VMEM((group_count, seq_count, local_rows, local_width), jnp.bfloat16),
            pltpu.SemaphoreType.DMA((group_count, seq_count - 1)),
            pltpu.SemaphoreType.DMA((group_count, seq_count - 1)),
            pltpu.SemaphoreType.DMA((group_count, seq_count - 1)),
            pltpu.SemaphoreType.DMA((group_count, seq_count - 1)),
            pltpu.SemaphoreType.DMA((2 * group_count,)),
        ],
        compiler_params=pltpu.CompilerParams(
            collective_id=1, has_side_effects=True, vmem_limit_bytes=48 * 1024 * 1024
        ),
        name="attend_forward",
    )(bounds, qkv)


def backward_kernel(
    seq_count, bound_ref, kept_ref, grad_ref, log_ref, out_ref,
    taken_scr, key_scr, query_scr, key_t_scr, head_query_scr, head_grad_scr, prob_scr, weight_scr,
    query_t_scr, key_sum_scr, value_sum_scr, back_scr,
    send_sem, recv_sem, back_send_sem, back_recv_sem, local_sem,
):
    group_count, local_rows, local_width = grad_ref.shape[1], grad_ref.shape[2], grad_ref.shape[3]
    total_rows = seq_count * local_rows
    heads = local_width // HEAD_DIM
    me = lax.axis_index("seq")
    grp = lax.axis_index("grp")
    others = [lax.rem(me + step, seq_count) for step in range(1, seq_count)]
    block = min(256, total_rows // 3)
    enter([(grp, other) for other in others])
    copies = []
    for group in range(group_count):
        own = pltpu.make_async_copy(grad_ref.at[me, group], taken_scr.at[me, group], local_sem.at[group])
        own.start()
        row = [own]
        for step, other in enumerate(others):
            copy = pltpu.make_async_remote_copy(
                grad_ref.at[other, group], taken_scr.at[me, group],
                send_sem.at[group, step], recv_sem.at[group, step],
                device_id=(grp, other), device_id_type=MESH,
            )
            copy.start()
            row.append(copy)
        copies.append(row)
    back = []
    for group in range(group_count):
        for copy in copies[group]:
            copy.wait()
        boundary = bound_ref[group]
        keys = kept_ref[:, group, 1].reshape(total_rows, local_width)
        key_scr[:, :local_width] = keys
        key_scr[:, local_width:] = utter_features(boundary, total_rows, True)
        query_scr[:, local_width:] = utter_features(boundary, total_rows, False)
        key_t_scr[...] = keys.astype(jnp.float32).T.astype(jnp.bfloat16)
        key_sum_scr[...] = jnp.zeros_like(key_sum_scr)
        value_sum_scr[...] = jnp.zeros_like(value_sum_scr)

        def one_head(head, carry):
            queries = head_lanes(kept_ref[:, group, 0].reshape(total_rows, local_width), head)
            head_query_scr[...] = queries
            query_scr[:, :local_width] = queries * jnp.bfloat16(HEAD_DIM ** (-0.5))
            head_grad_scr[...] = head_lanes(taken_scr[:, group].reshape(total_rows, local_width), head)
            for third in range(3):
                first_key, last_key = key_span(third, total_rows)
                chunks = range(first_key, last_key, block)

                def one_block(index, carry):
                    first_row = pl.multiple_of(third * (total_rows // 3) + index * block, block)
                    own_rows = pl.ds(first_row, block)
                    query_block = query_scr[own_rows, :]
                    grad_block = head_grad_scr[own_rows, :]
                    plain_block = head_query_scr[own_rows, :]
                    log_block = log_ref[group, head, :, own_rows]
                    row_dot = jnp.zeros((8, block), jnp.float32)
                    for first in chunks:
                        scores = dot_nt(key_scr[first:first + block, :], query_block)
                        prob = jnp.exp(scores - log_block)
                        values = kept_ref[
                            first // local_rows:(first + block - 1) // local_rows + 1, group, 2
                        ].reshape(-1, local_width)
                        skip = first % local_rows
                        weight_grad = dot_nt(values[skip:skip + block], grad_block)
                        prob_scr[first:first + block, :] = prob
                        weight_scr[first:first + block, :] = weight_grad
                        row_dot = row_dot + fold_rows(prob * weight_grad, jnp.sum)
                    row_dot = jnp.sum(row_dot, axis=0, keepdims=True)
                    rows = pl.ds(pl.multiple_of(head * HEAD_DIM, HEAD_DIM), HEAD_DIM)
                    turned = jnp.zeros((HEAD_DIM, block), jnp.float32)
                    for first in chunks:
                        prob = prob_scr[first:first + block, :]
                        score_grad = (
                            HEAD_DIM ** (-0.5) * (prob * (weight_scr[first:first + block, :] - row_dot))
                        ).astype(jnp.bfloat16)
                        key_sum_scr[first:first + block, :] += dot_nn(score_grad, plain_block)
                        value_sum_scr[first:first + block, :] += dot_nn(
                            prob.astype(jnp.bfloat16), grad_block
                        )
                        turned = turned + dot_nn(key_t_scr[rows, first:first + block], score_grad)
                    query_t_scr[rows, own_rows] = turned
                    return carry

                lax.fori_loop(0, total_rows // 3 // block, one_block, 0)
            return carry

        lax.fori_loop(0, heads, one_head, 0)
        shape = (seq_count, local_rows, local_width)
        back_scr[:, group, 0] = query_t_scr[...].T.astype(jnp.bfloat16).reshape(shape)
        back_scr[:, group, 1] = key_sum_scr[...].astype(jnp.bfloat16).reshape(shape)
        back_scr[:, group, 2] = value_sum_scr[...].astype(jnp.bfloat16).reshape(shape)
        own = pltpu.make_async_copy(
            back_scr.at[me, group], out_ref.at[me, group], local_sem.at[group_count + group]
        )
        own.start()
        back.append(own)
        for step, other in enumerate(others):
            copy = pltpu.make_async_remote_copy(
                back_scr.at[other, group], out_ref.at[me, group],
                back_send_sem.at[group, step], back_recv_sem.at[group, step],
                device_id=(grp, other), device_id_type=MESH,
            )
            copy.start()
            back.append(copy)
    for copy in back:
        copy.wait()


def attend_backward(bounds, kept, grad, log_total):
    seq_count, group_count, _, local_rows, local_width = kept.shape
    total_rows = seq_count * local_rows
    block = min(256, total_rows // 3)
    vmem = pl.BlockSpec(memory_space=pltpu.VMEM)
    return pl.pallas_call(
        functools.partial(backward_kernel, seq_count),
        out_shape=jax.ShapeDtypeStruct(kept.shape, jnp.bfloat16),
        in_specs=[
            pl.BlockSpec(memory_space=pltpu.SMEM), vmem, pl.BlockSpec(memory_space=pl.ANY), vmem
        ],
        out_specs=vmem,
        scratch_shapes=[
            pltpu.VMEM(grad.shape, jnp.bfloat16),
            pltpu.VMEM((total_rows, local_width + 128), jnp.bfloat16),
            pltpu.VMEM((total_rows, local_width + 128), jnp.bfloat16),
            pltpu.VMEM((local_width, total_rows), jnp.bfloat16),
            pltpu.VMEM((total_rows, local_width), jnp.bfloat16),
            pltpu.VMEM((total_rows, local_width), jnp.bfloat16),
            pltpu.VMEM((total_rows, block), jnp.float32),
            pltpu.VMEM((total_rows, block), jnp.float32),
            pltpu.VMEM((local_width, total_rows), jnp.float32),
            pltpu.VMEM((total_rows, local_width), jnp.float32),
            pltpu.VMEM((total_rows, local_width), jnp.float32),
            pltpu.VMEM(kept.shape, jnp.bfloat16),
            pltpu.SemaphoreType.DMA((group_count, seq_count - 1)),
            pltpu.SemaphoreType.DMA((group_count, seq_count - 1)),
            pltpu.SemaphoreType.DMA((group_count, seq_count - 1)),
            pltpu.SemaphoreType.DMA((group_count, seq_count - 1)),
            pltpu.SemaphoreType.DMA((2 * group_count,)),
        ],
        compiler_params=pltpu.CompilerParams(
            collective_id=2, has_side_effects=True, vmem_limit_bytes=48 * 1024 * 1024
        ),
        name="attend_backward",
    )(bounds, kept, grad, log_total)


def shards(
    frames,
    shortcut,
    time_embed,
    lengths,
    kept_mask,
    target,
    combine,
    modulation,
    projection,
    readout,
    expand,
    contract,
):
    gathered = (
        lax.all_gather(combine, "seq", axis=0, tiled=True),
        lax.all_gather(projection, "seq", axis=0, tiled=True),
        lax.all_gather(readout, "seq", axis=0, tiled=True),
        lax.all_gather(expand, "seq", axis=0, tiled=True),
        lax.all_gather(contract, "seq", axis=0, tiled=True),
    )
    combine_full, projection_full, readout_full, expand_full, contract_full = (
        gathered
    )
    group_count = frames.shape[0]
    local_rows = frames.shape[1]
    width = HEADS * HEAD_DIM
    row_count = group_count * local_rows
    seq_count = lax.axis_size("seq")
    group_frames = local_rows * seq_count
    all_frames = group_frames * lax.axis_size("grp") * group_count
    utter_count = time_embed.shape[1]
    kept_float = kept_mask.astype(jnp.float32).reshape(row_count)
    kept_total = lax.psum(jnp.sum(kept_float), ("grp", "seq"))
    local_index = lax.axis_index("seq") * local_rows + jnp.arange(local_rows, dtype=jnp.int32)

    def local_info(length_row):
        return segment_info(length_row, local_index)

    member_info = jax.vmap(local_info)(lengths)
    member_float = member_info[1].astype(jnp.float32)
    position = member_info[2]
    cos_table, sin_table = rotary_tables(position.reshape(row_count))
    joined = jnp.concatenate([frames, shortcut], axis=2).reshape(row_count, 2 * width)
    hidden = product(joined, combine_full)
    silu_value, silu_pull = jax.vjp(jax.nn.silu, time_embed)
    condition = silu_value.astype(jnp.bfloat16)
    shard_rows = modulation.shape[0]
    condition_part = lax.dynamic_slice_in_dim(
        condition, lax.axis_index("seq") * shard_rows, shard_rows, 2
    ).reshape(group_count * utter_count, shard_rows)
    modulation_utter = lax.psum(product(condition_part, modulation), "seq").reshape(
        group_count, utter_count, 6 * width
    )
    modulation_frame = jnp.einsum(
        "gtu,gue->gte",
        member_float,
        modulation_utter,
        precision=precise,
        preferred_element_type=jnp.float32,
    ).reshape(row_count, 6 * width)
    shift_first, scale_first, gate_first, shift_second, scale_second, gate_second = jnp.split(
        modulation_frame, 6, axis=1
    )
    normed_value, first_pull = jax.vjp(modulate, hidden, shift_first, scale_first)
    normed = normed_value.astype(jnp.bfloat16)
    packed = product(normed, projection_full)
    query_raw, key_raw, value_raw = jnp.split(packed, 3, axis=1)
    head_shape = (row_count, HEADS, HEAD_DIM)
    split_shape = (group_count, local_rows, width)

    def rotate_local(vectors):
        return rotate(vectors, cos_table, sin_table)

    query_turned, query_pull = jax.vjp(rotate_local, query_raw.reshape(head_shape))
    key_turned, key_pull = jax.vjp(rotate_local, key_raw.reshape(head_shape))
    local_width = width // seq_count

    def by_target(vectors):
        return vectors.reshape(group_count, local_rows, seq_count, local_width).astype(jnp.bfloat16)

    qkv = jnp.transpose(
        jnp.stack([by_target(query_turned), by_target(key_turned), by_target(value_raw)]),
        (3, 1, 0, 2, 4),
    )
    bounds = lengths[:, 0]
    kept_heads, mixture_blocks, log_total = attend_forward(bounds, qkv)
    mixture = jnp.transpose(mixture_blocks, (1, 2, 0, 3)).reshape(row_count, width)
    branch = product(mixture, readout_full)
    middle = hidden + gate_first * branch
    second_value, second_pull = jax.vjp(modulate, middle, shift_second, scale_second)
    normed_second = second_value.astype(jnp.bfloat16)
    expanded = product(normed_second, expand_full)
    active_value, gelu_pull = jax.vjp(gelu_tanh, expanded)
    active = active_value.astype(jnp.bfloat16)
    contracted = product(active, contract_full)
    output = middle + gate_second * contracted
    loss_scale = all_frames / kept_total
    output_grad = (
        loss_scale
        * kept_float[:, None]
        * (output - target.reshape(row_count, width).astype(jnp.float32))
    )
    combine_back, projection_back, readout_back, expand_back, contract_back = (
        gathered
    )
    gate_second_grad = output_grad * contracted
    contracted_grad = (gate_second * output_grad).astype(jnp.bfloat16)
    contract_part = product_left(active, contracted_grad)
    active_grad = product_right(contracted_grad, contract_back)
    expanded_grad = gelu_pull(active_grad)[0].astype(jnp.bfloat16)
    expand_part = product_left(normed_second, expanded_grad)
    normed_second_grad = product_right(expanded_grad, expand_back)
    middle_extra, shift_second_grad, scale_second_grad = second_pull(normed_second_grad)
    middle_grad = output_grad + middle_extra
    gate_first_grad = middle_grad * branch
    branch_grad = (gate_first * middle_grad).astype(jnp.bfloat16)
    readout_part = product_left(mixture, branch_grad)
    mixture_grad = product_right(branch_grad, readout_back).astype(jnp.bfloat16)
    back_blocks = attend_backward(
        bounds,
        kept_heads,
        jnp.transpose(
            mixture_grad.reshape(group_count, local_rows, seq_count, local_width), (2, 0, 1, 3)
        ),
        log_total,
    )
    query_back, key_back, value_back = jnp.transpose(back_blocks, (2, 1, 3, 0, 4)).reshape(
        3, group_count, local_rows, width
    )
    query_unturned = query_pull(query_back.reshape(head_shape).astype(jnp.float32))[0].reshape(
        row_count, width
    )
    key_unturned = key_pull(key_back.reshape(head_shape).astype(jnp.float32))[0].reshape(
        row_count, width
    )
    packed_grad = jnp.concatenate(
        [
            query_unturned.astype(jnp.bfloat16),
            key_unturned.astype(jnp.bfloat16),
            value_back.reshape(row_count, width),
        ],
        axis=1,
    )
    projection_part = product_left(normed, packed_grad)
    normed_grad = product_right(packed_grad, projection_back)
    hidden_extra, shift_first_grad, scale_first_grad = first_pull(normed_grad)
    hidden_grad = (middle_grad + hidden_extra).astype(jnp.bfloat16)
    combine_part = product_left(joined, hidden_grad)
    joined_grad = product_right(hidden_grad, combine_back)
    frames_grad = joined_grad[:, :width].reshape(split_shape)
    shortcut_grad = joined_grad[:, width:].reshape(split_shape)
    modulation_frame_grad = jnp.concatenate(
        [
            shift_first_grad,
            scale_first_grad,
            gate_first_grad,
            shift_second_grad,
            scale_second_grad,
            gate_second_grad,
        ],
        axis=1,
    )
    utter_part = jnp.einsum(
        "gtu,gte->gue",
        member_float,
        modulation_frame_grad.reshape(group_count, local_rows, 6 * width),
        precision=precise,
        preferred_element_type=jnp.float32,
    )
    utter_grad = lax.psum(utter_part.astype(jnp.bfloat16), "seq")
    utter_rows = utter_grad.reshape(group_count * utter_count, 6 * width)
    condition_grad = lax.all_gather(
        product_right(utter_rows, modulation), "seq", axis=1, tiled=True
    ).reshape(group_count, utter_count, width)
    time_grad = silu_pull(condition_grad)[0]
    modulation_part = product_left(condition_part, utter_rows)
    scattered = (
        lax.psum_scatter(
            combine_part.astype(jnp.bfloat16), "seq", scatter_dimension=0, tiled=True
        ).astype(jnp.float32),
        lax.psum_scatter(
            projection_part.astype(jnp.bfloat16), "seq", scatter_dimension=0, tiled=True
        ).astype(jnp.float32),
        lax.psum_scatter(
            readout_part.astype(jnp.bfloat16), "seq", scatter_dimension=0, tiled=True
        ).astype(jnp.float32),
        lax.psum_scatter(
            expand_part.astype(jnp.bfloat16), "seq", scatter_dimension=0, tiled=True
        ).astype(jnp.float32),
        lax.psum_scatter(
            contract_part.astype(jnp.bfloat16), "seq", scatter_dimension=0, tiled=True
        ).astype(jnp.float32),
    )
    summed = (
        lax.psum(scattered[0].astype(jnp.bfloat16), "grp").astype(jnp.float32),
        lax.psum(modulation_part.astype(jnp.bfloat16), "grp").astype(jnp.float32),
        lax.psum(scattered[1].astype(jnp.bfloat16), "grp").astype(jnp.float32),
        lax.psum(scattered[2].astype(jnp.bfloat16), "grp").astype(jnp.float32),
        lax.psum(scattered[3].astype(jnp.bfloat16), "grp").astype(jnp.float32),
        lax.psum(scattered[4].astype(jnp.bfloat16), "grp").astype(jnp.float32),
    )
    return (
        output.astype(jnp.bfloat16).reshape(split_shape),
        frames_grad,
        shortcut_grad,
        time_grad,
        summed[0],
        summed[1],
        summed[2],
        summed[3],
        summed[4],
        summed[5],
    )


def solution(mesh):
    return jax.shard_map(
        shards,
        mesh=mesh,
        in_specs=(
            P("grp", "seq", None),
            P("grp", "seq", None),
            P("grp", None, None),
            P("grp", None),
            P("grp", "seq"),
            P("grp", "seq", None),
            P("seq", None),
            P("seq", None),
            P("seq", None),
            P("seq", None),
            P("seq", None),
            P("seq", None),
        ),
        out_specs=(
            P("grp", "seq", None),
            P("grp", "seq", None),
            P("grp", "seq", None),
            P("grp", None, None),
            P("seq", None),
            P("seq", None),
            P("seq", None),
            P("seq", None),
            P("seq", None),
            P("seq", None),
        ),
        check_vma=False,
    )
```

```python
import functools
import math

import jax
import jax.numpy as jnp
from jax import lax
from jax.experimental import pallas as pl
from jax.experimental.pallas import tpu as pltpu
from jax.sharding import PartitionSpec as P

HEADS = 16
HEAD_DIM = 64


precise = lax.Precision.HIGHEST
epsilon = 1e-06
rope_base = 10000.0


def product(first_op, second_op):
    return jnp.dot(first_op, second_op, preferred_element_type=jnp.float32)


def product_left(first_op, second_op):
    return lax.dot_general(
        first_op, second_op, (((0,), (0,)), ((), ())), preferred_element_type=jnp.float32
    )


def product_right(first_op, second_op):
    return lax.dot_general(
        first_op, second_op, (((1,), (1,)), ((), ())), preferred_element_type=jnp.float32
    )


def gelu_tanh(values):
    return jax.nn.gelu(values, approximate=True)


def modulate(hidden, shift_part, scale_part):
    center = hidden - jnp.mean(hidden, axis=-1, keepdims=True)
    variance = jnp.mean(center * center, axis=-1, keepdims=True)
    return center * lax.rsqrt(variance + epsilon) * (1.0 + scale_part) + shift_part


def segment_info(lengths, frame_index):
    utter_count = lengths.shape[0]
    utter_ends = jnp.cumsum(lengths)
    starts = utter_ends - lengths
    segment = jnp.sum((frame_index[:, None] >= utter_ends[None, :]).astype(jnp.int32), axis=1)
    member = segment[:, None] == jnp.arange(utter_count, dtype=jnp.int32)[None, :]
    offset = jnp.sum(jnp.where(member, starts[None, :], 0), axis=1)
    return (segment, member, frame_index - offset)


def rotary_tables(position):
    half_dim = HEAD_DIM // 2
    ladder = jnp.arange(half_dim, dtype=jnp.float32) / half_dim
    inverse = jnp.exp(-jnp.log(rope_base) * ladder)
    angles = position.astype(jnp.float32)[:, None] * inverse[None, :]
    return (jnp.cos(angles)[:, None, :], jnp.sin(angles)[:, None, :])


def rotate(vectors, cos_table, sin_table):
    half_dim = vectors.shape[-1] // 2
    front_half = vectors[..., :half_dim]
    back_half = vectors[..., half_dim:]
    return jnp.concatenate(
        [
            front_half * cos_table - back_half * sin_table,
            back_half * cos_table + front_half * sin_table,
        ],
        axis=-1,
    )


MESH = pl.DeviceIdType.MESH
NEG = -1e30


def utter_features(boundary, total_rows, for_keys):
    row = lax.broadcasted_iota(jnp.int32, (total_rows, 128), 0)
    lane = lax.broadcasted_iota(jnp.int32, (total_rows, 128), 1)
    second = (row >= boundary).astype(jnp.float32)
    ahead = (lane == 0).astype(jnp.float32)
    after = (lane == 1).astype(jnp.float32)
    if for_keys:
        return (NEG * (second * ahead + (1.0 - second) * after)).astype(jnp.bfloat16)
    return (second * after + (1.0 - second) * ahead).astype(jnp.bfloat16)


def head_lanes(values, head):
    lane = lax.broadcasted_iota(jnp.int32, values.shape, 1)
    own = (lane >= head * HEAD_DIM) & (lane < (head + 1) * HEAD_DIM)
    return jnp.where(own, values.astype(jnp.float32), 0.0).astype(jnp.bfloat16)


def dot_nn(first_op, second_op):
    return jnp.dot(first_op, second_op, preferred_element_type=jnp.float32)


def dot_nt(first_op, second_op):
    return lax.dot_general(
        first_op, second_op, (((1,), (1,)), ((), ())), preferred_element_type=jnp.float32
    )


def fold_rows(values, combine):
    return combine(values.reshape(values.shape[0] // 8, 8, values.shape[1]), axis=0)


def enter(partners):
    barrier = pltpu.get_barrier_semaphore()
    for partner in partners:
        pl.semaphore_signal(barrier, inc=1, device_id=partner, device_id_type=MESH)
    pl.semaphore_wait(barrier, len(partners))


def key_span(third, total_rows):
    size = total_rows // 3
    return (max(third - 1, 0) * size, min(third + 2, 3) * size)


def forward_kernel(
    seq_count, bound_ref, qkv_ref, kept_ref, mixture_ref, log_ref,
    key_scr, query_scr, value_t_scr, score_scr, mix_t_scr, mix_scr,
    send_sem, recv_sem, back_send_sem, back_recv_sem, local_sem,
):
    group_count, local_rows, local_width = qkv_ref.shape[1], qkv_ref.shape[3], qkv_ref.shape[4]
    total_rows = seq_count * local_rows
    heads = local_width // HEAD_DIM
    me = lax.axis_index("seq")
    grp = lax.axis_index("grp")
    others = [lax.rem(me + step, seq_count) for step in range(1, seq_count)]
    origins = [lax.rem(me + seq_count - step, seq_count) for step in range(1, seq_count)]
    block = min(256, total_rows // 3)
    enter([(grp, other) for other in others])
    copies = []
    for group in range(group_count):
        own = pltpu.make_async_copy(qkv_ref.at[me, group], kept_ref.at[me, group], local_sem.at[group])
        own.start()
        row = [own]
        for step, other in enumerate(others):
            copy = pltpu.make_async_remote_copy(
                qkv_ref.at[other, group], kept_ref.at[me, group],
                send_sem.at[group, step], recv_sem.at[group, step],
                device_id=(grp, other), device_id_type=MESH,
            )
            copy.start()
            row.append(copy)
        copies.append(row)
    back = []
    for group in range(group_count):
        for copy in copies[group]:
            copy.wait()
        boundary = bound_ref[group]
        keys = kept_ref[:, group, 1].reshape(total_rows, local_width)
        values = kept_ref[:, group, 2].reshape(total_rows, local_width)
        key_scr[:, :local_width] = keys
        key_scr[:, local_width:] = utter_features(boundary, total_rows, True)
        query_scr[:, local_width:] = utter_features(boundary, total_rows, False)
        value_t_scr[...] = values.astype(jnp.float32).T.astype(jnp.bfloat16)

        def one_head(head, carry):
            queries = kept_ref[:, group, 0].reshape(total_rows, local_width)
            query_scr[:, :local_width] = head_lanes(queries, head) * jnp.bfloat16(HEAD_DIM ** (-0.5))
            for third in range(3):
                first_key, last_key = key_span(third, total_rows)
                chunks = range(first_key, last_key, block)

                def one_block(index, carry):
                    first_row = pl.multiple_of(third * (total_rows // 3) + index * block, block)
                    query_block = query_scr[pl.ds(first_row, block), :]
                    peak = jnp.full((8, block), -jnp.inf, jnp.float32)
                    for first in chunks:
                        scores = dot_nt(key_scr[first:first + block, :], query_block)
                        score_scr[first:first + block, :] = scores
                        peak = jnp.maximum(peak, fold_rows(scores, jnp.max))
                    peak = jnp.max(peak, axis=0, keepdims=True)
                    total = jnp.zeros((8, block), jnp.float32)
                    for first in chunks:
                        lifted = jnp.exp(score_scr[first:first + block, :] - peak)
                        score_scr[first:first + block, :] = lifted
                        total = total + fold_rows(lifted, jnp.sum)
                    total = jnp.sum(total, axis=0, keepdims=True)
                    inverse = 1.0 / total
                    mixed = jnp.zeros((HEAD_DIM, block), jnp.float32)
                    rows = pl.ds(pl.multiple_of(head * HEAD_DIM, HEAD_DIM), HEAD_DIM)
                    for first in chunks:
                        weight = (score_scr[first:first + block, :] * inverse).astype(jnp.bfloat16)
                        mixed = mixed + dot_nn(value_t_scr[rows, first:first + block], weight)
                    mix_t_scr[rows, pl.ds(first_row, block)] = mixed
                    log_ref[group, head, :, pl.ds(first_row, block)] = peak + jnp.log(total)
                    return carry

                lax.fori_loop(0, total_rows // 3 // block, one_block, 0)
            return carry

        lax.fori_loop(0, heads, one_head, 0)
        mix_scr[group] = mix_t_scr[...].T.astype(jnp.bfloat16).reshape(seq_count, local_rows, local_width)
        own = pltpu.make_async_copy(
            mix_scr.at[group, me], mixture_ref.at[me, group], local_sem.at[group_count + group]
        )
        own.start()
        back.append(own)
        for step, other in enumerate(others):
            copy = pltpu.make_async_remote_copy(
                mix_scr.at[group, other], mixture_ref.at[me, group],
                back_send_sem.at[group, step], back_recv_sem.at[group, step],
                device_id=(grp, other), device_id_type=MESH,
            )
            copy.start()
            back.append(copy)
    for copy in back:
        copy.wait()


def attend_forward(bounds, qkv):
    seq_count, group_count, _, local_rows, local_width = qkv.shape
    total_rows = seq_count * local_rows
    heads = local_width // HEAD_DIM
    block = min(256, total_rows // 3)
    vmem = pl.BlockSpec(memory_space=pltpu.VMEM)
    return pl.pallas_call(
        functools.partial(forward_kernel, seq_count),
        out_shape=(
            jax.ShapeDtypeStruct(qkv.shape, jnp.bfloat16),
            jax.ShapeDtypeStruct((seq_count, group_count, local_rows, local_width), jnp.bfloat16),
            jax.ShapeDtypeStruct((group_count, heads, 1, total_rows), jnp.float32),
        ),
        in_specs=[pl.BlockSpec(memory_space=pltpu.SMEM), pl.BlockSpec(memory_space=pl.ANY)],
        out_specs=(vmem, vmem, vmem),
        scratch_shapes=[
            pltpu.VMEM((total_rows, local_width + 128), jnp.bfloat16),
            pltpu.VMEM((total_rows, local_width + 128), jnp.bfloat16),
            pltpu.VMEM((local_width, total_rows), jnp.bfloat16),
            pltpu.VMEM((total_rows, block), jnp.float32),
            pltpu.VMEM((local_width, total_rows), jnp.float32),
            pltpu.VMEM((group_count, seq_count, local_rows, local_width), jnp.bfloat16),
            pltpu.SemaphoreType.DMA((group_count, seq_count - 1)),
            pltpu.SemaphoreType.DMA((group_count, seq_count - 1)),
            pltpu.SemaphoreType.DMA((group_count, seq_count - 1)),
            pltpu.SemaphoreType.DMA((group_count, seq_count - 1)),
            pltpu.SemaphoreType.DMA((2 * group_count,)),
        ],
        compiler_params=pltpu.CompilerParams(
            collective_id=1, has_side_effects=True, vmem_limit_bytes=48 * 1024 * 1024
        ),
        name="attend_forward",
    )(bounds, qkv)


def backward_kernel(
    seq_count, bound_ref, kept_ref, grad_ref, log_ref, out_ref,
    taken_scr, key_scr, query_scr, key_t_scr, head_query_scr, head_grad_scr, prob_scr, weight_scr,
    query_t_scr, key_sum_scr, value_sum_scr, back_scr,
    send_sem, recv_sem, back_send_sem, back_recv_sem, local_sem,
):
    group_count, local_rows, local_width = grad_ref.shape[1], grad_ref.shape[2], grad_ref.shape[3]
    total_rows = seq_count * local_rows
    heads = local_width // HEAD_DIM
    me = lax.axis_index("seq")
    grp = lax.axis_index("grp")
    others = [lax.rem(me + step, seq_count) for step in range(1, seq_count)]
    block = min(256, total_rows // 3)
    enter([(grp, other) for other in others])
    copies = []
    for group in range(group_count):
        own = pltpu.make_async_copy(grad_ref.at[me, group], taken_scr.at[me, group], local_sem.at[group])
        own.start()
        row = [own]
        for step, other in enumerate(others):
            copy = pltpu.make_async_remote_copy(
                grad_ref.at[other, group], taken_scr.at[me, group],
                send_sem.at[group, step], recv_sem.at[group, step],
                device_id=(grp, other), device_id_type=MESH,
            )
            copy.start()
            row.append(copy)
        copies.append(row)
    back = []
    for group in range(group_count):
        for copy in copies[group]:
            copy.wait()
        boundary = bound_ref[group]
        keys = kept_ref[:, group, 1].reshape(total_rows, local_width)
        key_scr[:, :local_width] = keys
        key_scr[:, local_width:] = utter_features(boundary, total_rows, True)
        query_scr[:, local_width:] = utter_features(boundary, total_rows, False)
        key_t_scr[...] = keys.astype(jnp.float32).T.astype(jnp.bfloat16)
        key_sum_scr[...] = jnp.zeros_like(key_sum_scr)
        value_sum_scr[...] = jnp.zeros_like(value_sum_scr)

        def one_head(head, carry):
            queries = head_lanes(kept_ref[:, group, 0].reshape(total_rows, local_width), head)
            head_query_scr[...] = queries
            query_scr[:, :local_width] = queries * jnp.bfloat16(HEAD_DIM ** (-0.5))
            head_grad_scr[...] = head_lanes(taken_scr[:, group].reshape(total_rows, local_width), head)
            for third in range(3):
                first_key, last_key = key_span(third, total_rows)
                chunks = range(first_key, last_key, block)

                def one_block(index, carry):
                    first_row = pl.multiple_of(third * (total_rows // 3) + index * block, block)
                    own_rows = pl.ds(first_row, block)
                    query_block = query_scr[own_rows, :]
                    grad_block = head_grad_scr[own_rows, :]
                    plain_block = head_query_scr[own_rows, :]
                    log_block = log_ref[group, head, :, own_rows]
                    row_dot = jnp.zeros((8, block), jnp.float32)
                    for first in chunks:
                        scores = dot_nt(key_scr[first:first + block, :], query_block)
                        prob = jnp.exp(scores - log_block)
                        values = kept_ref[
                            first // local_rows:(first + block - 1) // local_rows + 1, group, 2
                        ].reshape(-1, local_width)
                        skip = first % local_rows
                        weight_grad = dot_nt(values[skip:skip + block], grad_block)
                        prob_scr[first:first + block, :] = prob
                        weight_scr[first:first + block, :] = weight_grad
                        row_dot = row_dot + fold_rows(prob * weight_grad, jnp.sum)
                    row_dot = jnp.sum(row_dot, axis=0, keepdims=True)
                    rows = pl.ds(pl.multiple_of(head * HEAD_DIM, HEAD_DIM), HEAD_DIM)
                    turned = jnp.zeros((HEAD_DIM, block), jnp.float32)
                    for first in chunks:
                        prob = prob_scr[first:first + block, :]
                        score_grad = (
                            HEAD_DIM ** (-0.5) * (prob * (weight_scr[first:first + block, :] - row_dot))
                        ).astype(jnp.bfloat16)
                        key_sum_scr[first:first + block, :] += dot_nn(score_grad, plain_block)
                        value_sum_scr[first:first + block, :] += dot_nn(
                            prob.astype(jnp.bfloat16), grad_block
                        )
                        turned = turned + dot_nn(key_t_scr[rows, first:first + block], score_grad)
                    query_t_scr[rows, own_rows] = turned
                    return carry

                lax.fori_loop(0, total_rows // 3 // block, one_block, 0)
            return carry

        lax.fori_loop(0, heads, one_head, 0)
        shape = (seq_count, local_rows, local_width)
        back_scr[:, group, 0] = query_t_scr[...].T.astype(jnp.bfloat16).reshape(shape)
        back_scr[:, group, 1] = key_sum_scr[...].astype(jnp.bfloat16).reshape(shape)
        back_scr[:, group, 2] = value_sum_scr[...].astype(jnp.bfloat16).reshape(shape)
        own = pltpu.make_async_copy(
            back_scr.at[me, group], out_ref.at[me, group], local_sem.at[group_count + group]
        )
        own.start()
        back.append(own)
        for step, other in enumerate(others):
            copy = pltpu.make_async_remote_copy(
                back_scr.at[other, group], out_ref.at[me, group],
                back_send_sem.at[group, step], back_recv_sem.at[group, step],
                device_id=(grp, other), device_id_type=MESH,
            )
            copy.start()
            back.append(copy)
    for copy in back:
        copy.wait()


def attend_backward(bounds, kept, grad, log_total):
    seq_count, group_count, _, local_rows, local_width = kept.shape
    total_rows = seq_count * local_rows
    block = min(256, total_rows // 3)
    vmem = pl.BlockSpec(memory_space=pltpu.VMEM)
    return pl.pallas_call(
        functools.partial(backward_kernel, seq_count),
        out_shape=jax.ShapeDtypeStruct(kept.shape, jnp.bfloat16),
        in_specs=[
            pl.BlockSpec(memory_space=pltpu.SMEM), vmem, pl.BlockSpec(memory_space=pl.ANY), vmem
        ],
        out_specs=vmem,
        scratch_shapes=[
            pltpu.VMEM(grad.shape, jnp.bfloat16),
            pltpu.VMEM((total_rows, local_width + 128), jnp.bfloat16),
            pltpu.VMEM((total_rows, local_width + 128), jnp.bfloat16),
            pltpu.VMEM((local_width, total_rows), jnp.bfloat16),
            pltpu.VMEM((total_rows, local_width), jnp.bfloat16),
            pltpu.VMEM((total_rows, local_width), jnp.bfloat16),
            pltpu.VMEM((total_rows, block), jnp.float32),
            pltpu.VMEM((total_rows, block), jnp.float32),
            pltpu.VMEM((local_width, total_rows), jnp.float32),
            pltpu.VMEM((total_rows, local_width), jnp.float32),
            pltpu.VMEM((total_rows, local_width), jnp.float32),
            pltpu.VMEM(kept.shape, jnp.bfloat16),
            pltpu.SemaphoreType.DMA((group_count, seq_count - 1)),
            pltpu.SemaphoreType.DMA((group_count, seq_count - 1)),
            pltpu.SemaphoreType.DMA((group_count, seq_count - 1)),
            pltpu.SemaphoreType.DMA((group_count, seq_count - 1)),
            pltpu.SemaphoreType.DMA((2 * group_count,)),
        ],
        compiler_params=pltpu.CompilerParams(
            collective_id=2, has_side_effects=True, vmem_limit_bytes=48 * 1024 * 1024
        ),
        name="attend_backward",
    )(bounds, kept, grad, log_total)


def gather_kernel(plane, seq_count, count, *refs):
    shards, fulls = refs[:count], refs[count:2 * count]
    own_sem, z_send, z_recv, first_send, first_recv, second_send, second_recv, core_send, core_recv = refs[2 * count:]
    rows_y, cols_x = plane
    grp = lax.axis_index("grp")
    me = lax.axis_index("seq")
    gy, gx = grp // cols_x, lax.rem(grp, cols_x)
    layers = seq_count // 2
    layer, core = me // 2, lax.rem(me, 2)
    beside = [gy * cols_x + lax.rem(gx + step, cols_x) for step in range(1, cols_x)]
    beside_from = [lax.rem(gx + cols_x - step, cols_x) for step in range(1, cols_x)]
    along = [lax.rem(gy + step, rows_y) * cols_x + gx for step in range(1, rows_y)]
    along_from = [lax.rem(gy + rows_y - step, rows_y) for step in range(1, rows_y)]
    lines = [lax.rem(layer + step, layers) * 2 + core for step in range(1, layers)]
    line_from = [lax.rem(layer + layers - step, layers) * 2 + core for step in range(1, layers)]
    partner = layer * 2 + 1 - core
    enter(
        [(grp, line) for line in lines]
        + [(other, me) for other in beside + along]
        + [(grp, partner)]
    )
    started = []

    def push(src, dst, sends, recvs, slot, device):
        copy = pltpu.make_async_remote_copy(
            src, dst, sends.at[slot], recvs.at[slot], device_id=device, device_id_type=MESH
        )
        copy.start()
        started.append(copy)
        return copy

    def piece(index, owner, y_from, y_many, x_from, x_many):
        height = fulls[index].shape[1] // rows_y
        width = fulls[index].shape[2] // (2 * cols_x)
        return fulls[index].at[
            owner,
            pl.ds(pl.multiple_of(y_from * height, height), y_many * height),
            pl.ds(pl.multiple_of(x_from * width, width), x_many * width),
        ]

    own = []
    line_copies = []
    for index in range(count):
        height = shards[index].shape[0] // rows_y
        width = shards[index].shape[1] // cols_x
        source = shards[index].at[
            pl.ds(pl.multiple_of(gy * height, height), height),
            pl.ds(pl.multiple_of(gx * width, width), width),
        ]
        line_copies.append([
            push(source, piece(index, me, gy, 1, 2 * gx, 2), z_send, z_recv, (index, step), (grp, line))
            for step, line in enumerate(lines)
        ])
    for index in range(count):
        copy = pltpu.make_async_copy(shards[index], fulls[index].at[me], own_sem.at[index])
        copy.start()
        own.append(copy)
        push(shards[index], fulls[index].at[me], core_send, core_recv, (index, 0), (grp, partner))
    spread = {}

    def first(index, step):
        line_copies[index][step].wait_recv()
        owner = line_from[step]
        spread[index, step] = [
            push(part, part, first_send, first_recv, (index, step, 0, hop), (other, me))
            for hop, other in enumerate(beside)
            for part in [piece(index, owner, gy, 1, 2 * gx, 1)]
        ] + [
            push(part, part, first_send, first_recv, (index, step, 1, hop), (other, me))
            for hop, other in enumerate(along)
            for part in [piece(index, owner, gy, 1, 2 * gx + 1, 1)]
        ]

    def second(index, step):
        for copy in spread[index, step]:
            copy.wait_recv()
        owner = line_from[step]
        copies = []
        for hop, other in enumerate(along):
            for place, column in enumerate([gx] + beside_from):
                part = piece(index, owner, gy, 1, 2 * column, 1)
                copies.append(push(part, part, second_send, second_recv, (index, step, 0, hop, place), (other, me)))
        for hop, other in enumerate(beside):
            part = piece(index, owner, 0, rows_y, 2 * gx + 1, 1)
            copies.append(push(part, part, second_send, second_recv, (index, step, 1, hop, 0), (other, me)))
        spread[index, step] = copies

    def third(index, step):
        for copy in spread[index, step]:
            copy.wait_recv()
        part = fulls[index].at[line_from[step]]
        spread[index, step] = [push(part, part, core_send, core_recv, (index, step + 1), (grp, partner))]

    jobs = [(index, step) for index in range(count) for step in range(layers - 1)]
    lag = layers - 1
    for turn in range(len(jobs) + 2 * lag):
        if turn < len(jobs):
            first(*jobs[turn])
        if 0 <= turn - lag < len(jobs):
            second(*jobs[turn - lag])
        if 0 <= turn - 2 * lag < len(jobs):
            third(*jobs[turn - 2 * lag])
    for copy in started:
        copy.wait_send()
    for copies in spread.values():
        for copy in copies:
            copy.wait_recv()
    for index in range(count):
        pltpu.make_async_remote_copy(
            shards[index], fulls[index].at[me], core_send.at[index, 0], core_recv.at[index, 0],
            device_id=(grp, partner), device_id_type=MESH,
        ).wait_recv()
        own[index].wait()


def gather(collective, *shards):
    seq_count = lax.axis_size("seq")
    side = math.isqrt(lax.axis_size("grp"))
    plane = (side, side)
    layers = seq_count // 2
    count = len(shards)
    anywhere = pl.BlockSpec(memory_space=pl.ANY)
    dma = pltpu.SemaphoreType.DMA
    hops = max(side - 1, 1)
    outs = pl.pallas_call(
        functools.partial(gather_kernel, plane, seq_count, count),
        out_shape=tuple(jax.ShapeDtypeStruct((seq_count,) + part.shape, part.dtype) for part in shards),
        in_specs=[anywhere] * count,
        out_specs=(anywhere,) * count,
        scratch_shapes=[
            dma((count,)),
            dma((count, layers - 1)), dma((count, layers - 1)),
            dma((count, layers - 1, 2, hops)), dma((count, layers - 1, 2, hops)),
            dma((count, layers - 1, 2, hops, side)), dma((count, layers - 1, 2, hops, side)),
            dma((count, layers)), dma((count, layers)),
        ],
        compiler_params=pltpu.CompilerParams(collective_id=collective, has_side_effects=True),
        name="gather_weights_%d" % collective,
    )(*shards)
    return tuple(full.reshape(seq_count * part.shape[0], part.shape[1]) for full, part in zip(outs, shards))


def shards(
    frames,
    shortcut,
    time_embed,
    lengths,
    kept_mask,
    target,
    combine,
    modulation,
    projection,
    readout,
    expand,
    contract,
):
    gathered = gather(3, combine, projection, readout, expand, contract)
    combine_full, projection_full, readout_full, expand_full, contract_full = (
        gathered
    )
    group_count = frames.shape[0]
    local_rows = frames.shape[1]
    width = HEADS * HEAD_DIM
    row_count = group_count * local_rows
    seq_count = lax.axis_size("seq")
    group_frames = local_rows * seq_count
    all_frames = group_frames * lax.axis_size("grp") * group_count
    utter_count = time_embed.shape[1]
    kept_float = kept_mask.astype(jnp.float32).reshape(row_count)
    kept_total = lax.psum(jnp.sum(kept_float), ("grp", "seq"))
    local_index = lax.axis_index("seq") * local_rows + jnp.arange(local_rows, dtype=jnp.int32)

    def local_info(length_row):
        return segment_info(length_row, local_index)

    member_info = jax.vmap(local_info)(lengths)
    member_float = member_info[1].astype(jnp.float32)
    position = member_info[2]
    cos_table, sin_table = rotary_tables(position.reshape(row_count))
    joined = jnp.concatenate([frames, shortcut], axis=2).reshape(row_count, 2 * width)
    hidden = product(joined, combine_full)
    silu_value, silu_pull = jax.vjp(jax.nn.silu, time_embed)
    condition = silu_value.astype(jnp.bfloat16)
    shard_rows = modulation.shape[0]
    condition_part = lax.dynamic_slice_in_dim(
        condition, lax.axis_index("seq") * shard_rows, shard_rows, 2
    ).reshape(group_count * utter_count, shard_rows)
    modulation_utter = lax.psum(product(condition_part, modulation), "seq").reshape(
        group_count, utter_count, 6 * width
    )
    modulation_frame = jnp.einsum(
        "gtu,gue->gte",
        member_float,
        modulation_utter,
        precision=precise,
        preferred_element_type=jnp.float32,
    ).reshape(row_count, 6 * width)
    shift_first, scale_first, gate_first, shift_second, scale_second, gate_second = jnp.split(
        modulation_frame, 6, axis=1
    )
    normed_value, first_pull = jax.vjp(modulate, hidden, shift_first, scale_first)
    normed = normed_value.astype(jnp.bfloat16)
    packed = product(normed, projection_full)
    query_raw, key_raw, value_raw = jnp.split(packed, 3, axis=1)
    head_shape = (row_count, HEADS, HEAD_DIM)
    split_shape = (group_count, local_rows, width)

    def rotate_local(vectors):
        return rotate(vectors, cos_table, sin_table)

    query_turned, query_pull = jax.vjp(rotate_local, query_raw.reshape(head_shape))
    key_turned, key_pull = jax.vjp(rotate_local, key_raw.reshape(head_shape))
    local_width = width // seq_count

    def by_target(vectors):
        return vectors.reshape(group_count, local_rows, seq_count, local_width).astype(jnp.bfloat16)

    qkv = jnp.transpose(
        jnp.stack([by_target(query_turned), by_target(key_turned), by_target(value_raw)]),
        (3, 1, 0, 2, 4),
    )
    bounds = lengths[:, 0]
    kept_heads, mixture_blocks, log_total = attend_forward(bounds, qkv)
    mixture = jnp.transpose(mixture_blocks, (1, 2, 0, 3)).reshape(row_count, width)
    branch = product(mixture, readout_full)
    middle = hidden + gate_first * branch
    second_value, second_pull = jax.vjp(modulate, middle, shift_second, scale_second)
    normed_second = second_value.astype(jnp.bfloat16)
    expanded = product(normed_second, expand_full)
    active_value, gelu_pull = jax.vjp(gelu_tanh, expanded)
    active = active_value.astype(jnp.bfloat16)
    contracted = product(active, contract_full)
    output = middle + gate_second * contracted
    loss_scale = all_frames / kept_total
    output_grad = (
        loss_scale
        * kept_float[:, None]
        * (output - target.reshape(row_count, width).astype(jnp.float32))
    )
    combine_back, projection_back, readout_back, expand_back, contract_back = (
        gathered
    )
    gate_second_grad = output_grad * contracted
    contracted_grad = (gate_second * output_grad).astype(jnp.bfloat16)
    contract_part = product_left(active, contracted_grad)
    active_grad = product_right(contracted_grad, contract_back)
    expanded_grad = gelu_pull(active_grad)[0].astype(jnp.bfloat16)
    expand_part = product_left(normed_second, expanded_grad)
    normed_second_grad = product_right(expanded_grad, expand_back)
    middle_extra, shift_second_grad, scale_second_grad = second_pull(normed_second_grad)
    middle_grad = output_grad + middle_extra
    gate_first_grad = middle_grad * branch
    branch_grad = (gate_first * middle_grad).astype(jnp.bfloat16)
    readout_part = product_left(mixture, branch_grad)
    mixture_grad = product_right(branch_grad, readout_back).astype(jnp.bfloat16)
    back_blocks = attend_backward(
        bounds,
        kept_heads,
        jnp.transpose(
            mixture_grad.reshape(group_count, local_rows, seq_count, local_width), (2, 0, 1, 3)
        ),
        log_total,
    )
    query_back, key_back, value_back = jnp.transpose(back_blocks, (2, 1, 3, 0, 4)).reshape(
        3, group_count, local_rows, width
    )
    query_unturned = query_pull(query_back.reshape(head_shape).astype(jnp.float32))[0].reshape(
        row_count, width
    )
    key_unturned = key_pull(key_back.reshape(head_shape).astype(jnp.float32))[0].reshape(
        row_count, width
    )
    packed_grad = jnp.concatenate(
        [
            query_unturned.astype(jnp.bfloat16),
            key_unturned.astype(jnp.bfloat16),
            value_back.reshape(row_count, width),
        ],
        axis=1,
    )
    projection_part = product_left(normed, packed_grad)
    normed_grad = product_right(packed_grad, projection_back)
    hidden_extra, shift_first_grad, scale_first_grad = first_pull(normed_grad)
    hidden_grad = (middle_grad + hidden_extra).astype(jnp.bfloat16)
    combine_part = product_left(joined, hidden_grad)
    joined_grad = product_right(hidden_grad, combine_back)
    frames_grad = joined_grad[:, :width].reshape(split_shape)
    shortcut_grad = joined_grad[:, width:].reshape(split_shape)
    modulation_frame_grad = jnp.concatenate(
        [
            shift_first_grad,
            scale_first_grad,
            gate_first_grad,
            shift_second_grad,
            scale_second_grad,
            gate_second_grad,
        ],
        axis=1,
    )
    utter_part = jnp.einsum(
        "gtu,gte->gue",
        member_float,
        modulation_frame_grad.reshape(group_count, local_rows, 6 * width),
        precision=precise,
        preferred_element_type=jnp.float32,
    )
    utter_grad = lax.psum(utter_part.astype(jnp.bfloat16), "seq")
    utter_rows = utter_grad.reshape(group_count * utter_count, 6 * width)
    condition_grad = lax.all_gather(
        product_right(utter_rows, modulation), "seq", axis=1, tiled=True
    ).reshape(group_count, utter_count, width)
    time_grad = silu_pull(condition_grad)[0]
    modulation_part = product_left(condition_part, utter_rows)
    scattered = (
        lax.psum_scatter(
            combine_part.astype(jnp.bfloat16), "seq", scatter_dimension=0, tiled=True
        ).astype(jnp.float32),
        lax.psum_scatter(
            projection_part.astype(jnp.bfloat16), "seq", scatter_dimension=0, tiled=True
        ).astype(jnp.float32),
        lax.psum_scatter(
            readout_part.astype(jnp.bfloat16), "seq", scatter_dimension=0, tiled=True
        ).astype(jnp.float32),
        lax.psum_scatter(
            expand_part.astype(jnp.bfloat16), "seq", scatter_dimension=0, tiled=True
        ).astype(jnp.float32),
        lax.psum_scatter(
            contract_part.astype(jnp.bfloat16), "seq", scatter_dimension=0, tiled=True
        ).astype(jnp.float32),
    )
    summed = (
        lax.psum(scattered[0].astype(jnp.bfloat16), "grp").astype(jnp.float32),
        lax.psum(modulation_part.astype(jnp.bfloat16), "grp").astype(jnp.float32),
        lax.psum(scattered[1].astype(jnp.bfloat16), "grp").astype(jnp.float32),
        lax.psum(scattered[2].astype(jnp.bfloat16), "grp").astype(jnp.float32),
        lax.psum(scattered[3].astype(jnp.bfloat16), "grp").astype(jnp.float32),
        lax.psum(scattered[4].astype(jnp.bfloat16), "grp").astype(jnp.float32),
    )
    return (
        output.astype(jnp.bfloat16).reshape(split_shape),
        frames_grad,
        shortcut_grad,
        time_grad,
        summed[0],
        summed[1],
        summed[2],
        summed[3],
        summed[4],
        summed[5],
    )


def solution(mesh):
    return jax.shard_map(
        shards,
        mesh=mesh,
        in_specs=(
            P("grp", "seq", None),
            P("grp", "seq", None),
            P("grp", None, None),
            P("grp", None),
            P("grp", "seq"),
            P("grp", "seq", None),
            P("seq", None),
            P("seq", None),
            P("seq", None),
            P("seq", None),
            P("seq", None),
            P("seq", None),
        ),
        out_specs=(
            P("grp", "seq", None),
            P("grp", "seq", None),
            P("grp", "seq", None),
            P("grp", None, None),
            P("seq", None),
            P("seq", None),
            P("seq", None),
            P("seq", None),
            P("seq", None),
            P("seq", None),
        ),
        check_vma=False,
    )
```

```python
import functools
import math

import jax
import jax.numpy as jnp
from jax import lax
from jax.experimental import pallas as pl
from jax.experimental.pallas import tpu as pltpu
from jax.sharding import PartitionSpec as P

HEADS = 16
HEAD_DIM = 64


precise = lax.Precision.HIGHEST
epsilon = 1e-06
rope_base = 10000.0


def product(first_op, second_op):
    return jnp.dot(first_op, second_op, preferred_element_type=jnp.float32)


def product_left(first_op, second_op):
    return lax.dot_general(
        first_op, second_op, (((0,), (0,)), ((), ())), preferred_element_type=jnp.float32
    )


def product_right(first_op, second_op):
    return lax.dot_general(
        first_op, second_op, (((1,), (1,)), ((), ())), preferred_element_type=jnp.float32
    )


def gelu_tanh(values):
    return jax.nn.gelu(values, approximate=True)


def modulate(hidden, shift_part, scale_part):
    center = hidden - jnp.mean(hidden, axis=-1, keepdims=True)
    variance = jnp.mean(center * center, axis=-1, keepdims=True)
    return center * lax.rsqrt(variance + epsilon) * (1.0 + scale_part) + shift_part


def segment_info(lengths, frame_index):
    utter_count = lengths.shape[0]
    utter_ends = jnp.cumsum(lengths)
    starts = utter_ends - lengths
    segment = jnp.sum((frame_index[:, None] >= utter_ends[None, :]).astype(jnp.int32), axis=1)
    member = segment[:, None] == jnp.arange(utter_count, dtype=jnp.int32)[None, :]
    offset = jnp.sum(jnp.where(member, starts[None, :], 0), axis=1)
    return (segment, member, frame_index - offset)


def rotary_tables(position):
    half_dim = HEAD_DIM // 2
    ladder = jnp.arange(half_dim, dtype=jnp.float32) / half_dim
    inverse = jnp.exp(-jnp.log(rope_base) * ladder)
    angles = position.astype(jnp.float32)[:, None] * inverse[None, :]
    return (jnp.cos(angles)[:, None, :], jnp.sin(angles)[:, None, :])


def rotate(vectors, cos_table, sin_table):
    half_dim = vectors.shape[-1] // 2
    front_half = vectors[..., :half_dim]
    back_half = vectors[..., half_dim:]
    return jnp.concatenate(
        [
            front_half * cos_table - back_half * sin_table,
            back_half * cos_table + front_half * sin_table,
        ],
        axis=-1,
    )


MESH = pl.DeviceIdType.MESH
NEG = -1e30


def utter_features(boundary, total_rows, for_keys):
    row = lax.broadcasted_iota(jnp.int32, (total_rows, 128), 0)
    lane = lax.broadcasted_iota(jnp.int32, (total_rows, 128), 1)
    second = (row >= boundary).astype(jnp.float32)
    ahead = (lane == 0).astype(jnp.float32)
    after = (lane == 1).astype(jnp.float32)
    if for_keys:
        return (NEG * (second * ahead + (1.0 - second) * after)).astype(jnp.bfloat16)
    return (second * after + (1.0 - second) * ahead).astype(jnp.bfloat16)


def head_lanes(values, head):
    lane = lax.broadcasted_iota(jnp.int32, values.shape, 1)
    own = (lane >= head * HEAD_DIM) & (lane < (head + 1) * HEAD_DIM)
    return jnp.where(own, values.astype(jnp.float32), 0.0).astype(jnp.bfloat16)


def dot_nn(first_op, second_op):
    return jnp.dot(first_op, second_op, preferred_element_type=jnp.float32)


def dot_nt(first_op, second_op):
    return lax.dot_general(
        first_op, second_op, (((1,), (1,)), ((), ())), preferred_element_type=jnp.float32
    )


def fold_rows(values, combine):
    return combine(values.reshape(values.shape[0] // 8, 8, values.shape[1]), axis=0)


def enter(partners):
    barrier = pltpu.get_barrier_semaphore()
    for partner in partners:
        pl.semaphore_signal(barrier, inc=1, device_id=partner, device_id_type=MESH)
    pl.semaphore_wait(barrier, len(partners))


def key_span(third, total_rows):
    size = total_rows // 3
    return (max(third - 1, 0) * size, min(third + 2, 3) * size)


def forward_kernel(
    seq_count, bound_ref, qkv_ref, kept_ref, mixture_ref, log_ref,
    key_scr, query_scr, value_t_scr, score_scr, mix_t_scr, mix_scr,
    send_sem, recv_sem, back_send_sem, back_recv_sem, local_sem,
):
    group_count, local_rows, local_width = qkv_ref.shape[1], qkv_ref.shape[3], qkv_ref.shape[4]
    total_rows = seq_count * local_rows
    heads = local_width // HEAD_DIM
    me = lax.axis_index("seq")
    grp = lax.axis_index("grp")
    others = [lax.rem(me + step, seq_count) for step in range(1, seq_count)]
    origins = [lax.rem(me + seq_count - step, seq_count) for step in range(1, seq_count)]
    block = min(256, total_rows // 3)
    enter([(grp, other) for other in others])
    copies = []
    for group in range(group_count):
        own = pltpu.make_async_copy(qkv_ref.at[me, group], kept_ref.at[me, group], local_sem.at[group])
        own.start()
        row = [own]
        for step, other in enumerate(others):
            copy = pltpu.make_async_remote_copy(
                qkv_ref.at[other, group], kept_ref.at[me, group],
                send_sem.at[group, step], recv_sem.at[group, step],
                device_id=(grp, other), device_id_type=MESH,
            )
            copy.start()
            row.append(copy)
        copies.append(row)
    back = []
    for group in range(group_count):
        for copy in copies[group]:
            copy.wait()
        boundary = bound_ref[group]
        keys = kept_ref[:, group, 1].reshape(total_rows, local_width)
        values = kept_ref[:, group, 2].reshape(total_rows, local_width)
        key_scr[:, :local_width] = keys
        key_scr[:, local_width:] = utter_features(boundary, total_rows, True)
        query_scr[:, local_width:] = utter_features(boundary, total_rows, False)
        value_t_scr[...] = values.astype(jnp.float32).T.astype(jnp.bfloat16)

        def one_head(head, carry):
            queries = kept_ref[:, group, 0].reshape(total_rows, local_width)
            query_scr[:, :local_width] = head_lanes(queries, head) * jnp.bfloat16(HEAD_DIM ** (-0.5))
            for third in range(3):
                first_key, last_key = key_span(third, total_rows)
                chunks = range(first_key, last_key, block)

                def one_block(index, carry):
                    first_row = pl.multiple_of(third * (total_rows // 3) + index * block, block)
                    query_block = query_scr[pl.ds(first_row, block), :]
                    peak = jnp.full((8, block), -jnp.inf, jnp.float32)
                    for first in chunks:
                        scores = dot_nt(key_scr[first:first + block, :], query_block)
                        score_scr[first:first + block, :] = scores
                        peak = jnp.maximum(peak, fold_rows(scores, jnp.max))
                    peak = jnp.max(peak, axis=0, keepdims=True)
                    total = jnp.zeros((8, block), jnp.float32)
                    for first in chunks:
                        lifted = jnp.exp(score_scr[first:first + block, :] - peak)
                        score_scr[first:first + block, :] = lifted
                        total = total + fold_rows(lifted, jnp.sum)
                    total = jnp.sum(total, axis=0, keepdims=True)
                    inverse = 1.0 / total
                    mixed = jnp.zeros((HEAD_DIM, block), jnp.float32)
                    rows = pl.ds(pl.multiple_of(head * HEAD_DIM, HEAD_DIM), HEAD_DIM)
                    for first in chunks:
                        weight = (score_scr[first:first + block, :] * inverse).astype(jnp.bfloat16)
                        mixed = mixed + dot_nn(value_t_scr[rows, first:first + block], weight)
                    mix_t_scr[rows, pl.ds(first_row, block)] = mixed
                    log_ref[group, head, :, pl.ds(first_row, block)] = peak + jnp.log(total)
                    return carry

                lax.fori_loop(0, total_rows // 3 // block, one_block, 0)
            return carry

        lax.fori_loop(0, heads, one_head, 0)
        mix_scr[group] = mix_t_scr[...].T.astype(jnp.bfloat16).reshape(seq_count, local_rows, local_width)
        own = pltpu.make_async_copy(
            mix_scr.at[group, me], mixture_ref.at[me, group], local_sem.at[group_count + group]
        )
        own.start()
        back.append(own)
        for step, other in enumerate(others):
            copy = pltpu.make_async_remote_copy(
                mix_scr.at[group, other], mixture_ref.at[me, group],
                back_send_sem.at[group, step], back_recv_sem.at[group, step],
                device_id=(grp, other), device_id_type=MESH,
            )
            copy.start()
            back.append(copy)
    for copy in back:
        copy.wait()


def attend_forward(bounds, qkv):
    seq_count, group_count, _, local_rows, local_width = qkv.shape
    total_rows = seq_count * local_rows
    heads = local_width // HEAD_DIM
    block = min(256, total_rows // 3)
    vmem = pl.BlockSpec(memory_space=pltpu.VMEM)
    return pl.pallas_call(
        functools.partial(forward_kernel, seq_count),
        out_shape=(
            jax.ShapeDtypeStruct(qkv.shape, jnp.bfloat16),
            jax.ShapeDtypeStruct((seq_count, group_count, local_rows, local_width), jnp.bfloat16),
            jax.ShapeDtypeStruct((group_count, heads, 1, total_rows), jnp.float32),
        ),
        in_specs=[pl.BlockSpec(memory_space=pltpu.SMEM), pl.BlockSpec(memory_space=pl.ANY)],
        out_specs=(vmem, vmem, vmem),
        scratch_shapes=[
            pltpu.VMEM((total_rows, local_width + 128), jnp.bfloat16),
            pltpu.VMEM((total_rows, local_width + 128), jnp.bfloat16),
            pltpu.VMEM((local_width, total_rows), jnp.bfloat16),
            pltpu.VMEM((total_rows, block), jnp.float32),
            pltpu.VMEM((local_width, total_rows), jnp.float32),
            pltpu.VMEM((group_count, seq_count, local_rows, local_width), jnp.bfloat16),
            pltpu.SemaphoreType.DMA((group_count, seq_count - 1)),
            pltpu.SemaphoreType.DMA((group_count, seq_count - 1)),
            pltpu.SemaphoreType.DMA((group_count, seq_count - 1)),
            pltpu.SemaphoreType.DMA((group_count, seq_count - 1)),
            pltpu.SemaphoreType.DMA((2 * group_count,)),
        ],
        compiler_params=pltpu.CompilerParams(
            collective_id=1, has_side_effects=True, vmem_limit_bytes=48 * 1024 * 1024
        ),
        name="attend_forward",
    )(bounds, qkv)


def backward_kernel(
    seq_count, bound_ref, kept_ref, grad_ref, log_ref, out_ref,
    taken_scr, key_scr, query_scr, key_t_scr, head_query_scr, head_grad_scr, prob_scr, weight_scr,
    query_t_scr, key_sum_scr, value_sum_scr, back_scr,
    send_sem, recv_sem, back_send_sem, back_recv_sem, local_sem,
):
    group_count, local_rows, local_width = grad_ref.shape[1], grad_ref.shape[2], grad_ref.shape[3]
    total_rows = seq_count * local_rows
    heads = local_width // HEAD_DIM
    me = lax.axis_index("seq")
    grp = lax.axis_index("grp")
    others = [lax.rem(me + step, seq_count) for step in range(1, seq_count)]
    block = min(256, total_rows // 3)
    enter([(grp, other) for other in others])
    copies = []
    for group in range(group_count):
        own = pltpu.make_async_copy(grad_ref.at[me, group], taken_scr.at[me, group], local_sem.at[group])
        own.start()
        row = [own]
        for step, other in enumerate(others):
            copy = pltpu.make_async_remote_copy(
                grad_ref.at[other, group], taken_scr.at[me, group],
                send_sem.at[group, step], recv_sem.at[group, step],
                device_id=(grp, other), device_id_type=MESH,
            )
            copy.start()
            row.append(copy)
        copies.append(row)
    back = []
    for group in range(group_count):
        for copy in copies[group]:
            copy.wait()
        boundary = bound_ref[group]
        keys = kept_ref[:, group, 1].reshape(total_rows, local_width)
        key_scr[:, :local_width] = keys
        key_scr[:, local_width:] = utter_features(boundary, total_rows, True)
        query_scr[:, local_width:] = utter_features(boundary, total_rows, False)
        key_t_scr[...] = keys.astype(jnp.float32).T.astype(jnp.bfloat16)
        key_sum_scr[...] = jnp.zeros_like(key_sum_scr)
        value_sum_scr[...] = jnp.zeros_like(value_sum_scr)

        def one_head(head, carry):
            queries = head_lanes(kept_ref[:, group, 0].reshape(total_rows, local_width), head)
            head_query_scr[...] = queries
            query_scr[:, :local_width] = queries * jnp.bfloat16(HEAD_DIM ** (-0.5))
            head_grad_scr[...] = head_lanes(taken_scr[:, group].reshape(total_rows, local_width), head)
            for third in range(3):
                first_key, last_key = key_span(third, total_rows)
                chunks = range(first_key, last_key, block)

                def one_block(index, carry):
                    first_row = pl.multiple_of(third * (total_rows // 3) + index * block, block)
                    own_rows = pl.ds(first_row, block)
                    query_block = query_scr[own_rows, :]
                    grad_block = head_grad_scr[own_rows, :]
                    plain_block = head_query_scr[own_rows, :]
                    log_block = log_ref[group, head, :, own_rows]
                    row_dot = jnp.zeros((8, block), jnp.float32)
                    for first in chunks:
                        scores = dot_nt(key_scr[first:first + block, :], query_block)
                        prob = jnp.exp(scores - log_block)
                        values = kept_ref[
                            first // local_rows:(first + block - 1) // local_rows + 1, group, 2
                        ].reshape(-1, local_width)
                        skip = first % local_rows
                        weight_grad = dot_nt(values[skip:skip + block], grad_block)
                        prob_scr[first:first + block, :] = prob
                        weight_scr[first:first + block, :] = weight_grad
                        row_dot = row_dot + fold_rows(prob * weight_grad, jnp.sum)
                    row_dot = jnp.sum(row_dot, axis=0, keepdims=True)
                    rows = pl.ds(pl.multiple_of(head * HEAD_DIM, HEAD_DIM), HEAD_DIM)
                    turned = jnp.zeros((HEAD_DIM, block), jnp.float32)
                    for first in chunks:
                        prob = prob_scr[first:first + block, :]
                        score_grad = (
                            HEAD_DIM ** (-0.5) * (prob * (weight_scr[first:first + block, :] - row_dot))
                        ).astype(jnp.bfloat16)
                        key_sum_scr[first:first + block, :] += dot_nn(score_grad, plain_block)
                        value_sum_scr[first:first + block, :] += dot_nn(
                            prob.astype(jnp.bfloat16), grad_block
                        )
                        turned = turned + dot_nn(key_t_scr[rows, first:first + block], score_grad)
                    query_t_scr[rows, own_rows] = turned
                    return carry

                lax.fori_loop(0, total_rows // 3 // block, one_block, 0)
            return carry

        lax.fori_loop(0, heads, one_head, 0)
        shape = (seq_count, local_rows, local_width)
        back_scr[:, group, 0] = query_t_scr[...].T.astype(jnp.bfloat16).reshape(shape)
        back_scr[:, group, 1] = key_sum_scr[...].astype(jnp.bfloat16).reshape(shape)
        back_scr[:, group, 2] = value_sum_scr[...].astype(jnp.bfloat16).reshape(shape)
        own = pltpu.make_async_copy(
            back_scr.at[me, group], out_ref.at[me, group], local_sem.at[group_count + group]
        )
        own.start()
        back.append(own)
        for step, other in enumerate(others):
            copy = pltpu.make_async_remote_copy(
                back_scr.at[other, group], out_ref.at[me, group],
                back_send_sem.at[group, step], back_recv_sem.at[group, step],
                device_id=(grp, other), device_id_type=MESH,
            )
            copy.start()
            back.append(copy)
    for copy in back:
        copy.wait()


def attend_backward(bounds, kept, grad, log_total):
    seq_count, group_count, _, local_rows, local_width = kept.shape
    total_rows = seq_count * local_rows
    block = min(256, total_rows // 3)
    vmem = pl.BlockSpec(memory_space=pltpu.VMEM)
    return pl.pallas_call(
        functools.partial(backward_kernel, seq_count),
        out_shape=jax.ShapeDtypeStruct(kept.shape, jnp.bfloat16),
        in_specs=[
            pl.BlockSpec(memory_space=pltpu.SMEM), vmem, pl.BlockSpec(memory_space=pl.ANY), vmem
        ],
        out_specs=vmem,
        scratch_shapes=[
            pltpu.VMEM(grad.shape, jnp.bfloat16),
            pltpu.VMEM((total_rows, local_width + 128), jnp.bfloat16),
            pltpu.VMEM((total_rows, local_width + 128), jnp.bfloat16),
            pltpu.VMEM((local_width, total_rows), jnp.bfloat16),
            pltpu.VMEM((total_rows, local_width), jnp.bfloat16),
            pltpu.VMEM((total_rows, local_width), jnp.bfloat16),
            pltpu.VMEM((total_rows, block), jnp.float32),
            pltpu.VMEM((total_rows, block), jnp.float32),
            pltpu.VMEM((local_width, total_rows), jnp.float32),
            pltpu.VMEM((total_rows, local_width), jnp.float32),
            pltpu.VMEM((total_rows, local_width), jnp.float32),
            pltpu.VMEM(kept.shape, jnp.bfloat16),
            pltpu.SemaphoreType.DMA((group_count, seq_count - 1)),
            pltpu.SemaphoreType.DMA((group_count, seq_count - 1)),
            pltpu.SemaphoreType.DMA((group_count, seq_count - 1)),
            pltpu.SemaphoreType.DMA((group_count, seq_count - 1)),
            pltpu.SemaphoreType.DMA((2 * group_count,)),
        ],
        compiler_params=pltpu.CompilerParams(
            collective_id=2, has_side_effects=True, vmem_limit_bytes=48 * 1024 * 1024
        ),
        name="attend_backward",
    )(bounds, kept, grad, log_total)


def gather_kernel(plane, seq_count, count, *refs):
    shards, fulls = refs[:count], refs[count:2 * count]
    own_sem, z_send, z_recv, first_send, first_recv, second_send, second_recv, core_send, core_recv = refs[2 * count:]
    rows_y, cols_x = plane
    grp = lax.axis_index("grp")
    me = lax.axis_index("seq")
    gy, gx = grp // cols_x, lax.rem(grp, cols_x)
    layers = seq_count // 2
    layer, core = me // 2, lax.rem(me, 2)
    beside = [gy * cols_x + lax.rem(gx + step, cols_x) for step in range(1, cols_x)]
    beside_from = [lax.rem(gx + cols_x - step, cols_x) for step in range(1, cols_x)]
    along = [lax.rem(gy + step, rows_y) * cols_x + gx for step in range(1, rows_y)]
    along_from = [lax.rem(gy + rows_y - step, rows_y) for step in range(1, rows_y)]
    lines = [lax.rem(layer + step, layers) * 2 + core for step in range(1, layers)]
    line_from = [lax.rem(layer + layers - step, layers) * 2 + core for step in range(1, layers)]
    partner = layer * 2 + 1 - core
    enter(
        [(grp, line) for line in lines]
        + [(other, me) for other in beside + along]
        + [(grp, partner)]
    )
    started = []

    def push(src, dst, sends, recvs, slot, device):
        copy = pltpu.make_async_remote_copy(
            src, dst, sends.at[slot], recvs.at[slot], device_id=device, device_id_type=MESH
        )
        copy.start()
        started.append(copy)
        return copy

    def piece(index, owner, y_from, y_many, x_from, x_many):
        height = fulls[index].shape[1] // rows_y
        width = fulls[index].shape[2] // (2 * cols_x)
        return fulls[index].at[
            owner,
            pl.ds(pl.multiple_of(y_from * height, height), y_many * height),
            pl.ds(pl.multiple_of(x_from * width, width), x_many * width),
        ]

    own = []
    line_copies = []
    for index in range(count):
        height = shards[index].shape[0] // rows_y
        width = shards[index].shape[1] // cols_x
        source = shards[index].at[
            pl.ds(pl.multiple_of(gy * height, height), height),
            pl.ds(pl.multiple_of(gx * width, width), width),
        ]
        line_copies.append([
            push(source, piece(index, me, gy, 1, 2 * gx, 2), z_send, z_recv, (index, step), (grp, line))
            for step, line in enumerate(lines)
        ])
    for index in range(count):
        copy = pltpu.make_async_copy(shards[index], fulls[index].at[me], own_sem.at[index])
        copy.start()
        own.append(copy)
        push(shards[index], fulls[index].at[me], core_send, core_recv, (index, 0), (grp, partner))
    spread = {}

    def first(index, step):
        line_copies[index][step].wait_recv()
        owner = line_from[step]
        spread[index, step] = [
            push(part, part, first_send, first_recv, (index, step, 0, hop), (other, me))
            for hop, other in enumerate(beside)
            for part in [piece(index, owner, gy, 1, 2 * gx, 1)]
        ] + [
            push(part, part, first_send, first_recv, (index, step, 1, hop), (other, me))
            for hop, other in enumerate(along)
            for part in [piece(index, owner, gy, 1, 2 * gx + 1, 1)]
        ]

    def second(index, step):
        for copy in spread[index, step]:
            copy.wait_recv()
        owner = line_from[step]
        copies = []
        for hop, other in enumerate(along):
            for place, column in enumerate([gx] + beside_from):
                part = piece(index, owner, gy, 1, 2 * column, 1)
                copies.append(push(part, part, second_send, second_recv, (index, step, 0, hop, place), (other, me)))
        for hop, other in enumerate(beside):
            part = piece(index, owner, 0, rows_y, 2 * gx + 1, 1)
            copies.append(push(part, part, second_send, second_recv, (index, step, 1, hop, 0), (other, me)))
        spread[index, step] = copies

    def third(index, step):
        for copy in spread[index, step]:
            copy.wait_recv()
        part = fulls[index].at[line_from[step]]
        spread[index, step] = [push(part, part, core_send, core_recv, (index, step + 1), (grp, partner))]

    jobs = [(index, step) for index in range(count) for step in range(layers - 1)]
    lag = layers - 1
    for turn in range(len(jobs) + 2 * lag):
        if turn < len(jobs):
            first(*jobs[turn])
        if 0 <= turn - lag < len(jobs):
            second(*jobs[turn - lag])
        if 0 <= turn - 2 * lag < len(jobs):
            third(*jobs[turn - 2 * lag])
    for copy in started:
        copy.wait_send()
    for copies in spread.values():
        for copy in copies:
            copy.wait_recv()
    for index in range(count):
        pltpu.make_async_remote_copy(
            shards[index], fulls[index].at[me], core_send.at[index, 0], core_recv.at[index, 0],
            device_id=(grp, partner), device_id_type=MESH,
        ).wait_recv()
        own[index].wait()


def gather(collective, *shards):
    seq_count = lax.axis_size("seq")
    side = math.isqrt(lax.axis_size("grp"))
    plane = (side, side)
    layers = seq_count // 2
    count = len(shards)
    anywhere = pl.BlockSpec(memory_space=pl.ANY)
    dma = pltpu.SemaphoreType.DMA
    hops = max(side - 1, 1)
    outs = pl.pallas_call(
        functools.partial(gather_kernel, plane, seq_count, count),
        out_shape=tuple(jax.ShapeDtypeStruct((seq_count,) + part.shape, part.dtype) for part in shards),
        in_specs=[anywhere] * count,
        out_specs=(anywhere,) * count,
        scratch_shapes=[
            dma((count,)),
            dma((count, layers - 1)), dma((count, layers - 1)),
            dma((count, layers - 1, 2, hops)), dma((count, layers - 1, 2, hops)),
            dma((count, layers - 1, 2, hops, side)), dma((count, layers - 1, 2, hops, side)),
            dma((count, layers)), dma((count, layers)),
        ],
        compiler_params=pltpu.CompilerParams(collective_id=collective, has_side_effects=True),
        name="gather_weights_%d" % collective,
    )(*shards)
    return tuple(full.reshape(seq_count * part.shape[0], part.shape[1]) for full, part in zip(outs, shards))


def add_rows(target, source, first_row, rows, first_col, cols):
    step = 16
    col = pl.multiple_of(first_col, 128)

    def one(index, carry):
        at = pl.ds(pl.multiple_of(first_row + index * step, step), step)
        target[at, pl.ds(col, cols)] = target[at, pl.ds(col, cols)] + source[
            pl.ds(pl.multiple_of(index * step, step), step), :
        ]
        return carry

    lax.fori_loop(0, rows // step, one, 0)


def reduce_kernel(plane, seq_count, count, *refs):
    parts, outs = refs[:count], refs[count:2 * count]
    rest = refs[2 * count:]
    sums, partner_bufs, y_first, x_second, x_first, y_second, line_bufs = [
        rest[index * count:(index + 1) * count] for index in range(7)
    ]
    load_sem, core_send, core_recv, first_send, first_recv, second_send, second_recv, z_send, z_recv, spread_send, spread_recv, late_send, late_recv = rest[7 * count:]
    rows_y, cols_x = plane
    grp = lax.axis_index("grp")
    me = lax.axis_index("seq")
    gy, gx = grp // cols_x, lax.rem(grp, cols_x)
    layers = seq_count // 2
    layer, core = me // 2, lax.rem(me, 2)
    xs = [lax.rem(gx + step, cols_x) for step in range(1, cols_x)]
    ys = [lax.rem(gy + step, rows_y) for step in range(1, rows_y)]
    beside = [gy * cols_x + x for x in xs]
    along = [y * cols_x + gx for y in ys]
    beside_from = [lax.rem(gx + cols_x - step, cols_x) for step in range(1, cols_x)]
    far = [lax.rem(layer + step, layers) for step in range(1, layers)]
    partner = layer * 2 + 1 - core
    enter(
        [(grp, other * 2 + core) for other in far]
        + [(other, me) for other in beside + along]
        + [(grp, partner)]
    )
    started = []

    def push(src, dst, sends, recvs, slot, device):
        copy = pltpu.make_async_remote_copy(
            src, dst, sends.at[slot], recvs.at[slot], device_id=device, device_id_type=MESH
        )
        copy.start()
        started.append(copy)
        return copy

    def sizes(index):
        _, rows, cols = parts[index].shape
        return rows, cols, rows // rows_y, cols // (2 * cols_x)

    def window(ref, row, rows, col, cols):
        return ref.at[
            pl.ds(pl.multiple_of(row, 16), rows), pl.ds(pl.multiple_of(col, 128), cols)
        ]

    order = far + [layer]
    loads, swaps = {}, {}
    for index in range(count):
        for step, target in enumerate(order):
            copy = pltpu.make_async_copy(
                parts[index].at[target * 2 + core], sums[index].at[step], load_sem.at[index, step]
            )
            copy.start()
            loads[index, step] = copy
            swaps[index, step] = push(
                parts[index].at[target * 2 + 1 - core], partner_bufs[index].at[step],
                core_send, core_recv, (index, step), (grp, partner),
            )
    waiting = {}

    def first(index, step):
        rows, cols, height, width = sizes(index)
        loads[index, step].wait()
        swaps[index, step].wait_recv()
        total = sums[index].at[step]
        add_rows(total, partner_bufs[index].at[step], 0, rows, 0, cols)
        copies = []
        for hop, other in enumerate(along):
            for column in range(cols_x):
                copies.append(push(
                    window(total, ys[hop] * height, height, 2 * column * width, width),
                    y_first[index].at[step, hop, column],
                    first_send, first_recv, (index, step, 0, hop, column), (other, me),
                ))
        for hop, other in enumerate(beside):
            copies.append(push(
                window(total, 0, rows, (2 * xs[hop] + 1) * width, width),
                x_first[index].at[step, hop],
                first_send, first_recv, (index, step, 1, hop, 0), (other, me),
            ))
        waiting[index, step] = copies

    def second(index, step):
        rows, cols, height, width = sizes(index)
        for copy in waiting[index, step]:
            copy.wait_recv()
        total = sums[index].at[step]
        for hop in range(rows_y - 1):
            for column in range(cols_x):
                add_rows(total, y_first[index].at[step, hop, column], gy * height, height, 2 * column * width, width)
        for hop in range(cols_x - 1):
            add_rows(total, x_first[index].at[step, hop], 0, rows, (2 * gx + 1) * width, width)
        copies = []
        for hop, other in enumerate(beside):
            copies.append(push(
                window(total, gy * height, height, 2 * xs[hop] * width, width),
                x_second[index].at[step, hop],
                second_send, second_recv, (index, step, 0, hop), (other, me),
            ))
        for hop, other in enumerate(along):
            copies.append(push(
                window(total, ys[hop] * height, height, (2 * gx + 1) * width, width),
                y_second[index].at[step, hop],
                second_send, second_recv, (index, step, 1, hop), (other, me),
            ))
        waiting[index, step] = copies

    def third(index, step):
        rows, cols, height, width = sizes(index)
        for copy in waiting[index, step]:
            copy.wait_recv()
        total = sums[index].at[step]
        for hop in range(cols_x - 1):
            add_rows(total, x_second[index].at[step, hop], gy * height, height, 2 * gx * width, width)
        for hop in range(rows_y - 1):
            add_rows(total, y_second[index].at[step, hop], gy * height, height, (2 * gx + 1) * width, width)
        waiting[index, step] = []
        if step < layers - 1:
            waiting[index, step].append(push(
                window(total, gy * height, height, 2 * gx * width, 2 * width),
                line_bufs[index].at[step], z_send, z_recv, (index, step), (grp, order[step] * 2 + core),
            ))

    def fourth(index):
        rows, cols, height, width = sizes(index)
        for step in range(layers - 1):
            for copy in waiting[index, step]:
                copy.wait_recv()
        total = sums[index].at[layers - 1]
        low_row = gy * height
        low_col = pl.multiple_of(2 * gx * width, 128)

        def one(turn, carry):
            at = pl.ds(pl.multiple_of(low_row + turn * 16, 16), 16)
            off = pl.ds(pl.multiple_of(turn * 16, 16), 16)
            value = total[at, pl.ds(low_col, 2 * width)].astype(jnp.float32)
            for step in range(layers - 1):
                value = value + line_bufs[index][step, off, :].astype(jnp.float32)
            outs[index][at, pl.ds(low_col, 2 * width)] = value.astype(jnp.bfloat16)
            return carry

        lax.fori_loop(0, height // 16, one, 0)
        copies = []
        for hop, other in enumerate(beside):
            part = window(outs[index], low_row, height, 2 * gx * width, width)
            copies.append(push(part, part, spread_send, spread_recv, (index, 0, hop), (other, me)))
        for hop, other in enumerate(along):
            part = window(outs[index], low_row, height, (2 * gx + 1) * width, width)
            copies.append(push(part, part, spread_send, spread_recv, (index, 1, hop), (other, me)))
        waiting[index] = copies

    def fifth(index):
        rows, cols, height, width = sizes(index)
        for copy in waiting[index]:
            copy.wait_recv()
        copies = []
        for hop, other in enumerate(along):
            for place, column in enumerate([gx] + beside_from):
                part = window(outs[index], gy * height, height, 2 * column * width, width)
                copies.append(push(part, part, late_send, late_recv, (index, 0, hop, place), (other, me)))
        for hop, other in enumerate(beside):
            part = window(outs[index], 0, rows, (2 * gx + 1) * width, width)
            copies.append(push(part, part, late_send, late_recv, (index, 1, hop, 0), (other, me)))
        waiting[index] = copies

    jobs = [(index, step) for index in range(count) for step in range(layers)]
    lag = layers // 2
    for turn in range(len(jobs) + 6 * lag):
        if turn < len(jobs):
            first(*jobs[turn])
        if 0 <= turn - lag < len(jobs):
            second(*jobs[turn - lag])
        if 0 <= turn - 2 * lag < len(jobs):
            third(*jobs[turn - 2 * lag])
        done = turn - 4 * lag
        if 0 <= done < len(jobs) and done % layers == layers - 1:
            fourth(done // layers)
        done = turn - 6 * lag
        if 0 <= done < len(jobs) and done % layers == layers - 1:
            fifth(done // layers)
    for copy in started:
        copy.wait_send()
    for index in range(count):
        for copy in waiting[index]:
            copy.wait_recv()


def reduce_shares(collective, *parts):
    seq_count = lax.axis_size("seq")
    side = math.isqrt(lax.axis_size("grp"))
    layers = seq_count // 2
    count = len(parts)
    parts = [part.reshape(seq_count, part.shape[0] // seq_count, part.shape[1]) for part in parts]
    anywhere = pl.BlockSpec(memory_space=pl.ANY)
    vmem = pl.BlockSpec(memory_space=pltpu.VMEM)
    dma = pltpu.SemaphoreType.DMA
    hops = max(side - 1, 1)

    def buffers(lead, row_cut, col_cut):
        return [
            pltpu.VMEM(lead + (part.shape[1] // row_cut, part.shape[2] // col_cut), jnp.bfloat16)
            for part in parts
        ]

    return pl.pallas_call(
        functools.partial(reduce_kernel, (side, side), seq_count, count),
        out_shape=tuple(jax.ShapeDtypeStruct(part.shape[1:], part.dtype) for part in parts),
        in_specs=[anywhere] * count,
        out_specs=(vmem,) * count,
        scratch_shapes=buffers((layers,), 1, 1)
        + buffers((layers,), 1, 1)
        + buffers((layers, hops, side), side, 2 * side)
        + buffers((layers, hops), side, 2 * side)
        + buffers((layers, hops), 1, 2 * side)
        + buffers((layers, hops), side, 2 * side)
        + buffers((layers - 1,), side, side)
        + [
            dma((count, layers)), dma((count, layers)), dma((count, layers)),
            dma((count, layers, 2, hops, side)), dma((count, layers, 2, hops, side)),
            dma((count, layers, 2, hops)), dma((count, layers, 2, hops)),
            dma((count, layers - 1)), dma((count, layers - 1)),
            dma((count, 2, hops)), dma((count, 2, hops)),
            dma((count, 2, hops, side)), dma((count, 2, hops, side)),
        ],
        compiler_params=pltpu.CompilerParams(
            collective_id=collective, has_side_effects=True, vmem_limit_bytes=60 * 1024 * 1024
        ),
        name="reduce_shares_%d" % collective,
    )(*parts)


def shards(
    frames,
    shortcut,
    time_embed,
    lengths,
    kept_mask,
    target,
    combine,
    modulation,
    projection,
    readout,
    expand,
    contract,
):
    gathered = gather(3, combine, projection, readout, expand, contract)
    combine_full, projection_full, readout_full, expand_full, contract_full = (
        gathered
    )
    group_count = frames.shape[0]
    local_rows = frames.shape[1]
    width = HEADS * HEAD_DIM
    row_count = group_count * local_rows
    seq_count = lax.axis_size("seq")
    group_frames = local_rows * seq_count
    all_frames = group_frames * lax.axis_size("grp") * group_count
    utter_count = time_embed.shape[1]
    kept_float = kept_mask.astype(jnp.float32).reshape(row_count)
    kept_total = lax.psum(jnp.sum(kept_float), ("grp", "seq"))
    local_index = lax.axis_index("seq") * local_rows + jnp.arange(local_rows, dtype=jnp.int32)

    def local_info(length_row):
        return segment_info(length_row, local_index)

    member_info = jax.vmap(local_info)(lengths)
    member_float = member_info[1].astype(jnp.float32)
    position = member_info[2]
    cos_table, sin_table = rotary_tables(position.reshape(row_count))
    joined = jnp.concatenate([frames, shortcut], axis=2).reshape(row_count, 2 * width)
    hidden = product(joined, combine_full)
    silu_value, silu_pull = jax.vjp(jax.nn.silu, time_embed)
    condition = silu_value.astype(jnp.bfloat16)
    shard_rows = modulation.shape[0]
    condition_part = lax.dynamic_slice_in_dim(
        condition, lax.axis_index("seq") * shard_rows, shard_rows, 2
    ).reshape(group_count * utter_count, shard_rows)
    modulation_utter = lax.psum(product(condition_part, modulation), "seq").reshape(
        group_count, utter_count, 6 * width
    )
    modulation_frame = jnp.einsum(
        "gtu,gue->gte",
        member_float,
        modulation_utter,
        precision=precise,
        preferred_element_type=jnp.float32,
    ).reshape(row_count, 6 * width)
    shift_first, scale_first, gate_first, shift_second, scale_second, gate_second = jnp.split(
        modulation_frame, 6, axis=1
    )
    normed_value, first_pull = jax.vjp(modulate, hidden, shift_first, scale_first)
    normed = normed_value.astype(jnp.bfloat16)
    packed = product(normed, projection_full)
    query_raw, key_raw, value_raw = jnp.split(packed, 3, axis=1)
    head_shape = (row_count, HEADS, HEAD_DIM)
    split_shape = (group_count, local_rows, width)

    def rotate_local(vectors):
        return rotate(vectors, cos_table, sin_table)

    query_turned, query_pull = jax.vjp(rotate_local, query_raw.reshape(head_shape))
    key_turned, key_pull = jax.vjp(rotate_local, key_raw.reshape(head_shape))
    local_width = width // seq_count

    def by_target(vectors):
        return vectors.reshape(group_count, local_rows, seq_count, local_width).astype(jnp.bfloat16)

    qkv = jnp.transpose(
        jnp.stack([by_target(query_turned), by_target(key_turned), by_target(value_raw)]),
        (3, 1, 0, 2, 4),
    )
    bounds = lengths[:, 0]
    kept_heads, mixture_blocks, log_total = attend_forward(bounds, qkv)
    mixture = jnp.transpose(mixture_blocks, (1, 2, 0, 3)).reshape(row_count, width)
    branch = product(mixture, readout_full)
    middle = hidden + gate_first * branch
    second_value, second_pull = jax.vjp(modulate, middle, shift_second, scale_second)
    normed_second = second_value.astype(jnp.bfloat16)
    expanded = product(normed_second, expand_full)
    active_value, gelu_pull = jax.vjp(gelu_tanh, expanded)
    active = active_value.astype(jnp.bfloat16)
    contracted = product(active, contract_full)
    output = middle + gate_second * contracted
    loss_scale = all_frames / kept_total
    output_grad = (
        loss_scale
        * kept_float[:, None]
        * (output - target.reshape(row_count, width).astype(jnp.float32))
    )
    combine_back, projection_back, readout_back, expand_back, contract_back = (
        gathered
    )
    gate_second_grad = output_grad * contracted
    contracted_grad = (gate_second * output_grad).astype(jnp.bfloat16)
    contract_part = product_left(active, contracted_grad)
    active_grad = product_right(contracted_grad, contract_back)
    expanded_grad = gelu_pull(active_grad)[0].astype(jnp.bfloat16)
    expand_part = product_left(normed_second, expanded_grad)
    normed_second_grad = product_right(expanded_grad, expand_back)
    middle_extra, shift_second_grad, scale_second_grad = second_pull(normed_second_grad)
    middle_grad = output_grad + middle_extra
    gate_first_grad = middle_grad * branch
    branch_grad = (gate_first * middle_grad).astype(jnp.bfloat16)
    readout_part = product_left(mixture, branch_grad)
    mixture_grad = product_right(branch_grad, readout_back).astype(jnp.bfloat16)
    back_blocks = attend_backward(
        bounds,
        kept_heads,
        jnp.transpose(
            mixture_grad.reshape(group_count, local_rows, seq_count, local_width), (2, 0, 1, 3)
        ),
        log_total,
    )
    query_back, key_back, value_back = jnp.transpose(back_blocks, (2, 1, 3, 0, 4)).reshape(
        3, group_count, local_rows, width
    )
    query_unturned = query_pull(query_back.reshape(head_shape).astype(jnp.float32))[0].reshape(
        row_count, width
    )
    key_unturned = key_pull(key_back.reshape(head_shape).astype(jnp.float32))[0].reshape(
        row_count, width
    )
    packed_grad = jnp.concatenate(
        [
            query_unturned.astype(jnp.bfloat16),
            key_unturned.astype(jnp.bfloat16),
            value_back.reshape(row_count, width),
        ],
        axis=1,
    )
    projection_part = product_left(normed, packed_grad)
    normed_grad = product_right(packed_grad, projection_back)
    hidden_extra, shift_first_grad, scale_first_grad = first_pull(normed_grad)
    hidden_grad = (middle_grad + hidden_extra).astype(jnp.bfloat16)
    combine_part = product_left(joined, hidden_grad)
    joined_grad = product_right(hidden_grad, combine_back)
    frames_grad = joined_grad[:, :width].reshape(split_shape)
    shortcut_grad = joined_grad[:, width:].reshape(split_shape)
    modulation_frame_grad = jnp.concatenate(
        [
            shift_first_grad,
            scale_first_grad,
            gate_first_grad,
            shift_second_grad,
            scale_second_grad,
            gate_second_grad,
        ],
        axis=1,
    )
    utter_part = jnp.einsum(
        "gtu,gte->gue",
        member_float,
        modulation_frame_grad.reshape(group_count, local_rows, 6 * width),
        precision=precise,
        preferred_element_type=jnp.float32,
    )
    utter_grad = lax.psum(utter_part.astype(jnp.bfloat16), "seq")
    utter_rows = utter_grad.reshape(group_count * utter_count, 6 * width)
    condition_grad = lax.all_gather(
        product_right(utter_rows, modulation), "seq", axis=1, tiled=True
    ).reshape(group_count, utter_count, width)
    time_grad = silu_pull(condition_grad)[0]
    utter_all = lax.all_gather(utter_rows, "grp", axis=0, tiled=True)
    condition_all = lax.all_gather(condition_part, "grp", axis=0, tiled=True)
    modulation_grad = product_left(condition_all, utter_all)
    combine_grad, projection_grad, readout_grad, expand_grad, contract_grad = [
        share.astype(jnp.float32)
        for share in reduce_shares(
            4,
            combine_part.astype(jnp.bfloat16),
            projection_part.astype(jnp.bfloat16),
            readout_part.astype(jnp.bfloat16),
            expand_part.astype(jnp.bfloat16),
            contract_part.astype(jnp.bfloat16),
        )
    ]
    summed = (combine_grad, modulation_grad, projection_grad, readout_grad, expand_grad, contract_grad)
    return (
        output.astype(jnp.bfloat16).reshape(split_shape),
        frames_grad,
        shortcut_grad,
        time_grad,
        summed[0],
        summed[1],
        summed[2],
        summed[3],
        summed[4],
        summed[5],
    )


def solution(mesh):
    return jax.shard_map(
        shards,
        mesh=mesh,
        in_specs=(
            P("grp", "seq", None),
            P("grp", "seq", None),
            P("grp", None, None),
            P("grp", None),
            P("grp", "seq"),
            P("grp", "seq", None),
            P("seq", None),
            P("seq", None),
            P("seq", None),
            P("seq", None),
            P("seq", None),
            P("seq", None),
        ),
        out_specs=(
            P("grp", "seq", None),
            P("grp", "seq", None),
            P("grp", "seq", None),
            P("grp", None, None),
            P("seq", None),
            P("seq", None),
            P("seq", None),
            P("seq", None),
            P("seq", None),
            P("seq", None),
        ),
        check_vma=False,
    )
```

```python
import functools
import math

import jax
import jax.numpy as jnp
from jax import lax
from jax.experimental import pallas as pl
from jax.experimental.pallas import tpu as pltpu
from jax.sharding import PartitionSpec as P

HEADS = 16
HEAD_DIM = 64


precise = lax.Precision.HIGHEST
epsilon = 1e-06
rope_base = 10000.0


def product(first_op, second_op):
    return jnp.dot(first_op, second_op, preferred_element_type=jnp.float32)


def product_left(first_op, second_op):
    return lax.dot_general(
        first_op, second_op, (((0,), (0,)), ((), ())), preferred_element_type=jnp.float32
    )


def product_right(first_op, second_op):
    return lax.dot_general(
        first_op, second_op, (((1,), (1,)), ((), ())), preferred_element_type=jnp.float32
    )


def gelu_tanh(values):
    return jax.nn.gelu(values, approximate=True)


def modulate(hidden, shift_part, scale_part):
    center = hidden - jnp.mean(hidden, axis=-1, keepdims=True)
    variance = jnp.mean(center * center, axis=-1, keepdims=True)
    return center * lax.rsqrt(variance + epsilon) * (1.0 + scale_part) + shift_part


def segment_info(lengths, frame_index):
    utter_count = lengths.shape[0]
    utter_ends = jnp.cumsum(lengths)
    starts = utter_ends - lengths
    segment = jnp.sum((frame_index[:, None] >= utter_ends[None, :]).astype(jnp.int32), axis=1)
    member = segment[:, None] == jnp.arange(utter_count, dtype=jnp.int32)[None, :]
    offset = jnp.sum(jnp.where(member, starts[None, :], 0), axis=1)
    return (segment, member, frame_index - offset)


def rotary_tables(position):
    half_dim = HEAD_DIM // 2
    ladder = jnp.arange(half_dim, dtype=jnp.float32) / half_dim
    inverse = jnp.exp(-jnp.log(rope_base) * ladder)
    angles = position.astype(jnp.float32)[:, None] * inverse[None, :]
    return (jnp.cos(angles)[:, None, :], jnp.sin(angles)[:, None, :])


def rotate(vectors, cos_table, sin_table):
    half_dim = vectors.shape[-1] // 2
    front_half = vectors[..., :half_dim]
    back_half = vectors[..., half_dim:]
    return jnp.concatenate(
        [
            front_half * cos_table - back_half * sin_table,
            back_half * cos_table + front_half * sin_table,
        ],
        axis=-1,
    )


MESH = pl.DeviceIdType.MESH
NEG = -1e30


def utter_features(boundary, total_rows, for_keys):
    row = lax.broadcasted_iota(jnp.int32, (total_rows, 128), 0)
    lane = lax.broadcasted_iota(jnp.int32, (total_rows, 128), 1)
    second = (row >= boundary).astype(jnp.float32)
    ahead = (lane == 0).astype(jnp.float32)
    after = (lane == 1).astype(jnp.float32)
    if for_keys:
        return (NEG * (second * ahead + (1.0 - second) * after)).astype(jnp.bfloat16)
    return (second * after + (1.0 - second) * ahead).astype(jnp.bfloat16)


def head_lanes(values, head):
    lane = lax.broadcasted_iota(jnp.int32, values.shape, 1)
    own = (lane >= head * HEAD_DIM) & (lane < (head + 1) * HEAD_DIM)
    return jnp.where(own, values.astype(jnp.float32), 0.0).astype(jnp.bfloat16)


def dot_nn(first_op, second_op):
    return jnp.dot(first_op, second_op, preferred_element_type=jnp.float32)


def dot_nt(first_op, second_op):
    return lax.dot_general(
        first_op, second_op, (((1,), (1,)), ((), ())), preferred_element_type=jnp.float32
    )


def fold_rows(values, combine):
    return combine(values.reshape(values.shape[0] // 8, 8, values.shape[1]), axis=0)


def enter(partners):
    barrier = pltpu.get_barrier_semaphore()
    for partner in partners:
        pl.semaphore_signal(barrier, inc=1, device_id=partner, device_id_type=MESH)
    pl.semaphore_wait(barrier, len(partners))


def key_span(third, total_rows):
    size = total_rows // 3
    return (max(third - 1, 0) * size, min(third + 2, 3) * size)


class Place:
    def __init__(self, plane, seq_count):
        self.rows_y, self.cols_x = rows_y, cols_x = plane
        self.grp, self.me = grp, me = lax.axis_index("grp"), lax.axis_index("seq")
        self.gy, self.gx = gy, gx = grp // cols_x, lax.rem(grp, cols_x)
        self.layers = layers = seq_count // 2
        self.layer, self.core = layer, core = me // 2, lax.rem(me, 2)
        self.xs = [lax.rem(gx + step, cols_x) for step in range(1, cols_x)]
        self.ys = [lax.rem(gy + step, rows_y) for step in range(1, rows_y)]
        self.beside = [gy * cols_x + x for x in self.xs]
        self.along = [y * cols_x + gx for y in self.ys]
        self.beside_from = [lax.rem(gx + cols_x - step, cols_x) for step in range(1, cols_x)]
        self.far = [lax.rem(layer + step, layers) for step in range(1, layers)]
        self.line_from = [lax.rem(layer + layers - step, layers) * 2 + core for step in range(1, layers)]
        self.lines = [target * 2 + core for target in self.far]
        self.partner = layer * 2 + 1 - core
        self.others = [lax.rem(me + step, seq_count) for step in range(1, seq_count)]
        self.groups = [lax.rem(grp + step, rows_y * cols_x) for step in range(1, rows_y * cols_x)]
        self.started = []

    def push(self, src, dst, sends, recvs, slot, device):
        copy = pltpu.make_async_remote_copy(
            src, dst, sends.at[slot], recvs.at[slot], device_id=device, device_id_type=MESH
        )
        copy.start()
        self.started.append(copy)
        return copy

    def sent(self):
        for copy in self.started:
            copy.wait_send()
        self.started = []


def window(ref, row, rows, col, cols):
    return ref.at[pl.ds(pl.multiple_of(row, 16), rows), pl.ds(pl.multiple_of(col, 128), cols)]


def piece_segments(shapes, side, width):
    base, found = 0, []
    for rows, cols in shapes:
        height, many = rows // side, cols // side // width
        if many == 1:
            half = width // 2
            found.append([[(base, 0, height, half, 0)], [(base, half, height, half, half)]])
        else:
            blocks = [(base + spot * height, 0, height, width, spot * width) for spot in range(many)]
            found.append([blocks[:many // 2], blocks[many // 2:]])
        base += height * many
    return found, base


class PlaneGather:
    def __init__(self, place, shards, pieces, segments, fulls, own_sem, first_send, first_recv, second_send, second_recv, core_send, core_recv):
        self.place, self.shards, self.pieces, self.fulls = place, shards, pieces, fulls
        self.segments = segments
        self.own_sem = own_sem
        self.first = (first_send, first_recv)
        self.second = (second_send, second_recv)
        self.core = (core_send, core_recv)
        self.jobs = [(index, step) for step in range(place.layers - 1) for index in range(len(shards))]
        self.waiting, self.local, self.own = {}, {}, []

    def sizes(self, index):
        _, rows, cols = self.fulls[index].shape
        return rows, rows // self.place.rows_y, cols // (2 * self.place.cols_x)

    def begin(self):
        place = self.place
        for index, step in self.jobs:
            self.spread_first(index, step)
        for index, shard in enumerate(self.shards):
            copy = pltpu.make_async_copy(shard, self.fulls[index].at[place.me], self.own_sem.at[index, place.layers - 1, 0, 0])
            copy.start()
            push = place.push(shard, self.fulls[index].at[place.me], *self.core, (index, 0), (place.grp, place.partner))
            self.own.append((copy, push))

    def spread_first(self, index, step):
        place = self.place
        rows, height, width = self.sizes(index)
        full = self.fulls[index].at[place.line_from[step]]
        piece = self.pieces[step]
        first_row, first_col = place.gy * height, 2 * place.gx * width
        self.local[index, step] = []
        self.waiting[index, step] = []
        for half, partners in enumerate((place.beside, place.along)):
            for spot, (row, col, rows, cols, off) in enumerate(self.segments[index][half]):
                source = piece.at[pl.ds(row, rows), pl.ds(col, cols)]
                part = window(full, first_row, rows, first_col + off, cols)
                copy = pltpu.make_async_copy(source, part, self.own_sem.at[index, step, half, spot])
                copy.start()
                self.local[index, step].append(copy)
                for hop, other in enumerate(partners):
                    self.waiting[index, step].append(place.push(
                        source, part, *self.first, (index, step, half, hop, spot), (other, place.me)
                    ))

    def spread_second(self, index, step):
        place = self.place
        rows, height, width = self.sizes(index)
        for copy in self.local.get((index, step), []):
            copy.wait()
        for copy in self.waiting[index, step]:
            copy.wait_recv()
        full = self.fulls[index].at[place.line_from[step]]
        copies = []
        for hop, other in enumerate(place.along):
            for spot, column in enumerate([place.gx] + place.beside_from):
                part = window(full, place.gy * height, height, 2 * column * width, width)
                copies.append(place.push(part, part, *self.second, (index, step, 0, hop, spot), (other, place.me)))
        for hop, other in enumerate(place.beside):
            part = window(full, 0, rows, (2 * place.gx + 1) * width, width)
            copies.append(place.push(part, part, *self.second, (index, step, 1, hop, 0), (other, place.me)))
        self.waiting[index, step] = copies

    def over_core(self, index, step):
        place = self.place
        for copy in self.waiting[index, step]:
            copy.wait_recv()
        full = self.fulls[index].at[place.line_from[step]]
        self.waiting[index, step] = [
            place.push(full, full, *self.core, (index, step + 1), (place.grp, place.partner))
        ]

    def middle(self):
        for job in self.jobs:
            self.spread_second(*job)

    def late(self):
        return [functools.partial(self.over_core, *job) for job in self.jobs]

    def finish(self):
        self.place.sent()
        for job in self.jobs:
            for copy in self.waiting[job]:
                copy.wait_recv()
        for copy, push in self.own:
            copy.wait()
            push.wait_recv()


def add_rows(target, source, first_row, rows, first_col, cols, out=None):
    step = 16
    col = pl.multiple_of(first_col, 128)

    def one(index, carry):
        at = pl.ds(pl.multiple_of(first_row + index * step, step), step)
        off = pl.ds(pl.multiple_of(index * step, step), step)
        value = target[at, pl.ds(col, cols)] + source[off, :]
        if out is None:
            target[at, pl.ds(col, cols)] = value
        else:
            out[off, :] = value
        return carry

    lax.fori_loop(0, rows // step, one, 0)


def add_segments(target, source, first_row, first_col, segments, out):
    for row, col, rows, cols, off in segments:
        begin = off - segments[0][4]
        add_rows(
            target, source.at[:, pl.ds(begin, cols)], first_row, rows, first_col + off, cols,
            out.at[pl.ds(row, rows), pl.ds(col, cols)],
        )


def plane_sum_scratch(parts, side):
    layers = parts[0].shape[0] // 2
    hops = max(side - 1, 1)
    count = len(parts)
    dma = pltpu.SemaphoreType.DMA

    def buffers(lead, row_cut, col_cut):
        return [
            pltpu.VMEM(lead + (part.shape[1] // row_cut, part.shape[2] // col_cut), jnp.bfloat16)
            for part in parts
        ]

    return (
        buffers((layers,), 1, 1)
        + buffers((layers,), 1, 1)
        + buffers((layers, hops, side), side, 2 * side)
        + buffers((layers, hops), side, 2 * side)
        + buffers((layers, hops), 1, 2 * side)
        + buffers((layers, hops), side, 2 * side)
        + [
            dma((count, layers)), dma((count, layers)), dma((count, layers)),
            dma((count, layers, 2, hops, side)), dma((count, layers, 2, hops, side)),
            dma((count, layers, 2, hops)), dma((count, layers, 2, hops)),
        ]
    )


def by_owner(parts, seq_count):
    return [part.reshape(seq_count, part.shape[0] // seq_count, part.shape[1]) for part in parts]


class PlaneSum:
    def __init__(self, place, parts, pieces, segments, buffers, semaphores):
        self.place, self.parts, self.pieces, self.segments = place, parts, pieces, segments
        count = len(parts)
        self.sums, self.swapped, self.y_first, self.x_second, self.x_first, self.y_second = [
            buffers[index * count:(index + 1) * count] for index in range(6)
        ]
        self.load_sem = semaphores[0]
        self.core, self.first_sem, self.second_sem = semaphores[1:3], semaphores[3:5], semaphores[5:7]
        self.order = place.far + [place.layer]
        self.jobs = [(index, step) for index in range(count) for step in range(place.layers)]
        self.loads, self.swaps, self.waiting = {}, {}, {}

    def sizes(self, index):
        _, rows, cols = self.parts[index].shape
        return rows, cols, rows // self.place.rows_y, cols // (2 * self.place.cols_x)

    def begin(self):
        place = self.place
        for index, step in self.jobs:
            target = self.order[step]
            copy = pltpu.make_async_copy(
                self.parts[index].at[target * 2 + place.core], self.sums[index].at[step], self.load_sem.at[index, step]
            )
            copy.start()
            self.loads[index, step] = copy
            self.swaps[index, step] = place.push(
                self.parts[index].at[target * 2 + 1 - place.core], self.swapped[index].at[step],
                *self.core, (index, step), (place.grp, place.partner),
            )

    def first(self, index, step):
        place = self.place
        rows, cols, height, width = self.sizes(index)
        self.loads[index, step].wait()
        self.swaps[index, step].wait_recv()
        total = self.sums[index].at[step]
        add_rows(total, self.swapped[index].at[step], 0, rows, 0, cols)
        copies = []
        for hop, other in enumerate(place.along):
            for column in range(place.cols_x):
                copies.append(place.push(
                    window(total, place.ys[hop] * height, height, 2 * column * width, width),
                    self.y_first[index].at[step, hop, column],
                    *self.first_sem, (index, step, 0, hop, column), (other, place.me),
                ))
        for hop, other in enumerate(place.beside):
            copies.append(place.push(
                window(total, 0, rows, (2 * place.xs[hop] + 1) * width, width),
                self.x_first[index].at[step, hop],
                *self.first_sem, (index, step, 1, hop, 0), (other, place.me),
            ))
        self.waiting[index, step] = copies

    def second(self, index, step):
        place = self.place
        rows, cols, height, width = self.sizes(index)
        for copy in self.waiting[index, step]:
            copy.wait_recv()
        total = self.sums[index].at[step]
        for hop in range(place.rows_y - 1):
            for column in range(place.cols_x):
                add_rows(
                    total, self.y_first[index].at[step, hop, column],
                    place.gy * height, height, 2 * column * width, width,
                )
        for hop in range(place.cols_x - 1):
            add_rows(total, self.x_first[index].at[step, hop], 0, rows, (2 * place.gx + 1) * width, width)
        copies = []
        for hop, other in enumerate(place.beside):
            copies.append(place.push(
                window(total, place.gy * height, height, 2 * place.xs[hop] * width, width),
                self.x_second[index].at[step, hop],
                *self.second_sem, (index, step, 0, hop), (other, place.me),
            ))
        for hop, other in enumerate(place.along):
            copies.append(place.push(
                window(total, place.ys[hop] * height, height, (2 * place.gx + 1) * width, width),
                self.y_second[index].at[step, hop],
                *self.second_sem, (index, step, 1, hop), (other, place.me),
            ))
        self.waiting[index, step] = copies

    def third(self, index, step):
        place = self.place
        rows, cols, height, width = self.sizes(index)
        for copy in self.waiting[index, step]:
            copy.wait_recv()
        self.waiting[index, step] = []
        total = self.sums[index].at[step]
        out = self.pieces[index][step]
        row, col = place.gy * height, 2 * place.gx * width
        for hop in range(place.cols_x - 1):
            source = self.x_second[index].at[step, hop]
            if hop == place.cols_x - 2:
                add_segments(total, source, row, col, self.segments[index][0], out)
            else:
                add_rows(total, source, row, height, col, width)
        for hop in range(place.rows_y - 1):
            source = self.y_second[index].at[step, hop]
            if hop == place.rows_y - 2:
                add_segments(total, source, row, col, self.segments[index][1], out)
            else:
                add_rows(total, source, row, height, col + width, width)

    def steps(self, stage):
        return [functools.partial(stage, *job) for job in self.jobs]

    def finish(self):
        self.place.sent()


class PlaneSpread:
    def __init__(self, place, outs, first_send, first_recv, second_send, second_recv):
        self.place, self.outs = place, outs
        self.first_sem, self.second_sem = (first_send, first_recv), (second_send, second_recv)
        self.waiting = {}

    def sizes(self, index):
        rows, cols = self.outs[index].shape
        return rows, rows // self.place.rows_y, cols // (2 * self.place.cols_x)

    def total(self, index, piece, others, segments):
        place = self.place
        rows, height, width = self.sizes(index)
        row = place.gy * height
        col = pl.multiple_of(2 * place.gx * width, 128)
        for first, left, _, cols, off in segments[0] + segments[1]:

            def one(turn, carry):
                at = pl.ds(pl.multiple_of(first + turn * 16, 16), 16)
                value = piece[at, pl.ds(left, cols)].astype(jnp.float32)
                for other in others:
                    value = value + other[at, pl.ds(left, cols)].astype(jnp.float32)
                self.outs[index][
                    pl.ds(pl.multiple_of(row + turn * 16, 16), 16), pl.ds(pl.multiple_of(col + off, 128), cols)
                ] = value.astype(jnp.bfloat16)
                return carry

            lax.fori_loop(0, height // 16, one, 0)
        copies = []
        for hop, other in enumerate(place.beside):
            part = window(self.outs[index], row, height, 2 * place.gx * width, width)
            copies.append(place.push(part, part, *self.first_sem, (index, 0, hop), (other, place.me)))
        for hop, other in enumerate(place.along):
            part = window(self.outs[index], row, height, (2 * place.gx + 1) * width, width)
            copies.append(place.push(part, part, *self.first_sem, (index, 1, hop), (other, place.me)))
        self.waiting[index] = copies

    def second(self, index):
        place = self.place
        rows, height, width = self.sizes(index)
        for copy in self.waiting[index]:
            copy.wait_recv()
        copies = []
        for hop, other in enumerate(place.along):
            for spot, column in enumerate([place.gx] + place.beside_from):
                part = window(self.outs[index], place.gy * height, height, 2 * column * width, width)
                copies.append(place.push(part, part, *self.second_sem, (index, 0, hop, spot), (other, place.me)))
        for hop, other in enumerate(place.beside):
            part = window(self.outs[index], 0, rows, (2 * place.gx + 1) * width, width)
            copies.append(place.push(part, part, *self.second_sem, (index, 1, hop, 0), (other, place.me)))
        self.waiting[index] = copies

    def finish(self, index):
        for copy in self.waiting[index]:
            copy.wait_recv()


def small_rows(seq_count, values):
    rows = jnp.concatenate([values, jnp.zeros((32 - values.shape[0], values.shape[1]), jnp.float32)])
    return rows.reshape(seq_count, 32 // seq_count, values.shape[1])


class SmallSum:
    def __init__(self, place, source, total, scratch, first_send, first_recv, second_send, second_recv):
        self.place, self.source, self.total_ref, self.scratch = place, source, total, scratch
        self.first_sem, self.second_sem = (first_send, first_recv), (second_send, second_recv)

    def begin(self):
        place = self.place
        self.waiting = [
            place.push(self.source.at[other], self.scratch.at[step], *self.first_sem, step, (place.grp, other))
            for step, other in enumerate(place.others)
        ]

    def middle(self):
        place = self.place
        value = self.source[place.me]
        for step, copy in enumerate(self.waiting):
            copy.wait_recv()
            value = value + self.scratch[step]
        self.total_ref[place.me] = value
        part = self.total_ref.at[place.me]
        self.waiting = [
            place.push(part, part, *self.second_sem, step, (place.grp, other))
            for step, other in enumerate(place.others)
        ]

    def finish(self):
        for copy in self.waiting:
            copy.wait_recv()


def small_scratch(source):
    seq_count = source.shape[0]
    dma = pltpu.SemaphoreType.DMA
    return [pltpu.VMEM((seq_count - 1,) + source.shape[1:], jnp.float32)] + [dma((seq_count - 1,))] * 4


def forward_kernel(plane, seq_count, count, *refs):
    layers = seq_count // 2
    bound_ref, qkv_ref, shards = refs[0], refs[1], refs[2:2 + count]
    refs = refs[2 + count:]
    pieces, refs = refs[:layers - 1], refs[layers - 1:]
    kept_ref, mixture_ref, log_ref, fulls = refs[0], refs[1], refs[2], refs[3:3 + count]
    (
        key_scr, query_scr, value_t_scr, score_scr, mix_t_scr, mix_scr,
        send_sem, recv_sem, back_send_sem, back_recv_sem, local_sem,
    ) = refs[3 + count:14 + count]
    own_sem, first_send, first_recv, second_send, second_recv, core_send, core_recv = refs[14 + count:]
    group_count, local_rows, local_width = qkv_ref.shape[1], qkv_ref.shape[3], qkv_ref.shape[4]
    total_rows = seq_count * local_rows
    heads = local_width // HEAD_DIM
    me = lax.axis_index("seq")
    grp = lax.axis_index("grp")
    others = [lax.rem(me + step, seq_count) for step in range(1, seq_count)]
    origins = [lax.rem(me + seq_count - step, seq_count) for step in range(1, seq_count)]
    block = min(256, total_rows // 3)
    place = Place(plane, seq_count)
    enter([(grp, other) for other in others] + [(other, me) for other in place.beside + place.along])
    copies = []
    for group in range(group_count):
        own = pltpu.make_async_copy(qkv_ref.at[me, group], kept_ref.at[me, group], local_sem.at[group])
        own.start()
        row = [own]
        for step, other in enumerate(others):
            copy = pltpu.make_async_remote_copy(
                qkv_ref.at[other, group], kept_ref.at[me, group],
                send_sem.at[group, step], recv_sem.at[group, step],
                device_id=(grp, other), device_id_type=MESH,
            )
            copy.start()
            row.append(copy)
        copies.append(row)
    side = place.cols_x
    segments, _ = piece_segments(
        [shard.shape for shard in shards], side, min(shard.shape[1] for shard in shards) // side
    )
    spread = PlaneGather(
        place, shards, pieces, segments, fulls,
        own_sem, first_send, first_recv, second_send, second_recv, core_send, core_recv,
    )
    spread.begin()
    back = []
    for group in range(group_count):
        for copy in copies[group]:
            copy.wait()
        if group == 0:
            spread.middle()
            hooks = spread.late()
            held = len(hooks) // 3
        boundary = bound_ref[group]
        keys = kept_ref[:, group, 1].reshape(total_rows, local_width)
        values = kept_ref[:, group, 2].reshape(total_rows, local_width)
        key_scr[:, :local_width] = keys
        key_scr[:, local_width:] = utter_features(boundary, total_rows, True)
        query_scr[:, local_width:] = utter_features(boundary, total_rows, False)
        value_t_scr[...] = values.astype(jnp.float32).T.astype(jnp.bfloat16)

        for head in range(heads):
            queries = kept_ref[:, group, 0].reshape(total_rows, local_width)
            query_scr[:, :local_width] = head_lanes(queries, head) * jnp.bfloat16(HEAD_DIM ** (-0.5))
            for third in range(3):
                first_key, last_key = key_span(third, total_rows)
                chunks = range(first_key, last_key, block)

                def one_block(index, carry):
                    first_row = pl.multiple_of(third * (total_rows // 3) + index * block, block)
                    query_block = query_scr[pl.ds(first_row, block), :]
                    peak = jnp.full((8, block), -jnp.inf, jnp.float32)
                    for first in chunks:
                        scores = dot_nt(key_scr[first:first + block, :], query_block)
                        score_scr[first:first + block, :] = scores
                        peak = jnp.maximum(peak, fold_rows(scores, jnp.max))
                    peak = jnp.max(peak, axis=0, keepdims=True)
                    total = jnp.zeros((8, block), jnp.float32)
                    for first in chunks:
                        lifted = jnp.exp(score_scr[first:first + block, :] - peak)
                        score_scr[first:first + block, :] = lifted
                        total = total + fold_rows(lifted, jnp.sum)
                    total = jnp.sum(total, axis=0, keepdims=True)
                    inverse = 1.0 / total
                    mixed = jnp.zeros((HEAD_DIM, block), jnp.float32)
                    rows = slice(head * HEAD_DIM, (head + 1) * HEAD_DIM)
                    for first in chunks:
                        weight = (score_scr[first:first + block, :] * inverse).astype(jnp.bfloat16)
                        mixed = mixed + dot_nn(value_t_scr[rows, first:first + block], weight)
                    mix_t_scr[rows, pl.ds(first_row, block)] = mixed
                    log_ref[group, head, :, pl.ds(first_row, block)] = peak + jnp.log(total)
                    return carry

                lax.fori_loop(0, total_rows // 3 // block, one_block, 0)
                if group > 0 and len(hooks) > held:
                    hooks.pop(0)()
        mix_scr[group] = mix_t_scr[...].T.astype(jnp.bfloat16).reshape(seq_count, local_rows, local_width)
        own = pltpu.make_async_copy(
            mix_scr.at[group, me], mixture_ref.at[me, group], local_sem.at[group_count + group]
        )
        own.start()
        back.append(own)
        for step, other in enumerate(others):
            copy = pltpu.make_async_remote_copy(
                mix_scr.at[group, other], mixture_ref.at[me, group],
                back_send_sem.at[group, step], back_recv_sem.at[group, step],
                device_id=(grp, other), device_id_type=MESH,
            )
            copy.start()
            back.append(copy)
    for hook in hooks:
        hook()
    for copy in back:
        copy.wait()
    spread.finish()


def attend_forward(bounds, qkv, shards, pieces):
    side = math.isqrt(lax.axis_size("grp"))
    hops = max(side - 1, 1)
    count = len(shards)
    dma = pltpu.SemaphoreType.DMA
    anywhere = pl.BlockSpec(memory_space=pl.ANY)
    layers = qkv.shape[0] // 2
    seq_count, group_count, _, local_rows, local_width = qkv.shape
    total_rows = seq_count * local_rows
    heads = local_width // HEAD_DIM
    block = min(256, total_rows // 3)
    vmem = pl.BlockSpec(memory_space=pltpu.VMEM)
    return pl.pallas_call(
        functools.partial(forward_kernel, (side, side), seq_count, count),
        out_shape=(
            jax.ShapeDtypeStruct(qkv.shape, jnp.bfloat16),
            jax.ShapeDtypeStruct((seq_count, group_count, local_rows, local_width), jnp.bfloat16),
            jax.ShapeDtypeStruct((group_count, heads, 1, total_rows), jnp.float32),
        ) + tuple(jax.ShapeDtypeStruct((seq_count,) + part.shape, part.dtype) for part in shards),
        in_specs=[pl.BlockSpec(memory_space=pltpu.SMEM)] + [anywhere] * (count + layers),
        out_specs=(vmem, vmem, vmem) + (anywhere,) * count,
        scratch_shapes=[
            pltpu.VMEM((total_rows, local_width + 128), jnp.bfloat16),
            pltpu.VMEM((total_rows, local_width + 128), jnp.bfloat16),
            pltpu.VMEM((local_width, total_rows), jnp.bfloat16),
            pltpu.VMEM((total_rows, block), jnp.float32),
            pltpu.VMEM((local_width, total_rows), jnp.float32),
            pltpu.VMEM((group_count, seq_count, local_rows, local_width), jnp.bfloat16),
            pltpu.SemaphoreType.DMA((group_count, seq_count - 1)),
            pltpu.SemaphoreType.DMA((group_count, seq_count - 1)),
            pltpu.SemaphoreType.DMA((group_count, seq_count - 1)),
            pltpu.SemaphoreType.DMA((group_count, seq_count - 1)),
            pltpu.SemaphoreType.DMA((2 * group_count,)),
            dma((count, layers, 2, 2)),
            dma((count, layers - 1, 2, hops, 2)), dma((count, layers - 1, 2, hops, 2)),
            dma((count, layers - 1, 2, hops, side)), dma((count, layers - 1, 2, hops, side)),
            dma((count, layers)), dma((count, layers)),
        ],
        compiler_params=pltpu.CompilerParams(
            collective_id=1, has_side_effects=True, vmem_limit_bytes=48 * 1024 * 1024
        ),
        name="attend_forward",
    )(bounds, qkv, *shards, *pieces)


def backward_kernel(plane, seq_count, count, *refs):
    layers = seq_count // 2
    bound_ref, kept_ref, grad_ref, log_ref = refs[:4]
    parts, refs = refs[4:4 + count], refs[4 + count:]
    out_ref, refs = refs[0], refs[1:]
    pieces, refs = refs[:layers], refs[layers:]
    (
        taken_scr, key_scr, query_scr, key_t_scr, head_query_scr, head_grad_scr, prob_scr, weight_scr,
        query_t_scr, key_sum_scr, value_sum_scr, back_scr,
        send_sem, recv_sem, back_send_sem, back_recv_sem, local_sem,
    ) = refs[:17]
    buffers, semaphores = refs[17:17 + 6 * count], refs[17 + 6 * count:]
    group_count, local_rows, local_width = grad_ref.shape[1], grad_ref.shape[2], grad_ref.shape[3]
    total_rows = seq_count * local_rows
    heads = local_width // HEAD_DIM
    me = lax.axis_index("seq")
    grp = lax.axis_index("grp")
    others = [lax.rem(me + step, seq_count) for step in range(1, seq_count)]
    block = min(256, total_rows // 3)
    place = Place(plane, seq_count)
    enter([(grp, other) for other in others] + [(other, me) for other in place.beside + place.along])
    copies = []
    for group in range(group_count):
        own = pltpu.make_async_copy(grad_ref.at[me, group], taken_scr.at[me, group], local_sem.at[group])
        own.start()
        row = [own]
        for step, other in enumerate(others):
            copy = pltpu.make_async_remote_copy(
                grad_ref.at[other, group], taken_scr.at[me, group],
                send_sem.at[group, step], recv_sem.at[group, step],
                device_id=(grp, other), device_id_type=MESH,
            )
            copy.start()
            row.append(copy)
        copies.append(row)
    side = place.cols_x
    segments, _ = piece_segments(
        [part.shape[1:] for part in parts], side, min(part.shape[2] for part in parts) // side
    )
    plane_sum = PlaneSum(place, parts, [pieces] * count, segments, buffers, semaphores)
    plane_sum.begin()
    firsts = plane_sum.steps(plane_sum.first)
    seconds = plane_sum.steps(plane_sum.second)
    units = 3 * heads * group_count
    plan = [[] for _ in range(units + 1)]
    for spot, hook in enumerate(firsts):
        plan[spot * (units // 2 - 1) // len(firsts)].append(hook)
    for spot, hook in enumerate(seconds):
        plan[units - 5 + spot * 6 // len(seconds)].append(hook)
    back = []
    for group in range(group_count):
        for copy in copies[group]:
            copy.wait()
        boundary = bound_ref[group]
        keys = kept_ref[:, group, 1].reshape(total_rows, local_width)
        key_scr[:, :local_width] = keys
        key_scr[:, local_width:] = utter_features(boundary, total_rows, True)
        query_scr[:, local_width:] = utter_features(boundary, total_rows, False)
        key_t_scr[...] = keys.astype(jnp.float32).T.astype(jnp.bfloat16)
        key_sum_scr[...] = jnp.zeros_like(key_sum_scr)
        value_sum_scr[...] = jnp.zeros_like(value_sum_scr)

        for head in range(heads):
            queries = head_lanes(kept_ref[:, group, 0].reshape(total_rows, local_width), head)
            head_query_scr[...] = queries
            query_scr[:, :local_width] = queries * jnp.bfloat16(HEAD_DIM ** (-0.5))
            head_grad_scr[...] = head_lanes(taken_scr[:, group].reshape(total_rows, local_width), head)
            for third in range(3):
                first_key, last_key = key_span(third, total_rows)
                chunks = range(first_key, last_key, block)

                def one_block(index, carry):
                    first_row = pl.multiple_of(third * (total_rows // 3) + index * block, block)
                    own_rows = pl.ds(first_row, block)
                    query_block = query_scr[own_rows, :]
                    grad_block = head_grad_scr[own_rows, :]
                    plain_block = head_query_scr[own_rows, :]
                    log_block = log_ref[group, head, :, own_rows]
                    row_dot = jnp.zeros((8, block), jnp.float32)
                    for first in chunks:
                        scores = dot_nt(key_scr[first:first + block, :], query_block)
                        prob = jnp.exp(scores - log_block)
                        values = kept_ref[
                            first // local_rows:(first + block - 1) // local_rows + 1, group, 2
                        ].reshape(-1, local_width)
                        skip = first % local_rows
                        weight_grad = dot_nt(values[skip:skip + block], grad_block)
                        prob_scr[first:first + block, :] = prob
                        weight_scr[first:first + block, :] = weight_grad
                        row_dot = row_dot + fold_rows(prob * weight_grad, jnp.sum)
                    row_dot = jnp.sum(row_dot, axis=0, keepdims=True)
                    rows = slice(head * HEAD_DIM, (head + 1) * HEAD_DIM)
                    turned = jnp.zeros((HEAD_DIM, block), jnp.float32)
                    for first in chunks:
                        prob = prob_scr[first:first + block, :]
                        score_grad = (
                            HEAD_DIM ** (-0.5) * (prob * (weight_scr[first:first + block, :] - row_dot))
                        ).astype(jnp.bfloat16)
                        key_sum_scr[first:first + block, :] += dot_nn(score_grad, plain_block)
                        value_sum_scr[first:first + block, :] += dot_nn(
                            prob.astype(jnp.bfloat16), grad_block
                        )
                        turned = turned + dot_nn(key_t_scr[rows, first:first + block], score_grad)
                    query_t_scr[rows, own_rows] = turned
                    return carry

                lax.fori_loop(0, total_rows // 3 // block, one_block, 0)
                for hook in plan.pop(0):
                    hook()
        shape = (seq_count, local_rows, local_width)
        back_scr[:, group, 0] = query_t_scr[...].T.astype(jnp.bfloat16).reshape(shape)
        back_scr[:, group, 1] = key_sum_scr[...].astype(jnp.bfloat16).reshape(shape)
        back_scr[:, group, 2] = value_sum_scr[...].astype(jnp.bfloat16).reshape(shape)
        own = pltpu.make_async_copy(
            back_scr.at[me, group], out_ref.at[me, group], local_sem.at[group_count + group]
        )
        own.start()
        back.append(own)
        for step, other in enumerate(others):
            copy = pltpu.make_async_remote_copy(
                back_scr.at[other, group], out_ref.at[me, group],
                back_send_sem.at[group, step], back_recv_sem.at[group, step],
                device_id=(grp, other), device_id_type=MESH,
            )
            copy.start()
            back.append(copy)
    for hook in plan[0] + plane_sum.steps(plane_sum.third):
        hook()
    for copy in back:
        copy.wait()
    plane_sum.finish()


def attend_backward(bounds, kept, grad, log_total, parts):
    side = math.isqrt(lax.axis_size("grp"))
    count = len(parts)
    layers = kept.shape[0] // 2
    anywhere = pl.BlockSpec(memory_space=pl.ANY)
    parts = by_owner(parts, kept.shape[0])
    width = min(part.shape[2] for part in parts) // side
    _, piece_rows = piece_segments([part.shape[1:] for part in parts], side, width)
    seq_count, group_count, _, local_rows, local_width = kept.shape
    total_rows = seq_count * local_rows
    block = min(256, total_rows // 3)
    vmem = pl.BlockSpec(memory_space=pltpu.VMEM)
    return pl.pallas_call(
        functools.partial(backward_kernel, (side, side), seq_count, count),
        out_shape=(jax.ShapeDtypeStruct(kept.shape, jnp.bfloat16),) + tuple(
            jax.ShapeDtypeStruct((piece_rows, width), jnp.bfloat16) for _ in range(layers)
        ),
        in_specs=[pl.BlockSpec(memory_space=pltpu.SMEM), vmem, anywhere, vmem] + [anywhere] * count,
        out_specs=(vmem,) * (1 + layers),
        scratch_shapes=[
            pltpu.VMEM(grad.shape, jnp.bfloat16),
            pltpu.VMEM((total_rows, local_width + 128), jnp.bfloat16),
            pltpu.VMEM((total_rows, local_width + 128), jnp.bfloat16),
            pltpu.VMEM((local_width, total_rows), jnp.bfloat16),
            pltpu.VMEM((total_rows, local_width), jnp.bfloat16),
            pltpu.VMEM((total_rows, local_width), jnp.bfloat16),
            pltpu.VMEM((total_rows, block), jnp.float32),
            pltpu.VMEM((total_rows, block), jnp.float32),
            pltpu.VMEM((local_width, total_rows), jnp.float32),
            pltpu.VMEM((total_rows, local_width), jnp.float32),
            pltpu.VMEM((total_rows, local_width), jnp.float32),
            pltpu.VMEM(kept.shape, jnp.bfloat16),
            pltpu.SemaphoreType.DMA((group_count, seq_count - 1)),
            pltpu.SemaphoreType.DMA((group_count, seq_count - 1)),
            pltpu.SemaphoreType.DMA((group_count, seq_count - 1)),
            pltpu.SemaphoreType.DMA((group_count, seq_count - 1)),
            pltpu.SemaphoreType.DMA((2 * group_count,)),
        ] + plane_sum_scratch(parts, side),
        compiler_params=pltpu.CompilerParams(
            collective_id=2, has_side_effects=True, vmem_limit_bytes=60 * 1024 * 1024
        ),
        name="attend_backward",
    )(bounds, kept, grad, log_total, *parts)


class WholeGather(PlaneGather):
    def __init__(self, place, shards, fulls, line_send, line_recv, *semaphores):
        super().__init__(place, shards, None, None, fulls, *semaphores)
        self.line = (line_send, line_recv)
        self.jobs = [(index, step) for index in range(len(shards)) for step in range(place.layers - 1)]
        self.lines = {}

    def begin(self):
        place = self.place
        for index, step in self.jobs:
            rows, height, width = self.sizes(index)
            row, col = place.gy * height, 2 * place.gx * width
            self.lines[index, step] = place.push(
                window(self.shards[index], row, height, col, 2 * width),
                window(self.fulls[index].at[place.me], row, height, col, 2 * width),
                *self.line, (index, step), (place.grp, place.lines[step]),
            )
        for index, shard in enumerate(self.shards):
            copy = pltpu.make_async_copy(shard, self.fulls[index].at[place.me], self.own_sem.at[index, place.layers - 1, 0, 0])
            copy.start()
            push = place.push(shard, self.fulls[index].at[place.me], *self.core, (index, 0), (place.grp, place.partner))
            self.own.append((copy, push))

    def spread_first(self, index, step):
        place = self.place
        rows, height, width = self.sizes(index)
        self.lines[index, step].wait_recv()
        full = self.fulls[index].at[place.line_from[step]]
        row, col = place.gy * height, 2 * place.gx * width
        self.waiting[index, step] = []
        for half, partners in enumerate((place.beside, place.along)):
            part = window(full, row, height, col + half * width, width)
            for hop, other in enumerate(partners):
                self.waiting[index, step].append(
                    place.push(part, part, *self.first, (index, step, half, hop, 0), (other, place.me))
                )

    def steps(self):
        lag = self.place.layers - 1
        done = []
        for turn in range(len(self.jobs) + 2 * lag):
            if turn < len(self.jobs):
                done.append(functools.partial(self.spread_first, *self.jobs[turn]))
            if 0 <= turn - lag < len(self.jobs):
                done.append(functools.partial(self.spread_second, *self.jobs[turn - lag]))
            if 0 <= turn - 2 * lag < len(self.jobs):
                done.append(functools.partial(self.over_core, *self.jobs[turn - 2 * lag]))
        return done


def gather_kernel(plane, seq_count, count, *refs):
    shards, (partial_ref, token_ref), refs = refs[:count], refs[count:count + 2], refs[count + 2:]
    fulls, (total_ref, tokens_ref), refs = refs[:count], refs[count:count + 2], refs[count + 2:]
    token_scr, token_send, token_recv = refs[:3]
    small_refs, refs = refs[3:8], refs[8:]
    place = Place(plane, seq_count)
    enter([(place.grp, other) for other in place.others] + [(other, place.me) for other in place.groups])
    whole = WholeGather(place, shards, fulls, *refs)
    whole.begin()
    small = SmallSum(place, partial_ref, total_ref, *small_refs)
    small.begin()
    hooks = whole.steps()
    for hook in hooks[:len(hooks) // 2]:
        hook()
    small.middle()
    for hook in hooks[len(hooks) // 2:]:
        hook()
    small.finish()
    last = total_ref.shape[1] - 1
    token_scr[...] = token_ref[...]
    token_scr[4:5, :] = total_ref[seq_count - 1, last:last + 1, :128]
    tokens_ref[place.grp] = token_scr[...]
    tokens = [
        place.push(token_scr, tokens_ref.at[place.grp], token_send, token_recv, step, (other, place.me))
        for step, other in enumerate(place.groups)
    ]
    whole.finish()
    for copy in tokens:
        copy.wait_recv()


def gather(collective, partial, token, *shards):
    grp_count = lax.axis_size("grp")
    seq_count = lax.axis_size("seq")
    side = math.isqrt(grp_count)
    layers = seq_count // 2
    count = len(shards)
    anywhere = pl.BlockSpec(memory_space=pl.ANY)
    vmem = pl.BlockSpec(memory_space=pltpu.VMEM)
    dma = pltpu.SemaphoreType.DMA
    hops = max(side - 1, 1)
    outs = pl.pallas_call(
        functools.partial(gather_kernel, (side, side), seq_count, count),
        out_shape=tuple(
            jax.ShapeDtypeStruct((seq_count,) + part.shape, part.dtype) for part in shards
        ) + (
            jax.ShapeDtypeStruct(partial.shape, jnp.float32),
            jax.ShapeDtypeStruct((grp_count,) + token.shape, jnp.float32),
        ),
        in_specs=[anywhere] * count + [vmem] * 2,
        out_specs=(anywhere,) * count + (vmem,) * 2,
        scratch_shapes=[
            pltpu.VMEM(token.shape, jnp.float32), dma((grp_count - 1,)), dma((grp_count - 1,))
        ] + small_scratch(partial) + [
            dma((count, layers - 1)), dma((count, layers - 1)),
            dma((count, layers, 1, 1)),
            dma((count, layers - 1, 2, hops, 1)), dma((count, layers - 1, 2, hops, 1)),
            dma((count, layers - 1, 2, hops, side)), dma((count, layers - 1, 2, hops, side)),
            dma((count, layers)), dma((count, layers)),
        ],
        compiler_params=pltpu.CompilerParams(collective_id=collective, has_side_effects=True),
        name="gather_weights",
    )(*shards, partial, token)
    return outs[:count], outs[count], outs[count + 1]


def reduce_kernel(plane, seq_count, count, done_count, *refs):
    layers = seq_count // 2
    parts, refs = refs[:count], refs[count:]
    finished, refs = refs[:layers], refs[layers:]
    utter_ref, modulation_ref, refs = refs[0], refs[1], refs[2:]
    outs, refs = refs[:count + done_count], refs[count + done_count:]
    total_ref, utters_ref, conditions_ref, refs = refs[0], refs[1], refs[2], refs[3:]
    condition_scr, token_send, token_recv, last_send, last_recv, line_send, line_recv = refs[:7]
    small_refs, spread_sems, refs = refs[7:12], refs[12:16], refs[16:]
    lines, refs = refs[:count], refs[count:]
    pieces = [refs[index * layers:(index + 1) * layers] for index in range(count)]
    refs = refs[count * layers:]
    buffers, semaphores = refs[:6 * count], refs[6 * count:]
    place = Place(plane, seq_count)
    enter([(place.grp, other) for other in place.others] + [(other, place.me) for other in place.groups])
    side = place.cols_x
    segments = [
        piece_segments([part.shape[1:]], side, part.shape[2] // side)[0][0] for part in parts
    ]
    done_segments, _ = piece_segments(
        [out.shape for out in outs[count:]], side, min(out.shape[1] for out in outs[count:]) // side
    )
    plane_sum = PlaneSum(place, parts, pieces, segments, buffers, semaphores)
    plane_sum.begin()
    small = SmallSum(place, utter_ref, total_ref, *small_refs)
    small.begin()
    spread = PlaneSpread(place, outs, *spread_sems)
    late = []
    for index in range(done_count):
        spread.total(count + index, finished[0], finished[1:], done_segments[index])
        late.append(functools.partial(spread.second, count + index))
    arrived = {}

    def along_line(index, step):
        plane_sum.third(index, step)
        if step < layers - 1:
            arrived[index, step] = place.push(
                pieces[index][step], lines[index].at[step], line_send, line_recv, (index, step),
                (place.grp, place.lines[step]),
            )

    def last(index):
        for step in range(layers - 1):
            arrived[index, step].wait_recv()
        spread.total(index, pieces[index][layers - 1], [lines[index].at[step] for step in range(layers - 1)], segments[index])

    jobs = plane_sum.jobs
    lag = layers
    hooks = []
    for turn in range(len(jobs) + 4 * lag):
        if turn < len(jobs):
            hooks.append(functools.partial(plane_sum.first, *jobs[turn]))
        if turn >= lag + 1 and late:
            hooks.append(late.pop(0))
        if 0 <= turn - lag < len(jobs):
            hooks.append(functools.partial(plane_sum.second, *jobs[turn - lag]))
        if 0 <= turn - 2 * lag < len(jobs):
            hooks.append(functools.partial(along_line, *jobs[turn - 2 * lag]))
        done = turn - 3 * lag
        if 0 <= done < len(jobs) and done % layers == layers - 1:
            hooks.append(functools.partial(last, done // layers))
        done = turn - 4 * lag
        if 0 <= done < len(jobs) and done % layers == layers - 1:
            hooks.append(functools.partial(spread.second, done // layers))
    middle = len(hooks) // 3
    for hook in hooks[:middle]:
        hook()
    small.middle()
    for hook in hooks[middle:2 * middle]:
        hook()
    small.finish()
    utters_ref[place.grp] = total_ref[...]
    tokens = [
        place.push(total_ref, utters_ref.at[place.grp], token_send, token_recv, step, (other, place.me))
        for step, other in enumerate(place.groups)
    ]
    block, width = total_ref.shape[1], total_ref.shape[2]
    rows = modulation_ref.shape[1] // width
    utter_rows = utter_ref.shape[0] * block // 8
    condition_scr[...] = jnp.zeros_like(condition_scr)
    shard_rows = modulation_ref.shape[0]
    for spot in range(rows * utter_rows // block):
        part, row = spot * block // utter_rows, spot * block % utter_rows
        condition_scr[row:row + block, :shard_rows] += dot_nt(
            total_ref[spot].astype(jnp.bfloat16), modulation_ref[:, part * width:(part + 1) * width]
        )
    conditions_ref[place.me] = condition_scr[...]
    tokens += [
        place.push(condition_scr, conditions_ref.at[place.me], last_send, last_recv, step, (place.grp, other))
        for step, other in enumerate(place.others)
    ]
    for hook in hooks[2 * middle:]:
        hook()
    place.sent()
    for copy in tokens:
        copy.wait_recv()
    for index in range(count + done_count):
        spread.finish(index)


def reduce_shares(collective, utter, modulation, parts, finished, done_shapes):
    grp_count = lax.axis_size("grp")
    seq_count = lax.axis_size("seq")
    side = math.isqrt(grp_count)
    layers = seq_count // 2
    count, done_count = len(parts), len(done_shapes)
    parts = by_owner(parts, seq_count)
    anywhere = pl.BlockSpec(memory_space=pl.ANY)
    vmem = pl.BlockSpec(memory_space=pltpu.VMEM)
    dma = pltpu.SemaphoreType.DMA
    hops = max(side - 1, 1)
    pieces = [
        pltpu.VMEM((part.shape[1] // side, part.shape[2] // side), jnp.bfloat16)
        for part in parts for _ in range(layers)
    ]
    lines = [
        pltpu.VMEM((layers - 1, part.shape[1] // side, part.shape[2] // side), jnp.bfloat16) for part in parts
    ]
    total = count + done_count
    outs = pl.pallas_call(
        functools.partial(reduce_kernel, (side, side), seq_count, count, done_count),
        out_shape=tuple(jax.ShapeDtypeStruct(part.shape[1:], jnp.bfloat16) for part in parts) + tuple(
            jax.ShapeDtypeStruct(shape, jnp.bfloat16) for shape in done_shapes
        ) + (
            jax.ShapeDtypeStruct(utter.shape, jnp.float32),
            jax.ShapeDtypeStruct((grp_count,) + utter.shape, jnp.float32),
            jax.ShapeDtypeStruct((seq_count, 8, 128), jnp.float32),
        ),
        in_specs=[anywhere] * count + [vmem] * (layers + 2),
        out_specs=(vmem,) * (total + 3),
        scratch_shapes=[
            pltpu.VMEM((8, 128), jnp.float32),
            dma((grp_count - 1,)), dma((grp_count - 1,)),
            dma((seq_count - 1,)), dma((seq_count - 1,)),
            dma((count, layers - 1)), dma((count, layers - 1)),
        ] + small_scratch(utter) + [
            dma((total, 2, hops)), dma((total, 2, hops)),
            dma((total, 2, hops, side)), dma((total, 2, hops, side)),
        ] + lines + pieces + plane_sum_scratch(parts, side),
        compiler_params=pltpu.CompilerParams(
            collective_id=collective, has_side_effects=True, vmem_limit_bytes=60 * 1024 * 1024
        ),
        name="reduce_shares",
    )(*parts, *finished, utter, modulation)
    return outs[:total], outs[total + 1], outs[total + 2]


def line_shift(values, step):
    seq_count = lax.axis_size("seq")
    turned = [(spot, (spot + 2 * step) % seq_count) for spot in range(seq_count)]
    return lax.ppermute(values, "seq", turned)


def line_pieces(shards):
    side = math.isqrt(lax.axis_size("grp"))
    layers = lax.axis_size("seq") // 2
    grp = lax.axis_index("grp")
    width = min(shard.shape[1] for shard in shards) // side
    blocks = []
    for shard in shards:
        height, cols = shard.shape[0] // side, shard.shape[1] // side
        for off in range(0, cols, width):
            blocks.append(lax.dynamic_slice(
                shard, (grp // side * height, lax.rem(grp, side) * cols + off), (height, width)
            ))
    joined = jnp.concatenate(blocks)
    return [line_shift(joined, step) for step in range(1, layers)]


def shards(
    frames,
    shortcut,
    time_embed,
    lengths,
    kept_mask,
    target,
    combine,
    modulation,
    projection,
    readout,
    expand,
    contract,
):
    group_count = frames.shape[0]
    local_rows = frames.shape[1]
    width = HEADS * HEAD_DIM
    row_count = group_count * local_rows
    seq_count = lax.axis_size("seq")
    group_frames = local_rows * seq_count
    all_frames = group_frames * lax.axis_size("grp") * group_count
    utter_count = time_embed.shape[1]
    kept_float = kept_mask.astype(jnp.float32).reshape(row_count)
    local_index = lax.axis_index("seq") * local_rows + jnp.arange(local_rows, dtype=jnp.int32)

    def local_info(length_row):
        return segment_info(length_row, local_index)

    member_info = jax.vmap(local_info)(lengths)
    member_float = member_info[1].astype(jnp.float32)
    position = member_info[2]
    cos_table, sin_table = rotary_tables(position.reshape(row_count))
    silu_value, silu_pull = jax.vjp(jax.nn.silu, time_embed)
    condition = silu_value.astype(jnp.bfloat16)
    shard_rows = modulation.shape[0]
    utter_rows = group_count * utter_count
    condition_part = lax.dynamic_slice_in_dim(
        condition, lax.axis_index("seq") * shard_rows, shard_rows, 2
    ).reshape(utter_rows, shard_rows)
    partial = small_rows(
        seq_count, product(condition_part, modulation).reshape(6 * utter_rows, width)
    )
    partial = partial.at[seq_count - 1, 32 // seq_count - 1, 0].set(jnp.sum(kept_float))
    token = jnp.zeros((8, 128), jnp.float32)
    token = token.at[:utter_rows, :shard_rows].set(condition_part.astype(jnp.float32))
    late_shards = (readout, expand, contract)
    (combine_full, projection_full), partial_total, tokens = gather(3, partial, token, combine, projection)
    late_pieces = line_pieces(lax.optimization_barrier((late_shards, tokens))[0])
    combine_full = combine_full.reshape(2 * width, width)
    projection_full = projection_full.reshape(width, 3 * width)
    kept_total = jnp.sum(tokens[:, 4, 0])
    condition_all = tokens[:, :utter_rows, :shard_rows].reshape(-1, shard_rows).astype(jnp.bfloat16)
    joined = jnp.concatenate([frames, shortcut], axis=2).reshape(row_count, 2 * width)
    hidden = product(joined, combine_full)
    modulation_utter = partial_total.reshape(32, width)[:6 * utter_rows].reshape(
        group_count, utter_count, 6 * width
    )
    modulation_frame = jnp.einsum(
        "gtu,gue->gte",
        member_float,
        modulation_utter,
        precision=precise,
        preferred_element_type=jnp.float32,
    ).reshape(row_count, 6 * width)
    shift_first, scale_first, gate_first, shift_second, scale_second, gate_second = jnp.split(
        modulation_frame, 6, axis=1
    )
    normed_value, first_pull = jax.vjp(modulate, hidden, shift_first, scale_first)
    normed = normed_value.astype(jnp.bfloat16)
    packed = product(normed, projection_full)
    query_raw, key_raw, value_raw = jnp.split(packed, 3, axis=1)
    head_shape = (row_count, HEADS, HEAD_DIM)
    split_shape = (group_count, local_rows, width)

    def rotate_local(vectors):
        return rotate(vectors, cos_table, sin_table)

    query_turned, query_pull = jax.vjp(rotate_local, query_raw.reshape(head_shape))
    key_turned, key_pull = jax.vjp(rotate_local, key_raw.reshape(head_shape))
    local_width = width // seq_count

    def by_target(vectors):
        return vectors.reshape(group_count, local_rows, seq_count, local_width).astype(jnp.bfloat16)

    qkv = jnp.transpose(
        jnp.stack([by_target(query_turned), by_target(key_turned), by_target(value_raw)]),
        (3, 1, 0, 2, 4),
    )
    bounds = lengths[:, 0]
    kept_heads, mixture_blocks, log_total, *late_full = attend_forward(
        bounds, qkv, late_shards, late_pieces
    )
    readout_full = late_full[0].reshape(width, width)
    expand_full = late_full[1].reshape(width, -1)
    contract_full = late_full[2].reshape(-1, width)
    mixture = jnp.transpose(mixture_blocks, (1, 2, 0, 3)).reshape(row_count, width)
    branch = product(mixture, readout_full)
    middle = hidden + gate_first * branch
    second_value, second_pull = jax.vjp(modulate, middle, shift_second, scale_second)
    normed_second = second_value.astype(jnp.bfloat16)
    expanded = product(normed_second, expand_full)
    active_value, gelu_pull = jax.vjp(gelu_tanh, expanded)
    active = active_value.astype(jnp.bfloat16)
    contracted = product(active, contract_full)
    output = middle + gate_second * contracted
    loss_scale = all_frames / kept_total
    output_grad = (
        loss_scale
        * kept_float[:, None]
        * (output - target.reshape(row_count, width).astype(jnp.float32))
    )
    combine_back, projection_back, readout_back, expand_back, contract_back = (
        combine_full, projection_full, readout_full, expand_full, contract_full
    )
    gate_second_grad = output_grad * contracted
    contracted_grad = (gate_second * output_grad).astype(jnp.bfloat16)
    contract_part = product_left(active, contracted_grad)
    active_grad = product_right(contracted_grad, contract_back)
    expanded_grad = gelu_pull(active_grad)[0].astype(jnp.bfloat16)
    expand_part = product_left(normed_second, expanded_grad)
    normed_second_grad = product_right(expanded_grad, expand_back)
    middle_extra, shift_second_grad, scale_second_grad = second_pull(normed_second_grad)
    middle_grad = output_grad + middle_extra
    gate_first_grad = middle_grad * branch
    branch_grad = (gate_first * middle_grad).astype(jnp.bfloat16)
    readout_part = product_left(mixture, branch_grad)
    mixture_grad = product_right(branch_grad, readout_back).astype(jnp.bfloat16)
    back_blocks, *plane_pieces = attend_backward(
        bounds,
        kept_heads,
        jnp.transpose(
            mixture_grad.reshape(group_count, local_rows, seq_count, local_width), (2, 0, 1, 3)
        ),
        log_total,
        [part.astype(jnp.bfloat16) for part in (contract_part, expand_part, readout_part)],
    )
    layers = seq_count // 2
    finished = [plane_pieces[layers - 1]] + [
        line_shift(plane_pieces[step], step + 1) for step in range(layers - 1)
    ]
    query_back, key_back, value_back = jnp.transpose(back_blocks, (2, 1, 3, 0, 4)).reshape(
        3, group_count, local_rows, width
    )
    query_unturned = query_pull(query_back.reshape(head_shape).astype(jnp.float32))[0].reshape(
        row_count, width
    )
    key_unturned = key_pull(key_back.reshape(head_shape).astype(jnp.float32))[0].reshape(
        row_count, width
    )
    packed_grad = jnp.concatenate(
        [
            query_unturned.astype(jnp.bfloat16),
            key_unturned.astype(jnp.bfloat16),
            value_back.reshape(row_count, width),
        ],
        axis=1,
    )
    projection_part = product_left(normed, packed_grad)
    normed_grad = product_right(packed_grad, projection_back)
    hidden_extra, shift_first_grad, scale_first_grad = first_pull(normed_grad)
    hidden_grad = (middle_grad + hidden_extra).astype(jnp.bfloat16)
    combine_part = product_left(joined, hidden_grad)
    joined_grad = product_right(hidden_grad, combine_back)
    frames_grad = joined_grad[:, :width].reshape(split_shape)
    shortcut_grad = joined_grad[:, width:].reshape(split_shape)
    modulation_frame_grad = jnp.concatenate(
        [
            shift_first_grad,
            scale_first_grad,
            gate_first_grad,
            shift_second_grad,
            scale_second_grad,
            gate_second_grad,
        ],
        axis=1,
    )
    utter_part = jnp.einsum(
        "gtu,gte->gue",
        member_float,
        modulation_frame_grad.reshape(group_count, local_rows, 6 * width),
        precision=precise,
        preferred_element_type=jnp.float32,
    )
    utter_block = jnp.transpose(
        utter_part.reshape(utter_rows, 6, width), (1, 0, 2)
    ).reshape(6 * utter_rows, width)
    shares, utters, condition_back = reduce_shares(
        4,
        small_rows(seq_count, utter_block),
        modulation,
        [projection_part.astype(jnp.bfloat16), combine_part.astype(jnp.bfloat16)],
        finished,
        [contract.shape, expand.shape, readout.shape],
    )
    projection_grad, combine_grad, contract_grad, expand_grad, readout_grad = [
        share.astype(jnp.float32) for share in shares
    ]
    utter_all = jnp.transpose(
        utters.reshape(-1, 32, width)[:, :6 * utter_rows].reshape(-1, 6, utter_rows, width), (0, 2, 1, 3)
    ).reshape(-1, 6 * width).astype(jnp.bfloat16)
    modulation_grad = product_left(condition_all, utter_all)
    condition_grad = jnp.transpose(
        condition_back[:, :utter_rows, :shard_rows], (1, 0, 2)
    ).reshape(group_count, utter_count, width)
    time_grad = silu_pull(condition_grad)[0]
    summed = (combine_grad, modulation_grad, projection_grad, readout_grad, expand_grad, contract_grad)
    return (
        output.astype(jnp.bfloat16).reshape(split_shape),
        frames_grad,
        shortcut_grad,
        time_grad,
        summed[0],
        summed[1],
        summed[2],
        summed[3],
        summed[4],
        summed[5],
    )


def solution(mesh):
    return jax.shard_map(
        shards,
        mesh=mesh,
        in_specs=(
            P("grp", "seq", None),
            P("grp", "seq", None),
            P("grp", None, None),
            P("grp", None),
            P("grp", "seq"),
            P("grp", "seq", None),
            P("seq", None),
            P("seq", None),
            P("seq", None),
            P("seq", None),
            P("seq", None),
            P("seq", None),
        ),
        out_specs=(
            P("grp", "seq", None),
            P("grp", "seq", None),
            P("grp", "seq", None),
            P("grp", None, None),
            P("seq", None),
            P("seq", None),
            P("seq", None),
            P("seq", None),
            P("seq", None),
            P("seq", None),
        ),
        check_vma=False,
    )
```

```python
import functools
import math

import jax
import jax.numpy as jnp
from jax import lax
from jax.experimental import pallas as pl
from jax.experimental.pallas import tpu as pltpu
from jax.sharding import PartitionSpec as P

HEADS = 16
HEAD_DIM = 64


precise = lax.Precision.HIGHEST
epsilon = 1e-06
rope_base = 10000.0


def product(first_op, second_op):
    return jnp.dot(first_op, second_op, preferred_element_type=jnp.float32)


def product_left(first_op, second_op):
    return lax.dot_general(
        first_op, second_op, (((0,), (0,)), ((), ())), preferred_element_type=jnp.float32
    )


def product_right(first_op, second_op):
    return lax.dot_general(
        first_op, second_op, (((1,), (1,)), ((), ())), preferred_element_type=jnp.float32
    )


def gelu_tanh(values):
    return jax.nn.gelu(values, approximate=True)


def modulate(hidden, shift_part, scale_part):
    center = hidden - jnp.mean(hidden, axis=-1, keepdims=True)
    variance = jnp.mean(center * center, axis=-1, keepdims=True)
    return center * lax.rsqrt(variance + epsilon) * (1.0 + scale_part) + shift_part


def segment_info(lengths, frame_index):
    utter_count = lengths.shape[0]
    utter_ends = jnp.cumsum(lengths)
    starts = utter_ends - lengths
    segment = jnp.sum((frame_index[:, None] >= utter_ends[None, :]).astype(jnp.int32), axis=1)
    member = segment[:, None] == jnp.arange(utter_count, dtype=jnp.int32)[None, :]
    offset = jnp.sum(jnp.where(member, starts[None, :], 0), axis=1)
    return (segment, member, frame_index - offset)


def rotary_tables(position):
    half_dim = HEAD_DIM // 2
    ladder = jnp.arange(half_dim, dtype=jnp.float32) / half_dim
    inverse = jnp.exp(-jnp.log(rope_base) * ladder)
    angles = position.astype(jnp.float32)[:, None] * inverse[None, :]
    return (jnp.cos(angles)[:, None, :], jnp.sin(angles)[:, None, :])


def rotate(vectors, cos_table, sin_table):
    half_dim = vectors.shape[-1] // 2
    front_half = vectors[..., :half_dim]
    back_half = vectors[..., half_dim:]
    return jnp.concatenate(
        [
            front_half * cos_table - back_half * sin_table,
            back_half * cos_table + front_half * sin_table,
        ],
        axis=-1,
    )


MESH = pl.DeviceIdType.MESH
NEG = -1e30


def utter_features(boundary, total_rows, for_keys):
    row = lax.broadcasted_iota(jnp.int32, (total_rows, 128), 0)
    lane = lax.broadcasted_iota(jnp.int32, (total_rows, 128), 1)
    second = (row >= boundary).astype(jnp.float32)
    ahead = (lane == 0).astype(jnp.float32)
    after = (lane == 1).astype(jnp.float32)
    if for_keys:
        return (NEG * (second * ahead + (1.0 - second) * after)).astype(jnp.bfloat16)
    return (second * after + (1.0 - second) * ahead).astype(jnp.bfloat16)


def head_lanes(values, head):
    lane = lax.broadcasted_iota(jnp.int32, values.shape, 1)
    own = (lane >= head * HEAD_DIM) & (lane < (head + 1) * HEAD_DIM)
    return jnp.where(own, values.astype(jnp.float32), 0.0).astype(jnp.bfloat16)


def dot_nn(first_op, second_op):
    return jnp.dot(first_op, second_op, preferred_element_type=jnp.float32)


def dot_nt(first_op, second_op):
    return lax.dot_general(
        first_op, second_op, (((1,), (1,)), ((), ())), preferred_element_type=jnp.float32
    )


def fold_rows(values, combine):
    return combine(values.reshape(values.shape[0] // 8, 8, values.shape[1]), axis=0)


def enter(partners):
    barrier = pltpu.get_barrier_semaphore()
    for partner in partners:
        pl.semaphore_signal(barrier, inc=1, device_id=partner, device_id_type=MESH)
    pl.semaphore_wait(barrier, len(partners))


def key_span(third, total_rows):
    size = total_rows // 3
    return (max(third - 1, 0) * size, min(third + 2, 3) * size)


class Place:
    def __init__(self, plane, seq_count):
        self.rows_y, self.cols_x = rows_y, cols_x = plane
        self.grp, self.me = grp, me = lax.axis_index("grp"), lax.axis_index("seq")
        self.gy, self.gx = gy, gx = grp // cols_x, lax.rem(grp, cols_x)
        self.layers = layers = seq_count // 2
        self.layer, self.core = layer, core = me // 2, lax.rem(me, 2)
        self.xs = [lax.rem(gx + step, cols_x) for step in range(1, cols_x)]
        self.ys = [lax.rem(gy + step, rows_y) for step in range(1, rows_y)]
        self.beside = [gy * cols_x + x for x in self.xs]
        self.along = [y * cols_x + gx for y in self.ys]
        self.beside_from = [lax.rem(gx + cols_x - step, cols_x) for step in range(1, cols_x)]
        self.far = [lax.rem(layer + step, layers) for step in range(1, layers)]
        self.line_from = [lax.rem(layer + layers - step, layers) * 2 + core for step in range(1, layers)]
        self.lines = [target * 2 + core for target in self.far]
        self.partner = layer * 2 + 1 - core
        self.others = [lax.rem(me + step, seq_count) for step in range(1, seq_count)]
        self.groups = [lax.rem(grp + step, rows_y * cols_x) for step in range(1, rows_y * cols_x)]
        self.started = []

    def push(self, src, dst, sends, recvs, slot, device):
        copy = pltpu.make_async_remote_copy(
            src, dst, sends.at[slot], recvs.at[slot], device_id=device, device_id_type=MESH
        )
        copy.start()
        self.started.append(copy)
        return copy

    def sent(self):
        for copy in self.started:
            copy.wait_send()
        self.started = []


def window(ref, row, rows, col, cols):
    return ref.at[pl.ds(pl.multiple_of(row, 16), rows), pl.ds(pl.multiple_of(col, 128), cols)]


def piece_segments(shapes, side, width):
    base, found = 0, []
    for rows, cols in shapes:
        height, many = rows // side, cols // side // width
        if many == 1:
            half = width // 2
            found.append([[(base, 0, height, half, 0)], [(base, half, height, half, half)]])
        else:
            blocks = [(base + spot * height, 0, height, width, spot * width) for spot in range(many)]
            found.append([blocks[:many // 2], blocks[many // 2:]])
        base += height * many
    return found, base


class PlaneGather:
    def __init__(self, place, shards, pieces, segments, fulls, own_sem, first_send, first_recv, second_send, second_recv, core_send, core_recv):
        self.place, self.shards, self.pieces, self.fulls = place, shards, pieces, fulls
        self.segments = segments
        self.own_sem = own_sem
        self.first = (first_send, first_recv)
        self.second = (second_send, second_recv)
        self.core = (core_send, core_recv)
        self.jobs = [(index, step) for step in range(place.layers - 1) for index in range(len(shards))]
        self.waiting, self.local, self.own = {}, {}, []

    def sizes(self, index):
        _, rows, cols = self.fulls[index].shape
        return rows, rows // self.place.rows_y, cols // (2 * self.place.cols_x)

    def begin(self):
        place = self.place
        for index, step in self.jobs:
            self.spread_first(index, step)
        for index, shard in enumerate(self.shards):
            copy = pltpu.make_async_copy(shard, self.fulls[index].at[place.me], self.own_sem.at[index, place.layers - 1, 0, 0])
            copy.start()
            push = place.push(shard, self.fulls[index].at[place.me], *self.core, (index, 0), (place.grp, place.partner))
            self.own.append((copy, push))

    def spread_first(self, index, step):
        place = self.place
        rows, height, width = self.sizes(index)
        full = self.fulls[index].at[place.line_from[step]]
        piece = self.pieces[step]
        first_row, first_col = place.gy * height, 2 * place.gx * width
        self.local[index, step] = []
        self.waiting[index, step] = []
        for half, partners in enumerate((place.beside, place.along)):
            for spot, (row, col, rows, cols, off) in enumerate(self.segments[index][half]):
                source = piece.at[pl.ds(row, rows), pl.ds(col, cols)]
                part = window(full, first_row, rows, first_col + off, cols)
                copy = pltpu.make_async_copy(source, part, self.own_sem.at[index, step, half, spot])
                copy.start()
                self.local[index, step].append(copy)
                for hop, other in enumerate(partners):
                    self.waiting[index, step].append(place.push(
                        source, part, *self.first, (index, step, half, hop, spot), (other, place.me)
                    ))

    def spread_second(self, index, step):
        place = self.place
        rows, height, width = self.sizes(index)
        for copy in self.local.get((index, step), []):
            copy.wait()
        for copy in self.waiting[index, step]:
            copy.wait_recv()
        full = self.fulls[index].at[place.line_from[step]]
        copies = []
        for hop, other in enumerate(place.along):
            for spot, column in enumerate([place.gx] + place.beside_from):
                part = window(full, place.gy * height, height, 2 * column * width, width)
                copies.append(place.push(part, part, *self.second, (index, step, 0, hop, spot), (other, place.me)))
        for hop, other in enumerate(place.beside):
            part = window(full, 0, rows, (2 * place.gx + 1) * width, width)
            copies.append(place.push(part, part, *self.second, (index, step, 1, hop, 0), (other, place.me)))
        self.waiting[index, step] = copies

    def over_core(self, index, step):
        place = self.place
        for copy in self.waiting[index, step]:
            copy.wait_recv()
        full = self.fulls[index].at[place.line_from[step]]
        self.waiting[index, step] = [
            place.push(full, full, *self.core, (index, step + 1), (place.grp, place.partner))
        ]

    def middle(self):
        for job in self.jobs:
            self.spread_second(*job)

    def late(self):
        return [functools.partial(self.over_core, *job) for job in self.jobs]

    def finish(self):
        self.place.sent()
        for job in self.jobs:
            for copy in self.waiting[job]:
                copy.wait_recv()
        for copy, push in self.own:
            copy.wait()
            push.wait_recv()


def add_rows(target, source, first_row, rows, first_col, cols, out=None):
    step = 16
    col = pl.multiple_of(first_col, 128)

    def one(index, carry):
        at = pl.ds(pl.multiple_of(first_row + index * step, step), step)
        off = pl.ds(pl.multiple_of(index * step, step), step)
        value = target[at, pl.ds(col, cols)] + source[off, :]
        if out is None:
            target[at, pl.ds(col, cols)] = value
        else:
            out[off, :] = value
        return carry

    lax.fori_loop(0, rows // step, one, 0)


def add_segments(target, source, first_row, first_col, segments, out):
    for row, col, rows, cols, off in segments:
        begin = off - segments[0][4]
        add_rows(
            target, source.at[:, pl.ds(begin, cols)], first_row, rows, first_col + off, cols,
            out.at[pl.ds(row, rows), pl.ds(col, cols)],
        )


def plane_sum_scratch(parts, side, in_place=False):
    layers = parts[0].shape[0] // 2
    hops = max(side - 1, 1)
    count = len(parts)
    dma = pltpu.SemaphoreType.DMA

    def buffers(lead, row_cut, col_cut):
        return [
            pltpu.VMEM(lead + (part.shape[1] // row_cut, part.shape[2] // col_cut), jnp.bfloat16)
            for part in parts
        ]

    return (
        ([] if in_place else buffers((layers,), 1, 1))
        + buffers((layers,), 1, 1)
        + buffers((layers, hops, side), side, 2 * side)
        + buffers((layers, hops), side, 2 * side)
        + buffers((layers, hops), 1, 2 * side)
        + buffers((layers, hops), side, 2 * side)
        + [
            dma((count, layers)), dma((count, layers)), dma((count, layers)),
            dma((count, layers, 2, hops, side)), dma((count, layers, 2, hops, side)),
            dma((count, layers, 2, hops)), dma((count, layers, 2, hops)),
        ]
    )


def by_owner(parts, seq_count):
    return [part.reshape(seq_count, part.shape[0] // seq_count, part.shape[1]) for part in parts]


class PlaneSum:
    def __init__(self, place, parts, pieces, segments, buffers, semaphores, in_place=False):
        self.place, self.parts, self.pieces, self.segments = place, parts, pieces, segments
        count = len(parts)
        buffers = (() if in_place else buffers[:count], *[
            buffers[index * count:(index + 1) * count] for index in range(0 if in_place else 1, 5 if in_place else 6)
        ])
        self.in_place = in_place
        self.sums, self.swapped, self.y_first, self.x_second, self.x_first, self.y_second = buffers
        self.load_sem = semaphores[0]
        self.core, self.first_sem, self.second_sem = semaphores[1:3], semaphores[3:5], semaphores[5:7]
        self.order = place.far + [place.layer]
        self.jobs = [(index, step) for index in range(count) for step in range(place.layers)]
        self.loads, self.swaps, self.waiting = {}, {}, {}

    def sizes(self, index):
        _, rows, cols = self.parts[index].shape
        return rows, cols, rows // self.place.rows_y, cols // (2 * self.place.cols_x)

    def begin(self):
        place = self.place
        for index, step in self.jobs:
            target = self.order[step]
            copy = pltpu.make_async_copy(
                self.parts[index].at[target * 2 + place.core], self.sums[index].at[step], self.load_sem.at[index, step]
            )
            copy.start()
            self.loads[index, step] = copy
            self.swap(index, step)

    def swap(self, index, step):
        place = self.place
        self.swaps[index, step] = place.push(
            self.parts[index].at[self.order[step] * 2 + 1 - place.core], self.swapped[index].at[step],
            *self.core, (index, step), (place.grp, place.partner),
        )

    def running(self, index, step):
        if self.in_place:
            return self.parts[index].at[self.order[step] * 2 + self.place.core]
        return self.sums[index].at[step]

    def first(self, index, step):
        place = self.place
        rows, cols, height, width = self.sizes(index)
        if not self.in_place:
            self.loads[index, step].wait()
        self.swaps[index, step].wait_recv()
        total = self.running(index, step)
        add_rows(total, self.swapped[index].at[step], 0, rows, 0, cols)
        copies = []
        for hop, other in enumerate(place.along):
            for column in range(place.cols_x):
                copies.append(place.push(
                    window(total, place.ys[hop] * height, height, 2 * column * width, width),
                    self.y_first[index].at[step, hop, column],
                    *self.first_sem, (index, step, 0, hop, column), (other, place.me),
                ))
        for hop, other in enumerate(place.beside):
            copies.append(place.push(
                window(total, 0, rows, (2 * place.xs[hop] + 1) * width, width),
                self.x_first[index].at[step, hop],
                *self.first_sem, (index, step, 1, hop, 0), (other, place.me),
            ))
        self.waiting[index, step] = copies

    def second(self, index, step):
        place = self.place
        rows, cols, height, width = self.sizes(index)
        for copy in self.waiting[index, step]:
            copy.wait_recv()
        total = self.running(index, step)
        for hop in range(place.rows_y - 1):
            for column in range(place.cols_x):
                add_rows(
                    total, self.y_first[index].at[step, hop, column],
                    place.gy * height, height, 2 * column * width, width,
                )
        for hop in range(place.cols_x - 1):
            add_rows(total, self.x_first[index].at[step, hop], 0, rows, (2 * place.gx + 1) * width, width)
        copies = []
        for hop, other in enumerate(place.beside):
            copies.append(place.push(
                window(total, place.gy * height, height, 2 * place.xs[hop] * width, width),
                self.x_second[index].at[step, hop],
                *self.second_sem, (index, step, 0, hop), (other, place.me),
            ))
        for hop, other in enumerate(place.along):
            copies.append(place.push(
                window(total, place.ys[hop] * height, height, (2 * place.gx + 1) * width, width),
                self.y_second[index].at[step, hop],
                *self.second_sem, (index, step, 1, hop), (other, place.me),
            ))
        self.waiting[index, step] = copies

    def third(self, index, step):
        place = self.place
        rows, cols, height, width = self.sizes(index)
        for copy in self.waiting[index, step]:
            copy.wait_recv()
        self.waiting[index, step] = []
        total = self.running(index, step)
        out = self.pieces[index][step]
        row, col = place.gy * height, 2 * place.gx * width
        for hop in range(place.cols_x - 1):
            source = self.x_second[index].at[step, hop]
            if hop == place.cols_x - 2:
                add_segments(total, source, row, col, self.segments[index][0], out)
            else:
                add_rows(total, source, row, height, col, width)
        for hop in range(place.rows_y - 1):
            source = self.y_second[index].at[step, hop]
            if hop == place.rows_y - 2:
                add_segments(total, source, row, col, self.segments[index][1], out)
            else:
                add_rows(total, source, row, height, col + width, width)

    def steps(self, stage, only=None):
        return [functools.partial(stage, *job) for job in self.jobs if only is None or job[0] == only]

    def finish(self):
        self.place.sent()


class PlaneSpread:
    def __init__(self, place, outs, first_send, first_recv, second_send, second_recv):
        self.place, self.outs = place, outs
        self.first_sem, self.second_sem = (first_send, first_recv), (second_send, second_recv)
        self.waiting = {}

    def sizes(self, index):
        rows, cols = self.outs[index].shape
        return rows, rows // self.place.rows_y, cols // (2 * self.place.cols_x)

    def total(self, index, piece, others, segments):
        place = self.place
        rows, height, width = self.sizes(index)
        row = place.gy * height
        col = pl.multiple_of(2 * place.gx * width, 128)
        for first, left, _, cols, off in segments[0] + segments[1]:

            def one(turn, carry):
                at = pl.ds(pl.multiple_of(first + turn * 16, 16), 16)
                value = piece[at, pl.ds(left, cols)].astype(jnp.float32)
                for other in others:
                    value = value + other[at, pl.ds(left, cols)].astype(jnp.float32)
                self.outs[index][
                    pl.ds(pl.multiple_of(row + turn * 16, 16), 16), pl.ds(pl.multiple_of(col + off, 128), cols)
                ] = value.astype(jnp.bfloat16)
                return carry

            lax.fori_loop(0, height // 16, one, 0)
        copies = []
        for hop, other in enumerate(place.beside):
            part = window(self.outs[index], row, height, 2 * place.gx * width, width)
            copies.append(place.push(part, part, *self.first_sem, (index, 0, hop), (other, place.me)))
        for hop, other in enumerate(place.along):
            part = window(self.outs[index], row, height, (2 * place.gx + 1) * width, width)
            copies.append(place.push(part, part, *self.first_sem, (index, 1, hop), (other, place.me)))
        self.waiting[index] = copies

    def second(self, index):
        place = self.place
        rows, height, width = self.sizes(index)
        for copy in self.waiting[index]:
            copy.wait_recv()
        copies = []
        for hop, other in enumerate(place.along):
            for spot, column in enumerate([place.gx] + place.beside_from):
                part = window(self.outs[index], place.gy * height, height, 2 * column * width, width)
                copies.append(place.push(part, part, *self.second_sem, (index, 0, hop, spot), (other, place.me)))
        for hop, other in enumerate(place.beside):
            part = window(self.outs[index], 0, rows, (2 * place.gx + 1) * width, width)
            copies.append(place.push(part, part, *self.second_sem, (index, 1, hop, 0), (other, place.me)))
        self.waiting[index] = copies

    def finish(self, index):
        for copy in self.waiting[index]:
            copy.wait_recv()


def small_rows(seq_count, values):
    rows = jnp.concatenate([values, jnp.zeros((32 - values.shape[0], values.shape[1]), jnp.float32)])
    return rows.reshape(seq_count, 32 // seq_count, values.shape[1])


class SmallSum:
    def __init__(self, place, source, total, scratch, first_send, first_recv, second_send, second_recv):
        self.place, self.source, self.total_ref, self.scratch = place, source, total, scratch
        self.first_sem, self.second_sem = (first_send, first_recv), (second_send, second_recv)

    def begin(self):
        place = self.place
        self.waiting = [
            place.push(self.source.at[other], self.scratch.at[step], *self.first_sem, step, (place.grp, other))
            for step, other in enumerate(place.others)
        ]

    def middle(self):
        place = self.place
        value = self.source[place.me]
        for step, copy in enumerate(self.waiting):
            copy.wait_recv()
            value = value + self.scratch[step]
        self.total_ref[place.me] = value
        part = self.total_ref.at[place.me]
        self.waiting = [
            place.push(part, part, *self.second_sem, step, (place.grp, other))
            for step, other in enumerate(place.others)
        ]

    def finish(self):
        for copy in self.waiting:
            copy.wait_recv()


def small_scratch(source):
    seq_count = source.shape[0]
    dma = pltpu.SemaphoreType.DMA
    return [pltpu.VMEM((seq_count - 1,) + source.shape[1:], jnp.float32)] + [dma((seq_count - 1,))] * 4


def forward_kernel(plane, seq_count, count, *refs):
    layers = seq_count // 2
    bound_ref, qkv_ref, shards = refs[0], refs[1], refs[2:2 + count]
    refs = refs[2 + count:]
    pieces, refs = refs[:layers - 1], refs[layers - 1:]
    kept_ref, mixture_ref, log_ref, fulls = refs[0], refs[1], refs[2], refs[3:3 + count]
    (
        key_scr, query_scr, value_t_scr, score_scr, mix_t_scr, mix_scr,
        send_sem, recv_sem, back_send_sem, back_recv_sem, local_sem,
    ) = refs[3 + count:14 + count]
    own_sem, first_send, first_recv, second_send, second_recv, core_send, core_recv = refs[14 + count:]
    group_count, local_rows, local_width = qkv_ref.shape[1], qkv_ref.shape[3], qkv_ref.shape[4]
    total_rows = seq_count * local_rows
    heads = local_width // HEAD_DIM
    me = lax.axis_index("seq")
    grp = lax.axis_index("grp")
    others = [lax.rem(me + step, seq_count) for step in range(1, seq_count)]
    origins = [lax.rem(me + seq_count - step, seq_count) for step in range(1, seq_count)]
    block = min(256, total_rows // 3)
    place = Place(plane, seq_count)
    enter([(grp, other) for other in others] + [(other, me) for other in place.beside + place.along])
    copies = []
    for group in range(group_count):
        own = pltpu.make_async_copy(qkv_ref.at[me, group], kept_ref.at[me, group], local_sem.at[group])
        own.start()
        row = [own]
        for step, other in enumerate(others):
            copy = pltpu.make_async_remote_copy(
                qkv_ref.at[other, group], kept_ref.at[me, group],
                send_sem.at[group, step], recv_sem.at[group, step],
                device_id=(grp, other), device_id_type=MESH,
            )
            copy.start()
            row.append(copy)
        copies.append(row)
    side = place.cols_x
    segments, _ = piece_segments(
        [shard.shape for shard in shards], side, min(shard.shape[1] for shard in shards) // side
    )
    spread = PlaneGather(
        place, shards, pieces, segments, fulls,
        own_sem, first_send, first_recv, second_send, second_recv, core_send, core_recv,
    )
    spread.begin()
    back = []
    for group in range(group_count):
        for copy in copies[group]:
            copy.wait()
        if group == 0:
            spread.middle()
            hooks = spread.late()
            held = len(hooks) // 3
        boundary = bound_ref[group]
        keys = kept_ref[:, group, 1].reshape(total_rows, local_width)
        values = kept_ref[:, group, 2].reshape(total_rows, local_width)
        key_scr[:, :local_width] = keys
        key_scr[:, local_width:] = utter_features(boundary, total_rows, True)
        query_scr[:, local_width:] = utter_features(boundary, total_rows, False)
        value_t_scr[...] = values.astype(jnp.float32).T.astype(jnp.bfloat16)

        for head in range(heads):
            queries = kept_ref[:, group, 0].reshape(total_rows, local_width)
            query_scr[:, :local_width] = head_lanes(queries, head) * jnp.bfloat16(HEAD_DIM ** (-0.5))
            for third in range(3):
                first_key, last_key = key_span(third, total_rows)
                chunks = range(first_key, last_key, block)

                def one_block(index, carry):
                    first_row = pl.multiple_of(third * (total_rows // 3) + index * block, block)
                    query_block = query_scr[pl.ds(first_row, block), :]
                    peak = jnp.full((8, block), -jnp.inf, jnp.float32)
                    for first in chunks:
                        scores = dot_nt(key_scr[first:first + block, :], query_block)
                        score_scr[first:first + block, :] = scores
                        peak = jnp.maximum(peak, fold_rows(scores, jnp.max))
                    peak = jnp.max(peak, axis=0, keepdims=True)
                    total = jnp.zeros((8, block), jnp.float32)
                    for first in chunks:
                        lifted = jnp.exp(score_scr[first:first + block, :] - peak)
                        score_scr[first:first + block, :] = lifted
                        total = total + fold_rows(lifted, jnp.sum)
                    total = jnp.sum(total, axis=0, keepdims=True)
                    inverse = 1.0 / total
                    mixed = jnp.zeros((HEAD_DIM, block), jnp.float32)
                    rows = slice(head * HEAD_DIM, (head + 1) * HEAD_DIM)
                    for first in chunks:
                        weight = (score_scr[first:first + block, :] * inverse).astype(jnp.bfloat16)
                        mixed = mixed + dot_nn(value_t_scr[rows, first:first + block], weight)
                    mix_t_scr[rows, pl.ds(first_row, block)] = mixed
                    log_ref[group, head, :, pl.ds(first_row, block)] = peak + jnp.log(total)
                    return carry

                lax.fori_loop(0, total_rows // 3 // block, one_block, 0)
                if group > 0 and len(hooks) > held:
                    hooks.pop(0)()
        mix_scr[group] = mix_t_scr[...].T.astype(jnp.bfloat16).reshape(seq_count, local_rows, local_width)
        own = pltpu.make_async_copy(
            mix_scr.at[group, me], mixture_ref.at[me, group], local_sem.at[group_count + group]
        )
        own.start()
        back.append(own)
        for step, other in enumerate(others):
            copy = pltpu.make_async_remote_copy(
                mix_scr.at[group, other], mixture_ref.at[me, group],
                back_send_sem.at[group, step], back_recv_sem.at[group, step],
                device_id=(grp, other), device_id_type=MESH,
            )
            copy.start()
            back.append(copy)
    for hook in hooks:
        hook()
    for copy in back:
        copy.wait()
    spread.finish()


def attend_forward(bounds, qkv, shards, pieces):
    side = math.isqrt(lax.axis_size("grp"))
    hops = max(side - 1, 1)
    count = len(shards)
    dma = pltpu.SemaphoreType.DMA
    anywhere = pl.BlockSpec(memory_space=pl.ANY)
    layers = qkv.shape[0] // 2
    seq_count, group_count, _, local_rows, local_width = qkv.shape
    total_rows = seq_count * local_rows
    heads = local_width // HEAD_DIM
    block = min(256, total_rows // 3)
    vmem = pl.BlockSpec(memory_space=pltpu.VMEM)
    return pl.pallas_call(
        functools.partial(forward_kernel, (side, side), seq_count, count),
        out_shape=(
            jax.ShapeDtypeStruct(qkv.shape, jnp.bfloat16),
            jax.ShapeDtypeStruct((seq_count, group_count, local_rows, local_width), jnp.bfloat16),
            jax.ShapeDtypeStruct((group_count, heads, 1, total_rows), jnp.float32),
        ) + tuple(jax.ShapeDtypeStruct((seq_count,) + part.shape, part.dtype) for part in shards),
        in_specs=[pl.BlockSpec(memory_space=pltpu.SMEM)] + [anywhere] * (count + layers),
        out_specs=(vmem, vmem, vmem) + (anywhere,) * count,
        scratch_shapes=[
            pltpu.VMEM((total_rows, local_width + 128), jnp.bfloat16),
            pltpu.VMEM((total_rows, local_width + 128), jnp.bfloat16),
            pltpu.VMEM((local_width, total_rows), jnp.bfloat16),
            pltpu.VMEM((total_rows, block), jnp.float32),
            pltpu.VMEM((local_width, total_rows), jnp.float32),
            pltpu.VMEM((group_count, seq_count, local_rows, local_width), jnp.bfloat16),
            pltpu.SemaphoreType.DMA((group_count, seq_count - 1)),
            pltpu.SemaphoreType.DMA((group_count, seq_count - 1)),
            pltpu.SemaphoreType.DMA((group_count, seq_count - 1)),
            pltpu.SemaphoreType.DMA((group_count, seq_count - 1)),
            pltpu.SemaphoreType.DMA((2 * group_count,)),
            dma((count, layers, 2, 2)),
            dma((count, layers - 1, 2, hops, 2)), dma((count, layers - 1, 2, hops, 2)),
            dma((count, layers - 1, 2, hops, side)), dma((count, layers - 1, 2, hops, side)),
            dma((count, layers)), dma((count, layers)),
        ],
        compiler_params=pltpu.CompilerParams(
            collective_id=1, has_side_effects=True, vmem_limit_bytes=48 * 1024 * 1024
        ),
        name="attend_forward",
    )(bounds, qkv, *shards, *pieces)


def backward_kernel(plane, seq_count, count, *refs):
    layers = seq_count // 2
    bound_ref, kept_ref, grad_ref, log_ref = refs[:4]
    parts, refs = refs[4:4 + count], refs[4 + count:]
    out_ref, refs = refs[0], refs[1:]
    pieces, refs = refs[:layers], refs[layers:]
    (
        taken_scr, key_scr, query_scr, key_t_scr, head_query_scr, head_grad_scr, prob_scr, weight_scr,
        query_t_scr, key_sum_scr, value_sum_scr, back_scr,
        send_sem, recv_sem, back_send_sem, back_recv_sem, local_sem,
    ) = refs[:17]
    buffers, semaphores = refs[17:17 + 6 * count], refs[17 + 6 * count:]
    group_count, local_rows, local_width = grad_ref.shape[1], grad_ref.shape[2], grad_ref.shape[3]
    total_rows = seq_count * local_rows
    heads = local_width // HEAD_DIM
    me = lax.axis_index("seq")
    grp = lax.axis_index("grp")
    others = [lax.rem(me + step, seq_count) for step in range(1, seq_count)]
    block = min(256, total_rows // 3)
    place = Place(plane, seq_count)
    enter([(grp, other) for other in others] + [(other, me) for other in place.beside + place.along])
    copies = []
    for group in range(group_count):
        own = pltpu.make_async_copy(grad_ref.at[me, group], taken_scr.at[me, group], local_sem.at[group])
        own.start()
        row = [own]
        for step, other in enumerate(others):
            copy = pltpu.make_async_remote_copy(
                grad_ref.at[other, group], taken_scr.at[me, group],
                send_sem.at[group, step], recv_sem.at[group, step],
                device_id=(grp, other), device_id_type=MESH,
            )
            copy.start()
            row.append(copy)
        copies.append(row)
    side = place.cols_x
    segments, _ = piece_segments(
        [part.shape[1:] for part in parts], side, min(part.shape[2] for part in parts) // side
    )
    plane_sum = PlaneSum(place, parts, [pieces] * count, segments, buffers, semaphores)
    plane_sum.begin()
    firsts = plane_sum.steps(plane_sum.first)
    seconds = plane_sum.steps(plane_sum.second)
    units = 3 * heads * group_count
    plan = [[] for _ in range(units + 1)]
    for spot, hook in enumerate(firsts):
        plan[spot * (units // 2 - 1) // len(firsts)].append(hook)
    for spot, hook in enumerate(seconds):
        plan[units - 5 + spot * 6 // len(seconds)].append(hook)
    back = []
    for group in range(group_count):
        for copy in copies[group]:
            copy.wait()
        boundary = bound_ref[group]
        keys = kept_ref[:, group, 1].reshape(total_rows, local_width)
        key_scr[:, :local_width] = keys
        key_scr[:, local_width:] = utter_features(boundary, total_rows, True)
        query_scr[:, local_width:] = utter_features(boundary, total_rows, False)
        key_t_scr[...] = keys.astype(jnp.float32).T.astype(jnp.bfloat16)
        key_sum_scr[...] = jnp.zeros_like(key_sum_scr)
        value_sum_scr[...] = jnp.zeros_like(value_sum_scr)

        for head in range(heads):
            queries = head_lanes(kept_ref[:, group, 0].reshape(total_rows, local_width), head)
            head_query_scr[...] = queries
            query_scr[:, :local_width] = queries * jnp.bfloat16(HEAD_DIM ** (-0.5))
            head_grad_scr[...] = head_lanes(taken_scr[:, group].reshape(total_rows, local_width), head)
            for third in range(3):
                first_key, last_key = key_span(third, total_rows)
                chunks = range(first_key, last_key, block)

                def one_block(index, carry):
                    first_row = pl.multiple_of(third * (total_rows // 3) + index * block, block)
                    own_rows = pl.ds(first_row, block)
                    query_block = query_scr[own_rows, :]
                    grad_block = head_grad_scr[own_rows, :]
                    plain_block = head_query_scr[own_rows, :]
                    log_block = log_ref[group, head, :, own_rows]
                    row_dot = jnp.zeros((8, block), jnp.float32)
                    for first in chunks:
                        scores = dot_nt(key_scr[first:first + block, :], query_block)
                        prob = jnp.exp(scores - log_block)
                        values = kept_ref[
                            first // local_rows:(first + block - 1) // local_rows + 1, group, 2
                        ].reshape(-1, local_width)
                        skip = first % local_rows
                        weight_grad = dot_nt(values[skip:skip + block], grad_block)
                        prob_scr[first:first + block, :] = prob
                        weight_scr[first:first + block, :] = weight_grad
                        row_dot = row_dot + fold_rows(prob * weight_grad, jnp.sum)
                    row_dot = jnp.sum(row_dot, axis=0, keepdims=True)
                    rows = slice(head * HEAD_DIM, (head + 1) * HEAD_DIM)
                    turned = jnp.zeros((HEAD_DIM, block), jnp.float32)
                    for first in chunks:
                        prob = prob_scr[first:first + block, :]
                        score_grad = (
                            HEAD_DIM ** (-0.5) * (prob * (weight_scr[first:first + block, :] - row_dot))
                        ).astype(jnp.bfloat16)
                        key_sum_scr[first:first + block, :] += dot_nn(score_grad, plain_block)
                        value_sum_scr[first:first + block, :] += dot_nn(
                            prob.astype(jnp.bfloat16), grad_block
                        )
                        turned = turned + dot_nn(key_t_scr[rows, first:first + block], score_grad)
                    query_t_scr[rows, own_rows] = turned
                    return carry

                lax.fori_loop(0, total_rows // 3 // block, one_block, 0)
                for hook in plan.pop(0):
                    hook()
        shape = (seq_count, local_rows, local_width)
        back_scr[:, group, 0] = query_t_scr[...].T.astype(jnp.bfloat16).reshape(shape)
        back_scr[:, group, 1] = key_sum_scr[...].astype(jnp.bfloat16).reshape(shape)
        back_scr[:, group, 2] = value_sum_scr[...].astype(jnp.bfloat16).reshape(shape)
        own = pltpu.make_async_copy(
            back_scr.at[me, group], out_ref.at[me, group], local_sem.at[group_count + group]
        )
        own.start()
        back.append(own)
        for step, other in enumerate(others):
            copy = pltpu.make_async_remote_copy(
                back_scr.at[other, group], out_ref.at[me, group],
                back_send_sem.at[group, step], back_recv_sem.at[group, step],
                device_id=(grp, other), device_id_type=MESH,
            )
            copy.start()
            back.append(copy)
    for hook in plan[0] + plane_sum.steps(plane_sum.third):
        hook()
    for copy in back:
        copy.wait()
    plane_sum.finish()


def attend_backward(bounds, kept, grad, log_total, parts):
    side = math.isqrt(lax.axis_size("grp"))
    count = len(parts)
    layers = kept.shape[0] // 2
    anywhere = pl.BlockSpec(memory_space=pl.ANY)
    parts = by_owner(parts, kept.shape[0])
    width = min(part.shape[2] for part in parts) // side
    _, piece_rows = piece_segments([part.shape[1:] for part in parts], side, width)
    seq_count, group_count, _, local_rows, local_width = kept.shape
    total_rows = seq_count * local_rows
    block = min(256, total_rows // 3)
    vmem = pl.BlockSpec(memory_space=pltpu.VMEM)
    return pl.pallas_call(
        functools.partial(backward_kernel, (side, side), seq_count, count),
        out_shape=(jax.ShapeDtypeStruct(kept.shape, jnp.bfloat16),) + tuple(
            jax.ShapeDtypeStruct((piece_rows, width), jnp.bfloat16) for _ in range(layers)
        ),
        in_specs=[pl.BlockSpec(memory_space=pltpu.SMEM), vmem, anywhere, vmem] + [anywhere] * count,
        out_specs=(vmem,) * (1 + layers),
        scratch_shapes=[
            pltpu.VMEM(grad.shape, jnp.bfloat16),
            pltpu.VMEM((total_rows, local_width + 128), jnp.bfloat16),
            pltpu.VMEM((total_rows, local_width + 128), jnp.bfloat16),
            pltpu.VMEM((local_width, total_rows), jnp.bfloat16),
            pltpu.VMEM((total_rows, local_width), jnp.bfloat16),
            pltpu.VMEM((total_rows, local_width), jnp.bfloat16),
            pltpu.VMEM((total_rows, block), jnp.float32),
            pltpu.VMEM((total_rows, block), jnp.float32),
            pltpu.VMEM((local_width, total_rows), jnp.float32),
            pltpu.VMEM((total_rows, local_width), jnp.float32),
            pltpu.VMEM((total_rows, local_width), jnp.float32),
            pltpu.VMEM(kept.shape, jnp.bfloat16),
            pltpu.SemaphoreType.DMA((group_count, seq_count - 1)),
            pltpu.SemaphoreType.DMA((group_count, seq_count - 1)),
            pltpu.SemaphoreType.DMA((group_count, seq_count - 1)),
            pltpu.SemaphoreType.DMA((group_count, seq_count - 1)),
            pltpu.SemaphoreType.DMA((2 * group_count,)),
        ] + plane_sum_scratch(parts, side),
        compiler_params=pltpu.CompilerParams(
            collective_id=2, has_side_effects=True, vmem_limit_bytes=60 * 1024 * 1024
        ),
        name="attend_backward",
    )(bounds, kept, grad, log_total, *parts)


class WholeGather(PlaneGather):
    def __init__(self, place, shards, fulls, line_send, line_recv, *semaphores):
        super().__init__(place, shards, None, None, fulls, *semaphores)
        self.line = (line_send, line_recv)
        self.jobs = [(index, step) for index in range(len(shards)) for step in range(place.layers - 1)]
        self.lines = {}

    def begin(self):
        place = self.place
        for index, step in self.jobs:
            rows, height, width = self.sizes(index)
            row, col = place.gy * height, 2 * place.gx * width
            self.lines[index, step] = place.push(
                window(self.shards[index], row, height, col, 2 * width),
                window(self.fulls[index].at[place.me], row, height, col, 2 * width),
                *self.line, (index, step), (place.grp, place.lines[step]),
            )
        for index, shard in enumerate(self.shards):
            copy = pltpu.make_async_copy(shard, self.fulls[index].at[place.me], self.own_sem.at[index, place.layers - 1, 0, 0])
            copy.start()
            push = place.push(shard, self.fulls[index].at[place.me], *self.core, (index, 0), (place.grp, place.partner))
            self.own.append((copy, push))

    def spread_first(self, index, step):
        place = self.place
        rows, height, width = self.sizes(index)
        self.lines[index, step].wait_recv()
        full = self.fulls[index].at[place.line_from[step]]
        row, col = place.gy * height, 2 * place.gx * width
        self.waiting[index, step] = []
        for half, partners in enumerate((place.beside, place.along)):
            part = window(full, row, height, col + half * width, width)
            for hop, other in enumerate(partners):
                self.waiting[index, step].append(
                    place.push(part, part, *self.first, (index, step, half, hop, 0), (other, place.me))
                )

    def steps(self):
        lag = self.place.layers - 1
        done = []
        for turn in range(len(self.jobs) + 2 * lag):
            if turn < len(self.jobs):
                done.append(functools.partial(self.spread_first, *self.jobs[turn]))
            if 0 <= turn - lag < len(self.jobs):
                done.append(functools.partial(self.spread_second, *self.jobs[turn - lag]))
            if 0 <= turn - 2 * lag < len(self.jobs):
                done.append(functools.partial(self.over_core, *self.jobs[turn - 2 * lag]))
        return done


def gather_kernel(plane, seq_count, count, *refs):
    shards, (partial_ref, token_ref), refs = refs[:count], refs[count:count + 2], refs[count + 2:]
    fulls, (total_ref, tokens_ref), refs = refs[:count], refs[count:count + 2], refs[count + 2:]
    token_scr, token_send, token_recv = refs[:3]
    small_refs, refs = refs[3:8], refs[8:]
    place = Place(plane, seq_count)
    enter([(place.grp, other) for other in place.others] + [(other, place.me) for other in place.groups])
    whole = WholeGather(place, shards, fulls, *refs)
    whole.begin()
    small = SmallSum(place, partial_ref, total_ref, *small_refs)
    small.begin()
    hooks = whole.steps()
    for hook in hooks[:len(hooks) // 2]:
        hook()
    small.middle()
    for hook in hooks[len(hooks) // 2:]:
        hook()
    small.finish()
    last = total_ref.shape[1] - 1
    token_scr[...] = token_ref[...]
    token_scr[4:5, :] = total_ref[seq_count - 1, last:last + 1, :128]
    tokens_ref[place.grp] = token_scr[...]
    tokens = [
        place.push(token_scr, tokens_ref.at[place.grp], token_send, token_recv, step, (other, place.me))
        for step, other in enumerate(place.groups)
    ]
    whole.finish()
    for copy in tokens:
        copy.wait_recv()


def gather(collective, partial, token, *shards):
    grp_count = lax.axis_size("grp")
    seq_count = lax.axis_size("seq")
    side = math.isqrt(grp_count)
    layers = seq_count // 2
    count = len(shards)
    anywhere = pl.BlockSpec(memory_space=pl.ANY)
    vmem = pl.BlockSpec(memory_space=pltpu.VMEM)
    dma = pltpu.SemaphoreType.DMA
    hops = max(side - 1, 1)
    outs = pl.pallas_call(
        functools.partial(gather_kernel, (side, side), seq_count, count),
        out_shape=tuple(
            jax.ShapeDtypeStruct((seq_count,) + part.shape, part.dtype) for part in shards
        ) + (
            jax.ShapeDtypeStruct(partial.shape, jnp.float32),
            jax.ShapeDtypeStruct((grp_count,) + token.shape, jnp.float32),
        ),
        in_specs=[anywhere] * count + [vmem] * 2,
        out_specs=(anywhere,) * count + (vmem,) * 2,
        scratch_shapes=[
            pltpu.VMEM(token.shape, jnp.float32), dma((grp_count - 1,)), dma((grp_count - 1,))
        ] + small_scratch(partial) + [
            dma((count, layers - 1)), dma((count, layers - 1)),
            dma((count, layers, 1, 1)),
            dma((count, layers - 1, 2, hops, 1)), dma((count, layers - 1, 2, hops, 1)),
            dma((count, layers - 1, 2, hops, side)), dma((count, layers - 1, 2, hops, side)),
            dma((count, layers)), dma((count, layers)),
        ],
        compiler_params=pltpu.CompilerParams(collective_id=collective, has_side_effects=True),
        name="gather_weights",
    )(*shards, partial, token)
    return outs[:count], outs[count], outs[count + 1]


def turn_lanes(values, cos, sin):
    lane = lax.broadcasted_iota(jnp.int32, values.shape, 1)
    ahead = pltpu.roll(values, values.shape[1] - HEAD_DIM // 2, 1)
    behind = pltpu.roll(values, HEAD_DIM // 2, 1)
    other = jnp.where(lax.rem(lane, HEAD_DIM) < HEAD_DIM // 2, ahead, behind)
    return values * cos + other * sin


def second_mask(bound_ref, group, me, local_rows, first, rows):
    row = lax.broadcasted_iota(jnp.int32, (rows, 1), 0) + (me * local_rows + first)
    return row >= bound_ref[group]


def centered(values):
    center = values - jnp.mean(values, axis=-1, keepdims=True)
    scale = lax.rsqrt(jnp.mean(center * center, axis=-1, keepdims=True) + epsilon)
    return center * scale, scale


def back_kernel(plane, seq_count, *refs):
    layers = seq_count // 2
    (
        bound_ref, back_ref, cos_ref, sin_ref, normed_ref, hidden_ref, middle_ref, frames_ref, shortcut_ref,
        combine_ref, projection_ref, mods_ref, late_ref, modulation_ref,
    ) = refs[:14]
    finished, refs = refs[14:14 + layers], refs[14 + layers:]
    frames_out, shortcut_out, outs, refs = refs[0], refs[1], refs[2:7], refs[7:]
    utters_ref, conditions_ref, refs = refs[0], refs[1], refs[2:]
    (
        packed_scr, combine_scr, projection_scr, normed_t_scr, joined_t_scr, grad_scr, low_scr,
        frames_scr, shortcut_scr, total_ref, utter_scr, condition_scr,
    ) = refs[:12]
    parts, done_scr, lines, refs = refs[12:14], refs[14], refs[15:17], refs[17:]
    pieces = [refs[index * layers:(index + 1) * layers] for index in range(2)]
    refs = refs[2 * layers:]
    buffers, semaphores, refs = refs[:10], refs[10:17], refs[17:]
    small_refs, spread_sems, refs = refs[:5], refs[5:9], refs[9:]
    weight_sem, out_sem, token_send, token_recv, last_send, last_recv, line_send, line_recv, done_send, done_recv = refs
    group_count, local_rows, local_width = back_ref.shape[1], back_ref.shape[3], back_ref.shape[4]
    row_count, width = normed_ref.shape
    place = Place(plane, seq_count)
    me = place.me
    side = place.cols_x
    enter([(place.grp, other) for other in place.others] + [(other, me) for other in place.groups])
    arrived = {}
    for step in range(layers - 1):
        arrived[step] = place.push(
            finished[step], done_scr.at[step], done_send, done_recv, step, (place.grp, place.lines[step])
        )
    weights = [
        pltpu.make_async_copy(projection_ref, projection_scr, weight_sem.at[0]),
        pltpu.make_async_copy(combine_ref, combine_scr, weight_sem.at[1]),
    ]
    for copy in weights:
        copy.start()
    for source in range(seq_count):
        for kind in range(3):
            for group in range(group_count):
                packed_scr[
                    group * local_rows:(group + 1) * local_rows,
                    kind * width + source * local_width:kind * width + (source + 1) * local_width,
                ] = back_ref[source, group, kind]

    def turn(index, carry):
        lanes = pl.ds(pl.multiple_of(index * 128, 128), 128)
        packed_scr[:, lanes] = turn_lanes(
            packed_scr[:, lanes].astype(jnp.float32), cos_ref[...], -sin_ref[...]
        ).astype(jnp.bfloat16)
        return carry

    lax.fori_loop(0, 2 * width // 128, turn, 0)
    normed_t_scr[...] = normed_ref[...].astype(jnp.float32).T.astype(jnp.bfloat16)
    segments = [
        piece_segments([part.shape[1:]], side, part.shape[2] // side)[0][0] for part in parts
    ]
    done_segments, _ = piece_segments(
        [out.shape for out in outs[2:]], side, min(out.shape[1] for out in outs[2:]) // side
    )
    plane_sum = PlaneSum(place, parts, pieces, segments, buffers, semaphores, True)
    spread = PlaneSpread(place, outs, *spread_sems)

    def share(index, left, right, tile):
        rows = parts[index].shape[1]

        def fill(owner):
            at = pl.ds(pl.multiple_of(owner * rows, rows), rows)

            def one(turn, carry):
                lanes = pl.ds(pl.multiple_of(turn * tile, tile), tile)
                parts[index][owner, :, lanes] = dot_nn(left[at, :], right[:, lanes]).astype(jnp.bfloat16)
                return carry

            lax.fori_loop(0, parts[index].shape[2] // tile, one, 0)

        for step, target in enumerate(plane_sum.order):
            fill(target * 2 + 1 - place.core)
            plane_sum.swap(index, step)
        for target in plane_sum.order:
            fill(target * 2 + place.core)

    share(0, normed_t_scr, packed_scr, 512)
    weights[0].wait()

    def grad_tile(index, carry):
        at = pl.ds(pl.multiple_of(index * 256, 256), 256)
        grad_scr[:, at] = dot_nt(packed_scr[...], projection_scr[at, :])
        return carry

    lax.fori_loop(0, width // 256, grad_tile, 0)
    for hook in plane_sum.steps(plane_sum.first, 0):
        hook()
    block, utter_rows = utter_scr.shape[1], 2 * group_count
    utter_scr[...] = jnp.zeros_like(utter_scr)

    def put(part, utter, value):
        row = part * utter_rows + utter
        utter_scr[row // block, row % block:row % block + 1, :] = value

    for part in range(4):
        for utter in range(utter_rows):
            put(part + 2, utter, late_ref[part * utter_rows + utter:part * utter_rows + utter + 1, :])
    chunk = 32
    for group in range(group_count):

        def norm_back(index, sums):
            first = pl.multiple_of(index * chunk, chunk)
            at = pl.ds(pl.multiple_of(group * local_rows + first, chunk), chunk)
            second = second_mask(bound_ref, group, me, local_rows, first, chunk)
            row = group * 2 * 6
            scale_part = jnp.where(second, mods_ref[row + 7:row + 8, :], mods_ref[row + 1:row + 2, :])
            grad = grad_scr[at, :]
            normal, scale = centered(hidden_ref[at, :])
            inner = grad * (1.0 + scale_part)
            turned = scale * (
                inner
                - jnp.mean(inner, axis=-1, keepdims=True)
                - normal * jnp.mean(inner * normal, axis=-1, keepdims=True)
            )
            low_scr[at, :] = (middle_ref[at, :] + turned).astype(jnp.bfloat16)
            scaled = grad * normal
            later = second.astype(jnp.float32)
            shift_later, scale_later = grad * later, scaled * later
            return (
                sums[0] + fold_rows(grad - shift_later, jnp.sum),
                sums[1] + fold_rows(shift_later, jnp.sum),
                sums[2] + fold_rows(scaled - scale_later, jnp.sum),
                sums[3] + fold_rows(scale_later, jnp.sum),
            )

        zero = jnp.zeros((8, width), jnp.float32)
        sums = lax.fori_loop(0, local_rows // chunk, norm_back, (zero, zero, zero, zero))
        for spot, value in enumerate(sums):
            put(spot // 2, group * 2 + spot % 2, jnp.sum(value, axis=0, keepdims=True))
    small = SmallSum(place, utter_scr, total_ref, *small_refs)
    small.begin()
    joined_t_scr[:width, :] = frames_ref[...].astype(jnp.float32).T.astype(jnp.bfloat16)
    joined_t_scr[width:, :] = shortcut_ref[...].astype(jnp.float32).T.astype(jnp.bfloat16)
    share(1, joined_t_scr, low_scr, 512)
    for hook in plane_sum.steps(plane_sum.second, 0)[:layers // 2]:
        hook()
    weights[1].wait()

    def joined_tile(index, carry):
        at = pl.ds(pl.multiple_of(index * 256, 256), 256)
        late = pl.ds(pl.multiple_of(width + index * 256, 256), 256)
        frames_scr[:, at] = dot_nt(low_scr[...], combine_scr[at, :])
        shortcut_scr[:, at] = dot_nt(low_scr[...], combine_scr[late, :])
        return carry

    lax.fori_loop(0, width // 256, joined_tile, 0)
    grads = [
        pltpu.make_async_copy(frames_scr, frames_out, out_sem.at[0]),
        pltpu.make_async_copy(shortcut_scr, shortcut_out, out_sem.at[1]),
    ]
    for copy in grads:
        copy.start()
    for hook in plane_sum.steps(plane_sum.first, 1):
        hook()
    for hook in plane_sum.steps(plane_sum.second, 0)[layers // 2:]:
        hook()
    small.middle()

    def along_line(index, step):
        plane_sum.third(index, step)
        if step < layers - 1:
            arrived[index, step] = place.push(
                pieces[index][step], lines[index].at[step], line_send, line_recv, (index, step),
                (place.grp, place.lines[step]),
            )

    def last(index):
        for step in range(layers - 1):
            arrived[index, step].wait_recv()
        spread.total(
            index, pieces[index][layers - 1], [lines[index].at[step] for step in range(layers - 1)], segments[index]
        )

    for step in range(layers):
        plane_sum.second(1, step)
        along_line(0, step)
    small.finish()
    utters_ref[place.grp] = total_ref[...]
    tokens = [
        place.push(total_ref, utters_ref.at[place.grp], token_send, token_recv, step, (other, me))
        for step, other in enumerate(place.groups)
    ]
    condition_scr[...] = jnp.zeros_like(condition_scr)
    shard_rows = modulation_ref.shape[0]
    for spot in range(6 * utter_rows // block):
        part, row = spot * block // utter_rows, spot * block % utter_rows
        condition_scr[row:row + block, :shard_rows] += dot_nt(
            total_ref[spot].astype(jnp.bfloat16), modulation_ref[:, part * width:(part + 1) * width]
        )
    conditions_ref[me] = condition_scr[...]
    tokens += [
        place.push(condition_scr, conditions_ref.at[me], last_send, last_recv, step, (place.grp, other))
        for step, other in enumerate(place.others)
    ]
    for step in range(layers):
        along_line(1, step)
    for step in range(layers - 1):
        arrived[step].wait_recv()
    for index in range(2, 5):
        spread.total(
            index, finished[layers - 1], [done_scr.at[step] for step in range(layers - 1)], done_segments[index - 2]
        )
    last(0)
    for index in range(2, 5):
        spread.second(index)
    last(1)
    spread.second(0)
    spread.second(1)
    place.sent()
    for copy in tokens:
        copy.wait_recv()
    for copy in grads:
        copy.wait()
    for index in range(5):
        spread.finish(index)


def finish_backward(bounds, back, cos, sin, normed, hidden, middle_grad, frames, shortcut, combine, projection, mods, late, modulation, finished, done_shapes):
    grp_count = lax.axis_size("grp")
    seq_count = lax.axis_size("seq")
    side = math.isqrt(grp_count)
    layers = seq_count // 2
    hops = max(side - 1, 1)
    anywhere = pl.BlockSpec(memory_space=pl.ANY)
    vmem = pl.BlockSpec(memory_space=pltpu.VMEM)
    dma = pltpu.SemaphoreType.DMA
    row_count, width = normed.shape
    low, full = jnp.bfloat16, jnp.float32
    parts = [
        jax.ShapeDtypeStruct((seq_count, weight.shape[0] // seq_count, weight.shape[1]), low)
        for weight in (projection, combine)
    ]
    out_shapes = [part.shape[1:] for part in parts] + list(done_shapes)
    small = jax.ShapeDtypeStruct((seq_count, 32 // seq_count, width), full)
    return pl.pallas_call(
        functools.partial(back_kernel, (side, side), seq_count),
        out_shape=(
            jax.ShapeDtypeStruct((row_count, width), full),
            jax.ShapeDtypeStruct((row_count, width), full),
        ) + tuple(jax.ShapeDtypeStruct(shape, low) for shape in out_shapes) + (
            jax.ShapeDtypeStruct((grp_count,) + small.shape, full),
            jax.ShapeDtypeStruct((seq_count, 8, 128), full),
        ),
        in_specs=[pl.BlockSpec(memory_space=pltpu.SMEM)] + [vmem] * 8 + [anywhere] * 2 + [vmem] * (3 + layers),
        out_specs=(anywhere,) * 2 + (vmem,) * 7,
        scratch_shapes=[
            pltpu.VMEM((row_count, 3 * width), low),
            pltpu.VMEM(combine.shape, low),
            pltpu.VMEM(projection.shape, low),
            pltpu.VMEM((width, row_count), low),
            pltpu.VMEM((2 * width, row_count), low),
            pltpu.VMEM((row_count, width), full),
            pltpu.VMEM((row_count, width), low),
            pltpu.VMEM((row_count, width), full),
            pltpu.VMEM((row_count, width), full),
            pltpu.VMEM(small.shape, full),
            pltpu.VMEM(small.shape, full),
            pltpu.VMEM((8, 128), full),
        ] + [pltpu.VMEM(part.shape, low) for part in parts] + [
            pltpu.VMEM((layers - 1,) + finished[0].shape, low)
        ] + [
            pltpu.VMEM((layers - 1, part.shape[1] // side, part.shape[2] // side), low) for part in parts
        ] + [
            pltpu.VMEM((part.shape[1] // side, part.shape[2] // side), low)
            for part in parts for _ in range(layers)
        ] + plane_sum_scratch(parts, side, True) + small_scratch(small) + [
            dma((5, 2, hops)), dma((5, 2, hops)),
            dma((5, 2, hops, side)), dma((5, 2, hops, side)),
            dma((2,)), dma((2,)),
            dma((grp_count - 1,)), dma((grp_count - 1,)),
            dma((seq_count - 1,)), dma((seq_count - 1,)),
            dma((2, layers - 1)), dma((2, layers - 1)),
            dma((layers - 1,)), dma((layers - 1,)),
        ],
        compiler_params=pltpu.CompilerParams(
            collective_id=4, has_side_effects=True, vmem_limit_bytes=60 * 1024 * 1024
        ),
        name="finish_backward",
    )(bounds, back, cos, sin, normed, hidden, middle_grad, frames, shortcut, combine, projection, mods, late, modulation, *finished)


def line_shift(values, step):
    seq_count = lax.axis_size("seq")
    turned = [(spot, (spot + 2 * step) % seq_count) for spot in range(seq_count)]
    return lax.ppermute(values, "seq", turned)


def line_pieces(shards):
    side = math.isqrt(lax.axis_size("grp"))
    layers = lax.axis_size("seq") // 2
    grp = lax.axis_index("grp")
    width = min(shard.shape[1] for shard in shards) // side
    blocks = []
    for shard in shards:
        height, cols = shard.shape[0] // side, shard.shape[1] // side
        for off in range(0, cols, width):
            blocks.append(lax.dynamic_slice(
                shard, (grp // side * height, lax.rem(grp, side) * cols + off), (height, width)
            ))
    joined = jnp.concatenate(blocks)
    return [line_shift(joined, step) for step in range(1, layers)]


def shards(
    frames,
    shortcut,
    time_embed,
    lengths,
    kept_mask,
    target,
    combine,
    modulation,
    projection,
    readout,
    expand,
    contract,
):
    group_count = frames.shape[0]
    local_rows = frames.shape[1]
    width = HEADS * HEAD_DIM
    row_count = group_count * local_rows
    seq_count = lax.axis_size("seq")
    group_frames = local_rows * seq_count
    all_frames = group_frames * lax.axis_size("grp") * group_count
    utter_count = time_embed.shape[1]
    kept_float = kept_mask.astype(jnp.float32).reshape(row_count)
    local_index = lax.axis_index("seq") * local_rows + jnp.arange(local_rows, dtype=jnp.int32)

    def local_info(length_row):
        return segment_info(length_row, local_index)

    member_info = jax.vmap(local_info)(lengths)
    member_float = member_info[1].astype(jnp.float32)
    position = member_info[2]
    cos_table, sin_table = rotary_tables(position.reshape(row_count))
    cos_lanes = jnp.tile(cos_table[:, 0], (1, 4))
    sin_lanes = jnp.tile(jnp.concatenate([-sin_table[:, 0], sin_table[:, 0]], axis=1), (1, 2))
    silu_value, silu_pull = jax.vjp(jax.nn.silu, time_embed)
    condition = silu_value.astype(jnp.bfloat16)
    shard_rows = modulation.shape[0]
    utter_rows = group_count * utter_count
    condition_part = lax.dynamic_slice_in_dim(
        condition, lax.axis_index("seq") * shard_rows, shard_rows, 2
    ).reshape(utter_rows, shard_rows)
    partial = small_rows(
        seq_count, product(condition_part, modulation).reshape(6 * utter_rows, width)
    )
    partial = partial.at[seq_count - 1, 32 // seq_count - 1, 0].set(jnp.sum(kept_float))
    token = jnp.zeros((8, 128), jnp.float32)
    token = token.at[:utter_rows, :shard_rows].set(condition_part.astype(jnp.float32))
    late_shards = (readout, expand, contract)
    (combine_full, projection_full), partial_total, tokens = gather(3, partial, token, combine, projection)
    late_pieces = line_pieces(lax.optimization_barrier((late_shards, tokens))[0])
    combine_full = combine_full.reshape(2 * width, width)
    projection_full = projection_full.reshape(width, 3 * width)
    kept_total = jnp.sum(tokens[:, 4, 0])
    condition_all = tokens[:, :utter_rows, :shard_rows].reshape(-1, shard_rows).astype(jnp.bfloat16)
    joined = jnp.concatenate([frames, shortcut], axis=2).reshape(row_count, 2 * width)
    hidden = product(joined, combine_full)
    modulation_utter = partial_total.reshape(32, width)[:6 * utter_rows].reshape(
        group_count, utter_count, 6 * width
    )
    modulation_frame = jnp.einsum(
        "gtu,gue->gte",
        member_float,
        modulation_utter,
        precision=precise,
        preferred_element_type=jnp.float32,
    ).reshape(row_count, 6 * width)
    shift_first, scale_first, gate_first, shift_second, scale_second, gate_second = jnp.split(
        modulation_frame, 6, axis=1
    )
    normed_value, first_pull = jax.vjp(modulate, hidden, shift_first, scale_first)
    normed = normed_value.astype(jnp.bfloat16)
    packed = product(normed, projection_full)
    query_raw, key_raw, value_raw = jnp.split(packed, 3, axis=1)
    head_shape = (row_count, HEADS, HEAD_DIM)
    split_shape = (group_count, local_rows, width)

    def rotate_local(vectors):
        return rotate(vectors, cos_table, sin_table)

    query_turned, query_pull = jax.vjp(rotate_local, query_raw.reshape(head_shape))
    key_turned, key_pull = jax.vjp(rotate_local, key_raw.reshape(head_shape))
    local_width = width // seq_count

    def by_target(vectors):
        return vectors.reshape(group_count, local_rows, seq_count, local_width).astype(jnp.bfloat16)

    qkv = jnp.transpose(
        jnp.stack([by_target(query_turned), by_target(key_turned), by_target(value_raw)]),
        (3, 1, 0, 2, 4),
    )
    bounds = lengths[:, 0]
    kept_heads, mixture_blocks, log_total, *late_full = attend_forward(
        bounds, qkv, late_shards, late_pieces
    )
    readout_full = late_full[0].reshape(width, width)
    expand_full = late_full[1].reshape(width, -1)
    contract_full = late_full[2].reshape(-1, width)
    mixture = jnp.transpose(mixture_blocks, (1, 2, 0, 3)).reshape(row_count, width)
    branch = product(mixture, readout_full)
    middle = hidden + gate_first * branch
    second_value, second_pull = jax.vjp(modulate, middle, shift_second, scale_second)
    normed_second = second_value.astype(jnp.bfloat16)
    expanded = product(normed_second, expand_full)
    active_value, gelu_pull = jax.vjp(gelu_tanh, expanded)
    active = active_value.astype(jnp.bfloat16)
    contracted = product(active, contract_full)
    output = middle + gate_second * contracted
    loss_scale = all_frames / kept_total
    output_grad = (
        loss_scale
        * kept_float[:, None]
        * (output - target.reshape(row_count, width).astype(jnp.float32))
    )
    combine_back, projection_back, readout_back, expand_back, contract_back = (
        combine_full, projection_full, readout_full, expand_full, contract_full
    )
    gate_second_grad = output_grad * contracted
    contracted_grad = (gate_second * output_grad).astype(jnp.bfloat16)
    contract_part = product_left(active, contracted_grad)
    active_grad = product_right(contracted_grad, contract_back)
    expanded_grad = gelu_pull(active_grad)[0].astype(jnp.bfloat16)
    expand_part = product_left(normed_second, expanded_grad)
    normed_second_grad = product_right(expanded_grad, expand_back)
    middle_extra, shift_second_grad, scale_second_grad = second_pull(normed_second_grad)
    middle_grad = output_grad + middle_extra
    gate_first_grad = middle_grad * branch
    branch_grad = (gate_first * middle_grad).astype(jnp.bfloat16)
    readout_part = product_left(mixture, branch_grad)
    mixture_grad = product_right(branch_grad, readout_back).astype(jnp.bfloat16)
    back_blocks, *plane_pieces = attend_backward(
        bounds,
        kept_heads,
        jnp.transpose(
            mixture_grad.reshape(group_count, local_rows, seq_count, local_width), (2, 0, 1, 3)
        ),
        log_total,
        [part.astype(jnp.bfloat16) for part in (contract_part, expand_part, readout_part)],
    )
    late_grads = jnp.concatenate(
        [gate_first_grad, shift_second_grad, scale_second_grad, gate_second_grad], axis=1
    )
    late_part = jnp.einsum(
        "gtu,gte->gue",
        member_float,
        late_grads.reshape(group_count, local_rows, 4 * width),
        precision=precise,
        preferred_element_type=jnp.float32,
    )
    late_rows = jnp.transpose(
        late_part.reshape(utter_rows, 4, width), (1, 0, 2)
    ).reshape(4 * utter_rows, width)
    frames_grad, shortcut_grad, *shares, utters, condition_back = finish_backward(
        bounds,
        back_blocks,
        cos_lanes,
        sin_lanes,
        normed,
        hidden,
        middle_grad,
        frames.reshape(row_count, width),
        shortcut.reshape(row_count, width),
        combine_full,
        projection_full,
        partial_total.reshape(32, width),
        late_rows,
        modulation,
        plane_pieces,
        [contract.shape, expand.shape, readout.shape],
    )
    frames_grad = frames_grad.reshape(split_shape)
    shortcut_grad = shortcut_grad.reshape(split_shape)
    projection_grad, combine_grad, contract_grad, expand_grad, readout_grad = [
        share.astype(jnp.float32) for share in shares
    ]
    utter_all = jnp.transpose(
        utters.reshape(-1, 32, width)[:, :6 * utter_rows].reshape(-1, 6, utter_rows, width), (0, 2, 1, 3)
    ).reshape(-1, 6 * width).astype(jnp.bfloat16)
    modulation_grad = product_left(condition_all, utter_all)
    condition_grad = jnp.transpose(
        condition_back[:, :utter_rows, :shard_rows], (1, 0, 2)
    ).reshape(group_count, utter_count, width)
    time_grad = silu_pull(condition_grad)[0]
    summed = (combine_grad, modulation_grad, projection_grad, readout_grad, expand_grad, contract_grad)
    return (
        output.astype(jnp.bfloat16).reshape(split_shape),
        frames_grad,
        shortcut_grad,
        time_grad,
        summed[0],
        summed[1],
        summed[2],
        summed[3],
        summed[4],
        summed[5],
    )


def solution(mesh):
    return jax.shard_map(
        shards,
        mesh=mesh,
        in_specs=(
            P("grp", "seq", None),
            P("grp", "seq", None),
            P("grp", None, None),
            P("grp", None),
            P("grp", "seq"),
            P("grp", "seq", None),
            P("seq", None),
            P("seq", None),
            P("seq", None),
            P("seq", None),
            P("seq", None),
            P("seq", None),
        ),
        out_specs=(
            P("grp", "seq", None),
            P("grp", "seq", None),
            P("grp", "seq", None),
            P("grp", None, None),
            P("seq", None),
            P("seq", None),
            P("seq", None),
            P("seq", None),
            P("seq", None),
            P("seq", None),
        ),
        check_vma=False,
    )
```

```python
import functools
import math

import jax
import jax.numpy as jnp
from jax import lax
from jax.experimental import pallas as pl
from jax.experimental.pallas import tpu as pltpu
from jax.sharding import PartitionSpec as P

HEADS = 16
HEAD_DIM = 64


precise = lax.Precision.HIGHEST
epsilon = 1e-06
rope_base = 10000.0


def product(first_op, second_op):
    return jnp.dot(first_op, second_op, preferred_element_type=jnp.float32)


def product_left(first_op, second_op):
    return lax.dot_general(
        first_op, second_op, (((0,), (0,)), ((), ())), preferred_element_type=jnp.float32
    )


def product_right(first_op, second_op):
    return lax.dot_general(
        first_op, second_op, (((1,), (1,)), ((), ())), preferred_element_type=jnp.float32
    )


def gelu_tanh(values):
    return jax.nn.gelu(values, approximate=True)


def modulate(hidden, shift_part, scale_part):
    center = hidden - jnp.mean(hidden, axis=-1, keepdims=True)
    variance = jnp.mean(center * center, axis=-1, keepdims=True)
    return center * lax.rsqrt(variance + epsilon) * (1.0 + scale_part) + shift_part


def segment_info(lengths, frame_index):
    utter_count = lengths.shape[0]
    utter_ends = jnp.cumsum(lengths)
    starts = utter_ends - lengths
    segment = jnp.sum((frame_index[:, None] >= utter_ends[None, :]).astype(jnp.int32), axis=1)
    member = segment[:, None] == jnp.arange(utter_count, dtype=jnp.int32)[None, :]
    offset = jnp.sum(jnp.where(member, starts[None, :], 0), axis=1)
    return (segment, member, frame_index - offset)


def rotary_tables(position):
    half_dim = HEAD_DIM // 2
    ladder = jnp.arange(half_dim, dtype=jnp.float32) / half_dim
    inverse = jnp.exp(-jnp.log(rope_base) * ladder)
    angles = position.astype(jnp.float32)[:, None] * inverse[None, :]
    return (jnp.cos(angles)[:, None, :], jnp.sin(angles)[:, None, :])


def rotate(vectors, cos_table, sin_table):
    half_dim = vectors.shape[-1] // 2
    front_half = vectors[..., :half_dim]
    back_half = vectors[..., half_dim:]
    return jnp.concatenate(
        [
            front_half * cos_table - back_half * sin_table,
            back_half * cos_table + front_half * sin_table,
        ],
        axis=-1,
    )


MESH = pl.DeviceIdType.MESH
NEG = -1e30


def utter_features(boundary, total_rows, for_keys):
    row = lax.broadcasted_iota(jnp.int32, (total_rows, 128), 0)
    lane = lax.broadcasted_iota(jnp.int32, (total_rows, 128), 1)
    second = (row >= boundary).astype(jnp.float32)
    ahead = (lane == 0).astype(jnp.float32)
    after = (lane == 1).astype(jnp.float32)
    if for_keys:
        return (NEG * (second * ahead + (1.0 - second) * after)).astype(jnp.bfloat16)
    return (second * after + (1.0 - second) * ahead).astype(jnp.bfloat16)


def head_lanes(values, head):
    lane = lax.broadcasted_iota(jnp.int32, values.shape, 1)
    own = (lane >= head * HEAD_DIM) & (lane < (head + 1) * HEAD_DIM)
    return jnp.where(own, values.astype(jnp.float32), 0.0).astype(jnp.bfloat16)


def dot_nn(first_op, second_op):
    return jnp.dot(first_op, second_op, preferred_element_type=jnp.float32)


def dot_nt(first_op, second_op):
    return lax.dot_general(
        first_op, second_op, (((1,), (1,)), ((), ())), preferred_element_type=jnp.float32
    )


def fold_rows(values, combine):
    return combine(values.reshape(values.shape[0] // 8, 8, values.shape[1]), axis=0)


def enter(partners):
    barrier = pltpu.get_barrier_semaphore()
    for partner in partners:
        pl.semaphore_signal(barrier, inc=1, device_id=partner, device_id_type=MESH)
    pl.semaphore_wait(barrier, len(partners))


def key_span(third, total_rows):
    size = total_rows // 3
    return (max(third - 1, 0) * size, min(third + 2, 3) * size)


class Place:
    def __init__(self, plane, seq_count):
        self.rows_y, self.cols_x = rows_y, cols_x = plane
        self.grp, self.me = grp, me = lax.axis_index("grp"), lax.axis_index("seq")
        self.gy, self.gx = gy, gx = grp // cols_x, lax.rem(grp, cols_x)
        self.layers = layers = seq_count // 2
        self.layer, self.core = layer, core = me // 2, lax.rem(me, 2)
        self.xs = [lax.rem(gx + step, cols_x) for step in range(1, cols_x)]
        self.ys = [lax.rem(gy + step, rows_y) for step in range(1, rows_y)]
        self.beside = [gy * cols_x + x for x in self.xs]
        self.along = [y * cols_x + gx for y in self.ys]
        self.beside_from = [lax.rem(gx + cols_x - step, cols_x) for step in range(1, cols_x)]
        self.far = [lax.rem(layer + step, layers) for step in range(1, layers)]
        self.line_from = [lax.rem(layer + layers - step, layers) * 2 + core for step in range(1, layers)]
        self.lines = [target * 2 + core for target in self.far]
        self.partner = layer * 2 + 1 - core
        self.others = [lax.rem(me + step, seq_count) for step in range(1, seq_count)]
        self.groups = [lax.rem(grp + step, rows_y * cols_x) for step in range(1, rows_y * cols_x)]
        self.started = []

    def push(self, src, dst, sends, recvs, slot, device):
        copy = pltpu.make_async_remote_copy(
            src, dst, sends.at[slot], recvs.at[slot], device_id=device, device_id_type=MESH
        )
        copy.start()
        self.started.append(copy)
        return copy

    def sent(self):
        for copy in self.started:
            copy.wait_send()
        self.started = []


def window(ref, row, rows, col, cols):
    return ref.at[pl.ds(pl.multiple_of(row, 16), rows), pl.ds(pl.multiple_of(col, 128), cols)]


def piece_segments(shapes, side, width):
    base, found = 0, []
    for rows, cols in shapes:
        height, many = rows // side, cols // side // width
        if many == 1:
            half = width // 2
            found.append([[(base, 0, height, half, 0)], [(base, half, height, half, half)]])
        else:
            blocks = [(base + spot * height, 0, height, width, spot * width) for spot in range(many)]
            found.append([blocks[:many // 2], blocks[many // 2:]])
        base += height * many
    return found, base


class PlaneGather:
    def __init__(self, place, shards, pieces, segments, fulls, own_sem, first_send, first_recv, second_send, second_recv, core_send, core_recv):
        self.place, self.shards, self.pieces, self.fulls = place, shards, pieces, fulls
        self.segments = segments
        self.own_sem = own_sem
        self.first = (first_send, first_recv)
        self.second = (second_send, second_recv)
        self.core = (core_send, core_recv)
        self.jobs = [(index, step) for step in range(place.layers - 1) for index in range(len(shards))]
        self.waiting, self.local, self.own = {}, {}, []

    def sizes(self, index):
        _, rows, cols = self.fulls[index].shape
        return rows, rows // self.place.rows_y, cols // (2 * self.place.cols_x)

    def owner(self, step):
        return self.place.line_from[step]

    def begin(self):
        place = self.place
        for index, step in self.jobs:
            self.spread_first(index, step)
        for index, shard in enumerate(self.shards):
            copy = pltpu.make_async_copy(shard, self.fulls[index].at[place.me], self.own_sem.at[index, place.layers - 1, 0, 0])
            copy.start()
            push = place.push(shard, self.fulls[index].at[place.me], *self.core, (index, 0), (place.grp, place.partner))
            self.own.append((copy, push))

    def spread_first(self, index, step):
        place = self.place
        rows, height, width = self.sizes(index)
        full = self.fulls[index].at[self.owner(step)]
        piece = self.pieces.at[step]
        first_row, first_col = place.gy * height, 2 * place.gx * width
        self.local[index, step] = []
        self.waiting[index, step] = []
        for half, partners in enumerate((place.beside, place.along)):
            for spot, (row, col, rows, cols, off) in enumerate(self.segments[index][half]):
                source = piece.at[pl.ds(row, rows), pl.ds(col, cols)]
                part = window(full, first_row, rows, first_col + off, cols)
                copy = pltpu.make_async_copy(source, part, self.own_sem.at[index, step, half, spot])
                copy.start()
                self.local[index, step].append(copy)
                for hop, other in enumerate(partners):
                    self.waiting[index, step].append(place.push(
                        source, part, *self.first, (index, step, half, hop, spot), (other, place.me)
                    ))

    def spread_second(self, index, step):
        place = self.place
        rows, height, width = self.sizes(index)
        for copy in self.local.get((index, step), []):
            copy.wait()
        for copy in self.waiting[index, step]:
            copy.wait_recv()
        full = self.fulls[index].at[self.owner(step)]
        copies = []
        for hop, other in enumerate(place.along):
            for spot, column in enumerate([place.gx] + place.beside_from):
                part = window(full, place.gy * height, height, 2 * column * width, width)
                copies.append(place.push(part, part, *self.second, (index, step, 0, hop, spot), (other, place.me)))
        for hop, other in enumerate(place.beside):
            part = window(full, 0, rows, (2 * place.gx + 1) * width, width)
            copies.append(place.push(part, part, *self.second, (index, step, 1, hop, 0), (other, place.me)))
        self.waiting[index, step] = copies

    def over_core(self, index, step):
        place = self.place
        for copy in self.waiting[index, step]:
            copy.wait_recv()
        full = self.fulls[index].at[self.owner(step)]
        self.waiting[index, step] = [
            place.push(full, full, *self.core, (index, step + 1), (place.grp, place.partner))
        ]

    def middle(self):
        for job in self.jobs:
            self.spread_second(*job)

    def late(self):
        return [functools.partial(self.over_core, *job) for job in self.jobs]

    def arrive(self, index):
        for job in self.jobs:
            if job[0] == index:
                for copy in self.waiting[job]:
                    copy.wait_recv()
        copy, push = self.own[index]
        copy.wait()
        push.wait_recv()

    def finish(self):
        self.place.sent()


def add_rows(target, source, first_row, rows, first_col, cols, out=None):
    step = 16
    col = pl.multiple_of(first_col, 128)

    def one(index, carry):
        at = pl.ds(pl.multiple_of(first_row + index * step, step), step)
        off = pl.ds(pl.multiple_of(index * step, step), step)
        value = target[at, pl.ds(col, cols)] + source[off, :]
        if out is None:
            target[at, pl.ds(col, cols)] = value
        else:
            out[off, :] = value
        return carry

    lax.fori_loop(0, rows // step, one, 0)


def add_segments(target, source, first_row, first_col, segments, out):
    for row, col, rows, cols, off in segments:
        begin = off - segments[0][4]
        add_rows(
            target, source.at[:, pl.ds(begin, cols)], first_row, rows, first_col + off, cols,
            out.at[pl.ds(row, rows), pl.ds(col, cols)],
        )


def plane_sum_scratch(parts, side, in_place=False):
    layers = parts[0].shape[0] // 2
    hops = max(side - 1, 1)
    count = len(parts)
    dma = pltpu.SemaphoreType.DMA

    def buffers(lead, row_cut, col_cut):
        return [
            pltpu.VMEM(lead + (part.shape[1] // row_cut, part.shape[2] // col_cut), jnp.bfloat16)
            for part in parts
        ]

    return (
        ([] if in_place else buffers((layers,), 1, 1))
        + buffers((layers,), 1, 1)
        + buffers((layers, hops, side), side, 2 * side)
        + buffers((layers, hops), side, 2 * side)
        + buffers((layers, hops), 1, 2 * side)
        + buffers((layers, hops), side, 2 * side)
        + [
            dma((count, layers)), dma((count, layers)), dma((count, layers)),
            dma((count, layers, 2, hops, side)), dma((count, layers, 2, hops, side)),
            dma((count, layers, 2, hops)), dma((count, layers, 2, hops)),
        ]
    )


def by_owner(parts, seq_count):
    return [part.reshape(seq_count, part.shape[0] // seq_count, part.shape[1]) for part in parts]


class PlaneSum:
    def __init__(self, place, parts, pieces, segments, buffers, semaphores, in_place=False):
        self.place, self.parts, self.pieces, self.segments = place, parts, pieces, segments
        count = len(parts)
        buffers = (() if in_place else buffers[:count], *[
            buffers[index * count:(index + 1) * count] for index in range(0 if in_place else 1, 5 if in_place else 6)
        ])
        self.in_place = in_place
        self.sums, self.swapped, self.y_first, self.x_second, self.x_first, self.y_second = buffers
        self.load_sem = semaphores[0]
        self.core, self.first_sem, self.second_sem = semaphores[1:3], semaphores[3:5], semaphores[5:7]
        self.order = place.far + [place.layer]
        self.jobs = [(index, step) for index in range(count) for step in range(place.layers)]
        self.loads, self.swaps, self.waiting = {}, {}, {}

    def sizes(self, index):
        _, rows, cols = self.parts[index].shape
        return rows, cols, rows // self.place.rows_y, cols // (2 * self.place.cols_x)

    def begin(self):
        place = self.place
        for index, step in self.jobs:
            target = self.order[step]
            copy = pltpu.make_async_copy(
                self.parts[index].at[target * 2 + place.core], self.sums[index].at[step], self.load_sem.at[index, step]
            )
            copy.start()
            self.loads[index, step] = copy
            self.swap(index, step)

    def swap(self, index, step):
        place = self.place
        self.swaps[index, step] = place.push(
            self.parts[index].at[self.order[step] * 2 + 1 - place.core], self.swapped[index].at[step],
            *self.core, (index, step), (place.grp, place.partner),
        )

    def running(self, index, step):
        if self.in_place:
            return self.parts[index].at[self.order[step] * 2 + self.place.core]
        return self.sums[index].at[step]

    def first(self, index, step):
        place = self.place
        rows, cols, height, width = self.sizes(index)
        if not self.in_place:
            self.loads[index, step].wait()
        self.swaps[index, step].wait_recv()
        total = self.running(index, step)
        add_rows(total, self.swapped[index].at[step], 0, rows, 0, cols)
        copies = []
        for hop, other in enumerate(place.along):
            for column in range(place.cols_x):
                copies.append(place.push(
                    window(total, place.ys[hop] * height, height, 2 * column * width, width),
                    self.y_first[index].at[step, hop, column],
                    *self.first_sem, (index, step, 0, hop, column), (other, place.me),
                ))
        for hop, other in enumerate(place.beside):
            copies.append(place.push(
                window(total, 0, rows, (2 * place.xs[hop] + 1) * width, width),
                self.x_first[index].at[step, hop],
                *self.first_sem, (index, step, 1, hop, 0), (other, place.me),
            ))
        self.waiting[index, step] = copies

    def second(self, index, step):
        place = self.place
        rows, cols, height, width = self.sizes(index)
        for copy in self.waiting[index, step]:
            copy.wait_recv()
        total = self.running(index, step)
        for hop in range(place.rows_y - 1):
            for column in range(place.cols_x):
                add_rows(
                    total, self.y_first[index].at[step, hop, column],
                    place.gy * height, height, 2 * column * width, width,
                )
        for hop in range(place.cols_x - 1):
            add_rows(total, self.x_first[index].at[step, hop], 0, rows, (2 * place.gx + 1) * width, width)
        copies = []
        for hop, other in enumerate(place.beside):
            copies.append(place.push(
                window(total, place.gy * height, height, 2 * place.xs[hop] * width, width),
                self.x_second[index].at[step, hop],
                *self.second_sem, (index, step, 0, hop), (other, place.me),
            ))
        for hop, other in enumerate(place.along):
            copies.append(place.push(
                window(total, place.ys[hop] * height, height, (2 * place.gx + 1) * width, width),
                self.y_second[index].at[step, hop],
                *self.second_sem, (index, step, 1, hop), (other, place.me),
            ))
        self.waiting[index, step] = copies

    def third(self, index, step):
        place = self.place
        rows, cols, height, width = self.sizes(index)
        for copy in self.waiting[index, step]:
            copy.wait_recv()
        self.waiting[index, step] = []
        total = self.running(index, step)
        out = self.pieces[index][step]
        row, col = place.gy * height, 2 * place.gx * width
        for hop in range(place.cols_x - 1):
            source = self.x_second[index].at[step, hop]
            if hop == place.cols_x - 2:
                add_segments(total, source, row, col, self.segments[index][0], out)
            else:
                add_rows(total, source, row, height, col, width)
        for hop in range(place.rows_y - 1):
            source = self.y_second[index].at[step, hop]
            if hop == place.rows_y - 2:
                add_segments(total, source, row, col, self.segments[index][1], out)
            else:
                add_rows(total, source, row, height, col + width, width)

    def steps(self, stage, only=None):
        return [functools.partial(stage, *job) for job in self.jobs if only is None or job[0] == only]

    def finish(self):
        self.place.sent()


class PlaneSpread:
    def __init__(self, place, outs, first_send, first_recv, second_send, second_recv):
        self.place, self.outs = place, outs
        self.first_sem, self.second_sem = (first_send, first_recv), (second_send, second_recv)
        self.waiting = {}

    def sizes(self, index):
        rows, cols = self.outs[index].shape
        return rows, rows // self.place.rows_y, cols // (2 * self.place.cols_x)

    def total(self, index, piece, others, segments):
        place = self.place
        rows, height, width = self.sizes(index)
        row = place.gy * height
        col = pl.multiple_of(2 * place.gx * width, 128)
        for first, left, _, cols, off in segments[0] + segments[1]:

            def one(turn, carry):
                at = pl.ds(pl.multiple_of(first + turn * 16, 16), 16)
                value = piece[at, pl.ds(left, cols)].astype(jnp.float32)
                for other in others:
                    value = value + other[at, pl.ds(left, cols)].astype(jnp.float32)
                self.outs[index][
                    pl.ds(pl.multiple_of(row + turn * 16, 16), 16), pl.ds(pl.multiple_of(col + off, 128), cols)
                ] = value.astype(jnp.bfloat16)
                return carry

            lax.fori_loop(0, height // 16, one, 0)
        copies = []
        for hop, other in enumerate(place.beside):
            part = window(self.outs[index], row, height, 2 * place.gx * width, width)
            copies.append(place.push(part, part, *self.first_sem, (index, 0, hop), (other, place.me)))
        for hop, other in enumerate(place.along):
            part = window(self.outs[index], row, height, (2 * place.gx + 1) * width, width)
            copies.append(place.push(part, part, *self.first_sem, (index, 1, hop), (other, place.me)))
        self.waiting[index] = copies

    def second(self, index):
        place = self.place
        rows, height, width = self.sizes(index)
        for copy in self.waiting[index]:
            copy.wait_recv()
        copies = []
        for hop, other in enumerate(place.along):
            for spot, column in enumerate([place.gx] + place.beside_from):
                part = window(self.outs[index], place.gy * height, height, 2 * column * width, width)
                copies.append(place.push(part, part, *self.second_sem, (index, 0, hop, spot), (other, place.me)))
        for hop, other in enumerate(place.beside):
            part = window(self.outs[index], 0, rows, (2 * place.gx + 1) * width, width)
            copies.append(place.push(part, part, *self.second_sem, (index, 1, hop, 0), (other, place.me)))
        self.waiting[index] = copies

    def finish(self, index):
        for copy in self.waiting[index]:
            copy.wait_recv()


def small_rows(seq_count, values):
    rows = jnp.concatenate([values, jnp.zeros((32 - values.shape[0], values.shape[1]), jnp.float32)])
    return rows.reshape(seq_count, 32 // seq_count, values.shape[1])


class SmallSum:
    def __init__(self, place, source, total, scratch, first_send, first_recv, second_send, second_recv):
        self.place, self.source, self.total_ref, self.scratch = place, source, total, scratch
        self.first_sem, self.second_sem = (first_send, first_recv), (second_send, second_recv)

    def begin(self):
        place = self.place
        self.waiting = [
            place.push(self.source.at[other], self.scratch.at[step], *self.first_sem, step, (place.grp, other))
            for step, other in enumerate(place.others)
        ]

    def middle(self):
        place = self.place
        value = self.source[place.me]
        for step, copy in enumerate(self.waiting):
            copy.wait_recv()
            value = value + self.scratch[step]
        self.total_ref[place.me] = value
        part = self.total_ref.at[place.me]
        self.waiting = [
            place.push(part, part, *self.second_sem, step, (place.grp, other))
            for step, other in enumerate(place.others)
        ]

    def finish(self):
        for copy in self.waiting:
            copy.wait_recv()


def small_scratch(source):
    seq_count = source.shape[0]
    dma = pltpu.SemaphoreType.DMA
    return [pltpu.VMEM((seq_count - 1,) + source.shape[1:], jnp.float32)] + [dma((seq_count - 1,))] * 4


def forward_kernel(plane, seq_count, count, *refs):
    layers = seq_count // 2
    bound_ref, qkv_ref, shards = refs[0], refs[1], refs[2:2 + count]
    refs = refs[2 + count:]
    pieces, refs = refs[0], refs[1:]
    kept_ref, mixture_ref, log_ref, fulls = refs[0], refs[1], refs[2], refs[3:3 + count]
    (
        key_scr, query_scr, value_t_scr, score_scr, mix_t_scr, mix_scr,
        send_sem, recv_sem, back_send_sem, back_recv_sem, local_sem,
    ) = refs[3 + count:14 + count]
    own_sem, first_send, first_recv, second_send, second_recv, core_send, core_recv = refs[14 + count:]
    group_count, local_rows, local_width = qkv_ref.shape[1], qkv_ref.shape[3], qkv_ref.shape[4]
    total_rows = seq_count * local_rows
    heads = local_width // HEAD_DIM
    me = lax.axis_index("seq")
    grp = lax.axis_index("grp")
    others = [lax.rem(me + step, seq_count) for step in range(1, seq_count)]
    origins = [lax.rem(me + seq_count - step, seq_count) for step in range(1, seq_count)]
    block = min(256, total_rows // 3)
    place = Place(plane, seq_count)
    enter([(grp, other) for other in others] + [(other, me) for other in place.beside + place.along])
    copies = []

    def begin_group(group):
        own = pltpu.make_async_copy(qkv_ref.at[me, group], kept_ref.at[me, group], local_sem.at[group])
        own.start()
        row = [own]
        for step, other in enumerate(others):
            copy = pltpu.make_async_remote_copy(
                qkv_ref.at[other, group], kept_ref.at[me, group],
                send_sem.at[group, step], recv_sem.at[group, step],
                device_id=(grp, other), device_id_type=MESH,
            )
            copy.start()
            row.append(copy)
        copies.append(row)

    begin_group(0)
    side = place.cols_x
    segments, _ = piece_segments(
        [shard.shape for shard in shards], side, min(shard.shape[1] for shard in shards) // side
    )
    spread = PlaneGather(
        place, shards, pieces, segments, fulls,
        own_sem, first_send, first_recv, second_send, second_recv, core_send, core_recv,
    )
    spread.begin()
    back = []
    for group in range(group_count):
        for copy in copies[group]:
            copy.wait()
        if group + 1 < group_count:
            begin_group(group + 1)
        if group == 0:
            spread.middle()
            hooks = spread.late()
            held = len(hooks) // 3
        boundary = bound_ref[group]
        keys = kept_ref[:, group, 1].reshape(total_rows, local_width)
        values = kept_ref[:, group, 2].reshape(total_rows, local_width)
        key_scr[:, :local_width] = keys
        key_scr[:, local_width:] = utter_features(boundary, total_rows, True)
        query_scr[:, local_width:] = utter_features(boundary, total_rows, False)
        value_t_scr[...] = values.astype(jnp.float32).T.astype(jnp.bfloat16)

        for head in range(heads):
            queries = kept_ref[:, group, 0].reshape(total_rows, local_width)
            query_scr[:, :local_width] = head_lanes(queries, head) * jnp.bfloat16(HEAD_DIM ** (-0.5))
            for third in range(3):
                first_key, last_key = key_span(third, total_rows)
                chunks = range(first_key, last_key, block)

                def one_block(index, carry):
                    first_row = pl.multiple_of(third * (total_rows // 3) + index * block, block)
                    query_block = query_scr[pl.ds(first_row, block), :]
                    peak = jnp.full((8, block), -jnp.inf, jnp.float32)
                    for first in chunks:
                        scores = dot_nt(key_scr[first:first + block, :], query_block)
                        score_scr[first:first + block, :] = scores
                        peak = jnp.maximum(peak, fold_rows(scores, jnp.max))
                    peak = jnp.max(peak, axis=0, keepdims=True)
                    total = jnp.zeros((8, block), jnp.float32)
                    for first in chunks:
                        lifted = jnp.exp(score_scr[first:first + block, :] - peak)
                        score_scr[first:first + block, :] = lifted
                        total = total + fold_rows(lifted, jnp.sum)
                    total = jnp.sum(total, axis=0, keepdims=True)
                    inverse = 1.0 / total
                    mixed = jnp.zeros((HEAD_DIM, block), jnp.float32)
                    rows = slice(head * HEAD_DIM, (head + 1) * HEAD_DIM)
                    for first in chunks:
                        weight = (score_scr[first:first + block, :] * inverse).astype(jnp.bfloat16)
                        mixed = mixed + dot_nn(value_t_scr[rows, first:first + block], weight)
                    mix_t_scr[rows, pl.ds(first_row, block)] = mixed
                    log_ref[group, head, :, pl.ds(first_row, block)] = peak + jnp.log(total)
                    return carry

                lax.fori_loop(0, total_rows // 3 // block, one_block, 0)
                if group > 0 and len(hooks) > held:
                    hooks.pop(0)()
        mix_scr[group] = mix_t_scr[...].T.astype(jnp.bfloat16).reshape(seq_count, local_rows, local_width)
        own = pltpu.make_async_copy(
            mix_scr.at[group, me], mixture_ref.at[me, group], local_sem.at[group_count + group]
        )
        own.start()
        back.append(own)
        for step, other in enumerate(others):
            copy = pltpu.make_async_remote_copy(
                mix_scr.at[group, other], mixture_ref.at[me, group],
                back_send_sem.at[group, step], back_recv_sem.at[group, step],
                device_id=(grp, other), device_id_type=MESH,
            )
            copy.start()
            back.append(copy)
    for hook in hooks:
        hook()
    for copy in back:
        copy.wait()
    for index in range(count):
        spread.arrive(index)
    spread.finish()


def attend_forward(bounds, qkv, shards, pieces):
    side = math.isqrt(lax.axis_size("grp"))
    hops = max(side - 1, 1)
    count = len(shards)
    dma = pltpu.SemaphoreType.DMA
    anywhere = pl.BlockSpec(memory_space=pl.ANY)
    layers = qkv.shape[0] // 2
    seq_count, group_count, _, local_rows, local_width = qkv.shape
    total_rows = seq_count * local_rows
    heads = local_width // HEAD_DIM
    block = min(256, total_rows // 3)
    vmem = pl.BlockSpec(memory_space=pltpu.VMEM)
    return pl.pallas_call(
        functools.partial(forward_kernel, (side, side), seq_count, count),
        out_shape=(
            jax.ShapeDtypeStruct(qkv.shape, jnp.bfloat16),
            jax.ShapeDtypeStruct((seq_count, group_count, local_rows, local_width), jnp.bfloat16),
            jax.ShapeDtypeStruct((group_count, heads, 1, total_rows), jnp.float32),
        ) + tuple(jax.ShapeDtypeStruct((seq_count,) + part.shape, part.dtype) for part in shards),
        in_specs=[pl.BlockSpec(memory_space=pltpu.SMEM)] + [anywhere] * (2 + count),
        out_specs=(vmem, vmem, vmem) + (anywhere,) * count,
        scratch_shapes=[
            pltpu.VMEM((total_rows, local_width + 128), jnp.bfloat16),
            pltpu.VMEM((total_rows, local_width + 128), jnp.bfloat16),
            pltpu.VMEM((local_width, total_rows), jnp.bfloat16),
            pltpu.VMEM((total_rows, block), jnp.float32),
            pltpu.VMEM((local_width, total_rows), jnp.float32),
            pltpu.VMEM((group_count, seq_count, local_rows, local_width), jnp.bfloat16),
            pltpu.SemaphoreType.DMA((group_count, seq_count - 1)),
            pltpu.SemaphoreType.DMA((group_count, seq_count - 1)),
            pltpu.SemaphoreType.DMA((group_count, seq_count - 1)),
            pltpu.SemaphoreType.DMA((group_count, seq_count - 1)),
            pltpu.SemaphoreType.DMA((2 * group_count,)),
            dma((count, layers, 2, 2)),
            dma((count, layers - 1, 2, hops, 2)), dma((count, layers - 1, 2, hops, 2)),
            dma((count, layers - 1, 2, hops, side)), dma((count, layers - 1, 2, hops, side)),
            dma((count, layers)), dma((count, layers)),
        ],
        compiler_params=pltpu.CompilerParams(
            collective_id=1, has_side_effects=True, vmem_limit_bytes=48 * 1024 * 1024
        ),
        name="attend_forward",
    )(bounds, qkv, *shards, pieces)


def backward_kernel(plane, seq_count, count, *refs):
    layers = seq_count // 2
    bound_ref, kept_ref, grad_ref, log_ref = refs[:4]
    parts, refs = refs[4:4 + count], refs[4 + count:]
    out_ref, refs = refs[0], refs[1:]
    pieces, refs = refs[:layers], refs[layers:]
    (
        taken_scr, key_scr, query_scr, key_t_scr, head_query_scr, head_grad_scr, prob_scr, weight_scr,
        query_t_scr, key_sum_scr, value_sum_scr, back_scr,
        send_sem, recv_sem, back_send_sem, back_recv_sem, local_sem,
    ) = refs[:17]
    buffers, semaphores = refs[17:17 + 6 * count], refs[17 + 6 * count:]
    group_count, local_rows, local_width = grad_ref.shape[1], grad_ref.shape[2], grad_ref.shape[3]
    total_rows = seq_count * local_rows
    heads = local_width // HEAD_DIM
    me = lax.axis_index("seq")
    grp = lax.axis_index("grp")
    others = [lax.rem(me + step, seq_count) for step in range(1, seq_count)]
    block = min(256, total_rows // 3)
    place = Place(plane, seq_count)
    enter([(grp, other) for other in others] + [(other, me) for other in place.beside + place.along])
    copies = []

    def begin_group(group):
        own = pltpu.make_async_copy(grad_ref.at[me, group], taken_scr.at[me, group], local_sem.at[group])
        own.start()
        row = [own]
        for step, other in enumerate(others):
            copy = pltpu.make_async_remote_copy(
                grad_ref.at[other, group], taken_scr.at[me, group],
                send_sem.at[group, step], recv_sem.at[group, step],
                device_id=(grp, other), device_id_type=MESH,
            )
            copy.start()
            row.append(copy)
        copies.append(row)

    begin_group(0)
    side = place.cols_x
    segments, _ = piece_segments(
        [part.shape[1:] for part in parts], side, min(part.shape[2] for part in parts) // side
    )
    plane_sum = PlaneSum(place, parts, [pieces] * count, segments, buffers, semaphores)
    plane_sum.begin()
    firsts = plane_sum.steps(plane_sum.first)
    seconds = plane_sum.steps(plane_sum.second)
    units = 3 * heads * group_count
    plan = [[] for _ in range(units + 1)]
    for spot, hook in enumerate(firsts):
        plan[spot * (units // 2 - 1) // len(firsts)].append(hook)
    for spot, hook in enumerate(seconds):
        plan[units - 5 + spot * 6 // len(seconds)].append(hook)
    back = []
    for group in range(group_count):
        for copy in copies[group]:
            copy.wait()
        if group + 1 < group_count:
            begin_group(group + 1)
        boundary = bound_ref[group]
        keys = kept_ref[:, group, 1].reshape(total_rows, local_width)
        key_scr[:, :local_width] = keys
        key_scr[:, local_width:] = utter_features(boundary, total_rows, True)
        query_scr[:, local_width:] = utter_features(boundary, total_rows, False)
        key_t_scr[...] = keys.astype(jnp.float32).T.astype(jnp.bfloat16)
        key_sum_scr[...] = jnp.zeros_like(key_sum_scr)
        value_sum_scr[...] = jnp.zeros_like(value_sum_scr)

        for head in range(heads):
            queries = head_lanes(kept_ref[:, group, 0].reshape(total_rows, local_width), head)
            head_query_scr[...] = queries
            query_scr[:, :local_width] = queries * jnp.bfloat16(HEAD_DIM ** (-0.5))
            head_grad_scr[...] = head_lanes(taken_scr[:, group].reshape(total_rows, local_width), head)
            for third in range(3):
                first_key, last_key = key_span(third, total_rows)
                chunks = range(first_key, last_key, block)

                def one_block(index, carry):
                    first_row = pl.multiple_of(third * (total_rows // 3) + index * block, block)
                    own_rows = pl.ds(first_row, block)
                    query_block = query_scr[own_rows, :]
                    grad_block = head_grad_scr[own_rows, :]
                    plain_block = head_query_scr[own_rows, :]
                    log_block = log_ref[group, head, :, own_rows]
                    row_dot = jnp.zeros((8, block), jnp.float32)
                    for first in chunks:
                        scores = dot_nt(key_scr[first:first + block, :], query_block)
                        prob = jnp.exp(scores - log_block)
                        values = kept_ref[
                            first // local_rows:(first + block - 1) // local_rows + 1, group, 2
                        ].reshape(-1, local_width)
                        skip = first % local_rows
                        weight_grad = dot_nt(values[skip:skip + block], grad_block)
                        prob_scr[first:first + block, :] = prob
                        weight_scr[first:first + block, :] = weight_grad
                        row_dot = row_dot + fold_rows(prob * weight_grad, jnp.sum)
                    row_dot = jnp.sum(row_dot, axis=0, keepdims=True)
                    rows = slice(head * HEAD_DIM, (head + 1) * HEAD_DIM)
                    turned = jnp.zeros((HEAD_DIM, block), jnp.float32)
                    for first in chunks:
                        prob = prob_scr[first:first + block, :]
                        score_grad = (
                            HEAD_DIM ** (-0.5) * (prob * (weight_scr[first:first + block, :] - row_dot))
                        ).astype(jnp.bfloat16)
                        key_sum_scr[first:first + block, :] += dot_nn(score_grad, plain_block)
                        value_sum_scr[first:first + block, :] += dot_nn(
                            prob.astype(jnp.bfloat16), grad_block
                        )
                        turned = turned + dot_nn(key_t_scr[rows, first:first + block], score_grad)
                    query_t_scr[rows, own_rows] = turned
                    return carry

                lax.fori_loop(0, total_rows // 3 // block, one_block, 0)
                for hook in plan.pop(0):
                    hook()
        shape = (seq_count, local_rows, local_width)
        back_scr[:, group, 0] = query_t_scr[...].T.astype(jnp.bfloat16).reshape(shape)
        back_scr[:, group, 1] = key_sum_scr[...].astype(jnp.bfloat16).reshape(shape)
        back_scr[:, group, 2] = value_sum_scr[...].astype(jnp.bfloat16).reshape(shape)
        own = pltpu.make_async_copy(
            back_scr.at[me, group], out_ref.at[me, group], local_sem.at[group_count + group]
        )
        own.start()
        back.append(own)
        for step, other in enumerate(others):
            copy = pltpu.make_async_remote_copy(
                back_scr.at[other, group], out_ref.at[me, group],
                back_send_sem.at[group, step], back_recv_sem.at[group, step],
                device_id=(grp, other), device_id_type=MESH,
            )
            copy.start()
            back.append(copy)
    for hook in plan[0] + plane_sum.steps(plane_sum.third):
        hook()
    for copy in back:
        copy.wait()
    plane_sum.finish()


def attend_backward(bounds, kept, grad, log_total, parts):
    side = math.isqrt(lax.axis_size("grp"))
    count = len(parts)
    layers = kept.shape[0] // 2
    anywhere = pl.BlockSpec(memory_space=pl.ANY)
    parts = by_owner(parts, kept.shape[0])
    width = min(part.shape[2] for part in parts) // side
    _, piece_rows = piece_segments([part.shape[1:] for part in parts], side, width)
    seq_count, group_count, _, local_rows, local_width = kept.shape
    total_rows = seq_count * local_rows
    block = min(256, total_rows // 3)
    vmem = pl.BlockSpec(memory_space=pltpu.VMEM)
    return pl.pallas_call(
        functools.partial(backward_kernel, (side, side), seq_count, count),
        out_shape=(jax.ShapeDtypeStruct(kept.shape, jnp.bfloat16),) + tuple(
            jax.ShapeDtypeStruct((piece_rows, width), jnp.bfloat16) for _ in range(layers)
        ),
        in_specs=[pl.BlockSpec(memory_space=pltpu.SMEM), vmem, anywhere, vmem] + [anywhere] * count,
        out_specs=(vmem,) * (1 + layers),
        scratch_shapes=[
            pltpu.VMEM(grad.shape, jnp.bfloat16),
            pltpu.VMEM((total_rows, local_width + 128), jnp.bfloat16),
            pltpu.VMEM((total_rows, local_width + 128), jnp.bfloat16),
            pltpu.VMEM((local_width, total_rows), jnp.bfloat16),
            pltpu.VMEM((total_rows, local_width), jnp.bfloat16),
            pltpu.VMEM((total_rows, local_width), jnp.bfloat16),
            pltpu.VMEM((total_rows, block), jnp.float32),
            pltpu.VMEM((total_rows, block), jnp.float32),
            pltpu.VMEM((local_width, total_rows), jnp.float32),
            pltpu.VMEM((total_rows, local_width), jnp.float32),
            pltpu.VMEM((total_rows, local_width), jnp.float32),
            pltpu.VMEM(kept.shape, jnp.bfloat16),
            pltpu.SemaphoreType.DMA((group_count, seq_count - 1)),
            pltpu.SemaphoreType.DMA((group_count, seq_count - 1)),
            pltpu.SemaphoreType.DMA((group_count, seq_count - 1)),
            pltpu.SemaphoreType.DMA((group_count, seq_count - 1)),
            pltpu.SemaphoreType.DMA((2 * group_count,)),
        ] + plane_sum_scratch(parts, side),
        compiler_params=pltpu.CompilerParams(
            collective_id=2, has_side_effects=True, vmem_limit_bytes=60 * 1024 * 1024
        ),
        name="attend_backward",
    )(bounds, kept, grad, log_total, *parts)


class LineChain:
    def __init__(self, place, sources, slots, sends, recvs):
        self.place, self.sources, self.slots = place, sources, slots
        self.sends, self.recvs = sends, recvs
        self.pushed = []
        middle = []
        low, high = 0, place.layers - 2
        while low <= high:
            middle += [low] if low == high else [low, high]
            low, high = low + 1, high - 1
        first, last = place.layer == 0, place.layer == place.layers - 1
        self.ranks = [
            jnp.where(first, place.layers - 2 - rank, jnp.where(last, rank, step)).astype(jnp.int32)
            for rank, step in enumerate(middle)
        ]

    def owner(self, step):
        place = self.place
        return lax.rem(place.layer + place.layers - 1 - step, place.layers) * 2 + place.core

    def copy(self, index, source, owner, slot, target, send_slot):
        return pltpu.make_async_remote_copy(
            source, self.slots(index, owner, slot),
            self.sends.at[index, send_slot], self.recvs.at[index, slot],
            device_id=(self.place.grp, target * 2 + self.place.core), device_id_type=MESH,
        )

    def push(self, when, *given):
        self.pushed.append((when, given))

        @pl.when(when)
        def _():
            self.copy(*given).start()

    def begin(self, index):
        place = self.place
        source = self.sources[index]
        self.push(place.layer < place.layers - 1, index, source, place.me, 0, place.layer + 1, 0)
        self.push(place.layer > 0, index, source, place.me, place.layers - 2, place.layer - 1, 1)

    def forward(self, index, rank):
        place = self.place
        step = self.ranks[rank]
        owner = self.owner(step)
        held = self.slots(index, owner, step)
        self.copy(index, held, owner, step, place.layer, 0).wait_recv()
        below = step < place.layer
        going = (below & (place.layer < place.layers - 1)) | ((step >= place.layer) & (place.layer > 0))
        slot = jnp.where(below, step + 1, step - 1)
        target = jnp.where(below, place.layer + 1, place.layer - 1)
        self.push(going, index, held, owner, slot, target, rank + 2)
        return owner

    def sent(self):
        for when, given in self.pushed:

            @pl.when(when)
            def _(given=given):
                self.copy(*given).wait_send()


class WholeGather(PlaneGather):
    def __init__(self, place, shards, fulls, line_send, line_recv, *semaphores):
        super().__init__(place, shards, None, None, fulls, *semaphores)

        def piece(ref, index):
            rows, height, width = self.sizes(index)
            return window(ref, place.gy * height, height, 2 * place.gx * width, 2 * width)

        self.chain = LineChain(
            place, [piece(shard, index) for index, shard in enumerate(shards)],
            lambda index, owner, slot: piece(fulls[index].at[owner], index), line_send, line_recv,
        )
        self.jobs = [(index, rank) for index in range(len(shards)) for rank in range(place.layers - 1)]

    def owner(self, step):
        return self.chain.owner(self.chain.ranks[step])

    def begin(self):
        place = self.place
        for index in range(len(self.shards)):
            self.chain.begin(index)
        for index, shard in enumerate(self.shards):
            copy = pltpu.make_async_copy(shard, self.fulls[index].at[place.me], self.own_sem.at[index, place.layers - 1, 0, 0])
            copy.start()
            push = place.push(shard, self.fulls[index].at[place.me], *self.core, (index, 0), (place.grp, place.partner))
            self.own.append((copy, push))

    def spread_first(self, index, step):
        place = self.place
        rows, height, width = self.sizes(index)
        full = self.fulls[index].at[self.chain.forward(index, step)]
        row, col = place.gy * height, 2 * place.gx * width
        self.waiting[index, step] = []
        for half, partners in enumerate((place.beside, place.along)):
            part = window(full, row, height, col + half * width, width)
            for hop, other in enumerate(partners):
                self.waiting[index, step].append(
                    place.push(part, part, *self.first, (index, step, half, hop, 0), (other, place.me))
                )

    def finish(self):
        super().finish()
        self.chain.sent()


def turn_lanes(values, cos, sin):
    lane = lax.broadcasted_iota(jnp.int32, values.shape, 1)
    ahead = pltpu.roll(values, values.shape[1] - HEAD_DIM // 2, 1)
    behind = pltpu.roll(values, HEAD_DIM // 2, 1)
    other = jnp.where(lax.rem(lane, HEAD_DIM) < HEAD_DIM // 2, ahead, behind)
    return values * cos + other * sin


def second_mask(bound_ref, group, me, local_rows, first, rows):
    row = lax.broadcasted_iota(jnp.int32, (rows, 1), 0) + (me * local_rows + first)
    return row >= bound_ref[group]


def centered(values):
    center = values - jnp.mean(values, axis=-1, keepdims=True)
    scale = lax.rsqrt(jnp.mean(center * center, axis=-1, keepdims=True) + epsilon)
    return center * scale, scale


def front_kernel(plane, seq_count, late_count, *refs):
    layers = seq_count // 2
    bound_ref, frames_ref, shortcut_ref, cos_ref, sin_ref, partial_ref, token_ref = refs[:7]
    shards, late_shards, refs = refs[7:9], refs[9:9 + late_count], refs[9 + late_count:]
    fulls_out, late_out, refs = refs[:2], refs[2], refs[3:]
    hidden_ref, normed_ref, qkv_ref, total_ref, tokens_ref = refs[:5]
    fulls, refs = refs[5:7], refs[7:]
    token_scr, token_send, token_recv, out_sem = refs[:4]
    small_refs, (late_scr, late_send, late_recv, late_sem), refs = refs[4:9], refs[9:13], refs[13:]
    group_count, local_rows, local_width = qkv_ref.shape[1], qkv_ref.shape[3], qkv_ref.shape[4]
    row_count, width = hidden_ref.shape
    place = Place(plane, seq_count)
    me = place.me
    enter([(place.grp, other) for other in place.others] + [(other, me) for other in place.groups])
    whole = WholeGather(place, shards, fulls, *refs)
    whole.begin()
    small = SmallSum(place, partial_ref, total_ref, *small_refs)
    small.begin()
    side = place.cols_x
    cut = late_scr.shape[1]
    late_own, base = [], 0
    for index, shard in enumerate(late_shards):
        height, cols = shard.shape[0] // side, shard.shape[1] // side
        for spot in range(cols // cut):
            late_own.append(pltpu.make_async_copy(
                window(shard, place.gy * height, height, place.gx * cols + spot * cut, cut),
                late_scr.at[pl.ds(base, height), :],
                late_sem.at[len(late_own)],
            ))
            late_own[-1].start()
            base += height
    late_chain = LineChain(place, [late_scr], lambda index, owner, slot: late_out.at[slot], late_send, late_recv)
    combine_jobs = [job for job in whole.jobs if job[0] == 0]
    projection_jobs = [job for job in whole.jobs if job[0] == 1]
    for job in combine_jobs:
        whole.spread_first(*job)
    for job, late in zip(combine_jobs, projection_jobs):
        whole.spread_second(*job)
        whole.spread_first(*late)
    for copy in late_own:
        copy.wait()
    late_chain.begin(0)
    small.middle()
    for job, late in zip(combine_jobs, projection_jobs):
        whole.over_core(*job)
        whole.spread_second(*late)
    whole.arrive(0)
    outs = [pltpu.make_async_copy(fulls[0], fulls_out[0], out_sem.at[0])]
    outs[0].start()
    late_chain.forward(0, 0)
    half = seq_count // 2

    def hidden_tile(index, carry):
        at = pl.ds(pl.multiple_of(index * 256, 256), 256)
        upper = fulls[0][0:half, :, at].reshape(width, 256)
        lower = fulls[0][half:seq_count, :, at].reshape(width, 256)
        hidden_ref[:, at] = dot_nn(frames_ref[...], upper) + dot_nn(shortcut_ref[...], lower)
        return carry

    lax.fori_loop(0, width // 256, hidden_tile, 0)
    small.finish()
    last = total_ref.shape[1] - 1
    token_scr[...] = token_ref[...]
    token_scr[4:5, :] = total_ref[seq_count - 1, last:last + 1, :128]
    tokens_ref[place.grp] = token_scr[...]
    tokens = [
        place.push(token_scr, tokens_ref.at[place.grp], token_send, token_recv, step, (other, me))
        for step, other in enumerate(place.groups)
    ]
    block = total_ref.shape[1]

    def vector(group, part, second):
        def row(utter):
            at = (group * 2 + utter) * 6 + part
            return total_ref[at // block, at % block:at % block + 1, :]

        return jnp.where(second, row(1), row(0))

    chunk = 32
    for group in range(group_count):

        def norm_rows(index, carry):
            first = pl.multiple_of(index * chunk, chunk)
            at = pl.ds(pl.multiple_of(group * local_rows + first, chunk), chunk)
            second = second_mask(bound_ref, group, me, local_rows, first, chunk)
            normal, _ = centered(hidden_ref[at, :])
            normed_ref[at, :] = (
                normal * (1.0 + vector(group, 1, second)) + vector(group, 0, second)
            ).astype(jnp.bfloat16)
            return carry

        lax.fori_loop(0, local_rows // chunk, norm_rows, 0)
    for job in projection_jobs:
        whole.over_core(*job)
    whole.arrive(1)
    late_chain.forward(0, 1)
    outs.append(pltpu.make_async_copy(fulls[1], fulls_out[1], out_sem.at[1]))
    outs[1].start()
    each = 256 // local_width

    def head_tile(index, carry):
        for kind in range(3):
            at = pl.ds(pl.multiple_of(kind * width + index * 256, 256), 256)
            packed = dot_nn(normed_ref[...], fulls[1][:, :, at].reshape(width, 256))
            for half in range(2):
                lanes = packed[:, half * 128:(half + 1) * 128]
                if kind < 2:
                    lanes = turn_lanes(lanes, cos_ref[...], sin_ref[...])
                lanes = lanes.astype(jnp.bfloat16)
                for spot in range(each // 2):
                    cut = lanes[:, spot * local_width:(spot + 1) * local_width]
                    for group in range(group_count):
                        qkv_ref[index * each + half * (each // 2) + spot, group, kind] = cut[
                            group * local_rows:(group + 1) * local_rows
                        ]
        return carry

    lax.fori_loop(0, width // 256, head_tile, 0)
    for rank in range(2, layers - 1):
        late_chain.forward(0, rank)
    whole.finish()
    late_chain.sent()
    for copy in tokens:
        copy.wait_recv()
    for copy in outs:
        copy.wait()


def front(bounds, frames, shortcut, cos, sin, partial, token, combine, projection, late_shards):
    grp_count = lax.axis_size("grp")
    seq_count = lax.axis_size("seq")
    side = math.isqrt(grp_count)
    layers = seq_count // 2
    anywhere = pl.BlockSpec(memory_space=pl.ANY)
    vmem = pl.BlockSpec(memory_space=pltpu.VMEM)
    dma = pltpu.SemaphoreType.DMA
    hops = max(side - 1, 1)
    shards = (combine, projection)
    group_count = bounds.shape[0]
    row_count, width = frames.shape
    low, full = jnp.bfloat16, jnp.float32
    cut = min(shard.shape[1] for shard in late_shards) // side
    late_rows = sum(shard.shape[0] // side * (shard.shape[1] // side // cut) for shard in late_shards)
    most = max(shard.shape[1] // side // cut for shard in late_shards)
    wholes = [(seq_count,) + part.shape for part in shards]
    return pl.pallas_call(
        functools.partial(front_kernel, (side, side), seq_count, len(late_shards)),
        out_shape=tuple(jax.ShapeDtypeStruct(shape, low) for shape in wholes) + (
            jax.ShapeDtypeStruct((layers - 1, late_rows, cut), low),
            jax.ShapeDtypeStruct((row_count, width), full),
            jax.ShapeDtypeStruct((row_count, width), low),
            jax.ShapeDtypeStruct(
                (seq_count, group_count, 3, row_count // group_count, width // seq_count), low
            ),
            jax.ShapeDtypeStruct(partial.shape, full),
            jax.ShapeDtypeStruct((grp_count,) + token.shape, full),
        ),
        in_specs=[pl.BlockSpec(memory_space=pltpu.SMEM)] + [vmem] * 6 + [anywhere] * (2 + len(late_shards)),
        out_specs=(anywhere,) * 3 + (vmem,) * 5,
        scratch_shapes=[pltpu.VMEM(shape, low) for shape in wholes] + [
            pltpu.VMEM(token.shape, full), dma((grp_count - 1,)), dma((grp_count - 1,)), dma((2,)),
        ] + small_scratch(partial) + [
            pltpu.VMEM((late_rows, cut), low),
            dma((1, layers + 1)), dma((1, layers - 1)), dma((len(late_shards) * most,)),
            dma((2, layers + 1)), dma((2, layers - 1)),
            dma((2, layers, 1, 1)),
            dma((2, layers - 1, 2, hops, 1)), dma((2, layers - 1, 2, hops, 1)),
            dma((2, layers - 1, 2, hops, side)), dma((2, layers - 1, 2, hops, side)),
            dma((2, layers)), dma((2, layers)),
        ],
        compiler_params=pltpu.CompilerParams(
            collective_id=3, has_side_effects=True, vmem_limit_bytes=48 * 1024 * 1024
        ),
        name="front",
    )(bounds, frames, shortcut, cos, sin, partial, token, *shards, *late_shards)


def back_kernel(plane, seq_count, *refs):
    layers = seq_count // 2
    (
        bound_ref, back_ref, cos_ref, sin_ref, normed_ref, hidden_ref, middle_ref, frames_ref, shortcut_ref,
        combine_ref, projection_ref, mods_ref, late_ref, modulation_ref,
    ) = refs[:14]
    finished, refs = refs[14:14 + layers], refs[14 + layers:]
    frames_out, shortcut_out, outs, refs = refs[0], refs[1], refs[2:7], refs[7:]
    utters_ref, conditions_ref, refs = refs[0], refs[1], refs[2:]
    (
        packed_scr, combine_scr, projection_scr, normed_t_scr, joined_t_scr, grad_scr, low_scr,
        frames_scr, shortcut_scr, total_ref, utter_scr, condition_scr,
    ) = refs[:12]
    parts, done_scr, lines, refs = refs[12:14], refs[14], refs[15:17], refs[17:]
    pieces = [refs[index * layers:(index + 1) * layers] for index in range(2)]
    refs = refs[2 * layers:]
    buffers, semaphores, refs = refs[:10], refs[10:17], refs[17:]
    small_refs, spread_sems, refs = refs[:5], refs[5:9], refs[9:]
    weight_sem, out_sem, token_send, token_recv, last_send, last_recv, line_send, line_recv, done_send, done_recv = refs
    group_count, local_rows, local_width = back_ref.shape[1], back_ref.shape[3], back_ref.shape[4]
    row_count, width = normed_ref.shape
    place = Place(plane, seq_count)
    me = place.me
    side = place.cols_x
    enter([(place.grp, other) for other in place.others] + [(other, me) for other in place.groups])
    arrived = {}
    for step in range(layers - 1):
        arrived[step] = place.push(
            finished[step], done_scr.at[step], done_send, done_recv, step, (place.grp, place.lines[step])
        )
    weights = [
        pltpu.make_async_copy(projection_ref, projection_scr, weight_sem.at[0]),
        pltpu.make_async_copy(combine_ref, combine_scr, weight_sem.at[1]),
    ]
    for copy in weights:
        copy.start()
    for source in range(seq_count):
        for kind in range(3):
            for group in range(group_count):
                packed_scr[
                    group * local_rows:(group + 1) * local_rows,
                    kind * width + source * local_width:kind * width + (source + 1) * local_width,
                ] = back_ref[source, group, kind]

    def turn(index, carry):
        lanes = pl.ds(pl.multiple_of(index * 128, 128), 128)
        packed_scr[:, lanes] = turn_lanes(
            packed_scr[:, lanes].astype(jnp.float32), cos_ref[...], -sin_ref[...]
        ).astype(jnp.bfloat16)
        return carry

    lax.fori_loop(0, 2 * width // 128, turn, 0)
    normed_t_scr[...] = normed_ref[...].astype(jnp.float32).T.astype(jnp.bfloat16)
    segments = [
        piece_segments([part.shape[1:]], side, part.shape[2] // side)[0][0] for part in parts
    ]
    done_segments, _ = piece_segments(
        [out.shape for out in outs[2:]], side, min(out.shape[1] for out in outs[2:]) // side
    )
    plane_sum = PlaneSum(place, parts, pieces, segments, buffers, semaphores, True)
    spread = PlaneSpread(place, outs, *spread_sems)

    def share(index, left, right, tile):
        rows = parts[index].shape[1]

        def fill(owner):
            at = pl.ds(pl.multiple_of(owner * rows, rows), rows)

            def one(turn, carry):
                lanes = pl.ds(pl.multiple_of(turn * tile, tile), tile)
                parts[index][owner, :, lanes] = dot_nn(left[at, :], right[:, lanes]).astype(jnp.bfloat16)
                return carry

            lax.fori_loop(0, parts[index].shape[2] // tile, one, 0)

        for step, target in enumerate(plane_sum.order):
            fill(target * 2 + 1 - place.core)
            plane_sum.swap(index, step)
        for target in plane_sum.order:
            fill(target * 2 + place.core)

    share(0, normed_t_scr, packed_scr, 512)
    weights[0].wait()

    def grad_tile(index, carry):
        at = pl.ds(pl.multiple_of(index * 256, 256), 256)
        grad_scr[:, at] = dot_nt(packed_scr[...], projection_scr[at, :])
        return carry

    lax.fori_loop(0, width // 256, grad_tile, 0)
    for hook in plane_sum.steps(plane_sum.first, 0):
        hook()
    block, utter_rows = utter_scr.shape[1], 2 * group_count
    utter_scr[...] = jnp.zeros_like(utter_scr)

    def put(part, utter, value):
        row = part * utter_rows + utter
        utter_scr[row // block, row % block:row % block + 1, :] = value

    for part in range(4):
        for utter in range(utter_rows):
            put(part + 2, utter, late_ref[part * utter_rows + utter:part * utter_rows + utter + 1, :])
    chunk = 32
    for group in range(group_count):

        def norm_back(index, sums):
            first = pl.multiple_of(index * chunk, chunk)
            at = pl.ds(pl.multiple_of(group * local_rows + first, chunk), chunk)
            second = second_mask(bound_ref, group, me, local_rows, first, chunk)
            row = group * 2 * 6
            scale_part = jnp.where(second, mods_ref[row + 7:row + 8, :], mods_ref[row + 1:row + 2, :])
            grad = grad_scr[at, :]
            normal, scale = centered(hidden_ref[at, :])
            inner = grad * (1.0 + scale_part)
            turned = scale * (
                inner
                - jnp.mean(inner, axis=-1, keepdims=True)
                - normal * jnp.mean(inner * normal, axis=-1, keepdims=True)
            )
            low_scr[at, :] = (middle_ref[at, :] + turned).astype(jnp.bfloat16)
            scaled = grad * normal
            later = second.astype(jnp.float32)
            shift_later, scale_later = grad * later, scaled * later
            return (
                sums[0] + fold_rows(grad - shift_later, jnp.sum),
                sums[1] + fold_rows(shift_later, jnp.sum),
                sums[2] + fold_rows(scaled - scale_later, jnp.sum),
                sums[3] + fold_rows(scale_later, jnp.sum),
            )

        zero = jnp.zeros((8, width), jnp.float32)
        sums = lax.fori_loop(0, local_rows // chunk, norm_back, (zero, zero, zero, zero))
        for spot, value in enumerate(sums):
            put(spot // 2, group * 2 + spot % 2, jnp.sum(value, axis=0, keepdims=True))
    small = SmallSum(place, utter_scr, total_ref, *small_refs)
    small.begin()
    joined_t_scr[:width, :] = frames_ref[...].astype(jnp.float32).T.astype(jnp.bfloat16)
    joined_t_scr[width:, :] = shortcut_ref[...].astype(jnp.float32).T.astype(jnp.bfloat16)
    share(1, joined_t_scr, low_scr, 512)
    for hook in plane_sum.steps(plane_sum.second, 0)[:layers // 2]:
        hook()
    weights[1].wait()

    def joined_tile(index, carry):
        at = pl.ds(pl.multiple_of(index * 256, 256), 256)
        late = pl.ds(pl.multiple_of(width + index * 256, 256), 256)
        frames_scr[:, at] = dot_nt(low_scr[...], combine_scr[at, :])
        shortcut_scr[:, at] = dot_nt(low_scr[...], combine_scr[late, :])
        return carry

    lax.fori_loop(0, width // 256, joined_tile, 0)
    grads = [
        pltpu.make_async_copy(frames_scr, frames_out, out_sem.at[0]),
        pltpu.make_async_copy(shortcut_scr, shortcut_out, out_sem.at[1]),
    ]
    for copy in grads:
        copy.start()
    for hook in plane_sum.steps(plane_sum.first, 1):
        hook()
    for hook in plane_sum.steps(plane_sum.second, 0)[layers // 2:]:
        hook()
    small.middle()

    def along_line(index, step):
        plane_sum.third(index, step)
        if step < layers - 1:
            arrived[index, step] = place.push(
                pieces[index][step], lines[index].at[step], line_send, line_recv, (index, step),
                (place.grp, place.lines[step]),
            )

    def last(index):
        for step in range(layers - 1):
            arrived[index, step].wait_recv()
        spread.total(
            index, pieces[index][layers - 1], [lines[index].at[step] for step in range(layers - 1)], segments[index]
        )

    for step in range(layers):
        plane_sum.second(1, step)
        along_line(0, step)
    small.finish()
    utters_ref[place.grp] = total_ref[...]
    tokens = [
        place.push(total_ref, utters_ref.at[place.grp], token_send, token_recv, step, (other, me))
        for step, other in enumerate(place.groups)
    ]
    condition_scr[...] = jnp.zeros_like(condition_scr)
    shard_rows = modulation_ref.shape[0]
    for spot in range(6 * utter_rows // block):
        part, row = spot * block // utter_rows, spot * block % utter_rows
        condition_scr[row:row + block, :shard_rows] += dot_nt(
            total_ref[spot].astype(jnp.bfloat16), modulation_ref[:, part * width:(part + 1) * width]
        )
    conditions_ref[me] = condition_scr[...]
    tokens += [
        place.push(condition_scr, conditions_ref.at[me], last_send, last_recv, step, (place.grp, other))
        for step, other in enumerate(place.others)
    ]
    for step in range(layers):
        along_line(1, step)
    for step in range(layers - 1):
        arrived[step].wait_recv()
    for index in range(2, 5):
        spread.total(
            index, finished[layers - 1], [done_scr.at[step] for step in range(layers - 1)], done_segments[index - 2]
        )
    last(0)
    for index in range(2, 5):
        spread.second(index)
    last(1)
    spread.second(0)
    spread.second(1)
    place.sent()
    for copy in tokens:
        copy.wait_recv()
    for copy in grads:
        copy.wait()
    for index in range(5):
        spread.finish(index)


def finish_backward(bounds, back, cos, sin, normed, hidden, middle_grad, frames, shortcut, combine, projection, mods, late, modulation, finished, done_shapes):
    grp_count = lax.axis_size("grp")
    seq_count = lax.axis_size("seq")
    side = math.isqrt(grp_count)
    layers = seq_count // 2
    hops = max(side - 1, 1)
    anywhere = pl.BlockSpec(memory_space=pl.ANY)
    vmem = pl.BlockSpec(memory_space=pltpu.VMEM)
    dma = pltpu.SemaphoreType.DMA
    row_count, width = normed.shape
    low, full = jnp.bfloat16, jnp.float32
    parts = [
        jax.ShapeDtypeStruct((seq_count, weight.shape[0] // seq_count, weight.shape[1]), low)
        for weight in (projection, combine)
    ]
    out_shapes = [part.shape[1:] for part in parts] + list(done_shapes)
    small = jax.ShapeDtypeStruct((seq_count, 32 // seq_count, width), full)
    return pl.pallas_call(
        functools.partial(back_kernel, (side, side), seq_count),
        out_shape=(
            jax.ShapeDtypeStruct((row_count, width), full),
            jax.ShapeDtypeStruct((row_count, width), full),
        ) + tuple(jax.ShapeDtypeStruct(shape, low) for shape in out_shapes) + (
            jax.ShapeDtypeStruct((grp_count,) + small.shape, full),
            jax.ShapeDtypeStruct((seq_count, 8, 128), full),
        ),
        in_specs=[pl.BlockSpec(memory_space=pltpu.SMEM)] + [vmem] * 8 + [anywhere] * 2 + [vmem] * (3 + layers),
        out_specs=(anywhere,) * 2 + (vmem,) * 7,
        scratch_shapes=[
            pltpu.VMEM((row_count, 3 * width), low),
            pltpu.VMEM(combine.shape, low),
            pltpu.VMEM(projection.shape, low),
            pltpu.VMEM((width, row_count), low),
            pltpu.VMEM((2 * width, row_count), low),
            pltpu.VMEM((row_count, width), full),
            pltpu.VMEM((row_count, width), low),
            pltpu.VMEM((row_count, width), full),
            pltpu.VMEM((row_count, width), full),
            pltpu.VMEM(small.shape, full),
            pltpu.VMEM(small.shape, full),
            pltpu.VMEM((8, 128), full),
        ] + [pltpu.VMEM(part.shape, low) for part in parts] + [
            pltpu.VMEM((layers - 1,) + finished[0].shape, low)
        ] + [
            pltpu.VMEM((layers - 1, part.shape[1] // side, part.shape[2] // side), low) for part in parts
        ] + [
            pltpu.VMEM((part.shape[1] // side, part.shape[2] // side), low)
            for part in parts for _ in range(layers)
        ] + plane_sum_scratch(parts, side, True) + small_scratch(small) + [
            dma((5, 2, hops)), dma((5, 2, hops)),
            dma((5, 2, hops, side)), dma((5, 2, hops, side)),
            dma((2,)), dma((2,)),
            dma((grp_count - 1,)), dma((grp_count - 1,)),
            dma((seq_count - 1,)), dma((seq_count - 1,)),
            dma((2, layers - 1)), dma((2, layers - 1)),
            dma((layers - 1,)), dma((layers - 1,)),
        ],
        compiler_params=pltpu.CompilerParams(
            collective_id=4, has_side_effects=True, vmem_limit_bytes=60 * 1024 * 1024
        ),
        name="finish_backward",
    )(bounds, back, cos, sin, normed, hidden, middle_grad, frames, shortcut, combine, projection, mods, late, modulation, *finished)


def shards(
    frames,
    shortcut,
    time_embed,
    lengths,
    kept_mask,
    target,
    combine,
    modulation,
    projection,
    readout,
    expand,
    contract,
):
    group_count = frames.shape[0]
    local_rows = frames.shape[1]
    width = HEADS * HEAD_DIM
    row_count = group_count * local_rows
    seq_count = lax.axis_size("seq")
    group_frames = local_rows * seq_count
    all_frames = group_frames * lax.axis_size("grp") * group_count
    utter_count = time_embed.shape[1]
    kept_float = kept_mask.astype(jnp.float32).reshape(row_count)
    local_index = lax.axis_index("seq") * local_rows + jnp.arange(local_rows, dtype=jnp.int32)

    def local_info(length_row):
        return segment_info(length_row, local_index)

    member_info = jax.vmap(local_info)(lengths)
    member_float = member_info[1].astype(jnp.float32)
    position = member_info[2]
    cos_table, sin_table = rotary_tables(position.reshape(row_count))
    cos_lanes = jnp.tile(cos_table[:, 0], (1, 4))
    sin_lanes = jnp.tile(jnp.concatenate([-sin_table[:, 0], sin_table[:, 0]], axis=1), (1, 2))
    silu_value, silu_pull = jax.vjp(jax.nn.silu, time_embed)
    condition = silu_value.astype(jnp.bfloat16)
    shard_rows = modulation.shape[0]
    utter_rows = group_count * utter_count
    condition_part = lax.dynamic_slice_in_dim(
        condition, lax.axis_index("seq") * shard_rows, shard_rows, 2
    ).reshape(utter_rows, shard_rows)
    partial = small_rows(
        seq_count, product(condition_part, modulation).reshape(6 * utter_rows, width)
    )
    partial = partial.at[seq_count - 1, 32 // seq_count - 1, 0].set(jnp.sum(kept_float))
    token = jnp.zeros((8, 128), jnp.float32)
    token = token.at[:utter_rows, :shard_rows].set(condition_part.astype(jnp.float32))
    late_shards = (readout, expand, contract)
    bounds = lengths[:, 0]
    combine_full, projection_full, *rest = front(
        bounds,
        frames.reshape(row_count, width),
        shortcut.reshape(row_count, width),
        cos_lanes,
        sin_lanes,
        partial,
        token,
        combine,
        projection,
        late_shards,
    )
    late_pieces, hidden, normed, qkv, partial_total, tokens = rest
    combine_full = combine_full.reshape(2 * width, width)
    projection_full = projection_full.reshape(width, 3 * width)
    kept_total = jnp.sum(tokens[:, 4, 0])
    condition_all = tokens[:, :utter_rows, :shard_rows].reshape(-1, shard_rows).astype(jnp.bfloat16)
    modulation_utter = partial_total.reshape(32, width)[:6 * utter_rows].reshape(
        group_count, utter_count, 6 * width
    )
    modulation_frame = jnp.einsum(
        "gtu,gue->gte",
        member_float,
        modulation_utter,
        precision=precise,
        preferred_element_type=jnp.float32,
    ).reshape(row_count, 6 * width)
    shift_first, scale_first, gate_first, shift_second, scale_second, gate_second = jnp.split(
        modulation_frame, 6, axis=1
    )
    split_shape = (group_count, local_rows, width)
    local_width = width // seq_count
    kept_heads, mixture_blocks, log_total, *late_full = attend_forward(
        bounds, qkv, late_shards, late_pieces
    )
    readout_full = late_full[0].reshape(width, width)
    expand_full = late_full[1].reshape(width, -1)
    contract_full = late_full[2].reshape(-1, width)
    mixture = jnp.transpose(mixture_blocks, (1, 2, 0, 3)).reshape(row_count, width)
    branch = product(mixture, readout_full)
    middle = hidden + gate_first * branch
    second_value, second_pull = jax.vjp(modulate, middle, shift_second, scale_second)
    normed_second = second_value.astype(jnp.bfloat16)
    expanded = product(normed_second, expand_full)
    active_value, gelu_pull = jax.vjp(gelu_tanh, expanded)
    active = active_value.astype(jnp.bfloat16)
    contracted = product(active, contract_full)
    output = middle + gate_second * contracted
    loss_scale = all_frames / kept_total
    output_grad = (
        loss_scale
        * kept_float[:, None]
        * (output - target.reshape(row_count, width).astype(jnp.float32))
    )
    combine_back, projection_back, readout_back, expand_back, contract_back = (
        combine_full, projection_full, readout_full, expand_full, contract_full
    )
    gate_second_grad = output_grad * contracted
    contracted_grad = (gate_second * output_grad).astype(jnp.bfloat16)
    contract_part = product_left(active, contracted_grad)
    active_grad = product_right(contracted_grad, contract_back)
    expanded_grad = gelu_pull(active_grad)[0].astype(jnp.bfloat16)
    expand_part = product_left(normed_second, expanded_grad)
    normed_second_grad = product_right(expanded_grad, expand_back)
    middle_extra, shift_second_grad, scale_second_grad = second_pull(normed_second_grad)
    middle_grad = output_grad + middle_extra
    gate_first_grad = middle_grad * branch
    branch_grad = (gate_first * middle_grad).astype(jnp.bfloat16)
    readout_part = product_left(mixture, branch_grad)
    mixture_grad = product_right(branch_grad, readout_back).astype(jnp.bfloat16)
    back_blocks, *plane_pieces = attend_backward(
        bounds,
        kept_heads,
        jnp.transpose(
            mixture_grad.reshape(group_count, local_rows, seq_count, local_width), (2, 0, 1, 3)
        ),
        log_total,
        [part.astype(jnp.bfloat16) for part in (contract_part, expand_part, readout_part)],
    )
    late_grads = jnp.concatenate(
        [gate_first_grad, shift_second_grad, scale_second_grad, gate_second_grad], axis=1
    )
    late_part = jnp.einsum(
        "gtu,gte->gue",
        member_float,
        late_grads.reshape(group_count, local_rows, 4 * width),
        precision=precise,
        preferred_element_type=jnp.float32,
    )
    late_rows = jnp.transpose(
        late_part.reshape(utter_rows, 4, width), (1, 0, 2)
    ).reshape(4 * utter_rows, width)
    frames_grad, shortcut_grad, *shares, utters, condition_back = finish_backward(
        bounds,
        back_blocks,
        cos_lanes,
        sin_lanes,
        normed,
        hidden,
        middle_grad,
        frames.reshape(row_count, width),
        shortcut.reshape(row_count, width),
        combine_full,
        projection_full,
        partial_total.reshape(32, width),
        late_rows,
        modulation,
        plane_pieces,
        [contract.shape, expand.shape, readout.shape],
    )
    frames_grad = frames_grad.reshape(split_shape)
    shortcut_grad = shortcut_grad.reshape(split_shape)
    projection_grad, combine_grad, contract_grad, expand_grad, readout_grad = [
        share.astype(jnp.float32) for share in shares
    ]
    utter_all = jnp.transpose(
        utters.reshape(-1, 32, width)[:, :6 * utter_rows].reshape(-1, 6, utter_rows, width), (0, 2, 1, 3)
    ).reshape(-1, 6 * width).astype(jnp.bfloat16)
    modulation_grad = product_left(condition_all, utter_all)
    condition_grad = jnp.transpose(
        condition_back[:, :utter_rows, :shard_rows], (1, 0, 2)
    ).reshape(group_count, utter_count, width)
    time_grad = silu_pull(condition_grad)[0]
    summed = (combine_grad, modulation_grad, projection_grad, readout_grad, expand_grad, contract_grad)
    return (
        output.astype(jnp.bfloat16).reshape(split_shape),
        frames_grad,
        shortcut_grad,
        time_grad,
        summed[0],
        summed[1],
        summed[2],
        summed[3],
        summed[4],
        summed[5],
    )


def solution(mesh):
    return jax.shard_map(
        shards,
        mesh=mesh,
        in_specs=(
            P("grp", "seq", None),
            P("grp", "seq", None),
            P("grp", None, None),
            P("grp", None),
            P("grp", "seq"),
            P("grp", "seq", None),
            P("seq", None),
            P("seq", None),
            P("seq", None),
            P("seq", None),
            P("seq", None),
            P("seq", None),
        ),
        out_specs=(
            P("grp", "seq", None),
            P("grp", "seq", None),
            P("grp", "seq", None),
            P("grp", None, None),
            P("seq", None),
            P("seq", None),
            P("seq", None),
            P("seq", None),
            P("seq", None),
            P("seq", None),
        ),
        check_vma=False,
    )
```

```python
import functools
import math

import jax
import jax.numpy as jnp
from jax import lax
from jax.experimental import pallas as pl
from jax.experimental.pallas import tpu as pltpu
from jax.sharding import PartitionSpec as P

HEADS = 16
HEAD_DIM = 64


precise = lax.Precision.HIGHEST
epsilon = 1e-06
rope_base = 10000.0


def product(first_op, second_op):
    return jnp.dot(first_op, second_op, preferred_element_type=jnp.float32)


def product_left(first_op, second_op):
    return lax.dot_general(
        first_op, second_op, (((0,), (0,)), ((), ())), preferred_element_type=jnp.float32
    )


def product_right(first_op, second_op):
    return lax.dot_general(
        first_op, second_op, (((1,), (1,)), ((), ())), preferred_element_type=jnp.float32
    )


def gelu_tanh(values):
    return jax.nn.gelu(values, approximate=True)


def modulate(hidden, shift_part, scale_part):
    center = hidden - jnp.mean(hidden, axis=-1, keepdims=True)
    variance = jnp.mean(center * center, axis=-1, keepdims=True)
    return center * lax.rsqrt(variance + epsilon) * (1.0 + scale_part) + shift_part


def segment_info(lengths, frame_index):
    utter_count = lengths.shape[0]
    utter_ends = jnp.cumsum(lengths)
    starts = utter_ends - lengths
    segment = jnp.sum((frame_index[:, None] >= utter_ends[None, :]).astype(jnp.int32), axis=1)
    member = segment[:, None] == jnp.arange(utter_count, dtype=jnp.int32)[None, :]
    offset = jnp.sum(jnp.where(member, starts[None, :], 0), axis=1)
    return (segment, member, frame_index - offset)


def rotary_tables(position):
    half_dim = HEAD_DIM // 2
    ladder = jnp.arange(half_dim, dtype=jnp.float32) / half_dim
    inverse = jnp.exp(-jnp.log(rope_base) * ladder)
    angles = position.astype(jnp.float32)[:, None] * inverse[None, :]
    return (jnp.cos(angles)[:, None, :], jnp.sin(angles)[:, None, :])


def rotate(vectors, cos_table, sin_table):
    half_dim = vectors.shape[-1] // 2
    front_half = vectors[..., :half_dim]
    back_half = vectors[..., half_dim:]
    return jnp.concatenate(
        [
            front_half * cos_table - back_half * sin_table,
            back_half * cos_table + front_half * sin_table,
        ],
        axis=-1,
    )


MESH = pl.DeviceIdType.MESH
NEG = -1e30


def utter_features(boundary, total_rows, for_keys):
    row = lax.broadcasted_iota(jnp.int32, (total_rows, 128), 0)
    lane = lax.broadcasted_iota(jnp.int32, (total_rows, 128), 1)
    second = (row >= boundary).astype(jnp.float32)
    ahead = (lane == 0).astype(jnp.float32)
    after = (lane == 1).astype(jnp.float32)
    if for_keys:
        return (NEG * (second * ahead + (1.0 - second) * after)).astype(jnp.bfloat16)
    return (second * after + (1.0 - second) * ahead).astype(jnp.bfloat16)


def head_lanes(values, head):
    lane = lax.broadcasted_iota(jnp.int32, values.shape, 1)
    own = (lane >= head * HEAD_DIM) & (lane < (head + 1) * HEAD_DIM)
    return jnp.where(own, values.astype(jnp.float32), 0.0).astype(jnp.bfloat16)


def dot_nn(first_op, second_op):
    return jnp.dot(first_op, second_op, preferred_element_type=jnp.float32)


def dot_nt(first_op, second_op):
    return lax.dot_general(
        first_op, second_op, (((1,), (1,)), ((), ())), preferred_element_type=jnp.float32
    )


def fold_rows(values, combine):
    return combine(values.reshape(values.shape[0] // 8, 8, values.shape[1]), axis=0)


def enter(partners):
    barrier = pltpu.get_barrier_semaphore()
    for partner in partners:
        pl.semaphore_signal(barrier, inc=1, device_id=partner, device_id_type=MESH)
    pl.semaphore_wait(barrier, len(partners))


def key_span(third, total_rows):
    size = total_rows // 3
    return (max(third - 1, 0) * size, min(third + 2, 3) * size)


class Place:
    def __init__(self, plane, seq_count):
        self.rows_y, self.cols_x = rows_y, cols_x = plane
        self.grp, self.me = grp, me = lax.axis_index("grp"), lax.axis_index("seq")
        self.gy, self.gx = gy, gx = grp // cols_x, lax.rem(grp, cols_x)
        self.layers = layers = seq_count // 2
        self.layer, self.core = layer, core = me // 2, lax.rem(me, 2)
        self.xs = [lax.rem(gx + step, cols_x) for step in range(1, cols_x)]
        self.ys = [lax.rem(gy + step, rows_y) for step in range(1, rows_y)]
        self.beside = [gy * cols_x + x for x in self.xs]
        self.along = [y * cols_x + gx for y in self.ys]
        self.beside_from = [lax.rem(gx + cols_x - step, cols_x) for step in range(1, cols_x)]
        self.far = [lax.rem(layer + step, layers) for step in range(1, layers)]
        self.line_from = [lax.rem(layer + layers - step, layers) * 2 + core for step in range(1, layers)]
        self.lines = [target * 2 + core for target in self.far]
        self.partner = layer * 2 + 1 - core
        self.others = [lax.rem(me + step, seq_count) for step in range(1, seq_count)]
        self.groups = [lax.rem(grp + step, rows_y * cols_x) for step in range(1, rows_y * cols_x)]
        self.started = []

    def push(self, src, dst, sends, recvs, slot, device):
        copy = pltpu.make_async_remote_copy(
            src, dst, sends.at[slot], recvs.at[slot], device_id=device, device_id_type=MESH
        )
        copy.start()
        self.started.append(copy)
        return copy

    def sent(self):
        for copy in self.started:
            copy.wait_send()
        self.started = []


def window(ref, row, rows, col, cols):
    return ref.at[pl.ds(pl.multiple_of(row, 16), rows), pl.ds(pl.multiple_of(col, 128), cols)]


def piece_segments(shapes, side, width):
    base, found = 0, []
    for rows, cols in shapes:
        height, many = rows // side, cols // side // width
        if many == 1:
            half = width // 2
            found.append([[(base, 0, height, half, 0)], [(base, half, height, half, half)]])
        else:
            blocks = [(base + spot * height, 0, height, width, spot * width) for spot in range(many)]
            found.append([blocks[:many // 2], blocks[many // 2:]])
        base += height * many
    return found, base


class PlaneGather:
    def __init__(self, place, shards, pieces, segments, fulls, own_sem, first_send, first_recv, second_send, second_recv, core_send, core_recv):
        self.place, self.shards, self.pieces, self.fulls = place, shards, pieces, fulls
        self.segments = segments
        self.own_sem = own_sem
        self.first = (first_send, first_recv)
        self.second = (second_send, second_recv)
        self.core = (core_send, core_recv)
        self.jobs = [(index, step) for step in range(place.layers - 1) for index in range(len(shards))]
        self.waiting, self.local, self.own = {}, {}, []

    def sizes(self, index):
        _, rows, cols = self.fulls[index].shape
        return rows, rows // self.place.rows_y, cols // (2 * self.place.cols_x)

    def owner(self, step):
        return self.place.line_from[step]

    def begin(self):
        place = self.place
        for index, step in self.jobs:
            self.spread_first(index, step)
        for index, shard in enumerate(self.shards):
            copy = pltpu.make_async_copy(shard, self.fulls[index].at[place.me], self.own_sem.at[index, place.layers - 1, 0, 0])
            copy.start()
            push = place.push(shard, self.fulls[index].at[place.me], *self.core, (index, 0), (place.grp, place.partner))
            self.own.append((copy, push))

    def spread_first(self, index, step):
        place = self.place
        rows, height, width = self.sizes(index)
        full = self.fulls[index].at[self.owner(step)]
        piece = self.pieces.at[step]
        first_row, first_col = place.gy * height, 2 * place.gx * width
        self.local[index, step] = []
        self.waiting[index, step] = []
        for half, partners in enumerate((place.beside, place.along)):
            for spot, (row, col, rows, cols, off) in enumerate(self.segments[index][half]):
                source = piece.at[pl.ds(row, rows), pl.ds(col, cols)]
                part = window(full, first_row, rows, first_col + off, cols)
                copy = pltpu.make_async_copy(source, part, self.own_sem.at[index, step, half, spot])
                copy.start()
                self.local[index, step].append(copy)
                for hop, other in enumerate(partners):
                    self.waiting[index, step].append(place.push(
                        source, part, *self.first, (index, step, half, hop, spot), (other, place.me)
                    ))

    def spread_second(self, index, step):
        place = self.place
        rows, height, width = self.sizes(index)
        for copy in self.local.get((index, step), []):
            copy.wait()
        for copy in self.waiting[index, step]:
            copy.wait_recv()
        full = self.fulls[index].at[self.owner(step)]
        copies = []
        for hop, other in enumerate(place.along):
            for spot, column in enumerate([place.gx] + place.beside_from):
                part = window(full, place.gy * height, height, 2 * column * width, width)
                copies.append(place.push(part, part, *self.second, (index, step, 0, hop, spot), (other, place.me)))
        for hop, other in enumerate(place.beside):
            part = window(full, 0, rows, (2 * place.gx + 1) * width, width)
            copies.append(place.push(part, part, *self.second, (index, step, 1, hop, 0), (other, place.me)))
        self.waiting[index, step] = copies

    def over_core(self, index, step):
        place = self.place
        for copy in self.waiting[index, step]:
            copy.wait_recv()
        full = self.fulls[index].at[self.owner(step)]
        self.waiting[index, step] = [
            place.push(full, full, *self.core, (index, step + 1), (place.grp, place.partner))
        ]

    def middle(self):
        for job in self.jobs:
            self.spread_second(*job)

    def late(self):
        return [functools.partial(self.over_core, *job) for job in self.jobs]

    def arrive(self, index):
        for job in self.jobs:
            if job[0] == index:
                for copy in self.waiting[job]:
                    copy.wait_recv()
        copy, push = self.own[index]
        copy.wait()
        push.wait_recv()

    def finish(self):
        self.place.sent()


def add_rows(target, source, first_row, rows, first_col, cols, out=None):
    step = next(size for size in (64, 32, 16) if rows % size == 0)
    col = pl.multiple_of(first_col, 128)

    def one(index, carry):
        at = pl.ds(pl.multiple_of(first_row + index * step, 16), step)
        off = pl.ds(pl.multiple_of(index * step, step), step)
        value = target[at, pl.ds(col, cols)] + source[off, :]
        if out is None:
            target[at, pl.ds(col, cols)] = value
        else:
            out[off, :] = value
        return carry

    lax.fori_loop(0, rows // step, one, 0)


def add_segments(target, source, first_row, first_col, segments, out):
    for row, col, rows, cols, off in segments:
        begin = off - segments[0][4]
        add_rows(
            target, source.at[:, pl.ds(begin, cols)], first_row, rows, first_col + off, cols,
            out.at[pl.ds(row, rows), pl.ds(col, cols)],
        )


def plane_sum_scratch(parts, side, in_place=False):
    layers = parts[0].shape[0] // 2
    hops = max(side - 1, 1)
    count = len(parts)
    dma = pltpu.SemaphoreType.DMA

    def buffers(lead, row_cut, col_cut):
        return [
            pltpu.VMEM(lead + (part.shape[1] // row_cut, part.shape[2] // col_cut), jnp.bfloat16)
            for part in parts
        ]

    return (
        ([] if in_place else buffers((layers,), 1, 1))
        + buffers((layers,), 1, 1)
        + buffers((layers, hops, side), side, 2 * side)
        + buffers((layers, hops), side, 2 * side)
        + buffers((layers, hops), 1, 2 * side)
        + buffers((layers, hops), side, 2 * side)
        + [
            dma((count, layers)), dma((count, layers)), dma((count, layers)),
            dma((count, layers, 2, hops, side)), dma((count, layers, 2, hops, side)),
            dma((count, layers, 2, hops)), dma((count, layers, 2, hops)),
        ]
    )


def by_owner(parts, seq_count):
    return [part.reshape(seq_count, part.shape[0] // seq_count, part.shape[1]) for part in parts]


class PlaneSum:
    def __init__(self, place, parts, pieces, segments, buffers, semaphores, in_place=False):
        self.place, self.parts, self.pieces, self.segments = place, parts, pieces, segments
        count = len(parts)
        buffers = (() if in_place else buffers[:count], *[
            buffers[index * count:(index + 1) * count] for index in range(0 if in_place else 1, 5 if in_place else 6)
        ])
        self.in_place = in_place
        self.sums, self.swapped, self.y_first, self.x_second, self.x_first, self.y_second = buffers
        self.load_sem = semaphores[0]
        self.core, self.first_sem, self.second_sem = semaphores[1:3], semaphores[3:5], semaphores[5:7]
        self.order = place.far + [place.layer]
        self.jobs = [(index, step) for index in range(count) for step in range(place.layers)]
        self.loads, self.swaps, self.waiting = {}, {}, {}

    def sizes(self, index):
        _, rows, cols = self.parts[index].shape
        return rows, cols, rows // self.place.rows_y, cols // (2 * self.place.cols_x)

    def begin(self):
        place = self.place
        for index, step in self.jobs:
            target = self.order[step]
            copy = pltpu.make_async_copy(
                self.parts[index].at[target * 2 + place.core], self.sums[index].at[step], self.load_sem.at[index, step]
            )
            copy.start()
            self.loads[index, step] = copy
            self.swap(index, step)

    def swap(self, index, step):
        place = self.place
        self.swaps[index, step] = place.push(
            self.parts[index].at[self.order[step] * 2 + 1 - place.core], self.swapped[index].at[step],
            *self.core, (index, step), (place.grp, place.partner),
        )

    def running(self, index, step):
        if self.in_place:
            return self.parts[index].at[self.order[step] * 2 + self.place.core]
        return self.sums[index].at[step]

    def first(self, index, step):
        place = self.place
        rows, cols, height, width = self.sizes(index)
        if not self.in_place:
            self.loads[index, step].wait()
        self.swaps[index, step].wait_recv()
        total = self.running(index, step)
        add_rows(total, self.swapped[index].at[step], 0, rows, 0, cols)
        copies = []
        for hop, other in enumerate(place.along):
            for column in range(place.cols_x):
                copies.append(place.push(
                    window(total, place.ys[hop] * height, height, 2 * column * width, width),
                    self.y_first[index].at[step, hop, column],
                    *self.first_sem, (index, step, 0, hop, column), (other, place.me),
                ))
        for hop, other in enumerate(place.beside):
            copies.append(place.push(
                window(total, 0, rows, (2 * place.xs[hop] + 1) * width, width),
                self.x_first[index].at[step, hop],
                *self.first_sem, (index, step, 1, hop, 0), (other, place.me),
            ))
        self.waiting[index, step] = copies

    def second(self, index, step):
        place = self.place
        rows, cols, height, width = self.sizes(index)
        for copy in self.waiting[index, step]:
            copy.wait_recv()
        total = self.running(index, step)
        for hop in range(place.rows_y - 1):
            for column in range(place.cols_x):
                add_rows(
                    total, self.y_first[index].at[step, hop, column],
                    place.gy * height, height, 2 * column * width, width,
                )
        for hop in range(place.cols_x - 1):
            add_rows(total, self.x_first[index].at[step, hop], 0, rows, (2 * place.gx + 1) * width, width)
        copies = []
        for hop, other in enumerate(place.beside):
            copies.append(place.push(
                window(total, place.gy * height, height, 2 * place.xs[hop] * width, width),
                self.x_second[index].at[step, hop],
                *self.second_sem, (index, step, 0, hop), (other, place.me),
            ))
        for hop, other in enumerate(place.along):
            copies.append(place.push(
                window(total, place.ys[hop] * height, height, (2 * place.gx + 1) * width, width),
                self.y_second[index].at[step, hop],
                *self.second_sem, (index, step, 1, hop), (other, place.me),
            ))
        self.waiting[index, step] = copies

    def third(self, index, step):
        place = self.place
        rows, cols, height, width = self.sizes(index)
        for copy in self.waiting[index, step]:
            copy.wait_recv()
        self.waiting[index, step] = []
        total = self.running(index, step)
        out = self.pieces[index][step]
        row, col = place.gy * height, 2 * place.gx * width
        for hop in range(place.cols_x - 1):
            source = self.x_second[index].at[step, hop]
            if hop == place.cols_x - 2:
                add_segments(total, source, row, col, self.segments[index][0], out)
            else:
                add_rows(total, source, row, height, col, width)
        for hop in range(place.rows_y - 1):
            source = self.y_second[index].at[step, hop]
            if hop == place.rows_y - 2:
                add_segments(total, source, row, col, self.segments[index][1], out)
            else:
                add_rows(total, source, row, height, col + width, width)

    def steps(self, stage, only=None):
        return [functools.partial(stage, *job) for job in self.jobs if only is None or job[0] == only]

    def finish(self):
        self.place.sent()


class PlaneSpread:
    def __init__(self, place, outs, first_send, first_recv, second_send, second_recv):
        self.place, self.outs = place, outs
        self.first_sem, self.second_sem = (first_send, first_recv), (second_send, second_recv)
        self.waiting = {}

    def sizes(self, index):
        rows, cols = self.outs[index].shape
        return rows, rows // self.place.rows_y, cols // (2 * self.place.cols_x)

    def total(self, index, piece, others, segments):
        place = self.place
        rows, height, width = self.sizes(index)
        row = place.gy * height
        col = pl.multiple_of(2 * place.gx * width, 128)
        for first, left, _, cols, off in segments[0] + segments[1]:

            def one(turn, carry):
                at = pl.ds(pl.multiple_of(first + turn * 16, 16), 16)
                value = piece[at, pl.ds(left, cols)].astype(jnp.float32)
                for other in others:
                    value = value + other[at, pl.ds(left, cols)].astype(jnp.float32)
                self.outs[index][
                    pl.ds(pl.multiple_of(row + turn * 16, 16), 16), pl.ds(pl.multiple_of(col + off, 128), cols)
                ] = value.astype(jnp.bfloat16)
                return carry

            lax.fori_loop(0, height // 16, one, 0)
        copies = []
        for hop, other in enumerate(place.beside):
            part = window(self.outs[index], row, height, 2 * place.gx * width, width)
            copies.append(place.push(part, part, *self.first_sem, (index, 0, hop), (other, place.me)))
        for hop, other in enumerate(place.along):
            part = window(self.outs[index], row, height, (2 * place.gx + 1) * width, width)
            copies.append(place.push(part, part, *self.first_sem, (index, 1, hop), (other, place.me)))
        self.waiting[index] = copies

    def second(self, index):
        place = self.place
        rows, height, width = self.sizes(index)
        for copy in self.waiting[index]:
            copy.wait_recv()
        copies = []
        for hop, other in enumerate(place.along):
            for spot, column in enumerate([place.gx] + place.beside_from):
                part = window(self.outs[index], place.gy * height, height, 2 * column * width, width)
                copies.append(place.push(part, part, *self.second_sem, (index, 0, hop, spot), (other, place.me)))
        for hop, other in enumerate(place.beside):
            part = window(self.outs[index], 0, rows, (2 * place.gx + 1) * width, width)
            copies.append(place.push(part, part, *self.second_sem, (index, 1, hop, 0), (other, place.me)))
        self.waiting[index] = copies

    def finish(self, index):
        for copy in self.waiting[index]:
            copy.wait_recv()


def small_rows(seq_count, values):
    rows = jnp.concatenate([values, jnp.zeros((32 - values.shape[0], values.shape[1]), jnp.float32)])
    return rows.reshape(seq_count, 32 // seq_count, values.shape[1])


class SmallSum:
    def __init__(self, place, source, total, scratch, first_send, first_recv, second_send, second_recv):
        self.place, self.source, self.total_ref, self.scratch = place, source, total, scratch
        self.first_sem, self.second_sem = (first_send, first_recv), (second_send, second_recv)

    def begin(self):
        place = self.place
        self.waiting = [
            place.push(self.source.at[other], self.scratch.at[step], *self.first_sem, step, (place.grp, other))
            for step, other in enumerate(place.others)
        ]

    def middle(self):
        place = self.place
        value = self.source[place.me]
        for step, copy in enumerate(self.waiting):
            copy.wait_recv()
            value = value + self.scratch[step]
        self.total_ref[place.me] = value
        part = self.total_ref.at[place.me]
        self.waiting = [
            place.push(part, part, *self.second_sem, step, (place.grp, other))
            for step, other in enumerate(place.others)
        ]

    def finish(self):
        for copy in self.waiting:
            copy.wait_recv()


def small_scratch(source):
    seq_count = source.shape[0]
    dma = pltpu.SemaphoreType.DMA
    return [pltpu.VMEM((seq_count - 1,) + source.shape[1:], jnp.float32)] + [dma((seq_count - 1,))] * 4


def forward_kernel(plane, seq_count, count, *refs):
    layers = seq_count // 2
    bound_ref, qkv_ref, shards = refs[0], refs[1], refs[2:2 + count]
    refs = refs[2 + count:]
    pieces, refs = refs[0], refs[1:]
    kept_ref, mixture_ref, log_ref, fulls = refs[0], refs[1], refs[2], refs[3:3 + count]
    (
        key_scr, query_scr, value_t_scr, score_scr, mix_t_scr, mix_scr,
        send_sem, recv_sem, back_send_sem, back_recv_sem, local_sem,
    ) = refs[3 + count:14 + count]
    own_sem, first_send, first_recv, second_send, second_recv, core_send, core_recv = refs[14 + count:]
    group_count, local_rows, local_width = qkv_ref.shape[1], qkv_ref.shape[3], qkv_ref.shape[4]
    total_rows = seq_count * local_rows
    heads = local_width // HEAD_DIM
    me = lax.axis_index("seq")
    grp = lax.axis_index("grp")
    others = [lax.rem(me + step, seq_count) for step in range(1, seq_count)]
    origins = [lax.rem(me + seq_count - step, seq_count) for step in range(1, seq_count)]
    block = min(256, total_rows // 3)
    place = Place(plane, seq_count)
    enter([(grp, other) for other in others] + [(other, me) for other in place.beside + place.along])
    copies = []

    def begin_group(group):
        own = pltpu.make_async_copy(qkv_ref.at[me, group], kept_ref.at[me, group], local_sem.at[group])
        own.start()
        row = [own]
        for step, other in enumerate(others):
            copy = pltpu.make_async_remote_copy(
                qkv_ref.at[other, group], kept_ref.at[me, group],
                send_sem.at[group, step], recv_sem.at[group, step],
                device_id=(grp, other), device_id_type=MESH,
            )
            copy.start()
            row.append(copy)
        copies.append(row)

    begin_group(0)
    side = place.cols_x
    segments, _ = piece_segments(
        [shard.shape for shard in shards], side, min(shard.shape[1] for shard in shards) // side
    )
    spread = PlaneGather(
        place, shards, pieces, segments, fulls,
        own_sem, first_send, first_recv, second_send, second_recv, core_send, core_recv,
    )
    spread.begin()
    back = []
    for group in range(group_count):
        for copy in copies[group]:
            copy.wait()
        if group + 1 < group_count:
            begin_group(group + 1)
        if group == 0:
            spread.middle()
            hooks = spread.late()
            held = len(hooks) // 3
        boundary = bound_ref[group]
        keys = kept_ref[:, group, 1].reshape(total_rows, local_width)
        values = kept_ref[:, group, 2].reshape(total_rows, local_width)
        key_scr[:, :local_width] = keys
        key_scr[:, local_width:] = utter_features(boundary, total_rows, True)
        query_scr[:, local_width:] = utter_features(boundary, total_rows, False)
        value_t_scr[...] = values.astype(jnp.float32).T.astype(jnp.bfloat16)

        for head in range(heads):
            queries = kept_ref[:, group, 0].reshape(total_rows, local_width)
            query_scr[:, :local_width] = head_lanes(queries, head) * jnp.bfloat16(HEAD_DIM ** (-0.5))
            for third in range(3):
                first_key, last_key = key_span(third, total_rows)
                chunks = range(first_key, last_key, block)

                def one_block(index, carry):
                    first_row = pl.multiple_of(third * (total_rows // 3) + index * block, block)
                    query_block = query_scr[pl.ds(first_row, block), :]
                    peak = jnp.full((8, block), -jnp.inf, jnp.float32)
                    for first in chunks:
                        scores = dot_nt(key_scr[first:first + block, :], query_block)
                        score_scr[first:first + block, :] = scores
                        peak = jnp.maximum(peak, fold_rows(scores, jnp.max))
                    peak = jnp.max(peak, axis=0, keepdims=True)
                    total = jnp.zeros((8, block), jnp.float32)
                    for first in chunks:
                        lifted = jnp.exp(score_scr[first:first + block, :] - peak)
                        score_scr[first:first + block, :] = lifted
                        total = total + fold_rows(lifted, jnp.sum)
                    total = jnp.sum(total, axis=0, keepdims=True)
                    inverse = 1.0 / total
                    mixed = jnp.zeros((HEAD_DIM, block), jnp.float32)
                    rows = slice(head * HEAD_DIM, (head + 1) * HEAD_DIM)
                    for first in chunks:
                        weight = (score_scr[first:first + block, :] * inverse).astype(jnp.bfloat16)
                        mixed = mixed + dot_nn(value_t_scr[rows, first:first + block], weight)
                    mix_t_scr[rows, pl.ds(first_row, block)] = mixed
                    log_ref[group, head, :, pl.ds(first_row, block)] = peak + jnp.log(total)
                    return carry

                lax.fori_loop(0, total_rows // 3 // block, one_block, 0)
                if group > 0 and len(hooks) > held:
                    hooks.pop(0)()
        mix_scr[group] = mix_t_scr[...].T.astype(jnp.bfloat16).reshape(seq_count, local_rows, local_width)
        own = pltpu.make_async_copy(
            mix_scr.at[group, me], mixture_ref.at[me, group], local_sem.at[group_count + group]
        )
        own.start()
        back.append(own)
        for step, other in enumerate(others):
            copy = pltpu.make_async_remote_copy(
                mix_scr.at[group, other], mixture_ref.at[me, group],
                back_send_sem.at[group, step], back_recv_sem.at[group, step],
                device_id=(grp, other), device_id_type=MESH,
            )
            copy.start()
            back.append(copy)
    for hook in hooks:
        hook()
    for copy in back:
        copy.wait()
    for index in range(count):
        spread.arrive(index)
    spread.finish()


def attend_forward(bounds, qkv, shards, pieces):
    side = math.isqrt(lax.axis_size("grp"))
    hops = max(side - 1, 1)
    count = len(shards)
    dma = pltpu.SemaphoreType.DMA
    anywhere = pl.BlockSpec(memory_space=pl.ANY)
    layers = qkv.shape[0] // 2
    seq_count, group_count, _, local_rows, local_width = qkv.shape
    total_rows = seq_count * local_rows
    heads = local_width // HEAD_DIM
    block = min(256, total_rows // 3)
    vmem = pl.BlockSpec(memory_space=pltpu.VMEM)
    return pl.pallas_call(
        functools.partial(forward_kernel, (side, side), seq_count, count),
        out_shape=(
            jax.ShapeDtypeStruct(qkv.shape, jnp.bfloat16),
            jax.ShapeDtypeStruct((seq_count, group_count, local_rows, local_width), jnp.bfloat16),
            jax.ShapeDtypeStruct((group_count, heads, 1, total_rows), jnp.float32),
        ) + tuple(jax.ShapeDtypeStruct((seq_count,) + part.shape, part.dtype) for part in shards),
        in_specs=[pl.BlockSpec(memory_space=pltpu.SMEM)] + [anywhere] * (2 + count),
        out_specs=(vmem, vmem, vmem) + (anywhere,) * count,
        scratch_shapes=[
            pltpu.VMEM((total_rows, local_width + 128), jnp.bfloat16),
            pltpu.VMEM((total_rows, local_width + 128), jnp.bfloat16),
            pltpu.VMEM((local_width, total_rows), jnp.bfloat16),
            pltpu.VMEM((total_rows, block), jnp.float32),
            pltpu.VMEM((local_width, total_rows), jnp.float32),
            pltpu.VMEM((group_count, seq_count, local_rows, local_width), jnp.bfloat16),
            pltpu.SemaphoreType.DMA((group_count, seq_count - 1)),
            pltpu.SemaphoreType.DMA((group_count, seq_count - 1)),
            pltpu.SemaphoreType.DMA((group_count, seq_count - 1)),
            pltpu.SemaphoreType.DMA((group_count, seq_count - 1)),
            pltpu.SemaphoreType.DMA((2 * group_count,)),
            dma((count, layers, 2, 2)),
            dma((count, layers - 1, 2, hops, 2)), dma((count, layers - 1, 2, hops, 2)),
            dma((count, layers - 1, 2, hops, side)), dma((count, layers - 1, 2, hops, side)),
            dma((count, layers)), dma((count, layers)),
        ],
        compiler_params=pltpu.CompilerParams(
            collective_id=1, has_side_effects=True, vmem_limit_bytes=48 * 1024 * 1024
        ),
        name="attend_forward",
    )(bounds, qkv, *shards, pieces)


def backward_kernel(plane, seq_count, count, *refs):
    layers = seq_count // 2
    bound_ref, kept_ref, grad_ref, log_ref = refs[:4]
    parts, refs = refs[4:4 + count], refs[4 + count:]
    out_ref, refs = refs[0], refs[1:]
    pieces, refs = refs[:layers], refs[layers:]
    (
        taken_scr, key_scr, query_scr, key_t_scr, head_query_scr, head_grad_scr, prob_scr, weight_scr,
        query_t_scr, key_sum_scr, value_sum_scr, back_scr,
        send_sem, recv_sem, back_send_sem, back_recv_sem, local_sem,
    ) = refs[:17]
    buffers, semaphores = refs[17:17 + 6 * count], refs[17 + 6 * count:]
    group_count, local_rows, local_width = grad_ref.shape[1], grad_ref.shape[2], grad_ref.shape[3]
    total_rows = seq_count * local_rows
    heads = local_width // HEAD_DIM
    me = lax.axis_index("seq")
    grp = lax.axis_index("grp")
    others = [lax.rem(me + step, seq_count) for step in range(1, seq_count)]
    block = min(256, total_rows // 3)
    place = Place(plane, seq_count)
    enter([(grp, other) for other in others] + [(other, me) for other in place.beside + place.along])
    copies = []

    def begin_group(group):
        own = pltpu.make_async_copy(grad_ref.at[me, group], taken_scr.at[me, group], local_sem.at[group])
        own.start()
        row = [own]
        for step, other in enumerate(others):
            copy = pltpu.make_async_remote_copy(
                grad_ref.at[other, group], taken_scr.at[me, group],
                send_sem.at[group, step], recv_sem.at[group, step],
                device_id=(grp, other), device_id_type=MESH,
            )
            copy.start()
            row.append(copy)
        copies.append(row)

    begin_group(0)
    side = place.cols_x
    segments, _ = piece_segments(
        [part.shape[1:] for part in parts], side, min(part.shape[2] for part in parts) // side
    )
    plane_sum = PlaneSum(place, parts, [pieces] * count, segments, buffers, semaphores)
    plane_sum.begin()
    firsts = plane_sum.steps(plane_sum.first)
    seconds = plane_sum.steps(plane_sum.second)
    units = 3 * heads * group_count
    plan = [[] for _ in range(units + 1)]
    for spot, hook in enumerate(firsts):
        plan[spot * (units // 2 - 1) // len(firsts)].append(hook)
    for spot, hook in enumerate(seconds):
        plan[units - 5 + spot * 6 // len(seconds)].append(hook)
    back = []
    for group in range(group_count):
        for copy in copies[group]:
            copy.wait()
        if group + 1 < group_count:
            begin_group(group + 1)
        boundary = bound_ref[group]
        keys = kept_ref[:, group, 1].reshape(total_rows, local_width)
        key_scr[:, :local_width] = keys
        key_scr[:, local_width:] = utter_features(boundary, total_rows, True)
        query_scr[:, local_width:] = utter_features(boundary, total_rows, False)
        key_t_scr[...] = keys.astype(jnp.float32).T.astype(jnp.bfloat16)
        key_sum_scr[...] = jnp.zeros_like(key_sum_scr)
        value_sum_scr[...] = jnp.zeros_like(value_sum_scr)

        for head in range(heads):
            queries = head_lanes(kept_ref[:, group, 0].reshape(total_rows, local_width), head)
            head_query_scr[...] = queries
            query_scr[:, :local_width] = queries * jnp.bfloat16(HEAD_DIM ** (-0.5))
            head_grad_scr[...] = head_lanes(taken_scr[:, group].reshape(total_rows, local_width), head)
            for third in range(3):
                first_key, last_key = key_span(third, total_rows)
                chunks = range(first_key, last_key, block)

                def one_block(index, carry):
                    first_row = pl.multiple_of(third * (total_rows // 3) + index * block, block)
                    own_rows = pl.ds(first_row, block)
                    query_block = query_scr[own_rows, :]
                    grad_block = head_grad_scr[own_rows, :]
                    plain_block = head_query_scr[own_rows, :]
                    log_block = log_ref[group, head, :, own_rows]
                    row_dot = jnp.zeros((8, block), jnp.float32)
                    for first in chunks:
                        scores = dot_nt(key_scr[first:first + block, :], query_block)
                        prob = jnp.exp(scores - log_block)
                        values = kept_ref[
                            first // local_rows:(first + block - 1) // local_rows + 1, group, 2
                        ].reshape(-1, local_width)
                        skip = first % local_rows
                        weight_grad = dot_nt(values[skip:skip + block], grad_block)
                        prob_scr[first:first + block, :] = prob
                        weight_scr[first:first + block, :] = weight_grad
                        row_dot = row_dot + fold_rows(prob * weight_grad, jnp.sum)
                    row_dot = jnp.sum(row_dot, axis=0, keepdims=True)
                    rows = slice(head * HEAD_DIM, (head + 1) * HEAD_DIM)
                    turned = jnp.zeros((HEAD_DIM, block), jnp.float32)
                    for first in chunks:
                        prob = prob_scr[first:first + block, :]
                        score_grad = (
                            HEAD_DIM ** (-0.5) * (prob * (weight_scr[first:first + block, :] - row_dot))
                        ).astype(jnp.bfloat16)
                        key_sum_scr[first:first + block, :] += dot_nn(score_grad, plain_block)
                        value_sum_scr[first:first + block, :] += dot_nn(
                            prob.astype(jnp.bfloat16), grad_block
                        )
                        turned = turned + dot_nn(key_t_scr[rows, first:first + block], score_grad)
                    query_t_scr[rows, own_rows] = turned
                    return carry

                lax.fori_loop(0, total_rows // 3 // block, one_block, 0)
                for hook in plan.pop(0):
                    hook()
        shape = (seq_count, local_rows, local_width)
        back_scr[:, group, 0] = query_t_scr[...].T.astype(jnp.bfloat16).reshape(shape)
        back_scr[:, group, 1] = key_sum_scr[...].astype(jnp.bfloat16).reshape(shape)
        back_scr[:, group, 2] = value_sum_scr[...].astype(jnp.bfloat16).reshape(shape)
        own = pltpu.make_async_copy(
            back_scr.at[me, group], out_ref.at[me, group], local_sem.at[group_count + group]
        )
        own.start()
        back.append(own)
        for step, other in enumerate(others):
            copy = pltpu.make_async_remote_copy(
                back_scr.at[other, group], out_ref.at[me, group],
                back_send_sem.at[group, step], back_recv_sem.at[group, step],
                device_id=(grp, other), device_id_type=MESH,
            )
            copy.start()
            back.append(copy)
    for hook in plan[0] + plane_sum.steps(plane_sum.third):
        hook()
    for copy in back:
        copy.wait()
    plane_sum.finish()


def attend_backward(bounds, kept, grad, log_total, parts):
    side = math.isqrt(lax.axis_size("grp"))
    count = len(parts)
    layers = kept.shape[0] // 2
    anywhere = pl.BlockSpec(memory_space=pl.ANY)
    parts = by_owner(parts, kept.shape[0])
    width = min(part.shape[2] for part in parts) // side
    _, piece_rows = piece_segments([part.shape[1:] for part in parts], side, width)
    seq_count, group_count, _, local_rows, local_width = kept.shape
    total_rows = seq_count * local_rows
    block = min(256, total_rows // 3)
    vmem = pl.BlockSpec(memory_space=pltpu.VMEM)
    return pl.pallas_call(
        functools.partial(backward_kernel, (side, side), seq_count, count),
        out_shape=(jax.ShapeDtypeStruct(kept.shape, jnp.bfloat16),) + tuple(
            jax.ShapeDtypeStruct((piece_rows, width), jnp.bfloat16) for _ in range(layers)
        ),
        in_specs=[pl.BlockSpec(memory_space=pltpu.SMEM), vmem, anywhere, vmem] + [anywhere] * count,
        out_specs=(vmem,) * (1 + layers),
        scratch_shapes=[
            pltpu.VMEM(grad.shape, jnp.bfloat16),
            pltpu.VMEM((total_rows, local_width + 128), jnp.bfloat16),
            pltpu.VMEM((total_rows, local_width + 128), jnp.bfloat16),
            pltpu.VMEM((local_width, total_rows), jnp.bfloat16),
            pltpu.VMEM((total_rows, local_width), jnp.bfloat16),
            pltpu.VMEM((total_rows, local_width), jnp.bfloat16),
            pltpu.VMEM((total_rows, block), jnp.float32),
            pltpu.VMEM((total_rows, block), jnp.float32),
            pltpu.VMEM((local_width, total_rows), jnp.float32),
            pltpu.VMEM((total_rows, local_width), jnp.float32),
            pltpu.VMEM((total_rows, local_width), jnp.float32),
            pltpu.VMEM(kept.shape, jnp.bfloat16),
            pltpu.SemaphoreType.DMA((group_count, seq_count - 1)),
            pltpu.SemaphoreType.DMA((group_count, seq_count - 1)),
            pltpu.SemaphoreType.DMA((group_count, seq_count - 1)),
            pltpu.SemaphoreType.DMA((group_count, seq_count - 1)),
            pltpu.SemaphoreType.DMA((2 * group_count,)),
        ] + plane_sum_scratch(parts, side),
        compiler_params=pltpu.CompilerParams(
            collective_id=2, has_side_effects=True, vmem_limit_bytes=60 * 1024 * 1024
        ),
        name="attend_backward",
    )(bounds, kept, grad, log_total, *parts)


class LineChain:
    def __init__(self, place, sources, slots, sends, recvs):
        self.place, self.sources, self.slots = place, sources, slots
        self.sends, self.recvs = sends, recvs
        self.pushed = []
        middle = []
        low, high = 0, place.layers - 2
        while low <= high:
            middle += [low] if low == high else [low, high]
            low, high = low + 1, high - 1
        first, last = place.layer == 0, place.layer == place.layers - 1
        self.ranks = [
            jnp.where(first, place.layers - 2 - rank, jnp.where(last, rank, step)).astype(jnp.int32)
            for rank, step in enumerate(middle)
        ]

    def owner(self, step):
        place = self.place
        return lax.rem(place.layer + place.layers - 1 - step, place.layers) * 2 + place.core

    def copy(self, index, source, owner, slot, target, send_slot):
        return pltpu.make_async_remote_copy(
            source, self.slots(index, owner, slot),
            self.sends.at[index, send_slot], self.recvs.at[index, slot],
            device_id=(self.place.grp, target * 2 + self.place.core), device_id_type=MESH,
        )

    def push(self, when, *given):
        self.pushed.append((when, given))

        @pl.when(when)
        def _():
            self.copy(*given).start()

    def begin(self, index):
        place = self.place
        source = self.sources[index]
        self.push(place.layer < place.layers - 1, index, source, place.me, 0, place.layer + 1, 0)
        self.push(place.layer > 0, index, source, place.me, place.layers - 2, place.layer - 1, 1)

    def forward(self, index, rank):
        place = self.place
        step = self.ranks[rank]
        owner = self.owner(step)
        held = self.slots(index, owner, step)
        self.copy(index, held, owner, step, place.layer, 0).wait_recv()
        below = step < place.layer
        going = (below & (place.layer < place.layers - 1)) | ((step >= place.layer) & (place.layer > 0))
        slot = jnp.where(below, step + 1, step - 1)
        target = jnp.where(below, place.layer + 1, place.layer - 1)
        self.push(going, index, held, owner, slot, target, rank + 2)
        return owner

    def sent(self):
        for when, given in self.pushed:

            @pl.when(when)
            def _(given=given):
                self.copy(*given).wait_send()


class WholeGather(PlaneGather):
    def __init__(self, place, shards, fulls, line_send, line_recv, *semaphores):
        super().__init__(place, shards, None, None, fulls, *semaphores)

        def piece(ref, index):
            rows, height, width = self.sizes(index)
            return window(ref, place.gy * height, height, 2 * place.gx * width, 2 * width)

        self.chain = LineChain(
            place, [piece(shard, index) for index, shard in enumerate(shards)],
            lambda index, owner, slot: piece(fulls[index].at[owner], index), line_send, line_recv,
        )
        self.jobs = [(index, rank) for index in range(len(shards)) for rank in range(place.layers - 1)]

    def owner(self, step):
        return self.chain.owner(self.chain.ranks[step])

    def begin(self):
        place = self.place
        for index in range(len(self.shards)):
            self.chain.begin(index)
        for index, shard in enumerate(self.shards):
            copy = pltpu.make_async_copy(shard, self.fulls[index].at[place.me], self.own_sem.at[index, place.layers - 1, 0, 0])
            copy.start()
            push = place.push(shard, self.fulls[index].at[place.me], *self.core, (index, 0), (place.grp, place.partner))
            self.own.append((copy, push))

    def spread_first(self, index, step):
        place = self.place
        rows, height, width = self.sizes(index)
        full = self.fulls[index].at[self.chain.forward(index, step)]
        row, col = place.gy * height, 2 * place.gx * width
        self.waiting[index, step] = []
        for half, partners in enumerate((place.beside, place.along)):
            part = window(full, row, height, col + half * width, width)
            for hop, other in enumerate(partners):
                self.waiting[index, step].append(
                    place.push(part, part, *self.first, (index, step, half, hop, 0), (other, place.me))
                )

    def finish(self):
        super().finish()
        self.chain.sent()


def turn_lanes(values, cos, sin):
    lane = lax.broadcasted_iota(jnp.int32, values.shape, 1)
    ahead = pltpu.roll(values, values.shape[1] - HEAD_DIM // 2, 1)
    behind = pltpu.roll(values, HEAD_DIM // 2, 1)
    other = jnp.where(lax.rem(lane, HEAD_DIM) < HEAD_DIM // 2, ahead, behind)
    return values * cos + other * sin


def second_mask(bound_ref, group, me, local_rows, first, rows):
    row = lax.broadcasted_iota(jnp.int32, (rows, 1), 0) + (me * local_rows + first)
    return row >= bound_ref[group]


def centered(values):
    center = values - jnp.mean(values, axis=-1, keepdims=True)
    scale = lax.rsqrt(jnp.mean(center * center, axis=-1, keepdims=True) + epsilon)
    return center * scale, scale


def front_kernel(plane, seq_count, late_count, *refs):
    layers = seq_count // 2
    bound_ref, frames_ref, shortcut_ref, cos_ref, sin_ref, partial_ref, token_ref = refs[:7]
    shards, late_shards, refs = refs[7:9], refs[9:9 + late_count], refs[9 + late_count:]
    fulls_out, late_out, refs = refs[:2], refs[2], refs[3:]
    hidden_ref, normed_ref, qkv_ref, total_ref, tokens_ref = refs[:5]
    fulls, refs = refs[5:7], refs[7:]
    token_scr, token_send, token_recv, out_sem = refs[:4]
    small_refs, (late_scr, late_send, late_recv, late_sem), refs = refs[4:9], refs[9:13], refs[13:]
    group_count, local_rows, local_width = qkv_ref.shape[1], qkv_ref.shape[3], qkv_ref.shape[4]
    row_count, width = hidden_ref.shape
    place = Place(plane, seq_count)
    me = place.me
    enter([(place.grp, other) for other in place.others] + [(other, me) for other in place.groups])
    whole = WholeGather(place, shards, fulls, *refs)
    whole.begin()
    small = SmallSum(place, partial_ref, total_ref, *small_refs)
    small.begin()
    side = place.cols_x
    cut = late_scr.shape[1]
    late_own, base = [], 0
    for index, shard in enumerate(late_shards):
        height, cols = shard.shape[0] // side, shard.shape[1] // side
        for spot in range(cols // cut):
            late_own.append(pltpu.make_async_copy(
                window(shard, place.gy * height, height, place.gx * cols + spot * cut, cut),
                late_scr.at[pl.ds(base, height), :],
                late_sem.at[len(late_own)],
            ))
            late_own[-1].start()
            base += height
    late_chain = LineChain(place, [late_scr], lambda index, owner, slot: late_out.at[slot], late_send, late_recv)
    combine_jobs = [job for job in whole.jobs if job[0] == 0]
    projection_jobs = [job for job in whole.jobs if job[0] == 1]
    for job in combine_jobs:
        whole.spread_first(*job)
    for job, late in zip(combine_jobs, projection_jobs):
        whole.spread_second(*job)
        whole.spread_first(*late)
    for copy in late_own:
        copy.wait()
    late_chain.begin(0)
    small.middle()
    for job, late in zip(combine_jobs, projection_jobs):
        whole.over_core(*job)
        whole.spread_second(*late)
    whole.arrive(0)
    outs = [pltpu.make_async_copy(fulls[0], fulls_out[0], out_sem.at[0])]
    outs[0].start()
    late_chain.forward(0, 0)
    half = seq_count // 2

    def hidden_tile(index, carry):
        at = pl.ds(pl.multiple_of(index * 256, 256), 256)
        upper = fulls[0][0:half, :, at].reshape(width, 256)
        lower = fulls[0][half:seq_count, :, at].reshape(width, 256)
        hidden_ref[:, at] = dot_nn(frames_ref[...], upper) + dot_nn(shortcut_ref[...], lower)
        return carry

    lax.fori_loop(0, width // 256, hidden_tile, 0)
    small.finish()
    last = total_ref.shape[1] - 1
    token_scr[...] = token_ref[...]
    token_scr[4:5, :] = total_ref[seq_count - 1, last:last + 1, :128]
    tokens_ref[place.grp] = token_scr[...]
    tokens = [
        place.push(token_scr, tokens_ref.at[place.grp], token_send, token_recv, step, (other, me))
        for step, other in enumerate(place.groups)
    ]
    block = total_ref.shape[1]

    def vector(group, part, second):
        def row(utter):
            at = (group * 2 + utter) * 6 + part
            return total_ref[at // block, at % block:at % block + 1, :]

        return jnp.where(second, row(1), row(0))

    chunk = 32
    for group in range(group_count):

        def norm_rows(index, carry):
            first = pl.multiple_of(index * chunk, chunk)
            at = pl.ds(pl.multiple_of(group * local_rows + first, chunk), chunk)
            second = second_mask(bound_ref, group, me, local_rows, first, chunk)
            normal, _ = centered(hidden_ref[at, :])
            normed_ref[at, :] = (
                normal * (1.0 + vector(group, 1, second)) + vector(group, 0, second)
            ).astype(jnp.bfloat16)
            return carry

        lax.fori_loop(0, local_rows // chunk, norm_rows, 0)
    for job in projection_jobs:
        whole.over_core(*job)
    whole.arrive(1)
    late_chain.forward(0, 1)
    outs.append(pltpu.make_async_copy(fulls[1], fulls_out[1], out_sem.at[1]))
    outs[1].start()
    each = 256 // local_width

    def head_tile(index, carry):
        for kind in range(3):
            at = pl.ds(pl.multiple_of(kind * width + index * 256, 256), 256)
            packed = dot_nn(normed_ref[...], fulls[1][:, :, at].reshape(width, 256))
            for half in range(2):
                lanes = packed[:, half * 128:(half + 1) * 128]
                if kind < 2:
                    lanes = turn_lanes(lanes, cos_ref[...], sin_ref[...])
                lanes = lanes.astype(jnp.bfloat16)
                for spot in range(each // 2):
                    cut = lanes[:, spot * local_width:(spot + 1) * local_width]
                    for group in range(group_count):
                        qkv_ref[index * each + half * (each // 2) + spot, group, kind] = cut[
                            group * local_rows:(group + 1) * local_rows
                        ]
        return carry

    lax.fori_loop(0, width // 256, head_tile, 0)
    for rank in range(2, layers - 1):
        late_chain.forward(0, rank)
    whole.finish()
    late_chain.sent()
    for copy in tokens:
        copy.wait_recv()
    for copy in outs:
        copy.wait()


def front(bounds, frames, shortcut, cos, sin, partial, token, combine, projection, late_shards):
    grp_count = lax.axis_size("grp")
    seq_count = lax.axis_size("seq")
    side = math.isqrt(grp_count)
    layers = seq_count // 2
    anywhere = pl.BlockSpec(memory_space=pl.ANY)
    vmem = pl.BlockSpec(memory_space=pltpu.VMEM)
    dma = pltpu.SemaphoreType.DMA
    hops = max(side - 1, 1)
    shards = (combine, projection)
    group_count = bounds.shape[0]
    row_count, width = frames.shape
    low, full = jnp.bfloat16, jnp.float32
    cut = min(shard.shape[1] for shard in late_shards) // side
    late_rows = sum(shard.shape[0] // side * (shard.shape[1] // side // cut) for shard in late_shards)
    most = max(shard.shape[1] // side // cut for shard in late_shards)
    wholes = [(seq_count,) + part.shape for part in shards]
    return pl.pallas_call(
        functools.partial(front_kernel, (side, side), seq_count, len(late_shards)),
        out_shape=tuple(jax.ShapeDtypeStruct(shape, low) for shape in wholes) + (
            jax.ShapeDtypeStruct((layers - 1, late_rows, cut), low),
            jax.ShapeDtypeStruct((row_count, width), full),
            jax.ShapeDtypeStruct((row_count, width), low),
            jax.ShapeDtypeStruct(
                (seq_count, group_count, 3, row_count // group_count, width // seq_count), low
            ),
            jax.ShapeDtypeStruct(partial.shape, full),
            jax.ShapeDtypeStruct((grp_count,) + token.shape, full),
        ),
        in_specs=[pl.BlockSpec(memory_space=pltpu.SMEM)] + [vmem] * 6 + [anywhere] * (2 + len(late_shards)),
        out_specs=(anywhere,) * 3 + (vmem,) * 5,
        scratch_shapes=[pltpu.VMEM(shape, low) for shape in wholes] + [
            pltpu.VMEM(token.shape, full), dma((grp_count - 1,)), dma((grp_count - 1,)), dma((2,)),
        ] + small_scratch(partial) + [
            pltpu.VMEM((late_rows, cut), low),
            dma((1, layers + 1)), dma((1, layers - 1)), dma((len(late_shards) * most,)),
            dma((2, layers + 1)), dma((2, layers - 1)),
            dma((2, layers, 1, 1)),
            dma((2, layers - 1, 2, hops, 1)), dma((2, layers - 1, 2, hops, 1)),
            dma((2, layers - 1, 2, hops, side)), dma((2, layers - 1, 2, hops, side)),
            dma((2, layers)), dma((2, layers)),
        ],
        compiler_params=pltpu.CompilerParams(
            collective_id=3, has_side_effects=True, vmem_limit_bytes=48 * 1024 * 1024
        ),
        name="front",
    )(bounds, frames, shortcut, cos, sin, partial, token, *shards, *late_shards)


def middle_kernel(seq_count, *refs):
    (
        bound_ref, mixture_ref, hidden_ref, target_ref, kept_ref, mods_ref, scale_ref,
        readout_ref, expand_ref, contract_ref,
    ) = refs[:10]
    result_ref, middle_grad_ref, mixture_grad_ref, late_ref, contract_part, expand_part, readout_part = refs[10:17]
    (
        readout_scr, expand_scr, contract_scr, mixture_scr, branch_scr, middle_scr, normed_scr, slope_scr, active_scr,
        active_t_scr, wide_scr, grad_scr, low_scr, left_t_scr, stage_scr, value_scr, weight_sem, stage_sem,
    ) = refs[17:]
    row_count, width = hidden_ref.shape
    wide = expand_ref.shape[1]
    group_count = mods_ref.shape[0] // 12
    local_rows = row_count // group_count
    local_width = width // seq_count
    me = lax.axis_index("seq")
    weights = [
        pltpu.make_async_copy(source, scratch, weight_sem.at[index])
        for index, (source, scratch) in enumerate(
            ((readout_ref, readout_scr), (expand_ref, expand_scr), (contract_ref, contract_scr))
        )
    ]
    weights[0].start()
    for source in range(seq_count):
        for group in range(group_count):
            mixture_scr[
                group * local_rows:(group + 1) * local_rows, source * local_width:(source + 1) * local_width
            ] = mixture_ref[source, group]
    chunk = 32
    tile = 256

    def tiles(count, body):
        def one(index, carry):
            body(pl.ds(pl.multiple_of(index * tile, tile), tile))
            return carry

        lax.fori_loop(0, count // tile, one, 0)

    def chunks(body, many):
        sums = []
        for group in range(group_count):

            def one(index, carry, group=group):
                first = pl.multiple_of(index * chunk, chunk)
                at = pl.ds(pl.multiple_of(group * local_rows + first, chunk), chunk)
                second = second_mask(bound_ref, group, me, local_rows, first, chunk)

                def vector(part):
                    row = group * 12 + part
                    return jnp.where(second, mods_ref[row + 6:row + 7, :], mods_ref[row:row + 1, :])

                later = second.astype(jnp.float32)
                found = body(at, vector)
                out = []
                for spot, value in enumerate(found):
                    late = value * later
                    out.append(carry[2 * spot] + fold_rows(value - late, jnp.sum))
                    out.append(carry[2 * spot + 1] + fold_rows(late, jnp.sum))
                return tuple(out)

            zero = jnp.zeros((8, width), jnp.float32)
            sums.append(lax.fori_loop(0, local_rows // chunk, one, (zero,) * (2 * many)))
        return sums

    def put(part, spot, sums):
        for group in range(group_count):
            for utter in range(2):
                row = part * 2 * group_count + group * 2 + utter
                late_ref[row:row + 1, :] = jnp.sum(sums[group][2 * spot + utter], axis=0, keepdims=True)

    weights[0].wait()
    weights[1].start()
    weights[2].start()
    tiles(width, lambda at: branch_scr.__setitem__((slice(None), at), dot_nn(mixture_scr[...], readout_scr[:, at])))

    def second_norm(at, vector):
        middle = hidden_ref[at, :] + vector(2) * branch_scr[at, :]
        middle_scr[at, :] = middle
        normal, _ = centered(middle)
        normed_scr[at, :] = (normal * (1.0 + vector(4)) + vector(3)).astype(jnp.bfloat16)
        return ()

    chunks(second_norm, 0)
    weights[1].wait()

    def expand_dot(index, slot):
        at = pl.ds(pl.multiple_of(jnp.minimum(index, wide // tile - 1) * tile, tile), tile)
        value_scr[slot] = dot_nn(normed_scr[...], expand_scr[:, at])

    def bend(index, slot):
        at = pl.ds(pl.multiple_of(index * tile, tile), tile)
        value = value_scr[slot]
        square = value * value
        factor = (2.0 / math.pi) ** 0.5
        bent = jnp.tanh(value * (factor + (factor * 0.044715) * square))
        half = 0.5 + 0.5 * bent
        active_scr[:, at] = (value * half).astype(jnp.bfloat16)
        slope_scr[:, at] = half + (0.5 * value * (1.0 - bent * bent)) * (factor + (factor * 3 * 0.044715) * square)

    def expand_pair(index, carry):
        expand_dot(2 * index + 1, 1)
        bend(2 * index, 0)
        expand_dot(2 * index + 2, 0)
        bend(2 * index + 1, 1)
        return carry

    expand_dot(0, 0)
    lax.fori_loop(0, wide // tile // 2, expand_pair, 0)
    weights[2].wait()
    tiles(width, lambda at: grad_scr.__setitem__((slice(None), at), dot_nn(active_scr[...], contract_scr[:, at])))
    loss_scale = scale_ref[0]

    def close(at, vector):
        contracted = grad_scr[at, :]
        gate = vector(5)
        output = middle_scr[at, :] + gate * contracted
        result_ref[at, :] = output.astype(jnp.bfloat16)
        output_grad = loss_scale * kept_ref[at, :] * (output - target_ref[at, :].astype(jnp.float32))
        middle_grad_ref[at, :] = output_grad
        low_scr[at, :] = (gate * output_grad).astype(jnp.bfloat16)
        return (output_grad * contracted,)

    put(3, 0, chunks(close, 1))
    def share_out(left, right, dest, across):
        many = dest.shape[1 if across else 0] // width

        def copy(index, slot):
            block = pl.ds(index * width, width)
            return pltpu.make_async_copy(
                stage_scr.at[slot], dest.at[:, block] if across else dest.at[block, :], stage_sem.at[slot]
            )

        for block in range(many):
            slot = block % 2
            if block >= 2:
                copy(block - 2, slot).wait()

            def one(index, carry, block=block, slot=slot):
                at = pl.ds(pl.multiple_of(index * tile, tile), tile)
                first = left[...] if across else left[block * width:(block + 1) * width, :]
                lanes = pl.ds(pl.multiple_of(index * tile + (block * width if across else 0), tile), tile)
                stage_scr[slot, :, at] = dot_nn(first, right[:, lanes]).astype(jnp.bfloat16)
                return carry

            lax.fori_loop(0, width // tile, one, 0)
            copy(block, slot).start()
        return [copy(last, last % 2) for last in range(max(many - 2, 0), many)]

    def active_dot(index, slot):
        at = pl.ds(pl.multiple_of(jnp.minimum(index, wide // tile - 1) * tile, tile), tile)
        value_scr[slot] = dot_nt(low_scr[...], contract_scr[at, :])

    def unbend(index, slot):
        at = pl.ds(pl.multiple_of(index * tile, tile), tile)
        active_t_scr[at, :] = active_scr[:, at].T
        wide_scr[:, at] = (value_scr[slot] * slope_scr[:, at]).astype(jnp.bfloat16)

    def active_pair(index, carry):
        active_dot(2 * index + 1, 1)
        unbend(2 * index, 0)
        active_dot(2 * index + 2, 0)
        unbend(2 * index + 1, 1)
        return carry

    active_dot(0, 0)
    lax.fori_loop(0, wide // tile // 2, active_pair, 0)

    out = share_out(active_t_scr, low_scr, contract_part, False)
    tiles(width, lambda at: grad_scr.__setitem__((slice(None), at), dot_nt(wide_scr[...], expand_scr[at, :])))
    tiles(width, lambda at: left_t_scr.__setitem__(
        (at, slice(None)), normed_scr[:, at].astype(jnp.float32).T.astype(jnp.bfloat16)
    ))

    for copy in out:
        copy.wait()
    out = share_out(left_t_scr, wide_scr, expand_part, True)

    def norm_back(at, vector):
        grad = grad_scr[at, :]
        normal, scale = centered(middle_scr[at, :])
        inner = grad * (1.0 + vector(4))
        turned = scale * (
            inner
            - jnp.mean(inner, axis=-1, keepdims=True)
            - normal * jnp.mean(inner * normal, axis=-1, keepdims=True)
        )
        middle_grad = middle_grad_ref[at, :] + turned
        middle_grad_ref[at, :] = middle_grad
        low_scr[at, :] = (vector(2) * middle_grad).astype(jnp.bfloat16)
        return middle_grad * branch_scr[at, :], grad, grad * normal

    sums = chunks(norm_back, 3)
    for spot in range(3):
        put(spot, spot, sums)

    def mixture_tile(at):
        left_t_scr[at, :] = mixture_scr[:, at].astype(jnp.float32).T.astype(jnp.bfloat16)
        grad_scr[:, at] = dot_nt(low_scr[...], readout_scr[at, :])

    tiles(width, mixture_tile)
    for source in range(seq_count):
        for group in range(group_count):
            mixture_grad_ref[source, group] = grad_scr[
                group * local_rows:(group + 1) * local_rows, source * local_width:(source + 1) * local_width
            ].astype(jnp.bfloat16)

    for copy in out:
        copy.wait()
    for copy in share_out(left_t_scr, low_scr, readout_part, False):
        copy.wait()


def middle(bounds, mixture, hidden, target, kept, mods, loss_scale, readout, expand, contract):
    seq_count, group_count, local_rows, local_width = mixture.shape
    row_count, width = hidden.shape
    wide = expand.shape[1]
    anywhere = pl.BlockSpec(memory_space=pl.ANY)
    vmem = pl.BlockSpec(memory_space=pltpu.VMEM)
    smem = pl.BlockSpec(memory_space=pltpu.SMEM)
    low, full = jnp.bfloat16, jnp.float32
    dma = pltpu.SemaphoreType.DMA
    return pl.pallas_call(
        functools.partial(middle_kernel, seq_count),
        out_shape=(
            jax.ShapeDtypeStruct((row_count, width), low),
            jax.ShapeDtypeStruct((row_count, width), full),
            jax.ShapeDtypeStruct(mixture.shape, low),
            jax.ShapeDtypeStruct((8 * group_count, width), full),
            jax.ShapeDtypeStruct(contract.shape, low),
            jax.ShapeDtypeStruct(expand.shape, low),
            jax.ShapeDtypeStruct(readout.shape, low),
        ),
        in_specs=[smem] + [vmem] * 5 + [smem] + [anywhere] * 3,
        out_specs=(vmem,) * 4 + (anywhere,) * 3,
        scratch_shapes=[
            pltpu.VMEM(readout.shape, low),
            pltpu.VMEM(expand.shape, low),
            pltpu.VMEM(contract.shape, low),
            pltpu.VMEM((row_count, width), low),
            pltpu.VMEM((row_count, width), full),
            pltpu.VMEM((row_count, width), full),
            pltpu.VMEM((row_count, width), low),
            pltpu.VMEM((row_count, wide), full),
            pltpu.VMEM((row_count, wide), low),
            pltpu.VMEM((wide, row_count), low),
            pltpu.VMEM((row_count, wide), low),
            pltpu.VMEM((row_count, width), full),
            pltpu.VMEM((row_count, width), low),
            pltpu.VMEM((width, row_count), low),
            pltpu.VMEM((2, width, width), low),
            pltpu.VMEM((2, row_count, 256), full),
            dma((3,)),
            dma((2,)),
        ],
        compiler_params=pltpu.CompilerParams(vmem_limit_bytes=60 * 1024 * 1024),
        name="feed_forward",
    )(bounds, mixture, hidden, target, kept, mods, loss_scale, readout, expand, contract)


def back_kernel(plane, seq_count, *refs):
    layers = seq_count // 2
    (
        bound_ref, back_ref, cos_ref, sin_ref, normed_ref, hidden_ref, middle_ref, frames_ref, shortcut_ref,
        combine_ref, projection_ref, mods_ref, late_ref, modulation_ref,
    ) = refs[:14]
    finished, refs = refs[14:14 + layers], refs[14 + layers:]
    frames_out, shortcut_out, outs, refs = refs[0], refs[1], refs[2:7], refs[7:]
    utters_ref, conditions_ref, refs = refs[0], refs[1], refs[2:]
    (
        packed_scr, combine_scr, projection_scr, normed_t_scr, joined_t_scr, grad_scr, low_scr,
        frames_scr, shortcut_scr, total_ref, utter_scr, condition_scr,
    ) = refs[:12]
    parts, done_scr, lines, refs = refs[12:14], refs[14], refs[15:17], refs[17:]
    pieces = [refs[index * layers:(index + 1) * layers] for index in range(2)]
    refs = refs[2 * layers:]
    buffers, semaphores, refs = refs[:10], refs[10:17], refs[17:]
    small_refs, spread_sems, refs = refs[:5], refs[5:9], refs[9:]
    weight_sem, out_sem, token_send, token_recv, last_send, last_recv, line_send, line_recv, done_send, done_recv = refs
    group_count, local_rows, local_width = back_ref.shape[1], back_ref.shape[3], back_ref.shape[4]
    row_count, width = normed_ref.shape
    place = Place(plane, seq_count)
    me = place.me
    side = place.cols_x
    enter([(place.grp, other) for other in place.others] + [(other, me) for other in place.groups])
    arrived = {}
    for step in range(layers - 1):
        arrived[step] = place.push(
            finished[step], done_scr.at[step], done_send, done_recv, step, (place.grp, place.lines[step])
        )
    weights = [
        pltpu.make_async_copy(projection_ref, projection_scr, weight_sem.at[0]),
        pltpu.make_async_copy(combine_ref, combine_scr, weight_sem.at[1]),
    ]
    for copy in weights:
        copy.start()
    for source in range(seq_count):
        for kind in range(3):
            for group in range(group_count):
                packed_scr[
                    group * local_rows:(group + 1) * local_rows,
                    kind * width + source * local_width:kind * width + (source + 1) * local_width,
                ] = back_ref[source, group, kind]

    def turn(index, carry):
        lanes = pl.ds(pl.multiple_of(index * 128, 128), 128)
        packed_scr[:, lanes] = turn_lanes(
            packed_scr[:, lanes].astype(jnp.float32), cos_ref[...], -sin_ref[...]
        ).astype(jnp.bfloat16)
        return carry

    lax.fori_loop(0, 2 * width // 128, turn, 0)
    normed_t_scr[...] = normed_ref[...].astype(jnp.float32).T.astype(jnp.bfloat16)
    segments = [
        piece_segments([part.shape[1:]], side, part.shape[2] // side)[0][0] for part in parts
    ]
    done_segments, _ = piece_segments(
        [out.shape for out in outs[2:]], side, min(out.shape[1] for out in outs[2:]) // side
    )
    plane_sum = PlaneSum(place, parts, pieces, segments, buffers, semaphores, True)
    spread = PlaneSpread(place, outs, *spread_sems)

    def share(index, left, right, tile):
        rows = parts[index].shape[1]

        def fill(owner):
            at = pl.ds(pl.multiple_of(owner * rows, rows), rows)

            def one(turn, carry):
                lanes = pl.ds(pl.multiple_of(turn * tile, tile), tile)
                parts[index][owner, :, lanes] = dot_nn(left[at, :], right[:, lanes]).astype(jnp.bfloat16)
                return carry

            lax.fori_loop(0, parts[index].shape[2] // tile, one, 0)

        for step, target in enumerate(plane_sum.order):
            fill(target * 2 + 1 - place.core)
            plane_sum.swap(index, step)
        for target in plane_sum.order:
            fill(target * 2 + place.core)

    share(0, normed_t_scr, packed_scr, 512)
    weights[0].wait()

    def grad_tile(index, carry):
        at = pl.ds(pl.multiple_of(index * 256, 256), 256)
        grad_scr[:, at] = dot_nt(packed_scr[...], projection_scr[at, :])
        return carry

    lax.fori_loop(0, width // 256, grad_tile, 0)
    for hook in plane_sum.steps(plane_sum.first, 0):
        hook()
    block, utter_rows = utter_scr.shape[1], 2 * group_count
    utter_scr[...] = jnp.zeros_like(utter_scr)

    def put(part, utter, value):
        row = part * utter_rows + utter
        utter_scr[row // block, row % block:row % block + 1, :] = value

    for part in range(4):
        for utter in range(utter_rows):
            put(part + 2, utter, late_ref[part * utter_rows + utter:part * utter_rows + utter + 1, :])
    chunk = 32
    for group in range(group_count):

        def norm_back(index, sums):
            first = pl.multiple_of(index * chunk, chunk)
            at = pl.ds(pl.multiple_of(group * local_rows + first, chunk), chunk)
            second = second_mask(bound_ref, group, me, local_rows, first, chunk)
            row = group * 2 * 6
            scale_part = jnp.where(second, mods_ref[row + 7:row + 8, :], mods_ref[row + 1:row + 2, :])
            grad = grad_scr[at, :]
            normal, scale = centered(hidden_ref[at, :])
            inner = grad * (1.0 + scale_part)
            turned = scale * (
                inner
                - jnp.mean(inner, axis=-1, keepdims=True)
                - normal * jnp.mean(inner * normal, axis=-1, keepdims=True)
            )
            low_scr[at, :] = (middle_ref[at, :] + turned).astype(jnp.bfloat16)
            scaled = grad * normal
            later = second.astype(jnp.float32)
            shift_later, scale_later = grad * later, scaled * later
            return (
                sums[0] + fold_rows(grad - shift_later, jnp.sum),
                sums[1] + fold_rows(shift_later, jnp.sum),
                sums[2] + fold_rows(scaled - scale_later, jnp.sum),
                sums[3] + fold_rows(scale_later, jnp.sum),
            )

        zero = jnp.zeros((8, width), jnp.float32)
        sums = lax.fori_loop(0, local_rows // chunk, norm_back, (zero, zero, zero, zero))
        for spot, value in enumerate(sums):
            put(spot // 2, group * 2 + spot % 2, jnp.sum(value, axis=0, keepdims=True))
    small = SmallSum(place, utter_scr, total_ref, *small_refs)
    small.begin()
    joined_t_scr[:width, :] = frames_ref[...].astype(jnp.float32).T.astype(jnp.bfloat16)
    joined_t_scr[width:, :] = shortcut_ref[...].astype(jnp.float32).T.astype(jnp.bfloat16)
    share(1, joined_t_scr, low_scr, 512)
    for hook in plane_sum.steps(plane_sum.second, 0)[:layers // 2]:
        hook()
    weights[1].wait()

    def joined_tile(index, carry):
        at = pl.ds(pl.multiple_of(index * 256, 256), 256)
        late = pl.ds(pl.multiple_of(width + index * 256, 256), 256)
        frames_scr[:, at] = dot_nt(low_scr[...], combine_scr[at, :])
        shortcut_scr[:, at] = dot_nt(low_scr[...], combine_scr[late, :])
        return carry

    lax.fori_loop(0, width // 256, joined_tile, 0)
    grads = [
        pltpu.make_async_copy(frames_scr, frames_out, out_sem.at[0]),
        pltpu.make_async_copy(shortcut_scr, shortcut_out, out_sem.at[1]),
    ]
    for copy in grads:
        copy.start()
    for hook in plane_sum.steps(plane_sum.first, 1):
        hook()
    for hook in plane_sum.steps(plane_sum.second, 0)[layers // 2:]:
        hook()
    small.middle()

    def along_line(index, step):
        plane_sum.third(index, step)
        if step < layers - 1:
            arrived[index, step] = place.push(
                pieces[index][step], lines[index].at[step], line_send, line_recv, (index, step),
                (place.grp, place.lines[step]),
            )

    def last(index):
        for step in range(layers - 1):
            arrived[index, step].wait_recv()
        spread.total(
            index, pieces[index][layers - 1], [lines[index].at[step] for step in range(layers - 1)], segments[index]
        )

    for step in range(layers):
        plane_sum.second(1, step)
        along_line(0, step)
    small.finish()
    utters_ref[place.grp] = total_ref[...]
    tokens = [
        place.push(total_ref, utters_ref.at[place.grp], token_send, token_recv, step, (other, me))
        for step, other in enumerate(place.groups)
    ]
    condition_scr[...] = jnp.zeros_like(condition_scr)
    shard_rows = modulation_ref.shape[0]
    for spot in range(6 * utter_rows // block):
        part, row = spot * block // utter_rows, spot * block % utter_rows
        condition_scr[row:row + block, :shard_rows] += dot_nt(
            total_ref[spot].astype(jnp.bfloat16), modulation_ref[:, part * width:(part + 1) * width]
        )
    conditions_ref[me] = condition_scr[...]
    tokens += [
        place.push(condition_scr, conditions_ref.at[me], last_send, last_recv, step, (place.grp, other))
        for step, other in enumerate(place.others)
    ]
    for step in range(layers):
        along_line(1, step)
    for step in range(layers - 1):
        arrived[step].wait_recv()
    for index in range(2, 5):
        spread.total(
            index, finished[layers - 1], [done_scr.at[step] for step in range(layers - 1)], done_segments[index - 2]
        )
    last(0)
    for index in range(2, 5):
        spread.second(index)
    last(1)
    spread.second(0)
    spread.second(1)
    place.sent()
    for copy in tokens:
        copy.wait_recv()
    for copy in grads:
        copy.wait()
    for index in range(5):
        spread.finish(index)


def finish_backward(bounds, back, cos, sin, normed, hidden, middle_grad, frames, shortcut, combine, projection, mods, late, modulation, finished, done_shapes):
    grp_count = lax.axis_size("grp")
    seq_count = lax.axis_size("seq")
    side = math.isqrt(grp_count)
    layers = seq_count // 2
    hops = max(side - 1, 1)
    anywhere = pl.BlockSpec(memory_space=pl.ANY)
    vmem = pl.BlockSpec(memory_space=pltpu.VMEM)
    dma = pltpu.SemaphoreType.DMA
    row_count, width = normed.shape
    low, full = jnp.bfloat16, jnp.float32
    parts = [
        jax.ShapeDtypeStruct((seq_count, weight.shape[0] // seq_count, weight.shape[1]), low)
        for weight in (projection, combine)
    ]
    out_shapes = [part.shape[1:] for part in parts] + list(done_shapes)
    small = jax.ShapeDtypeStruct((seq_count, 32 // seq_count, width), full)
    return pl.pallas_call(
        functools.partial(back_kernel, (side, side), seq_count),
        out_shape=(
            jax.ShapeDtypeStruct((row_count, width), full),
            jax.ShapeDtypeStruct((row_count, width), full),
        ) + tuple(jax.ShapeDtypeStruct(shape, low) for shape in out_shapes) + (
            jax.ShapeDtypeStruct((grp_count,) + small.shape, full),
            jax.ShapeDtypeStruct((seq_count, 8, 128), full),
        ),
        in_specs=[pl.BlockSpec(memory_space=pltpu.SMEM)] + [vmem] * 8 + [anywhere] * 2 + [vmem] * (3 + layers),
        out_specs=(anywhere,) * 2 + (vmem,) * 7,
        scratch_shapes=[
            pltpu.VMEM((row_count, 3 * width), low),
            pltpu.VMEM(combine.shape, low),
            pltpu.VMEM(projection.shape, low),
            pltpu.VMEM((width, row_count), low),
            pltpu.VMEM((2 * width, row_count), low),
            pltpu.VMEM((row_count, width), full),
            pltpu.VMEM((row_count, width), low),
            pltpu.VMEM((row_count, width), full),
            pltpu.VMEM((row_count, width), full),
            pltpu.VMEM(small.shape, full),
            pltpu.VMEM(small.shape, full),
            pltpu.VMEM((8, 128), full),
        ] + [pltpu.VMEM(part.shape, low) for part in parts] + [
            pltpu.VMEM((layers - 1,) + finished[0].shape, low)
        ] + [
            pltpu.VMEM((layers - 1, part.shape[1] // side, part.shape[2] // side), low) for part in parts
        ] + [
            pltpu.VMEM((part.shape[1] // side, part.shape[2] // side), low)
            for part in parts for _ in range(layers)
        ] + plane_sum_scratch(parts, side, True) + small_scratch(small) + [
            dma((5, 2, hops)), dma((5, 2, hops)),
            dma((5, 2, hops, side)), dma((5, 2, hops, side)),
            dma((2,)), dma((2,)),
            dma((grp_count - 1,)), dma((grp_count - 1,)),
            dma((seq_count - 1,)), dma((seq_count - 1,)),
            dma((2, layers - 1)), dma((2, layers - 1)),
            dma((layers - 1,)), dma((layers - 1,)),
        ],
        compiler_params=pltpu.CompilerParams(
            collective_id=4, has_side_effects=True, vmem_limit_bytes=60 * 1024 * 1024
        ),
        name="finish_backward",
    )(bounds, back, cos, sin, normed, hidden, middle_grad, frames, shortcut, combine, projection, mods, late, modulation, *finished)


def shards(
    frames,
    shortcut,
    time_embed,
    lengths,
    kept_mask,
    target,
    combine,
    modulation,
    projection,
    readout,
    expand,
    contract,
):
    group_count = frames.shape[0]
    local_rows = frames.shape[1]
    width = HEADS * HEAD_DIM
    row_count = group_count * local_rows
    seq_count = lax.axis_size("seq")
    group_frames = local_rows * seq_count
    all_frames = group_frames * lax.axis_size("grp") * group_count
    utter_count = time_embed.shape[1]
    kept_float = kept_mask.astype(jnp.float32).reshape(row_count)
    local_index = lax.axis_index("seq") * local_rows + jnp.arange(local_rows, dtype=jnp.int32)

    def local_info(length_row):
        return segment_info(length_row, local_index)

    member_info = jax.vmap(local_info)(lengths)
    member_float = member_info[1].astype(jnp.float32)
    position = member_info[2]
    cos_table, sin_table = rotary_tables(position.reshape(row_count))
    cos_lanes = jnp.tile(cos_table[:, 0], (1, 4))
    sin_lanes = jnp.tile(jnp.concatenate([-sin_table[:, 0], sin_table[:, 0]], axis=1), (1, 2))
    silu_value, silu_pull = jax.vjp(jax.nn.silu, time_embed)
    condition = silu_value.astype(jnp.bfloat16)
    shard_rows = modulation.shape[0]
    utter_rows = group_count * utter_count
    condition_part = lax.dynamic_slice_in_dim(
        condition, lax.axis_index("seq") * shard_rows, shard_rows, 2
    ).reshape(utter_rows, shard_rows)
    partial = small_rows(
        seq_count, product(condition_part, modulation).reshape(6 * utter_rows, width)
    )
    partial = partial.at[seq_count - 1, 32 // seq_count - 1, 0].set(jnp.sum(kept_float))
    token = jnp.zeros((8, 128), jnp.float32)
    token = token.at[:utter_rows, :shard_rows].set(condition_part.astype(jnp.float32))
    late_shards = (readout, expand, contract)
    bounds = lengths[:, 0]
    combine_full, projection_full, *rest = front(
        bounds,
        frames.reshape(row_count, width),
        shortcut.reshape(row_count, width),
        cos_lanes,
        sin_lanes,
        partial,
        token,
        combine,
        projection,
        late_shards,
    )
    late_pieces, hidden, normed, qkv, partial_total, tokens = rest
    combine_full = combine_full.reshape(2 * width, width)
    projection_full = projection_full.reshape(width, 3 * width)
    kept_total = jnp.sum(tokens[:, 4, 0])
    condition_all = tokens[:, :utter_rows, :shard_rows].reshape(-1, shard_rows).astype(jnp.bfloat16)
    split_shape = (group_count, local_rows, width)
    mods = partial_total.reshape(32, width)
    kept_heads, mixture_blocks, log_total, *late_full = attend_forward(
        bounds, qkv, late_shards, late_pieces
    )
    readout_full = late_full[0].reshape(width, width)
    expand_full = late_full[1].reshape(width, -1)
    contract_full = late_full[2].reshape(-1, width)
    result, middle_grad, mixture_grad, late_rows, contract_part, expand_part, readout_part = middle(
        bounds,
        mixture_blocks,
        hidden,
        target.reshape(row_count, width),
        kept_float[:, None],
        mods[:6 * utter_rows],
        (all_frames / kept_total).reshape(1),
        late_full[0].reshape(width, width),
        late_full[1].reshape(width, -1),
        late_full[2].reshape(-1, width),
    )
    back_blocks, *plane_pieces = attend_backward(
        bounds,
        kept_heads,
        mixture_grad,
        log_total,
        (contract_part, expand_part, readout_part),
    )
    frames_grad, shortcut_grad, *shares, utters, condition_back = finish_backward(
        bounds,
        back_blocks,
        cos_lanes,
        sin_lanes,
        normed,
        hidden,
        middle_grad,
        frames.reshape(row_count, width),
        shortcut.reshape(row_count, width),
        combine_full,
        projection_full,
        mods,
        late_rows,
        modulation,
        plane_pieces,
        [contract.shape, expand.shape, readout.shape],
    )
    frames_grad = frames_grad.reshape(split_shape)
    shortcut_grad = shortcut_grad.reshape(split_shape)
    projection_grad, combine_grad, contract_grad, expand_grad, readout_grad = [
        share.astype(jnp.float32) for share in shares
    ]
    utter_all = jnp.transpose(
        utters.reshape(-1, 32, width)[:, :6 * utter_rows].reshape(-1, 6, utter_rows, width), (0, 2, 1, 3)
    ).reshape(-1, 6 * width).astype(jnp.bfloat16)
    modulation_grad = product_left(condition_all, utter_all)
    condition_grad = jnp.transpose(
        condition_back[:, :utter_rows, :shard_rows], (1, 0, 2)
    ).reshape(group_count, utter_count, width)
    time_grad = silu_pull(condition_grad)[0]
    summed = (combine_grad, modulation_grad, projection_grad, readout_grad, expand_grad, contract_grad)
    return (
        result.reshape(split_shape),
        frames_grad,
        shortcut_grad,
        time_grad,
        summed[0],
        summed[1],
        summed[2],
        summed[3],
        summed[4],
        summed[5],
    )


def solution(mesh):
    return jax.shard_map(
        shards,
        mesh=mesh,
        in_specs=(
            P("grp", "seq", None),
            P("grp", "seq", None),
            P("grp", None, None),
            P("grp", None),
            P("grp", "seq"),
            P("grp", "seq", None),
            P("seq", None),
            P("seq", None),
            P("seq", None),
            P("seq", None),
            P("seq", None),
            P("seq", None),
        ),
        out_specs=(
            P("grp", "seq", None),
            P("grp", "seq", None),
            P("grp", "seq", None),
            P("grp", None, None),
            P("seq", None),
            P("seq", None),
            P("seq", None),
            P("seq", None),
            P("seq", None),
            P("seq", None),
        ),
        check_vma=False,
    )
```

```python
import functools
import math

import jax
import jax.numpy as jnp
from jax import lax
from jax.experimental import pallas as pl
from jax.experimental.pallas import tpu as pltpu
from jax.sharding import PartitionSpec as P

HEADS = 16
HEAD_DIM = 64


precise = lax.Precision.HIGHEST
epsilon = 1e-06
rope_base = 10000.0


def product(first_op, second_op):
    return jnp.dot(first_op, second_op, preferred_element_type=jnp.float32)


def product_left(first_op, second_op):
    return lax.dot_general(
        first_op, second_op, (((0,), (0,)), ((), ())), preferred_element_type=jnp.float32
    )


def product_right(first_op, second_op):
    return lax.dot_general(
        first_op, second_op, (((1,), (1,)), ((), ())), preferred_element_type=jnp.float32
    )


def gelu_tanh(values):
    return jax.nn.gelu(values, approximate=True)


def modulate(hidden, shift_part, scale_part):
    center = hidden - jnp.mean(hidden, axis=-1, keepdims=True)
    variance = jnp.mean(center * center, axis=-1, keepdims=True)
    return center * lax.rsqrt(variance + epsilon) * (1.0 + scale_part) + shift_part


def segment_info(lengths, frame_index):
    utter_count = lengths.shape[0]
    utter_ends = jnp.cumsum(lengths)
    starts = utter_ends - lengths
    segment = jnp.sum((frame_index[:, None] >= utter_ends[None, :]).astype(jnp.int32), axis=1)
    member = segment[:, None] == jnp.arange(utter_count, dtype=jnp.int32)[None, :]
    offset = jnp.sum(jnp.where(member, starts[None, :], 0), axis=1)
    return (segment, member, frame_index - offset)


def rotary_tables(position):
    half_dim = HEAD_DIM // 2
    ladder = jnp.arange(half_dim, dtype=jnp.float32) / half_dim
    inverse = jnp.exp(-jnp.log(rope_base) * ladder)
    angles = position.astype(jnp.float32)[:, None] * inverse[None, :]
    return (jnp.cos(angles)[:, None, :], jnp.sin(angles)[:, None, :])


def rotate(vectors, cos_table, sin_table):
    half_dim = vectors.shape[-1] // 2
    front_half = vectors[..., :half_dim]
    back_half = vectors[..., half_dim:]
    return jnp.concatenate(
        [
            front_half * cos_table - back_half * sin_table,
            back_half * cos_table + front_half * sin_table,
        ],
        axis=-1,
    )


MESH = pl.DeviceIdType.MESH
NEG = -1e30


def utter_features(boundary, total_rows, for_keys):
    row = lax.broadcasted_iota(jnp.int32, (total_rows, 128), 0)
    lane = lax.broadcasted_iota(jnp.int32, (total_rows, 128), 1)
    second = (row >= boundary).astype(jnp.float32)
    ahead = (lane == 0).astype(jnp.float32)
    after = (lane == 1).astype(jnp.float32)
    if for_keys:
        return (NEG * (second * ahead + (1.0 - second) * after)).astype(jnp.bfloat16)
    return (second * after + (1.0 - second) * ahead).astype(jnp.bfloat16)


def head_lanes(values, head):
    lane = lax.broadcasted_iota(jnp.int32, values.shape, 1)
    own = (lane >= head * HEAD_DIM) & (lane < (head + 1) * HEAD_DIM)
    return jnp.where(own, values.astype(jnp.float32), 0.0).astype(jnp.bfloat16)


def dot_nn(first_op, second_op):
    return jnp.dot(first_op, second_op, preferred_element_type=jnp.float32)


def dot_nt(first_op, second_op):
    return lax.dot_general(
        first_op, second_op, (((1,), (1,)), ((), ())), preferred_element_type=jnp.float32
    )


def fold_rows(values, combine):
    return combine(values.reshape(values.shape[0] // 8, 8, values.shape[1]), axis=0)


def enter(partners):
    barrier = pltpu.get_barrier_semaphore()
    for partner in partners:
        pl.semaphore_signal(barrier, inc=1, device_id=partner, device_id_type=MESH)
    pl.semaphore_wait(barrier, len(partners))


def key_span(third, total_rows):
    size = total_rows // 3
    return (max(third - 1, 0) * size, min(third + 2, 3) * size)


class Place:
    def __init__(self, plane, seq_count):
        self.rows_y, self.cols_x = rows_y, cols_x = plane
        self.grp, self.me = grp, me = lax.axis_index("grp"), lax.axis_index("seq")
        self.gy, self.gx = gy, gx = grp // cols_x, lax.rem(grp, cols_x)
        self.layers = layers = seq_count // 2
        self.layer, self.core = layer, core = me // 2, lax.rem(me, 2)
        self.xs = [lax.rem(gx + step, cols_x) for step in range(1, cols_x)]
        self.ys = [lax.rem(gy + step, rows_y) for step in range(1, rows_y)]
        self.beside = [gy * cols_x + x for x in self.xs]
        self.along = [y * cols_x + gx for y in self.ys]
        self.beside_from = [lax.rem(gx + cols_x - step, cols_x) for step in range(1, cols_x)]
        self.far = [lax.rem(layer + step, layers) for step in range(1, layers)]
        self.line_from = [lax.rem(layer + layers - step, layers) * 2 + core for step in range(1, layers)]
        self.lines = [target * 2 + core for target in self.far]
        self.partner = layer * 2 + 1 - core
        self.others = [lax.rem(me + step, seq_count) for step in range(1, seq_count)]
        self.groups = [lax.rem(grp + step, rows_y * cols_x) for step in range(1, rows_y * cols_x)]
        self.started = []

    def push(self, src, dst, sends, recvs, slot, device):
        copy = pltpu.make_async_remote_copy(
            src, dst, sends.at[slot], recvs.at[slot], device_id=device, device_id_type=MESH
        )
        copy.start()
        self.started.append(copy)
        return copy

    def sent(self):
        for copy in self.started:
            copy.wait_send()
        self.started = []


def window(ref, row, rows, col, cols):
    return ref.at[pl.ds(pl.multiple_of(row, 16), rows), pl.ds(pl.multiple_of(col, 128), cols)]


def piece_segments(shapes, side, width):
    base, found = 0, []
    for rows, cols in shapes:
        height, many = rows // side, cols // side // width
        if many == 1:
            half = width // 2
            found.append([[(base, 0, height, half, 0)], [(base, half, height, half, half)]])
        else:
            blocks = [(base + spot * height, 0, height, width, spot * width) for spot in range(many)]
            found.append([blocks[:many // 2], blocks[many // 2:]])
        base += height * many
    return found, base


class PlaneGather:
    def __init__(self, place, shards, pieces, segments, fulls, own_sem, first_send, first_recv, second_send, second_recv, core_send, core_recv):
        self.place, self.shards, self.pieces, self.fulls = place, shards, pieces, fulls
        self.segments = segments
        self.own_sem = own_sem
        self.first = (first_send, first_recv)
        self.second = (second_send, second_recv)
        self.core = (core_send, core_recv)
        self.jobs = [(index, step) for step in range(place.layers - 1) for index in range(len(shards))]
        self.waiting, self.local, self.own = {}, {}, []

    def sizes(self, index):
        _, rows, cols = self.fulls[index].shape
        return rows, rows // self.place.rows_y, cols // (2 * self.place.cols_x)

    def owner(self, step):
        return self.place.line_from[step]

    def begin(self):
        place = self.place
        for index, step in self.jobs:
            self.spread_first(index, step)
        for index, shard in enumerate(self.shards):
            copy = pltpu.make_async_copy(shard, self.fulls[index].at[place.me], self.own_sem.at[index, place.layers - 1, 0, 0])
            copy.start()
            push = place.push(shard, self.fulls[index].at[place.me], *self.core, (index, 0), (place.grp, place.partner))
            self.own.append((copy, push))

    def spread_first(self, index, step):
        place = self.place
        rows, height, width = self.sizes(index)
        full = self.fulls[index].at[self.owner(step)]
        piece = self.pieces.at[step]
        first_row, first_col = place.gy * height, 2 * place.gx * width
        self.local[index, step] = []
        self.waiting[index, step] = []
        for half, partners in enumerate((place.beside, place.along)):
            for spot, (row, col, rows, cols, off) in enumerate(self.segments[index][half]):
                source = piece.at[pl.ds(row, rows), pl.ds(col, cols)]
                part = window(full, first_row, rows, first_col + off, cols)
                copy = pltpu.make_async_copy(source, part, self.own_sem.at[index, step, half, spot])
                copy.start()
                self.local[index, step].append(copy)
                for hop, other in enumerate(partners):
                    self.waiting[index, step].append(place.push(
                        source, part, *self.first, (index, step, half, hop, spot), (other, place.me)
                    ))

    def spread_second(self, index, step):
        place = self.place
        rows, height, width = self.sizes(index)
        for copy in self.local.get((index, step), []):
            copy.wait()
        for copy in self.waiting[index, step]:
            copy.wait_recv()
        full = self.fulls[index].at[self.owner(step)]
        copies = []
        for hop, other in enumerate(place.along):
            for spot, column in enumerate([place.gx] + place.beside_from):
                part = window(full, place.gy * height, height, 2 * column * width, width)
                copies.append(place.push(part, part, *self.second, (index, step, 0, hop, spot), (other, place.me)))
        for hop, other in enumerate(place.beside):
            part = window(full, 0, rows, (2 * place.gx + 1) * width, width)
            copies.append(place.push(part, part, *self.second, (index, step, 1, hop, 0), (other, place.me)))
        self.waiting[index, step] = copies

    def over_core(self, index, step):
        place = self.place
        for copy in self.waiting[index, step]:
            copy.wait_recv()
        full = self.fulls[index].at[self.owner(step)]
        self.waiting[index, step] = [
            place.push(full, full, *self.core, (index, step + 1), (place.grp, place.partner))
        ]

    def middle(self):
        for job in self.jobs:
            self.spread_second(*job)

    def late(self):
        return [functools.partial(self.over_core, *job) for job in self.jobs]

    def arrive(self, index):
        for job in self.jobs:
            if job[0] == index:
                for copy in self.waiting[job]:
                    copy.wait_recv()
        copy, push = self.own[index]
        copy.wait()
        push.wait_recv()

    def finish(self):
        self.place.sent()


def add_rows(target, source, first_row, rows, first_col, cols, out=None):
    step = next(size for size in (64, 32, 16) if rows % size == 0)
    col = pl.multiple_of(first_col, 128)

    def one(index, carry):
        at = pl.ds(pl.multiple_of(first_row + index * step, 16), step)
        off = pl.ds(pl.multiple_of(index * step, step), step)
        value = target[at, pl.ds(col, cols)] + source[off, :]
        if out is None:
            target[at, pl.ds(col, cols)] = value
        else:
            out[off, :] = value
        return carry

    lax.fori_loop(0, rows // step, one, 0)


def add_segments(target, source, first_row, first_col, segments, out):
    for row, col, rows, cols, off in segments:
        begin = off - segments[0][4]
        add_rows(
            target, source.at[:, pl.ds(begin, cols)], first_row, rows, first_col + off, cols,
            out.at[pl.ds(row, rows), pl.ds(col, cols)],
        )


def plane_sum_scratch(parts, side, in_place=False):
    layers = parts[0].shape[0] // 2
    hops = max(side - 1, 1)
    count = len(parts)
    dma = pltpu.SemaphoreType.DMA

    def buffers(lead, row_cut, col_cut):
        return [
            pltpu.VMEM(lead + (part.shape[1] // row_cut, part.shape[2] // col_cut), jnp.bfloat16)
            for part in parts
        ]

    return (
        ([] if in_place else buffers((layers,), 1, 1))
        + buffers((layers,), 1, 1)
        + buffers((layers, hops, side), side, 2 * side)
        + buffers((layers, hops), side, 2 * side)
        + buffers((layers, hops), 1, 2 * side)
        + buffers((layers, hops), side, 2 * side)
        + [
            dma((count, layers)), dma((count, layers)), dma((count, layers)),
            dma((count, layers, 2, hops, side)), dma((count, layers, 2, hops, side)),
            dma((count, layers, 2, hops)), dma((count, layers, 2, hops)),
        ]
    )


def by_owner(parts, seq_count):
    return [part.reshape(seq_count, part.shape[0] // seq_count, part.shape[1]) for part in parts]


class PlaneSum:
    def __init__(self, place, parts, pieces, segments, buffers, semaphores, in_place=False):
        self.place, self.parts, self.pieces, self.segments = place, parts, pieces, segments
        count = len(parts)
        buffers = (() if in_place else buffers[:count], *[
            buffers[index * count:(index + 1) * count] for index in range(0 if in_place else 1, 5 if in_place else 6)
        ])
        self.in_place = in_place
        self.sums, self.swapped, self.y_first, self.x_second, self.x_first, self.y_second = buffers
        self.load_sem = semaphores[0]
        self.core, self.first_sem, self.second_sem = semaphores[1:3], semaphores[3:5], semaphores[5:7]
        self.order = place.far + [place.layer]
        self.jobs = [(index, step) for index in range(count) for step in range(place.layers)]
        self.loads, self.swaps, self.waiting = {}, {}, {}

    def sizes(self, index):
        _, rows, cols = self.parts[index].shape
        return rows, cols, rows // self.place.rows_y, cols // (2 * self.place.cols_x)

    def begin(self):
        place = self.place
        for index, step in self.jobs:
            target = self.order[step]
            copy = pltpu.make_async_copy(
                self.parts[index].at[target * 2 + place.core], self.sums[index].at[step], self.load_sem.at[index, step]
            )
            copy.start()
            self.loads[index, step] = copy
            self.swap(index, step)

    def swap(self, index, step):
        place = self.place
        self.swaps[index, step] = place.push(
            self.parts[index].at[self.order[step] * 2 + 1 - place.core], self.swapped[index].at[step],
            *self.core, (index, step), (place.grp, place.partner),
        )

    def running(self, index, step):
        if self.in_place:
            return self.parts[index].at[self.order[step] * 2 + self.place.core]
        return self.sums[index].at[step]

    def first(self, index, step):
        place = self.place
        rows, cols, height, width = self.sizes(index)
        if not self.in_place:
            self.loads[index, step].wait()
        self.swaps[index, step].wait_recv()
        total = self.running(index, step)
        add_rows(total, self.swapped[index].at[step], 0, rows, 0, cols)
        copies = []
        for hop, other in enumerate(place.along):
            for column in range(place.cols_x):
                copies.append(place.push(
                    window(total, place.ys[hop] * height, height, 2 * column * width, width),
                    self.y_first[index].at[step, hop, column],
                    *self.first_sem, (index, step, 0, hop, column), (other, place.me),
                ))
        for hop, other in enumerate(place.beside):
            copies.append(place.push(
                window(total, 0, rows, (2 * place.xs[hop] + 1) * width, width),
                self.x_first[index].at[step, hop],
                *self.first_sem, (index, step, 1, hop, 0), (other, place.me),
            ))
        self.waiting[index, step] = copies

    def second(self, index, step):
        place = self.place
        rows, cols, height, width = self.sizes(index)
        for copy in self.waiting[index, step]:
            copy.wait_recv()
        total = self.running(index, step)
        for hop in range(place.rows_y - 1):
            for column in range(place.cols_x):
                add_rows(
                    total, self.y_first[index].at[step, hop, column],
                    place.gy * height, height, 2 * column * width, width,
                )
        for hop in range(place.cols_x - 1):
            add_rows(total, self.x_first[index].at[step, hop], 0, rows, (2 * place.gx + 1) * width, width)
        copies = []
        for hop, other in enumerate(place.beside):
            copies.append(place.push(
                window(total, place.gy * height, height, 2 * place.xs[hop] * width, width),
                self.x_second[index].at[step, hop],
                *self.second_sem, (index, step, 0, hop), (other, place.me),
            ))
        for hop, other in enumerate(place.along):
            copies.append(place.push(
                window(total, place.ys[hop] * height, height, (2 * place.gx + 1) * width, width),
                self.y_second[index].at[step, hop],
                *self.second_sem, (index, step, 1, hop), (other, place.me),
            ))
        self.waiting[index, step] = copies

    def third(self, index, step):
        place = self.place
        rows, cols, height, width = self.sizes(index)
        for copy in self.waiting[index, step]:
            copy.wait_recv()
        self.waiting[index, step] = []
        total = self.running(index, step)
        out = self.pieces[index][step]
        row, col = place.gy * height, 2 * place.gx * width
        for hop in range(place.cols_x - 1):
            source = self.x_second[index].at[step, hop]
            if hop == place.cols_x - 2:
                add_segments(total, source, row, col, self.segments[index][0], out)
            else:
                add_rows(total, source, row, height, col, width)
        for hop in range(place.rows_y - 1):
            source = self.y_second[index].at[step, hop]
            if hop == place.rows_y - 2:
                add_segments(total, source, row, col, self.segments[index][1], out)
            else:
                add_rows(total, source, row, height, col + width, width)

    def steps(self, stage, only=None):
        return [functools.partial(stage, *job) for job in self.jobs if only is None or job[0] == only]

    def finish(self):
        self.place.sent()


class LineSum:
    def __init__(self, place, pieces, sums, sends, recvs):
        self.place, self.pieces, self.sums = place, pieces, sums
        self.sends, self.recvs = sends, recvs
        self.pushed = []

    def mine(self, owner):
        place = self.place
        return self.pieces.at[lax.rem(place.layers + owner - place.layer - 1, place.layers)]

    def slot(self, way, owner, layer):
        return owner if way == 0 else jnp.where(layer == owner, self.place.layers, owner)

    def copy(self, way, owner):
        place = self.place
        target = place.layer + (1 if way == 0 else -1)
        return pltpu.make_async_remote_copy(
            self.mine(owner), self.sums.at[self.slot(way, owner, target)],
            self.sends.at[way, owner], self.recvs.at[way, owner],
            device_id=(place.grp, target * 2 + place.core), device_id_type=MESH,
        )

    def push(self, when, way, owner, add):
        self.pushed.append((when, way, owner))

        @pl.when(when)
        def _():
            if add:
                self.arrived(way, owner)
                mine, other = self.mine(owner), self.sums.at[self.slot(way, owner, self.place.layer)]
                rows = mine.shape[0]
                step = next(size for size in (64, 32, 16) if rows % size == 0)

                def one(index, carry):
                    at = pl.ds(pl.multiple_of(index * step, 16), step)
                    mine[at, :] = mine[at, :] + other[at, :]
                    return carry

                lax.fori_loop(0, rows // step, one, 0)
            self.copy(way, owner).start()

    def arrived(self, way, owner):
        place = self.place
        part = self.sums.at[self.slot(way, owner, place.layer)]
        pltpu.make_async_remote_copy(
            part, part, self.sends.at[way, owner], self.recvs.at[way, owner],
            device_id=(place.grp, place.me), device_id_type=MESH,
        ).wait_recv()

    def begin(self):
        place, last = self.place, self.place.layers - 1
        for hop in range(last):
            self.push(place.layer == 0, 0, last - hop, False)
            self.push(place.layer == last, 1, hop, False)

    def round(self, turn):
        place, last = self.place, self.place.layers - 1
        for owner in range(place.layers):
            up = turn + 1 - (last - owner)
            if 1 <= up < owner:
                self.push(place.layer == up, 0, owner, True)
            down = turn + 1 - owner
            if 1 <= down < last - owner:
                self.push(place.layer == last - down, 1, owner, True)

    def rounds(self):
        return [functools.partial(self.round, turn) for turn in range(2 * self.place.layers - 5)]

    def close(self):
        place, last = self.place, self.place.layers - 1
        for owner in range(place.layers):
            for way, ends in ((0, owner == 0), (1, owner == last)):

                @pl.when(place.layer == owner)
                def _(way=way, ends=ends, owner=owner):
                    if ends:
                        spot = owner if way == 0 else place.layers
                        self.sums[spot] = jnp.zeros(self.sums.shape[1:], jnp.bfloat16)
                    else:
                        self.arrived(way, owner)

        return self.pieces.at[last], [self.sums.at[place.layer], self.sums.at[place.layers]]

    def sent(self):
        for when, way, owner in self.pushed:

            @pl.when(when)
            def _(way=way, owner=owner):
                self.copy(way, owner).wait_send()


class PlaneSpread:
    def __init__(self, place, outs, first_send, first_recv, second_send, second_recv):
        self.place, self.outs = place, outs
        self.first_sem, self.second_sem = (first_send, first_recv), (second_send, second_recv)
        self.waiting = {}

    def sizes(self, index):
        rows, cols = self.outs[index].shape
        return rows, rows // self.place.rows_y, cols // (2 * self.place.cols_x)

    def total(self, index, piece, others, segments):
        place = self.place
        rows, height, width = self.sizes(index)
        row = place.gy * height
        col = pl.multiple_of(2 * place.gx * width, 128)
        for first, left, _, cols, off in segments[0] + segments[1]:

            def one(turn, carry):
                at = pl.ds(pl.multiple_of(first + turn * 16, 16), 16)
                value = piece[at, pl.ds(left, cols)].astype(jnp.float32)
                for other in others:
                    value = value + other[at, pl.ds(left, cols)].astype(jnp.float32)
                self.outs[index][
                    pl.ds(pl.multiple_of(row + turn * 16, 16), 16), pl.ds(pl.multiple_of(col + off, 128), cols)
                ] = value.astype(jnp.bfloat16)
                return carry

            lax.fori_loop(0, height // 16, one, 0)
        copies = []
        for hop, other in enumerate(place.beside):
            part = window(self.outs[index], row, height, 2 * place.gx * width, width)
            copies.append(place.push(part, part, *self.first_sem, (index, 0, hop), (other, place.me)))
        for hop, other in enumerate(place.along):
            part = window(self.outs[index], row, height, (2 * place.gx + 1) * width, width)
            copies.append(place.push(part, part, *self.first_sem, (index, 1, hop), (other, place.me)))
        self.waiting[index] = copies

    def second(self, index):
        place = self.place
        rows, height, width = self.sizes(index)
        for copy in self.waiting[index]:
            copy.wait_recv()
        copies = []
        for hop, other in enumerate(place.along):
            for spot, column in enumerate([place.gx] + place.beside_from):
                part = window(self.outs[index], place.gy * height, height, 2 * column * width, width)
                copies.append(place.push(part, part, *self.second_sem, (index, 0, hop, spot), (other, place.me)))
        for hop, other in enumerate(place.beside):
            part = window(self.outs[index], 0, rows, (2 * place.gx + 1) * width, width)
            copies.append(place.push(part, part, *self.second_sem, (index, 1, hop, 0), (other, place.me)))
        self.waiting[index] = copies

    def finish(self, index):
        for copy in self.waiting[index]:
            copy.wait_recv()


class SmallSum:
    def __init__(self, place, source, total, scratch, first_send, first_recv, second_send, second_recv):
        self.place, self.source, self.total_ref, self.scratch = place, source, total, scratch
        self.first_sem, self.second_sem = (first_send, first_recv), (second_send, second_recv)

    def begin(self):
        place = self.place
        self.waiting = [
            place.push(self.source.at[other], self.scratch.at[step], *self.first_sem, step, (place.grp, other))
            for step, other in enumerate(place.others)
        ]

    def middle(self):
        place = self.place
        value = self.source[place.me]
        for step, copy in enumerate(self.waiting):
            copy.wait_recv()
            value = value + self.scratch[step]
        self.total_ref[place.me] = value
        part = self.total_ref.at[place.me]
        self.waiting = [
            place.push(part, part, *self.second_sem, step, (place.grp, other))
            for step, other in enumerate(place.others)
        ]

    def finish(self):
        for copy in self.waiting:
            copy.wait_recv()


def small_scratch(source):
    seq_count = source.shape[0]
    dma = pltpu.SemaphoreType.DMA
    return [pltpu.VMEM((seq_count - 1,) + source.shape[1:], jnp.float32)] + [dma((seq_count - 1,))] * 4


def forward_kernel(plane, seq_count, count, *refs):
    layers = seq_count // 2
    bound_ref, qkv_ref, shards = refs[0], refs[1], refs[2:2 + count]
    refs = refs[2 + count:]
    pieces, refs = refs[0], refs[1:]
    kept_ref, mixture_ref, log_ref, fulls = refs[0], refs[1], refs[2], refs[3:3 + count]
    (
        key_scr, query_scr, value_t_scr, score_scr, mix_t_scr, mix_scr,
        send_sem, recv_sem, back_send_sem, back_recv_sem, local_sem,
    ) = refs[3 + count:14 + count]
    own_sem, first_send, first_recv, second_send, second_recv, core_send, core_recv = refs[14 + count:]
    group_count, local_rows, local_width = qkv_ref.shape[1], qkv_ref.shape[3], qkv_ref.shape[4]
    total_rows = seq_count * local_rows
    heads = local_width // HEAD_DIM
    me = lax.axis_index("seq")
    grp = lax.axis_index("grp")
    others = [lax.rem(me + step, seq_count) for step in range(1, seq_count)]
    origins = [lax.rem(me + seq_count - step, seq_count) for step in range(1, seq_count)]
    block = min(256, total_rows // 3)
    place = Place(plane, seq_count)
    enter([(grp, other) for other in others] + [(other, me) for other in place.beside + place.along])
    copies = []

    def begin_group(group):
        own = pltpu.make_async_copy(qkv_ref.at[me, group], kept_ref.at[me, group], local_sem.at[group])
        own.start()
        row = [own]
        for step, other in enumerate(others):
            copy = pltpu.make_async_remote_copy(
                qkv_ref.at[other, group], kept_ref.at[me, group],
                send_sem.at[group, step], recv_sem.at[group, step],
                device_id=(grp, other), device_id_type=MESH,
            )
            copy.start()
            row.append(copy)
        copies.append(row)

    begin_group(0)
    side = place.cols_x
    segments, _ = piece_segments(
        [shard.shape for shard in shards], side, min(shard.shape[1] for shard in shards) // side
    )
    spread = PlaneGather(
        place, shards, pieces, segments, fulls,
        own_sem, first_send, first_recv, second_send, second_recv, core_send, core_recv,
    )
    spread.begin()
    back = []
    for group in range(group_count):
        for copy in copies[group]:
            copy.wait()
        if group + 1 < group_count:
            begin_group(group + 1)
        if group == 0:
            spread.middle()
            hooks = spread.late()
            held = len(hooks) // 3
        boundary = bound_ref[group]
        keys = kept_ref[:, group, 1].reshape(total_rows, local_width)
        values = kept_ref[:, group, 2].reshape(total_rows, local_width)
        key_scr[:, :local_width] = keys
        key_scr[:, local_width:] = utter_features(boundary, total_rows, True)
        query_scr[:, local_width:] = utter_features(boundary, total_rows, False)
        value_t_scr[...] = values.astype(jnp.float32).T.astype(jnp.bfloat16)

        for head in range(heads):
            queries = kept_ref[:, group, 0].reshape(total_rows, local_width)
            query_scr[:, :local_width] = head_lanes(queries, head) * jnp.bfloat16(HEAD_DIM ** (-0.5))
            for third in range(3):
                first_key, last_key = key_span(third, total_rows)
                chunks = range(first_key, last_key, block)

                def one_block(index, carry):
                    first_row = pl.multiple_of(third * (total_rows // 3) + index * block, block)
                    query_block = query_scr[pl.ds(first_row, block), :]
                    peak = jnp.full((8, block), -jnp.inf, jnp.float32)
                    for first in chunks:
                        scores = dot_nt(key_scr[first:first + block, :], query_block)
                        score_scr[first:first + block, :] = scores
                        peak = jnp.maximum(peak, fold_rows(scores, jnp.max))
                    peak = jnp.max(peak, axis=0, keepdims=True)
                    total = jnp.zeros((8, block), jnp.float32)
                    for first in chunks:
                        lifted = jnp.exp(score_scr[first:first + block, :] - peak)
                        score_scr[first:first + block, :] = lifted
                        total = total + fold_rows(lifted, jnp.sum)
                    total = jnp.sum(total, axis=0, keepdims=True)
                    inverse = 1.0 / total
                    mixed = jnp.zeros((HEAD_DIM, block), jnp.float32)
                    rows = slice(head * HEAD_DIM, (head + 1) * HEAD_DIM)
                    for first in chunks:
                        weight = (score_scr[first:first + block, :] * inverse).astype(jnp.bfloat16)
                        mixed = mixed + dot_nn(value_t_scr[rows, first:first + block], weight)
                    mix_t_scr[rows, pl.ds(first_row, block)] = mixed
                    log_ref[group, head, :, pl.ds(first_row, block)] = peak + jnp.log(total)
                    return carry

                lax.fori_loop(0, total_rows // 3 // block, one_block, 0)
                if group > 0 and len(hooks) > held:
                    hooks.pop(0)()
        mix_scr[group] = mix_t_scr[...].T.astype(jnp.bfloat16).reshape(seq_count, local_rows, local_width)
        own = pltpu.make_async_copy(
            mix_scr.at[group, me], mixture_ref.at[me, group], local_sem.at[group_count + group]
        )
        own.start()
        back.append(own)
        for step, other in enumerate(others):
            copy = pltpu.make_async_remote_copy(
                mix_scr.at[group, other], mixture_ref.at[me, group],
                back_send_sem.at[group, step], back_recv_sem.at[group, step],
                device_id=(grp, other), device_id_type=MESH,
            )
            copy.start()
            back.append(copy)
    for hook in hooks:
        hook()
    for copy in back:
        copy.wait()
    for index in range(count):
        spread.arrive(index)
    spread.finish()


def attend_forward(bounds, qkv, shards, pieces):
    side = math.isqrt(lax.axis_size("grp"))
    hops = max(side - 1, 1)
    count = len(shards)
    dma = pltpu.SemaphoreType.DMA
    anywhere = pl.BlockSpec(memory_space=pl.ANY)
    layers = qkv.shape[0] // 2
    seq_count, group_count, _, local_rows, local_width = qkv.shape
    total_rows = seq_count * local_rows
    heads = local_width // HEAD_DIM
    block = min(256, total_rows // 3)
    vmem = pl.BlockSpec(memory_space=pltpu.VMEM)
    return pl.pallas_call(
        functools.partial(forward_kernel, (side, side), seq_count, count),
        out_shape=(
            jax.ShapeDtypeStruct(qkv.shape, jnp.bfloat16),
            jax.ShapeDtypeStruct((seq_count, group_count, local_rows, local_width), jnp.bfloat16),
            jax.ShapeDtypeStruct((group_count, heads, 1, total_rows), jnp.float32),
        ) + tuple(jax.ShapeDtypeStruct((seq_count,) + part.shape, part.dtype) for part in shards),
        in_specs=[pl.BlockSpec(memory_space=pltpu.SMEM)] + [anywhere] * (2 + count),
        out_specs=(vmem, vmem, vmem) + (anywhere,) * count,
        scratch_shapes=[
            pltpu.VMEM((total_rows, local_width + 128), jnp.bfloat16),
            pltpu.VMEM((total_rows, local_width + 128), jnp.bfloat16),
            pltpu.VMEM((local_width, total_rows), jnp.bfloat16),
            pltpu.VMEM((total_rows, block), jnp.float32),
            pltpu.VMEM((local_width, total_rows), jnp.float32),
            pltpu.VMEM((group_count, seq_count, local_rows, local_width), jnp.bfloat16),
            pltpu.SemaphoreType.DMA((group_count, seq_count - 1)),
            pltpu.SemaphoreType.DMA((group_count, seq_count - 1)),
            pltpu.SemaphoreType.DMA((group_count, seq_count - 1)),
            pltpu.SemaphoreType.DMA((group_count, seq_count - 1)),
            pltpu.SemaphoreType.DMA((2 * group_count,)),
            dma((count, layers, 2, 2)),
            dma((count, layers - 1, 2, hops, 2)), dma((count, layers - 1, 2, hops, 2)),
            dma((count, layers - 1, 2, hops, side)), dma((count, layers - 1, 2, hops, side)),
            dma((count, layers)), dma((count, layers)),
        ],
        compiler_params=pltpu.CompilerParams(
            collective_id=1, has_side_effects=True, vmem_limit_bytes=48 * 1024 * 1024
        ),
        name="attend_forward",
    )(bounds, qkv, *shards, pieces)


def backward_kernel(plane, seq_count, count, *refs):
    layers = seq_count // 2
    bound_ref, kept_ref, grad_ref, log_ref = refs[:4]
    parts, refs = refs[4:4 + count], refs[4 + count:]
    out_ref, refs = refs[0], refs[1:]
    pieces, refs = refs[0], refs[1:]
    (
        taken_scr, key_scr, query_scr, key_t_scr, head_query_scr, head_grad_scr, prob_scr, weight_scr,
        query_t_scr, key_sum_scr, value_sum_scr, back_scr,
        send_sem, recv_sem, back_send_sem, back_recv_sem, local_sem,
    ) = refs[:17]
    buffers, semaphores = refs[17:17 + 6 * count], refs[17 + 6 * count:]
    group_count, local_rows, local_width = grad_ref.shape[1], grad_ref.shape[2], grad_ref.shape[3]
    total_rows = seq_count * local_rows
    heads = local_width // HEAD_DIM
    me = lax.axis_index("seq")
    grp = lax.axis_index("grp")
    others = [lax.rem(me + step, seq_count) for step in range(1, seq_count)]
    block = min(256, total_rows // 3)
    place = Place(plane, seq_count)
    enter([(grp, other) for other in others] + [(other, me) for other in place.beside + place.along])
    copies = []

    def begin_group(group):
        own = pltpu.make_async_copy(grad_ref.at[me, group], taken_scr.at[me, group], local_sem.at[group])
        own.start()
        row = [own]
        for step, other in enumerate(others):
            copy = pltpu.make_async_remote_copy(
                grad_ref.at[other, group], taken_scr.at[me, group],
                send_sem.at[group, step], recv_sem.at[group, step],
                device_id=(grp, other), device_id_type=MESH,
            )
            copy.start()
            row.append(copy)
        copies.append(row)

    begin_group(0)
    side = place.cols_x
    segments, _ = piece_segments(
        [part.shape[1:] for part in parts], side, min(part.shape[2] for part in parts) // side
    )
    plane_sum = PlaneSum(
        place, parts, [[pieces.at[step] for step in range(layers)]] * count, segments, buffers, semaphores
    )
    plane_sum.begin()
    firsts = plane_sum.steps(plane_sum.first)
    seconds = plane_sum.steps(plane_sum.second)
    units = 3 * heads * group_count
    plan = [[] for _ in range(units + 1)]
    for spot, hook in enumerate(firsts):
        plan[spot * (units // 2 - 1) // len(firsts)].append(hook)
    for spot, hook in enumerate(seconds):
        plan[units - 5 + spot * 6 // len(seconds)].append(hook)
    back = []
    for group in range(group_count):
        for copy in copies[group]:
            copy.wait()
        if group + 1 < group_count:
            begin_group(group + 1)
        boundary = bound_ref[group]
        keys = kept_ref[:, group, 1].reshape(total_rows, local_width)
        key_scr[:, :local_width] = keys
        key_scr[:, local_width:] = utter_features(boundary, total_rows, True)
        query_scr[:, local_width:] = utter_features(boundary, total_rows, False)
        key_t_scr[...] = keys.astype(jnp.float32).T.astype(jnp.bfloat16)
        key_sum_scr[...] = jnp.zeros_like(key_sum_scr)
        value_sum_scr[...] = jnp.zeros_like(value_sum_scr)

        for head in range(heads):
            queries = head_lanes(kept_ref[:, group, 0].reshape(total_rows, local_width), head)
            head_query_scr[...] = queries
            query_scr[:, :local_width] = queries * jnp.bfloat16(HEAD_DIM ** (-0.5))
            head_grad_scr[...] = head_lanes(taken_scr[:, group].reshape(total_rows, local_width), head)
            for third in range(3):
                first_key, last_key = key_span(third, total_rows)
                chunks = range(first_key, last_key, block)

                def one_block(index, carry):
                    first_row = pl.multiple_of(third * (total_rows // 3) + index * block, block)
                    own_rows = pl.ds(first_row, block)
                    query_block = query_scr[own_rows, :]
                    grad_block = head_grad_scr[own_rows, :]
                    plain_block = head_query_scr[own_rows, :]
                    log_block = log_ref[group, head, :, own_rows]
                    row_dot = jnp.zeros((8, block), jnp.float32)
                    for first in chunks:
                        scores = dot_nt(key_scr[first:first + block, :], query_block)
                        prob = jnp.exp(scores - log_block)
                        values = kept_ref[
                            first // local_rows:(first + block - 1) // local_rows + 1, group, 2
                        ].reshape(-1, local_width)
                        skip = first % local_rows
                        weight_grad = dot_nt(values[skip:skip + block], grad_block)
                        prob_scr[first:first + block, :] = prob
                        weight_scr[first:first + block, :] = weight_grad
                        row_dot = row_dot + fold_rows(prob * weight_grad, jnp.sum)
                    row_dot = jnp.sum(row_dot, axis=0, keepdims=True)
                    rows = slice(head * HEAD_DIM, (head + 1) * HEAD_DIM)
                    turned = jnp.zeros((HEAD_DIM, block), jnp.float32)
                    for first in chunks:
                        prob = prob_scr[first:first + block, :]
                        score_grad = (
                            HEAD_DIM ** (-0.5) * (prob * (weight_scr[first:first + block, :] - row_dot))
                        ).astype(jnp.bfloat16)
                        key_sum_scr[first:first + block, :] += dot_nn(score_grad, plain_block)
                        value_sum_scr[first:first + block, :] += dot_nn(
                            prob.astype(jnp.bfloat16), grad_block
                        )
                        turned = turned + dot_nn(key_t_scr[rows, first:first + block], score_grad)
                    query_t_scr[rows, own_rows] = turned
                    return carry

                lax.fori_loop(0, total_rows // 3 // block, one_block, 0)
                for hook in plan.pop(0):
                    hook()
        shape = (seq_count, local_rows, local_width)
        back_scr[:, group, 0] = query_t_scr[...].T.astype(jnp.bfloat16).reshape(shape)
        back_scr[:, group, 1] = key_sum_scr[...].astype(jnp.bfloat16).reshape(shape)
        back_scr[:, group, 2] = value_sum_scr[...].astype(jnp.bfloat16).reshape(shape)
        own = pltpu.make_async_copy(
            back_scr.at[me, group], out_ref.at[me, group], local_sem.at[group_count + group]
        )
        own.start()
        back.append(own)
        for step, other in enumerate(others):
            copy = pltpu.make_async_remote_copy(
                back_scr.at[other, group], out_ref.at[me, group],
                back_send_sem.at[group, step], back_recv_sem.at[group, step],
                device_id=(grp, other), device_id_type=MESH,
            )
            copy.start()
            back.append(copy)
    for hook in plan[0] + plane_sum.steps(plane_sum.third):
        hook()
    for copy in back:
        copy.wait()
    plane_sum.finish()


def attend_backward(bounds, kept, grad, log_total, parts):
    side = math.isqrt(lax.axis_size("grp"))
    count = len(parts)
    layers = kept.shape[0] // 2
    anywhere = pl.BlockSpec(memory_space=pl.ANY)
    parts = by_owner(parts, kept.shape[0])
    width = min(part.shape[2] for part in parts) // side
    _, piece_rows = piece_segments([part.shape[1:] for part in parts], side, width)
    seq_count, group_count, _, local_rows, local_width = kept.shape
    total_rows = seq_count * local_rows
    block = min(256, total_rows // 3)
    vmem = pl.BlockSpec(memory_space=pltpu.VMEM)
    return pl.pallas_call(
        functools.partial(backward_kernel, (side, side), seq_count, count),
        out_shape=(jax.ShapeDtypeStruct(kept.shape, jnp.bfloat16),) + tuple(
            jax.ShapeDtypeStruct((layers, piece_rows, width), jnp.bfloat16) for _ in range(1)
        ),
        in_specs=[pl.BlockSpec(memory_space=pltpu.SMEM), vmem, anywhere, vmem] + [anywhere] * count,
        out_specs=(vmem,) * 2,
        scratch_shapes=[
            pltpu.VMEM(grad.shape, jnp.bfloat16),
            pltpu.VMEM((total_rows, local_width + 128), jnp.bfloat16),
            pltpu.VMEM((total_rows, local_width + 128), jnp.bfloat16),
            pltpu.VMEM((local_width, total_rows), jnp.bfloat16),
            pltpu.VMEM((total_rows, local_width), jnp.bfloat16),
            pltpu.VMEM((total_rows, local_width), jnp.bfloat16),
            pltpu.VMEM((total_rows, block), jnp.float32),
            pltpu.VMEM((total_rows, block), jnp.float32),
            pltpu.VMEM((local_width, total_rows), jnp.float32),
            pltpu.VMEM((total_rows, local_width), jnp.float32),
            pltpu.VMEM((total_rows, local_width), jnp.float32),
            pltpu.VMEM(kept.shape, jnp.bfloat16),
            pltpu.SemaphoreType.DMA((group_count, seq_count - 1)),
            pltpu.SemaphoreType.DMA((group_count, seq_count - 1)),
            pltpu.SemaphoreType.DMA((group_count, seq_count - 1)),
            pltpu.SemaphoreType.DMA((group_count, seq_count - 1)),
            pltpu.SemaphoreType.DMA((2 * group_count,)),
        ] + plane_sum_scratch(parts, side),
        compiler_params=pltpu.CompilerParams(
            collective_id=2, has_side_effects=True, vmem_limit_bytes=60 * 1024 * 1024
        ),
        name="attend_backward",
    )(bounds, kept, grad, log_total, *parts)


class LineChain:
    def __init__(self, place, sources, slots, sends, recvs):
        self.place, self.sources, self.slots = place, sources, slots
        self.sends, self.recvs = sends, recvs
        self.pushed = []
        middle = []
        low, high = 0, place.layers - 2
        while low <= high:
            middle += [low] if low == high else [low, high]
            low, high = low + 1, high - 1
        first, last = place.layer == 0, place.layer == place.layers - 1
        self.ranks = [
            jnp.where(first, place.layers - 2 - rank, jnp.where(last, rank, step)).astype(jnp.int32)
            for rank, step in enumerate(middle)
        ]

    def owner(self, step):
        place = self.place
        return lax.rem(place.layer + place.layers - 1 - step, place.layers) * 2 + place.core

    def copy(self, index, source, owner, slot, target, send_slot):
        return pltpu.make_async_remote_copy(
            source, self.slots(index, owner, slot),
            self.sends.at[index, send_slot], self.recvs.at[index, slot],
            device_id=(self.place.grp, target * 2 + self.place.core), device_id_type=MESH,
        )

    def push(self, when, *given):
        self.pushed.append((when, given))

        @pl.when(when)
        def _():
            self.copy(*given).start()

    def begin(self, index):
        place = self.place
        source = self.sources[index]
        self.push(place.layer < place.layers - 1, index, source, place.me, 0, place.layer + 1, 0)
        self.push(place.layer > 0, index, source, place.me, place.layers - 2, place.layer - 1, 1)

    def forward(self, index, rank):
        place = self.place
        step = self.ranks[rank]
        owner = self.owner(step)
        held = self.slots(index, owner, step)
        self.copy(index, held, owner, step, place.layer, 0).wait_recv()
        below = step < place.layer
        going = (below & (place.layer < place.layers - 1)) | ((step >= place.layer) & (place.layer > 0))
        slot = jnp.where(below, step + 1, step - 1)
        target = jnp.where(below, place.layer + 1, place.layer - 1)
        self.push(going, index, held, owner, slot, target, rank + 2)
        return owner

    def sent(self):
        for when, given in self.pushed:

            @pl.when(when)
            def _(given=given):
                self.copy(*given).wait_send()


class WholeGather(PlaneGather):
    def __init__(self, place, shards, fulls, line_send, line_recv, *semaphores):
        super().__init__(place, shards, None, None, fulls, *semaphores)

        def piece(ref, index):
            rows, height, width = self.sizes(index)
            return window(ref, place.gy * height, height, 2 * place.gx * width, 2 * width)

        self.chain = LineChain(
            place, [piece(shard, index) for index, shard in enumerate(shards)],
            lambda index, owner, slot: piece(fulls[index].at[owner], index), line_send, line_recv,
        )
        self.jobs = [(index, rank) for index in range(len(shards)) for rank in range(place.layers - 1)]

    def owner(self, step):
        return self.chain.owner(self.chain.ranks[step])

    def begin(self):
        place = self.place
        for index in range(len(self.shards)):
            self.chain.begin(index)
        for index, shard in enumerate(self.shards):
            copy = pltpu.make_async_copy(shard, self.fulls[index].at[place.me], self.own_sem.at[index, place.layers - 1, 0, 0])
            copy.start()
            push = place.push(shard, self.fulls[index].at[place.me], *self.core, (index, 0), (place.grp, place.partner))
            self.own.append((copy, push))

    def spread_first(self, index, step):
        place = self.place
        rows, height, width = self.sizes(index)
        full = self.fulls[index].at[self.chain.forward(index, step)]
        row, col = place.gy * height, 2 * place.gx * width
        self.waiting[index, step] = []
        for half, partners in enumerate((place.beside, place.along)):
            part = window(full, row, height, col + half * width, width)
            for hop, other in enumerate(partners):
                self.waiting[index, step].append(
                    place.push(part, part, *self.first, (index, step, half, hop, 0), (other, place.me))
                )

    def finish(self):
        super().finish()
        self.chain.sent()


def turn_lanes(values, cos, sin):
    lane = lax.broadcasted_iota(jnp.int32, values.shape, 1)
    ahead = pltpu.roll(values, values.shape[1] - HEAD_DIM // 2, 1)
    behind = pltpu.roll(values, HEAD_DIM // 2, 1)
    other = jnp.where(lax.rem(lane, HEAD_DIM) < HEAD_DIM // 2, ahead, behind)
    return values * cos + other * sin


def second_mask(bound_ref, group, me, local_rows, first, rows):
    row = lax.broadcasted_iota(jnp.int32, (rows, 1), 0) + (me * local_rows + first)
    return row >= bound_ref[group]


def centered(values):
    center = values - jnp.mean(values, axis=-1, keepdims=True)
    scale = lax.rsqrt(jnp.mean(center * center, axis=-1, keepdims=True) + epsilon)
    return center * scale, scale


def front_kernel(plane, seq_count, late_count, *refs):
    layers = seq_count // 2
    bound_ref, frames_ref, shortcut_ref, ladder_ref, kept_ref, token_ref, modulation_ref = refs[:7]
    shards, late_shards, refs = refs[7:9], refs[9:9 + late_count], refs[9 + late_count:]
    fulls_out, late_out, refs = refs[:2], refs[2], refs[3:]
    hidden_ref, normed_ref, qkv_ref, cos_ref, sin_ref, mods_ref, scale_ref, tokens_ref = refs[:8]
    partial_ref, total_ref, refs = refs[8], refs[9], refs[10:]
    fulls, refs = refs[:2], refs[2:]
    token_scr, token_send, token_recv, out_sem = refs[:4]
    small_refs, (late_scr, late_send, late_recv, late_sem), refs = refs[4:9], refs[9:13], refs[13:]
    group_count, local_rows, local_width = qkv_ref.shape[1], qkv_ref.shape[3], qkv_ref.shape[4]
    row_count, width = hidden_ref.shape
    rows_all = plane[0] * plane[1]
    place = Place(plane, seq_count)
    me = place.me
    enter([(place.grp, other) for other in place.others] + [(other, me) for other in place.groups])
    whole = WholeGather(place, shards, fulls, *refs)
    whole.begin()
    block = partial_ref.shape[1]
    partial_ref[...] = jnp.zeros_like(partial_ref)
    shard_rows = modulation_ref.shape[0]
    factor = token_ref[:, :shard_rows].astype(jnp.bfloat16)
    for part in range(6):
        found = dot_nn(factor, modulation_ref[:, part * width:(part + 1) * width])
        for utter in range(2 * group_count):
            spot = utter * 6 + part
            partial_ref[spot // block, spot % block:spot % block + 1, :] = found[utter:utter + 1, :]
    kept = jnp.sum(jnp.sum(kept_ref[...], axis=1, keepdims=True), axis=0, keepdims=True)
    partial_ref[seq_count - 1, block - 1:block, :] = jnp.broadcast_to(kept, (1, width))
    small = SmallSum(place, partial_ref, total_ref, *small_refs)
    small.begin()
    for group in range(group_count):
        rows = slice(group * local_rows, (group + 1) * local_rows)
        frame = lax.broadcasted_iota(jnp.int32, (local_rows, 1), 0) + me * local_rows
        place_in = frame - jnp.where(frame >= bound_ref[group], bound_ref[group], 0)
        angles = place_in.astype(jnp.float32) * ladder_ref[0:1, :]
        cos_ref[rows, :] = jnp.cos(angles)
        sin_ref[rows, :] = jnp.sin(angles) * ladder_ref[1:2, :]
    side = place.cols_x
    cut = late_scr.shape[1]
    late_own, base = [], 0
    for index, shard in enumerate(late_shards):
        height, cols = shard.shape[0] // side, shard.shape[1] // side
        for spot in range(cols // cut):
            late_own.append(pltpu.make_async_copy(
                window(shard, place.gy * height, height, place.gx * cols + spot * cut, cut),
                late_scr.at[pl.ds(base, height), :],
                late_sem.at[len(late_own)],
            ))
            late_own[-1].start()
            base += height
    late_chain = LineChain(place, [late_scr], lambda index, owner, slot: late_out.at[slot], late_send, late_recv)
    combine_jobs = [job for job in whole.jobs if job[0] == 0]
    projection_jobs = [job for job in whole.jobs if job[0] == 1]
    for job in combine_jobs:
        whole.spread_first(*job)
    for job, late in zip(combine_jobs, projection_jobs):
        whole.spread_second(*job)
        whole.spread_first(*late)
    for copy in late_own:
        copy.wait()
    late_chain.begin(0)
    small.middle()
    for job, late in zip(combine_jobs, projection_jobs):
        whole.over_core(*job)
        whole.spread_second(*late)
    whole.arrive(0)
    outs = [pltpu.make_async_copy(fulls[0], fulls_out[0], out_sem.at[0])]
    outs[0].start()
    late_chain.forward(0, 0)
    half = seq_count // 2

    def hidden_tile(index, carry):
        at = pl.ds(pl.multiple_of(index * 256, 256), 256)
        upper = fulls[0][0:half, :, at].reshape(width, 256)
        lower = fulls[0][half:seq_count, :, at].reshape(width, 256)
        hidden_ref[:, at] = dot_nn(frames_ref[...], upper) + dot_nn(shortcut_ref[...], lower)
        return carry

    lax.fori_loop(0, width // 256, hidden_tile, 0)
    small.finish()
    last = total_ref.shape[1] - 1
    token_scr[...] = token_ref[...]
    token_scr[4:5, :] = total_ref[seq_count - 1, last:last + 1, :128]
    tokens_ref[place.grp] = token_scr[...]
    tokens = [
        place.push(token_scr, tokens_ref.at[place.grp], token_send, token_recv, step, (other, me))
        for step, other in enumerate(place.groups)
    ]
    for spot in range(seq_count):
        mods_ref[spot * block:(spot + 1) * block, :] = total_ref[spot]

    def vector(group, part, second):
        def row(utter):
            at = (group * 2 + utter) * 6 + part
            return mods_ref[at:at + 1, :]

        return jnp.where(second, row(1), row(0))

    chunk = 32
    for group in range(group_count):

        def norm_rows(index, carry):
            first = pl.multiple_of(index * chunk, chunk)
            at = pl.ds(pl.multiple_of(group * local_rows + first, chunk), chunk)
            second = second_mask(bound_ref, group, me, local_rows, first, chunk)
            normal, _ = centered(hidden_ref[at, :])
            normed_ref[at, :] = (
                normal * (1.0 + vector(group, 1, second)) + vector(group, 0, second)
            ).astype(jnp.bfloat16)
            return carry

        lax.fori_loop(0, local_rows // chunk, norm_rows, 0)
    for job in projection_jobs:
        whole.over_core(*job)
    whole.arrive(1)
    late_chain.forward(0, 1)
    outs.append(pltpu.make_async_copy(fulls[1], fulls_out[1], out_sem.at[1]))
    outs[1].start()
    each = 256 // local_width

    def head_tile(index, carry):
        for kind in range(3):
            at = pl.ds(pl.multiple_of(kind * width + index * 256, 256), 256)
            packed = dot_nn(normed_ref[...], fulls[1][:, :, at].reshape(width, 256))
            for half in range(2):
                lanes = packed[:, half * 128:(half + 1) * 128]
                if kind < 2:
                    lanes = turn_lanes(lanes, cos_ref[...], sin_ref[...])
                lanes = lanes.astype(jnp.bfloat16)
                for spot in range(each // 2):
                    cut = lanes[:, spot * local_width:(spot + 1) * local_width]
                    for group in range(group_count):
                        qkv_ref[index * each + half * (each // 2) + spot, group, kind] = cut[
                            group * local_rows:(group + 1) * local_rows
                        ]
        return carry

    lax.fori_loop(0, width // 256, head_tile, 0)
    for rank in range(2, layers - 1):
        late_chain.forward(0, rank)
    whole.finish()
    late_chain.sent()
    for copy in tokens:
        copy.wait_recv()
    kept = tokens_ref[0, 4:5, :]
    for group in range(1, rows_all):
        kept = kept + tokens_ref[group, 4:5, :]
    frames_all = float(rows_all * group_count * local_rows * seq_count)
    scale_ref[...] = jnp.broadcast_to(frames_all / kept, scale_ref.shape)
    for copy in outs:
        copy.wait()


def front(bounds, frames, shortcut, ladder, kept, token, modulation, combine, projection, late_shards):
    grp_count = lax.axis_size("grp")
    seq_count = lax.axis_size("seq")
    side = math.isqrt(grp_count)
    layers = seq_count // 2
    anywhere = pl.BlockSpec(memory_space=pl.ANY)
    vmem = pl.BlockSpec(memory_space=pltpu.VMEM)
    dma = pltpu.SemaphoreType.DMA
    hops = max(side - 1, 1)
    shards = (combine, projection)
    group_count = bounds.shape[0]
    row_count, width = frames.shape
    low, full = jnp.bfloat16, jnp.float32
    cut = min(shard.shape[1] for shard in late_shards) // side
    late_rows = sum(shard.shape[0] // side * (shard.shape[1] // side // cut) for shard in late_shards)
    most = max(shard.shape[1] // side // cut for shard in late_shards)
    small = jax.ShapeDtypeStruct((seq_count, 32 // seq_count, width), full)
    wholes = [(seq_count,) + part.shape for part in shards]
    return pl.pallas_call(
        functools.partial(front_kernel, (side, side), seq_count, len(late_shards)),
        out_shape=tuple(jax.ShapeDtypeStruct(shape, low) for shape in wholes) + (
            jax.ShapeDtypeStruct((layers - 1, late_rows, cut), low),
            jax.ShapeDtypeStruct((row_count, width), full),
            jax.ShapeDtypeStruct((row_count, width), low),
            jax.ShapeDtypeStruct(
                (seq_count, group_count, 3, row_count // group_count, width // seq_count), low
            ),
            jax.ShapeDtypeStruct((row_count, 128), full),
            jax.ShapeDtypeStruct((row_count, 128), full),
            jax.ShapeDtypeStruct((32, width), full),
            jax.ShapeDtypeStruct(token.shape, full),
            jax.ShapeDtypeStruct((grp_count,) + token.shape, full),
        ),
        in_specs=[pl.BlockSpec(memory_space=pltpu.SMEM)] + [vmem] * 6 + [anywhere] * (2 + len(late_shards)),
        out_specs=(anywhere,) * 3 + (vmem,) * 8,
        scratch_shapes=[pltpu.VMEM(small.shape, full)] * 2 + [pltpu.VMEM(shape, low) for shape in wholes] + [
            pltpu.VMEM(token.shape, full), dma((grp_count - 1,)), dma((grp_count - 1,)), dma((2,)),
        ] + small_scratch(small) + [
            pltpu.VMEM((late_rows, cut), low),
            dma((1, layers + 1)), dma((1, layers - 1)), dma((len(late_shards) * most,)),
            dma((2, layers + 1)), dma((2, layers - 1)),
            dma((2, layers, 1, 1)),
            dma((2, layers - 1, 2, hops, 1)), dma((2, layers - 1, 2, hops, 1)),
            dma((2, layers - 1, 2, hops, side)), dma((2, layers - 1, 2, hops, side)),
            dma((2, layers)), dma((2, layers)),
        ],
        compiler_params=pltpu.CompilerParams(
            collective_id=3, has_side_effects=True, vmem_limit_bytes=48 * 1024 * 1024
        ),
        name="front",
    )(bounds, frames, shortcut, ladder, kept, token, modulation, *shards, *late_shards)


def middle_kernel(seq_count, *refs):
    (
        bound_ref, mixture_ref, hidden_ref, target_ref, kept_ref, mods_ref, scale_ref,
        readout_ref, expand_ref, contract_ref,
    ) = refs[:10]
    result_ref, middle_grad_ref, mixture_grad_ref, late_ref, contract_part, expand_part, readout_part = refs[10:17]
    (
        readout_scr, expand_scr, contract_scr, mixture_scr, branch_scr, middle_scr, normed_scr, slope_scr, active_scr,
        active_t_scr, wide_scr, grad_scr, low_scr, left_t_scr, stage_scr, value_scr, weight_sem, stage_sem,
    ) = refs[17:]
    row_count, width = hidden_ref.shape
    wide = expand_ref.shape[1]
    group_count = mixture_ref.shape[1]
    local_rows = row_count // group_count
    local_width = width // seq_count
    me = lax.axis_index("seq")
    weights = [
        pltpu.make_async_copy(source, scratch, weight_sem.at[index])
        for index, (source, scratch) in enumerate(
            ((readout_ref, readout_scr), (expand_ref, expand_scr), (contract_ref, contract_scr))
        )
    ]
    weights[0].start()
    for source in range(seq_count):
        for group in range(group_count):
            mixture_scr[
                group * local_rows:(group + 1) * local_rows, source * local_width:(source + 1) * local_width
            ] = mixture_ref[source, group]
    chunk = 32
    tile = 256

    def tiles(count, body):
        def one(index, carry):
            body(pl.ds(pl.multiple_of(index * tile, tile), tile))
            return carry

        lax.fori_loop(0, count // tile, one, 0)

    def chunks(body, many):
        sums = []
        for group in range(group_count):

            def one(index, carry, group=group):
                first = pl.multiple_of(index * chunk, chunk)
                at = pl.ds(pl.multiple_of(group * local_rows + first, chunk), chunk)
                second = second_mask(bound_ref, group, me, local_rows, first, chunk)

                def vector(part):
                    row = group * 12 + part
                    return jnp.where(second, mods_ref[row + 6:row + 7, :], mods_ref[row:row + 1, :])

                later = second.astype(jnp.float32)
                found = body(at, vector)
                out = []
                for spot, value in enumerate(found):
                    late = value * later
                    out.append(carry[2 * spot] + fold_rows(value - late, jnp.sum))
                    out.append(carry[2 * spot + 1] + fold_rows(late, jnp.sum))
                return tuple(out)

            zero = jnp.zeros((8, width), jnp.float32)
            sums.append(lax.fori_loop(0, local_rows // chunk, one, (zero,) * (2 * many)))
        return sums

    def put(part, spot, sums):
        for group in range(group_count):
            for utter in range(2):
                row = part * 2 * group_count + group * 2 + utter
                late_ref[row:row + 1, :] = jnp.sum(sums[group][2 * spot + utter], axis=0, keepdims=True)

    weights[0].wait()
    weights[1].start()
    weights[2].start()
    tiles(width, lambda at: branch_scr.__setitem__((slice(None), at), dot_nn(mixture_scr[...], readout_scr[:, at])))

    def second_norm(at, vector):
        middle = hidden_ref[at, :] + vector(2) * branch_scr[at, :]
        middle_scr[at, :] = middle
        normal, _ = centered(middle)
        normed_scr[at, :] = (normal * (1.0 + vector(4)) + vector(3)).astype(jnp.bfloat16)
        return ()

    chunks(second_norm, 0)
    weights[1].wait()

    def expand_dot(index, slot):
        at = pl.ds(pl.multiple_of(jnp.minimum(index, wide // tile - 1) * tile, tile), tile)
        value_scr[slot] = dot_nn(normed_scr[...], expand_scr[:, at])

    def bend(index, slot):
        at = pl.ds(pl.multiple_of(index * tile, tile), tile)
        value = value_scr[slot]
        square = value * value
        factor = (2.0 / math.pi) ** 0.5
        bent = jnp.tanh(value * (factor + (factor * 0.044715) * square))
        half = 0.5 + 0.5 * bent
        active_scr[:, at] = (value * half).astype(jnp.bfloat16)
        slope_scr[:, at] = half + (0.5 * value * (1.0 - bent * bent)) * (factor + (factor * 3 * 0.044715) * square)

    def expand_pair(index, carry):
        expand_dot(2 * index + 1, 1)
        bend(2 * index, 0)
        expand_dot(2 * index + 2, 0)
        bend(2 * index + 1, 1)
        return carry

    expand_dot(0, 0)
    lax.fori_loop(0, wide // tile // 2, expand_pair, 0)
    weights[2].wait()
    tiles(width, lambda at: grad_scr.__setitem__((slice(None), at), dot_nn(active_scr[...], contract_scr[:, at])))
    loss_scale = scale_ref[0:1, 0:1]

    def close(at, vector):
        contracted = grad_scr[at, :]
        gate = vector(5)
        output = middle_scr[at, :] + gate * contracted
        result_ref[at, :] = output.astype(jnp.bfloat16)
        output_grad = loss_scale * kept_ref[at, :] * (output - target_ref[at, :].astype(jnp.float32))
        middle_grad_ref[at, :] = output_grad
        low_scr[at, :] = (gate * output_grad).astype(jnp.bfloat16)
        return (output_grad * contracted,)

    put(3, 0, chunks(close, 1))
    def share_out(left, right, dest, across):
        many = dest.shape[1 if across else 0] // width

        def copy(index, slot):
            block = pl.ds(index * width, width)
            return pltpu.make_async_copy(
                stage_scr.at[slot], dest.at[:, block] if across else dest.at[block, :], stage_sem.at[slot]
            )

        for block in range(many):
            slot = block % 2
            if block >= 2:
                copy(block - 2, slot).wait()

            def one(index, carry, block=block, slot=slot):
                at = pl.ds(pl.multiple_of(index * tile, tile), tile)
                first = left[...] if across else left[block * width:(block + 1) * width, :]
                lanes = pl.ds(pl.multiple_of(index * tile + (block * width if across else 0), tile), tile)
                stage_scr[slot, :, at] = dot_nn(first, right[:, lanes]).astype(jnp.bfloat16)
                return carry

            lax.fori_loop(0, width // tile, one, 0)
            copy(block, slot).start()
        return [copy(last, last % 2) for last in range(max(many - 2, 0), many)]

    def active_dot(index, slot):
        at = pl.ds(pl.multiple_of(jnp.minimum(index, wide // tile - 1) * tile, tile), tile)
        value_scr[slot] = dot_nt(low_scr[...], contract_scr[at, :])

    def unbend(index, slot):
        at = pl.ds(pl.multiple_of(index * tile, tile), tile)
        active_t_scr[at, :] = active_scr[:, at].T
        wide_scr[:, at] = (value_scr[slot] * slope_scr[:, at]).astype(jnp.bfloat16)

    def active_pair(index, carry):
        active_dot(2 * index + 1, 1)
        unbend(2 * index, 0)
        active_dot(2 * index + 2, 0)
        unbend(2 * index + 1, 1)
        return carry

    active_dot(0, 0)
    lax.fori_loop(0, wide // tile // 2, active_pair, 0)

    out = share_out(active_t_scr, low_scr, contract_part, False)
    tiles(width, lambda at: grad_scr.__setitem__((slice(None), at), dot_nt(wide_scr[...], expand_scr[at, :])))
    tiles(width, lambda at: left_t_scr.__setitem__(
        (at, slice(None)), normed_scr[:, at].astype(jnp.float32).T.astype(jnp.bfloat16)
    ))

    for copy in out:
        copy.wait()
    out = share_out(left_t_scr, wide_scr, expand_part, True)

    def norm_back(at, vector):
        grad = grad_scr[at, :]
        normal, scale = centered(middle_scr[at, :])
        inner = grad * (1.0 + vector(4))
        turned = scale * (
            inner
            - jnp.mean(inner, axis=-1, keepdims=True)
            - normal * jnp.mean(inner * normal, axis=-1, keepdims=True)
        )
        middle_grad = middle_grad_ref[at, :] + turned
        middle_grad_ref[at, :] = middle_grad
        low_scr[at, :] = (vector(2) * middle_grad).astype(jnp.bfloat16)
        return middle_grad * branch_scr[at, :], grad, grad * normal

    sums = chunks(norm_back, 3)
    for spot in range(3):
        put(spot, spot, sums)

    def mixture_tile(at):
        left_t_scr[at, :] = mixture_scr[:, at].astype(jnp.float32).T.astype(jnp.bfloat16)
        grad_scr[:, at] = dot_nt(low_scr[...], readout_scr[at, :])

    tiles(width, mixture_tile)
    for source in range(seq_count):
        for group in range(group_count):
            mixture_grad_ref[source, group] = grad_scr[
                group * local_rows:(group + 1) * local_rows, source * local_width:(source + 1) * local_width
            ].astype(jnp.bfloat16)

    for copy in out:
        copy.wait()
    for copy in share_out(left_t_scr, low_scr, readout_part, False):
        copy.wait()


def middle(bounds, mixture, hidden, target, kept, mods, loss_scale, readout, expand, contract):
    seq_count, group_count, local_rows, local_width = mixture.shape
    row_count, width = hidden.shape
    wide = expand.shape[1]
    anywhere = pl.BlockSpec(memory_space=pl.ANY)
    vmem = pl.BlockSpec(memory_space=pltpu.VMEM)
    smem = pl.BlockSpec(memory_space=pltpu.SMEM)
    low, full = jnp.bfloat16, jnp.float32
    dma = pltpu.SemaphoreType.DMA
    return pl.pallas_call(
        functools.partial(middle_kernel, seq_count),
        out_shape=(
            jax.ShapeDtypeStruct((row_count, width), low),
            jax.ShapeDtypeStruct((row_count, width), full),
            jax.ShapeDtypeStruct(mixture.shape, low),
            jax.ShapeDtypeStruct((8 * group_count, width), full),
            jax.ShapeDtypeStruct(contract.shape, low),
            jax.ShapeDtypeStruct(expand.shape, low),
            jax.ShapeDtypeStruct(readout.shape, low),
        ),
        in_specs=[smem] + [vmem] * 6 + [anywhere] * 3,
        out_specs=(vmem,) * 4 + (anywhere,) * 3,
        scratch_shapes=[
            pltpu.VMEM(readout.shape, low),
            pltpu.VMEM(expand.shape, low),
            pltpu.VMEM(contract.shape, low),
            pltpu.VMEM((row_count, width), low),
            pltpu.VMEM((row_count, width), full),
            pltpu.VMEM((row_count, width), full),
            pltpu.VMEM((row_count, width), low),
            pltpu.VMEM((row_count, wide), full),
            pltpu.VMEM((row_count, wide), low),
            pltpu.VMEM((wide, row_count), low),
            pltpu.VMEM((row_count, wide), low),
            pltpu.VMEM((row_count, width), full),
            pltpu.VMEM((row_count, width), low),
            pltpu.VMEM((width, row_count), low),
            pltpu.VMEM((2, width, width), low),
            pltpu.VMEM((2, row_count, 256), full),
            dma((3,)),
            dma((2,)),
        ],
        compiler_params=pltpu.CompilerParams(vmem_limit_bytes=60 * 1024 * 1024),
        name="feed_forward",
    )(bounds, mixture, hidden, target, kept, mods, loss_scale, readout, expand, contract)


def back_kernel(plane, seq_count, *refs):
    layers = seq_count // 2
    (
        bound_ref, back_ref, cos_ref, sin_ref, normed_ref, hidden_ref, middle_ref, frames_ref, shortcut_ref,
        combine_ref, projection_ref, mods_ref, late_ref, modulation_ref,
    ) = refs[:14]
    finished, refs = refs[14], refs[15:]
    frames_out, shortcut_out, outs, refs = refs[0], refs[1], refs[2:7], refs[7:]
    utters_ref, conditions_ref, refs = refs[0], refs[1], refs[2:]
    (
        packed_scr, combine_scr, projection_scr, normed_t_scr, joined_t_scr, grad_scr, low_scr,
        shortcut_scr, total_ref, utter_scr, flat_scr, condition_scr,
    ) = refs[:12]
    frames_scr = grad_scr
    parts, line_refs, refs = refs[12:14], refs[14:20], refs[20:]
    buffers, semaphores, refs = refs[:10], refs[10:17], refs[17:]
    small_refs, spread_sems, refs = refs[:5], refs[5:9], refs[9:]
    weight_sem, out_sem, token_send, token_recv, last_send, last_recv, *line_sems = refs
    group_count, local_rows, local_width = back_ref.shape[1], back_ref.shape[3], back_ref.shape[4]
    row_count, width = normed_ref.shape
    place = Place(plane, seq_count)
    me = place.me
    side = place.cols_x
    enter([(place.grp, other) for other in place.others] + [(other, me) for other in place.groups])
    chains = [
        LineSum(place, *line_refs[2 * index:2 * index + 2], *line_sems[2 * index:2 * index + 2])
        for index in range(3)
    ]
    held = pltpu.make_async_copy(finished, line_refs[4], weight_sem.at[2])
    held.start()
    weights = [
        pltpu.make_async_copy(projection_ref, projection_scr, weight_sem.at[0]),
        pltpu.make_async_copy(combine_ref, combine_scr, weight_sem.at[1]),
    ]
    for copy in weights:
        copy.start()
    held.wait()
    chains[2].begin()
    for source in range(seq_count):
        for kind in range(3):
            for group in range(group_count):
                packed_scr[
                    group * local_rows:(group + 1) * local_rows,
                    kind * width + source * local_width:kind * width + (source + 1) * local_width,
                ] = back_ref[source, group, kind]

    def turn(index, carry):
        lanes = pl.ds(pl.multiple_of(index * 128, 128), 128)
        packed_scr[:, lanes] = turn_lanes(
            packed_scr[:, lanes].astype(jnp.float32), cos_ref[...], -sin_ref[...]
        ).astype(jnp.bfloat16)
        return carry

    lax.fori_loop(0, 2 * width // 128, turn, 0)
    normed_t_scr[...] = normed_ref[...].T
    joined_t_scr[:width, :] = frames_ref[...].T
    joined_t_scr[width:, :] = shortcut_ref[...].T
    segments = [
        piece_segments([part.shape[1:]], side, part.shape[2] // side)[0][0] for part in parts
    ]
    done_segments, _ = piece_segments(
        [out.shape for out in outs[2:]], side, min(out.shape[1] for out in outs[2:]) // side
    )
    pieces = [[line_refs[2 * index].at[step] for step in range(layers)] for index in range(2)]
    plane_sum = PlaneSum(place, parts, pieces, segments, buffers, semaphores, True)
    late_rounds = chains[2].rounds()
    spread = PlaneSpread(place, outs, *spread_sems)

    def share(index, left, right, tile):
        rows, columns = parts[index].shape[1:]

        def one(turn, carry):
            lanes = pl.ds(pl.multiple_of(turn * tile, tile), tile)
            parts[index][:, :, lanes] = dot_nn(left[...], right[:, lanes]).astype(jnp.bfloat16).reshape(
                seq_count, rows, tile
            )
            return carry

        lax.fori_loop(0, columns // tile, one, 0)
        for step in range(layers):
            plane_sum.swap(index, step)

    share(0, normed_t_scr, packed_scr, 256)
    weights[0].wait()

    def grad_tile(index, carry):
        at = pl.ds(pl.multiple_of(index * 256, 256), 256)
        grad_scr[:, at] = dot_nt(packed_scr[...], projection_scr[at, :])
        return carry

    lax.fori_loop(0, width // 256, grad_tile, 0)
    for hook in plane_sum.steps(plane_sum.first, 0):
        hook()
    block, utter_rows = utter_scr.shape[1], 2 * group_count
    utter_scr[...] = jnp.zeros_like(utter_scr)

    def put(part, utter, value):
        row = part * utter_rows + utter
        utter_scr[row // block, row % block:row % block + 1, :] = value

    for part in range(4):
        for utter in range(utter_rows):
            put(part + 2, utter, late_ref[part * utter_rows + utter:part * utter_rows + utter + 1, :])
    chunk = 32
    for group in range(group_count):

        def norm_back(index, sums):
            first = pl.multiple_of(index * chunk, chunk)
            at = pl.ds(pl.multiple_of(group * local_rows + first, chunk), chunk)
            second = second_mask(bound_ref, group, me, local_rows, first, chunk)
            row = group * 2 * 6
            scale_part = jnp.where(second, mods_ref[row + 7:row + 8, :], mods_ref[row + 1:row + 2, :])
            grad = grad_scr[at, :]
            normal, scale = centered(hidden_ref[at, :])
            inner = grad * (1.0 + scale_part)
            turned = scale * (
                inner
                - jnp.mean(inner, axis=-1, keepdims=True)
                - normal * jnp.mean(inner * normal, axis=-1, keepdims=True)
            )
            low_scr[at, :] = (middle_ref[at, :] + turned).astype(jnp.bfloat16)
            scaled = grad * normal
            later = second.astype(jnp.float32)
            shift_later, scale_later = grad * later, scaled * later
            return (
                sums[0] + fold_rows(grad - shift_later, jnp.sum),
                sums[1] + fold_rows(shift_later, jnp.sum),
                sums[2] + fold_rows(scaled - scale_later, jnp.sum),
                sums[3] + fold_rows(scale_later, jnp.sum),
            )

        zero = jnp.zeros((8, width), jnp.float32)
        sums = lax.fori_loop(0, local_rows // chunk, norm_back, (zero, zero, zero, zero))
        for spot, value in enumerate(sums):
            put(spot // 2, group * 2 + spot % 2, jnp.sum(value, axis=0, keepdims=True))
    small = SmallSum(place, utter_scr, total_ref, *small_refs)
    small.begin()
    share(1, joined_t_scr, low_scr, 256)
    late_rounds[0]()
    for hook in plane_sum.steps(plane_sum.first, 1) + plane_sum.steps(plane_sum.second, 0):
        hook()
    weights[1].wait()

    def joined_tile(index, carry):
        at = pl.ds(pl.multiple_of(index * 256, 256), 256)
        late = pl.ds(pl.multiple_of(width + index * 256, 256), 256)
        frames_scr[:, at] = dot_nt(low_scr[...], combine_scr[at, :])
        shortcut_scr[:, at] = dot_nt(low_scr[...], combine_scr[late, :])
        return carry

    lax.fori_loop(0, width // 256, joined_tile, 0)
    grads = [
        pltpu.make_async_copy(frames_scr, frames_out, out_sem.at[0]),
        pltpu.make_async_copy(shortcut_scr, shortcut_out, out_sem.at[1]),
    ]
    for copy in grads:
        copy.start()
    for hook in late_rounds[1:]:
        hook()
    small.middle()
    for hook in plane_sum.steps(plane_sum.second, 1) + plane_sum.steps(plane_sum.third, 0):
        hook()
    chains[0].begin()
    small.finish()
    for spot in range(seq_count):
        flat_scr[spot * block:(spot + 1) * block, :] = total_ref[spot]
    utters_ref[place.grp] = flat_scr[...].astype(jnp.bfloat16)
    tokens = [
        place.push(utters_ref.at[place.grp], utters_ref.at[place.grp], token_send, token_recv, step, (other, me))
        for step, other in enumerate(place.groups)
    ]
    condition_scr[...] = jnp.zeros_like(condition_scr)
    shard_rows = modulation_ref.shape[0]
    for spot in range(6 * utter_rows // block):
        part, row = spot * block // utter_rows, spot * block % utter_rows
        condition_scr[row:row + block, :shard_rows] += dot_nt(
            total_ref[spot].astype(jnp.bfloat16), modulation_ref[:, part * width:(part + 1) * width]
        )
    conditions_ref[me] = condition_scr[...]
    tokens += [
        place.push(condition_scr, conditions_ref.at[me], last_send, last_recv, step, (place.grp, other))
        for step, other in enumerate(place.others)
    ]
    rounds = [chains[0].rounds(), chains[1].rounds()]
    piece, others = chains[2].close()
    for index in range(2, 5):
        spread.total(index, piece, others, done_segments[index - 2])
    rounds[0][0]()
    for hook in plane_sum.steps(plane_sum.third, 1):
        hook()
    chains[1].begin()
    for hook in rounds[0][1:]:
        hook()
    for index in range(2, 5):
        spread.second(index)
    piece, others = chains[0].close()
    spread.total(0, piece, others, segments[0])
    for hook in rounds[1]:
        hook()
    piece, others = chains[1].close()
    spread.total(1, piece, others, segments[1])
    spread.second(0)
    spread.second(1)
    for chain in chains:
        chain.sent()
    place.sent()
    for copy in tokens:
        copy.wait_recv()
    for copy in grads:
        copy.wait()
    for index in range(5):
        spread.finish(index)


def finish_backward(bounds, back, cos, sin, normed, hidden, middle_grad, frames, shortcut, combine, projection, mods, late, modulation, finished, done_shapes):
    grp_count = lax.axis_size("grp")
    seq_count = lax.axis_size("seq")
    side = math.isqrt(grp_count)
    layers = seq_count // 2
    hops = max(side - 1, 1)
    anywhere = pl.BlockSpec(memory_space=pl.ANY)
    vmem = pl.BlockSpec(memory_space=pltpu.VMEM)
    dma = pltpu.SemaphoreType.DMA
    row_count, width = normed.shape
    low, full = jnp.bfloat16, jnp.float32
    parts = [
        jax.ShapeDtypeStruct((seq_count, weight.shape[0] // seq_count, weight.shape[1]), low)
        for weight in (projection, combine)
    ]
    out_shapes = [part.shape[1:] for part in parts] + list(done_shapes)
    small = jax.ShapeDtypeStruct((seq_count, 32 // seq_count, width), full)
    return pl.pallas_call(
        functools.partial(back_kernel, (side, side), seq_count),
        out_shape=(
            jax.ShapeDtypeStruct((row_count, width), full),
            jax.ShapeDtypeStruct((row_count, width), full),
        ) + tuple(jax.ShapeDtypeStruct(shape, low) for shape in out_shapes) + (
            jax.ShapeDtypeStruct((grp_count, 32, width), low),
            jax.ShapeDtypeStruct((seq_count, 8, 128), full),
        ),
        in_specs=[pl.BlockSpec(memory_space=pltpu.SMEM)] + [vmem] * 8 + [anywhere] * 2 + [vmem] * 3 + [anywhere],
        out_specs=(anywhere,) * 2 + (vmem,) * 7,
        scratch_shapes=[
            pltpu.VMEM((row_count, 3 * width), low),
            pltpu.VMEM(combine.shape, low),
            pltpu.VMEM(projection.shape, low),
            pltpu.VMEM((width, row_count), low),
            pltpu.VMEM((2 * width, row_count), low),
            pltpu.VMEM((row_count, width), full),
            pltpu.VMEM((row_count, width), low),
            pltpu.VMEM((row_count, width), full),
            pltpu.VMEM(small.shape, full),
            pltpu.VMEM(small.shape, full),
            pltpu.VMEM((32, width), full),
            pltpu.VMEM((8, 128), full),
        ] + [pltpu.VMEM(part.shape, low) for part in parts] + [
            pltpu.VMEM((layers + more,) + shape, low)
            for shape in [
                (part.shape[1] // side, part.shape[2] // side) for part in parts
            ] + [finished.shape[1:]] for more in range(2)
        ] + plane_sum_scratch(parts, side, True) + small_scratch(small) + [
            dma((5, 2, hops)), dma((5, 2, hops)),
            dma((5, 2, hops, side)), dma((5, 2, hops, side)),
            dma((3,)), dma((2,)),
            dma((grp_count - 1,)), dma((grp_count - 1,)),
            dma((seq_count - 1,)), dma((seq_count - 1,)),
        ] + [dma((2, layers))] * 6 + [
        ],
        compiler_params=pltpu.CompilerParams(
            collective_id=4, has_side_effects=True, vmem_limit_bytes=60 * 1024 * 1024
        ),
        name="finish_backward",
    )(bounds, back, cos, sin, normed, hidden, middle_grad, frames, shortcut, combine, projection, mods, late, modulation, finished)


def shards(
    frames,
    shortcut,
    time_embed,
    lengths,
    kept_mask,
    target,
    combine,
    modulation,
    projection,
    readout,
    expand,
    contract,
):
    group_count = frames.shape[0]
    local_rows = frames.shape[1]
    width = HEADS * HEAD_DIM
    row_count = group_count * local_rows
    seq_count = lax.axis_size("seq")
    utter_count = time_embed.shape[1]
    kept_float = kept_mask.astype(jnp.float32)
    half_dim = HEAD_DIM // 2
    inverse = jnp.exp(-jnp.log(rope_base) * (jnp.arange(half_dim, dtype=jnp.float32) / half_dim))
    signs = jnp.where(jnp.arange(128) % HEAD_DIM < half_dim, -1.0, 1.0).astype(jnp.float32)
    ladder = jnp.zeros((8, 128), jnp.float32).at[0].set(jnp.tile(inverse, 128 // half_dim)).at[1].set(signs)
    silu_value, silu_pull = jax.vjp(jax.nn.silu, time_embed)
    condition = silu_value.astype(jnp.bfloat16)
    shard_rows = modulation.shape[0]
    utter_rows = group_count * utter_count
    condition_part = lax.dynamic_slice_in_dim(
        condition, lax.axis_index("seq") * shard_rows, shard_rows, 2
    ).reshape(utter_rows, shard_rows)
    token = jnp.zeros((8, 128), jnp.float32)
    token = token.at[:utter_rows, :shard_rows].set(condition_part.astype(jnp.float32))
    late_shards = (readout, expand, contract)
    bounds = lengths[:, 0]
    combine_full, projection_full, *rest = front(
        bounds,
        frames.reshape(row_count, width),
        shortcut.reshape(row_count, width),
        ladder,
        kept_float,
        token,
        modulation,
        combine,
        projection,
        late_shards,
    )
    late_pieces, hidden, normed, qkv, cos_lanes, sin_lanes, mods, loss_scale, tokens = rest
    combine_full = combine_full.reshape(2 * width, width)
    projection_full = projection_full.reshape(width, 3 * width)
    condition_all = tokens[:, :utter_rows, :shard_rows].reshape(-1, shard_rows).astype(jnp.bfloat16)
    split_shape = (group_count, local_rows, width)
    kept_heads, mixture_blocks, log_total, *late_full = attend_forward(
        bounds, qkv, late_shards, late_pieces
    )
    readout_full = late_full[0].reshape(width, width)
    expand_full = late_full[1].reshape(width, -1)
    contract_full = late_full[2].reshape(-1, width)
    result, middle_grad, mixture_grad, late_rows, contract_part, expand_part, readout_part = middle(
        bounds,
        mixture_blocks,
        hidden,
        target.reshape(row_count, width),
        kept_float.reshape(row_count, 1),
        mods,
        loss_scale,
        late_full[0].reshape(width, width),
        late_full[1].reshape(width, -1),
        late_full[2].reshape(-1, width),
    )
    back_blocks, plane_pieces = attend_backward(
        bounds,
        kept_heads,
        mixture_grad,
        log_total,
        (contract_part, expand_part, readout_part),
    )
    frames_grad, shortcut_grad, *shares, utters, condition_back = finish_backward(
        bounds,
        back_blocks,
        cos_lanes,
        sin_lanes,
        normed,
        hidden,
        middle_grad,
        frames.reshape(row_count, width),
        shortcut.reshape(row_count, width),
        combine_full,
        projection_full,
        mods,
        late_rows,
        modulation,
        plane_pieces,
        [contract.shape, expand.shape, readout.shape],
    )
    frames_grad = frames_grad.reshape(split_shape)
    shortcut_grad = shortcut_grad.reshape(split_shape)
    projection_grad, combine_grad, contract_grad, expand_grad, readout_grad = [
        share.astype(jnp.float32) for share in shares
    ]
    utter_all = jnp.transpose(
        utters[:, :6 * utter_rows].reshape(-1, 6, utter_rows, width), (0, 2, 1, 3)
    ).reshape(-1, 6 * width)
    modulation_grad = product_left(condition_all, utter_all)
    condition_grad = jnp.transpose(
        condition_back[:, :utter_rows, :shard_rows], (1, 0, 2)
    ).reshape(group_count, utter_count, width)
    time_grad = silu_pull(condition_grad)[0]
    summed = (combine_grad, modulation_grad, projection_grad, readout_grad, expand_grad, contract_grad)
    return (
        result.reshape(split_shape),
        frames_grad,
        shortcut_grad,
        time_grad,
        summed[0],
        summed[1],
        summed[2],
        summed[3],
        summed[4],
        summed[5],
    )


def solution(mesh):
    return jax.shard_map(
        shards,
        mesh=mesh,
        in_specs=(
            P("grp", "seq", None),
            P("grp", "seq", None),
            P("grp", None, None),
            P("grp", None),
            P("grp", "seq"),
            P("grp", "seq", None),
            P("seq", None),
            P("seq", None),
            P("seq", None),
            P("seq", None),
            P("seq", None),
            P("seq", None),
        ),
        out_specs=(
            P("grp", "seq", None),
            P("grp", "seq", None),
            P("grp", "seq", None),
            P("grp", None, None),
            P("seq", None),
            P("seq", None),
            P("seq", None),
            P("seq", None),
            P("seq", None),
            P("seq", None),
        ),
        check_vma=False,
    )
```

```python
import functools
import math

import jax
import jax.numpy as jnp
from jax import lax
from jax.experimental import pallas as pl
from jax.experimental.pallas import tpu as pltpu
from jax.sharding import PartitionSpec as P

HEADS = 16
HEAD_DIM = 64


precise = lax.Precision.HIGHEST
epsilon = 1e-06
rope_base = 10000.0


def product(first_op, second_op):
    return jnp.dot(first_op, second_op, preferred_element_type=jnp.float32)


def product_left(first_op, second_op):
    return lax.dot_general(
        first_op, second_op, (((0,), (0,)), ((), ())), preferred_element_type=jnp.float32
    )


def product_right(first_op, second_op):
    return lax.dot_general(
        first_op, second_op, (((1,), (1,)), ((), ())), preferred_element_type=jnp.float32
    )


def gelu_tanh(values):
    return jax.nn.gelu(values, approximate=True)


def modulate(hidden, shift_part, scale_part):
    center = hidden - jnp.mean(hidden, axis=-1, keepdims=True)
    variance = jnp.mean(center * center, axis=-1, keepdims=True)
    return center * lax.rsqrt(variance + epsilon) * (1.0 + scale_part) + shift_part


def segment_info(lengths, frame_index):
    utter_count = lengths.shape[0]
    utter_ends = jnp.cumsum(lengths)
    starts = utter_ends - lengths
    segment = jnp.sum((frame_index[:, None] >= utter_ends[None, :]).astype(jnp.int32), axis=1)
    member = segment[:, None] == jnp.arange(utter_count, dtype=jnp.int32)[None, :]
    offset = jnp.sum(jnp.where(member, starts[None, :], 0), axis=1)
    return (segment, member, frame_index - offset)


def rotary_tables(position):
    half_dim = HEAD_DIM // 2
    ladder = jnp.arange(half_dim, dtype=jnp.float32) / half_dim
    inverse = jnp.exp(-jnp.log(rope_base) * ladder)
    angles = position.astype(jnp.float32)[:, None] * inverse[None, :]
    return (jnp.cos(angles)[:, None, :], jnp.sin(angles)[:, None, :])


def rotate(vectors, cos_table, sin_table):
    half_dim = vectors.shape[-1] // 2
    front_half = vectors[..., :half_dim]
    back_half = vectors[..., half_dim:]
    return jnp.concatenate(
        [
            front_half * cos_table - back_half * sin_table,
            back_half * cos_table + front_half * sin_table,
        ],
        axis=-1,
    )


MESH = pl.DeviceIdType.MESH
PLAN_FIRST, PLAN_RATE = 2, 4
NEG = -1e30


def utter_features(boundary, total_rows, for_keys):
    row = lax.broadcasted_iota(jnp.int32, (total_rows, 128), 0)
    lane = lax.broadcasted_iota(jnp.int32, (total_rows, 128), 1)
    second = (row >= boundary).astype(jnp.float32)
    ahead = (lane == 0).astype(jnp.float32)
    after = (lane == 1).astype(jnp.float32)
    if for_keys:
        return (NEG * (second * ahead + (1.0 - second) * after)).astype(jnp.bfloat16)
    return (second * after + (1.0 - second) * ahead).astype(jnp.bfloat16)


def head_lanes(values, head):
    lane = lax.broadcasted_iota(jnp.int32, values.shape, 1)
    own = (lane >= head * HEAD_DIM) & (lane < (head + 1) * HEAD_DIM)
    return jnp.where(own, values.astype(jnp.float32), 0.0).astype(jnp.bfloat16)


def dot_nn(first_op, second_op):
    return jnp.dot(first_op, second_op, preferred_element_type=jnp.float32)


def dot_nt(first_op, second_op):
    return lax.dot_general(
        first_op, second_op, (((1,), (1,)), ((), ())), preferred_element_type=jnp.float32
    )


def fold_rows(values, combine):
    return combine(values.reshape(values.shape[0] // 8, 8, values.shape[1]), axis=0)


def enter(partners):
    barrier = pltpu.get_barrier_semaphore()
    for partner in partners:
        pl.semaphore_signal(barrier, inc=1, device_id=partner, device_id_type=MESH)
    pl.semaphore_wait(barrier, len(partners))


def key_span(third, total_rows):
    size = total_rows // 3
    return (max(third - 1, 0) * size, min(third + 2, 3) * size)


class Place:
    def __init__(self, plane, seq_count):
        self.rows_y, self.cols_x = rows_y, cols_x = plane
        self.grp, self.me = grp, me = lax.axis_index("grp"), lax.axis_index("seq")
        self.gy, self.gx = gy, gx = grp // cols_x, lax.rem(grp, cols_x)
        self.layers = layers = seq_count // 2
        self.layer, self.core = layer, core = me // 2, lax.rem(me, 2)
        self.xs = [lax.rem(gx + step, cols_x) for step in range(1, cols_x)]
        self.ys = [lax.rem(gy + step, rows_y) for step in range(1, rows_y)]
        self.beside = [gy * cols_x + x for x in self.xs]
        self.along = [y * cols_x + gx for y in self.ys]
        self.beside_from = [lax.rem(gx + cols_x - step, cols_x) for step in range(1, cols_x)]
        self.far = [lax.rem(layer + step, layers) for step in range(1, layers)]
        self.line_from = [lax.rem(layer + layers - step, layers) * 2 + core for step in range(1, layers)]
        self.lines = [target * 2 + core for target in self.far]
        self.partner = layer * 2 + 1 - core
        self.others = [lax.rem(me + step, seq_count) for step in range(1, seq_count)]
        self.groups = [lax.rem(grp + step, rows_y * cols_x) for step in range(1, rows_y * cols_x)]
        self.started = []

    def push(self, src, dst, sends, recvs, slot, device):
        copy = pltpu.make_async_remote_copy(
            src, dst, sends.at[slot], recvs.at[slot], device_id=device, device_id_type=MESH
        )
        copy.start()
        self.started.append(copy)
        return copy

    def sent(self):
        for copy in self.started:
            copy.wait_send()
        self.started = []


def window(ref, row, rows, col, cols):
    return ref.at[pl.ds(pl.multiple_of(row, 16), rows), pl.ds(pl.multiple_of(col, 128), cols)]


def piece_segments(shapes, side, width):
    base, found = 0, []
    for rows, cols in shapes:
        height, many = rows // side, cols // side // width
        if many == 1:
            half = width // 2
            found.append([[(base, 0, height, half, 0)], [(base, half, height, half, half)]])
        else:
            blocks = [(base + spot * height, 0, height, width, spot * width) for spot in range(many)]
            found.append([blocks[:many // 2], blocks[many // 2:]])
        base += height * many
    return found, base


class PlaneGather:
    def __init__(self, place, shards, pieces, segments, fulls, own_sem, first_send, first_recv, second_send, second_recv, core_send, core_recv):
        self.place, self.shards, self.pieces, self.fulls = place, shards, pieces, fulls
        self.segments = segments
        self.own_sem = own_sem
        self.first = (first_send, first_recv)
        self.second = (second_send, second_recv)
        self.core = (core_send, core_recv)
        self.jobs = [(index, step) for step in range(place.layers - 1) for index in range(len(shards))]
        self.waiting, self.local, self.own = {}, {}, []

    def sizes(self, index):
        _, rows, cols = self.fulls[index].shape
        return rows, rows // self.place.rows_y, cols // (2 * self.place.cols_x)

    def owner(self, step):
        return self.place.line_from[step]

    def begin(self):
        place = self.place
        for index, step in self.jobs:
            self.spread_first(index, step)
        for index, shard in enumerate(self.shards):
            copy = pltpu.make_async_copy(shard, self.fulls[index].at[place.me], self.own_sem.at[index, place.layers - 1, 0, 0])
            copy.start()
            push = place.push(shard, self.fulls[index].at[place.me], *self.core, (index, 0), (place.grp, place.partner))
            self.own.append((copy, push))

    def spread_first(self, index, step):
        place = self.place
        rows, height, width = self.sizes(index)
        full = self.fulls[index].at[self.owner(step)]
        piece = self.pieces.at[step]
        first_row, first_col = place.gy * height, 2 * place.gx * width
        self.local[index, step] = []
        self.waiting[index, step] = []
        for half, partners in enumerate((place.beside, place.along)):
            for spot, (row, col, rows, cols, off) in enumerate(self.segments[index][half]):
                source = piece.at[pl.ds(row, rows), pl.ds(col, cols)]
                part = window(full, first_row, rows, first_col + off, cols)
                copy = pltpu.make_async_copy(source, part, self.own_sem.at[index, step, half, spot])
                copy.start()
                self.local[index, step].append(copy)
                for hop, other in enumerate(partners):
                    self.waiting[index, step].append(place.push(
                        source, part, *self.first, (index, step, half, hop, spot), (other, place.me)
                    ))

    def spread_second(self, index, step):
        place = self.place
        rows, height, width = self.sizes(index)
        for copy in self.local.get((index, step), []):
            copy.wait()
        for copy in self.waiting[index, step]:
            copy.wait_recv()
        full = self.fulls[index].at[self.owner(step)]
        copies = []
        for hop, other in enumerate(place.along):
            for spot, column in enumerate([place.gx] + place.beside_from):
                part = window(full, place.gy * height, height, 2 * column * width, width)
                copies.append(place.push(part, part, *self.second, (index, step, 0, hop, spot), (other, place.me)))
        for hop, other in enumerate(place.beside):
            part = window(full, 0, rows, (2 * place.gx + 1) * width, width)
            copies.append(place.push(part, part, *self.second, (index, step, 1, hop, 0), (other, place.me)))
        self.waiting[index, step] = copies

    def over_core(self, index, step):
        place = self.place
        for copy in self.waiting[index, step]:
            copy.wait_recv()
        full = self.fulls[index].at[self.owner(step)]
        self.waiting[index, step] = [
            place.push(full, full, *self.core, (index, step + 1), (place.grp, place.partner))
        ]

    def middle(self):
        for job in self.jobs:
            self.spread_second(*job)

    def late(self):
        return [functools.partial(self.over_core, *job) for job in self.jobs]

    def arrive(self, index):
        for job in self.jobs:
            if job[0] == index:
                for copy in self.waiting[job]:
                    copy.wait_recv()
        copy, push = self.own[index]
        copy.wait()
        push.wait_recv()

    def finish(self):
        self.place.sent()


def add_rows(target, source, first_row, rows, first_col, cols, out=None):
    step = next(size for size in (64, 32, 16) if rows % size == 0)
    col = pl.multiple_of(first_col, 128)

    def one(index, carry):
        at = pl.ds(pl.multiple_of(first_row + index * step, 16), step)
        off = pl.ds(pl.multiple_of(index * step, step), step)
        value = target[at, pl.ds(col, cols)] + source[off, :]
        if out is None:
            target[at, pl.ds(col, cols)] = value
        else:
            out[off, :] = value
        return carry

    lax.fori_loop(0, rows // step, one, 0)


def add_segments(target, source, first_row, first_col, segments, out):
    for row, col, rows, cols, off in segments:
        begin = off - segments[0][4]
        add_rows(
            target, source.at[:, pl.ds(begin, cols)], first_row, rows, first_col + off, cols,
            out.at[pl.ds(row, rows), pl.ds(col, cols)],
        )


def plane_sum_scratch(parts, side, in_place=False):
    layers = parts[0].shape[0] // 2 if in_place else parts[0].shape[0]
    hops = max(side - 1, 1)
    count = len(parts)
    dma = pltpu.SemaphoreType.DMA

    def buffers(lead, row_cut, col_cut):
        return [
            pltpu.VMEM(lead + (part.shape[1] // row_cut, part.shape[2] // col_cut), jnp.bfloat16)
            for part in parts
        ]

    return (
        ([] if in_place else buffers((layers,), 1, 1))
        + buffers((layers,), 1, 1)
        + buffers((layers, hops, side), side, 2 * side)
        + buffers((layers, hops), side, 2 * side)
        + buffers((layers, hops), 1, 2 * side)
        + buffers((layers, hops), side, 2 * side)
        + [
            dma((count, layers)), dma((count, layers)), dma((count, layers)),
            dma((count, layers, 2, hops, side)), dma((count, layers, 2, hops, side)),
            dma((count, layers, 2, hops)), dma((count, layers, 2, hops)),
        ]
    )


class PlaneSum:
    def __init__(self, place, parts, pieces, segments, buffers, semaphores, in_place=False, given=None):
        self.given = given
        self.place, self.parts, self.pieces, self.segments = place, parts, pieces, segments
        count = len(parts)
        buffers = (() if in_place else buffers[:count], *[
            buffers[index * count:(index + 1) * count] for index in range(0 if in_place else 1, 5 if in_place else 6)
        ])
        self.in_place = in_place
        self.sums, self.swapped, self.y_first, self.x_second, self.x_first, self.y_second = buffers
        self.load_sem = semaphores[0]
        self.core, self.first_sem, self.second_sem = semaphores[1:3], semaphores[3:5], semaphores[5:7]
        self.order = place.far + [place.layer]
        self.jobs = [(index, step) for index in range(count) for step in range(place.layers)]
        self.loads, self.swaps, self.waiting = {}, {}, {}

    def sizes(self, index):
        _, rows, cols = self.parts[index].shape
        return rows, cols, rows // self.place.rows_y, cols // (2 * self.place.cols_x)

    def begin(self):
        place = self.place
        for index, step in self.jobs:
            target = self.order[step]
            for source, kept, sem in (
                (self.parts, self.sums, self.load_sem), (self.given, self.swapped, self.core[0]),
            ):
                copy = pltpu.make_async_copy(source[index].at[target], kept[index].at[step], sem.at[index, step])
                copy.start()
                self.loads.setdefault((index, step), []).append(copy)

    def swap(self, index, step):
        place = self.place
        self.swaps[index, step] = place.push(
            self.parts[index].at[self.order[step] * 2 + 1 - place.core], self.swapped[index].at[step],
            *self.core, (index, step), (place.grp, place.partner),
        )

    def running(self, index, step):
        if self.in_place:
            return self.parts[index].at[self.order[step] * 2 + self.place.core]
        return self.sums[index].at[step]

    def first(self, index, step):
        place = self.place
        rows, cols, height, width = self.sizes(index)
        for copy in self.loads.get((index, step), []):
            copy.wait()
        if self.given is None:
            self.swaps[index, step].wait_recv()
        total = self.running(index, step)
        add_rows(total, self.swapped[index].at[step], 0, rows, 0, cols)
        copies = []
        for hop, other in enumerate(place.along):
            for column in range(place.cols_x):
                copies.append(place.push(
                    window(total, place.ys[hop] * height, height, 2 * column * width, width),
                    self.y_first[index].at[step, hop, column],
                    *self.first_sem, (index, step, 0, hop, column), (other, place.me),
                ))
        for hop, other in enumerate(place.beside):
            copies.append(place.push(
                window(total, 0, rows, (2 * place.xs[hop] + 1) * width, width),
                self.x_first[index].at[step, hop],
                *self.first_sem, (index, step, 1, hop, 0), (other, place.me),
            ))
        self.waiting[index, step] = copies

    def second(self, index, step):
        place = self.place
        rows, cols, height, width = self.sizes(index)
        for copy in self.waiting[index, step]:
            copy.wait_recv()
        total = self.running(index, step)
        for hop in range(place.rows_y - 1):
            for column in range(place.cols_x):
                add_rows(
                    total, self.y_first[index].at[step, hop, column],
                    place.gy * height, height, 2 * column * width, width,
                )
        for hop in range(place.cols_x - 1):
            add_rows(total, self.x_first[index].at[step, hop], 0, rows, (2 * place.gx + 1) * width, width)
        copies = []
        for hop, other in enumerate(place.beside):
            copies.append(place.push(
                window(total, place.gy * height, height, 2 * place.xs[hop] * width, width),
                self.x_second[index].at[step, hop],
                *self.second_sem, (index, step, 0, hop), (other, place.me),
            ))
        for hop, other in enumerate(place.along):
            copies.append(place.push(
                window(total, place.ys[hop] * height, height, (2 * place.gx + 1) * width, width),
                self.y_second[index].at[step, hop],
                *self.second_sem, (index, step, 1, hop), (other, place.me),
            ))
        self.waiting[index, step] = copies

    def third(self, index, step):
        place = self.place
        rows, cols, height, width = self.sizes(index)
        for copy in self.waiting[index, step]:
            copy.wait_recv()
        self.waiting[index, step] = []
        total = self.running(index, step)
        out = self.pieces[index][step]
        row, col = place.gy * height, 2 * place.gx * width
        for hop in range(place.cols_x - 1):
            source = self.x_second[index].at[step, hop]
            if hop == place.cols_x - 2:
                add_segments(total, source, row, col, self.segments[index][0], out)
            else:
                add_rows(total, source, row, height, col, width)
        for hop in range(place.rows_y - 1):
            source = self.y_second[index].at[step, hop]
            if hop == place.rows_y - 2:
                add_segments(total, source, row, col, self.segments[index][1], out)
            else:
                add_rows(total, source, row, height, col + width, width)

    def steps(self, stage, only=None):
        return [functools.partial(stage, *job) for job in self.jobs if only is None or job[0] == only]

    def finish(self):
        self.place.sent()


class LineSum:
    def __init__(self, place, pieces, sums, sends, recvs):
        self.place, self.pieces, self.sums = place, pieces, sums
        self.sends, self.recvs = sends, recvs
        self.pushed = []

    def mine(self, owner):
        place = self.place
        return self.pieces.at[lax.rem(place.layers + owner - place.layer - 1, place.layers)]

    def slot(self, way, owner, layer):
        return owner if way == 0 else jnp.where(layer == owner, self.place.layers, owner)

    def copy(self, way, owner):
        place = self.place
        target = place.layer + (1 if way == 0 else -1)
        return pltpu.make_async_remote_copy(
            self.mine(owner), self.sums.at[self.slot(way, owner, target)],
            self.sends.at[way, owner], self.recvs.at[way, owner],
            device_id=(place.grp, target * 2 + place.core), device_id_type=MESH,
        )

    def push(self, when, way, owner, add):
        self.pushed.append((when, way, owner))

        @pl.when(when)
        def _():
            if add:
                self.arrived(way, owner)
                mine, other = self.mine(owner), self.sums.at[self.slot(way, owner, self.place.layer)]
                rows = mine.shape[0]
                step = next(size for size in (64, 32, 16) if rows % size == 0)

                def one(index, carry):
                    at = pl.ds(pl.multiple_of(index * step, 16), step)
                    mine[at, :] = mine[at, :] + other[at, :]
                    return carry

                lax.fori_loop(0, rows // step, one, 0)
            self.copy(way, owner).start()

    def arrived(self, way, owner):
        place = self.place
        part = self.sums.at[self.slot(way, owner, place.layer)]
        pltpu.make_async_remote_copy(
            part, part, self.sends.at[way, owner], self.recvs.at[way, owner],
            device_id=(place.grp, place.me), device_id_type=MESH,
        ).wait_recv()

    def begin(self):
        place, last = self.place, self.place.layers - 1
        for hop in range(last):
            self.push(place.layer == 0, 0, last - hop, False)
            self.push(place.layer == last, 1, hop, False)

    def round(self, turn):
        place, last = self.place, self.place.layers - 1
        for owner in range(place.layers):
            up = turn + 1 - (last - owner)
            if 1 <= up < owner:
                self.push(place.layer == up, 0, owner, True)
            down = turn + 1 - owner
            if 1 <= down < last - owner:
                self.push(place.layer == last - down, 1, owner, True)

    def rounds(self):
        return [functools.partial(self.round, turn) for turn in range(2 * self.place.layers - 5)]

    def close(self):
        place, last = self.place, self.place.layers - 1
        for owner in range(place.layers):
            for way, ends in ((0, owner == 0), (1, owner == last)):

                @pl.when(place.layer == owner)
                def _(way=way, ends=ends, owner=owner):
                    if ends:
                        spot = owner if way == 0 else place.layers
                        self.sums[spot] = jnp.zeros(self.sums.shape[1:], jnp.bfloat16)
                    else:
                        self.arrived(way, owner)

        return self.pieces.at[last], [self.sums.at[place.layer], self.sums.at[place.layers]]

    def sent(self):
        for when, way, owner in self.pushed:

            @pl.when(when)
            def _(way=way, owner=owner):
                self.copy(way, owner).wait_send()


class PlaneSpread:
    def __init__(self, place, outs, first_send, first_recv, second_send, second_recv):
        self.place, self.outs = place, outs
        self.first_sem, self.second_sem = (first_send, first_recv), (second_send, second_recv)
        self.waiting = {}

    def sizes(self, index):
        rows, cols = self.outs[index].shape
        return rows, rows // self.place.rows_y, cols // (2 * self.place.cols_x)

    def total(self, index, piece, others, segments):
        place = self.place
        rows, height, width = self.sizes(index)
        row = place.gy * height
        col = pl.multiple_of(2 * place.gx * width, 128)
        for first, left, _, cols, off in segments[0] + segments[1]:

            def one(turn, carry):
                at = pl.ds(pl.multiple_of(first + turn * 16, 16), 16)
                value = piece[at, pl.ds(left, cols)].astype(jnp.float32)
                for other in others:
                    value = value + other[at, pl.ds(left, cols)].astype(jnp.float32)
                self.outs[index][
                    pl.ds(pl.multiple_of(row + turn * 16, 16), 16), pl.ds(pl.multiple_of(col + off, 128), cols)
                ] = value.astype(jnp.bfloat16)
                return carry

            lax.fori_loop(0, height // 16, one, 0)
        copies = []
        for hop, other in enumerate(place.beside):
            part = window(self.outs[index], row, height, 2 * place.gx * width, width)
            copies.append(place.push(part, part, *self.first_sem, (index, 0, hop), (other, place.me)))
        for hop, other in enumerate(place.along):
            part = window(self.outs[index], row, height, (2 * place.gx + 1) * width, width)
            copies.append(place.push(part, part, *self.first_sem, (index, 1, hop), (other, place.me)))
        self.waiting[index] = copies

    def second(self, index):
        place = self.place
        rows, height, width = self.sizes(index)
        for copy in self.waiting[index]:
            copy.wait_recv()
        copies = []
        for hop, other in enumerate(place.along):
            for spot, column in enumerate([place.gx] + place.beside_from):
                part = window(self.outs[index], place.gy * height, height, 2 * column * width, width)
                copies.append(place.push(part, part, *self.second_sem, (index, 0, hop, spot), (other, place.me)))
        for hop, other in enumerate(place.beside):
            part = window(self.outs[index], 0, rows, (2 * place.gx + 1) * width, width)
            copies.append(place.push(part, part, *self.second_sem, (index, 1, hop, 0), (other, place.me)))
        self.waiting[index] = copies

    def finish(self, index):
        for copy in self.waiting[index]:
            copy.wait_recv()


class SmallSum:
    def __init__(self, place, source, total, scratch, first_send, first_recv, second_send, second_recv):
        self.place, self.source, self.total_ref, self.scratch = place, source, total, scratch
        self.first_sem, self.second_sem = (first_send, first_recv), (second_send, second_recv)

    def begin(self):
        place = self.place
        self.waiting = [
            place.push(self.source.at[other], self.scratch.at[step], *self.first_sem, step, (place.grp, other))
            for step, other in enumerate(place.others)
        ]

    def middle(self):
        place = self.place
        value = self.source[place.me]
        for step, copy in enumerate(self.waiting):
            copy.wait_recv()
            value = value + self.scratch[step]
        self.total_ref[place.me] = value
        part = self.total_ref.at[place.me]
        self.waiting = [
            place.push(part, part, *self.second_sem, step, (place.grp, other))
            for step, other in enumerate(place.others)
        ]

    def finish(self):
        for copy in self.waiting:
            copy.wait_recv()


def small_scratch(source):
    seq_count = source.shape[0]
    dma = pltpu.SemaphoreType.DMA
    return [pltpu.VMEM((seq_count - 1,) + source.shape[1:], jnp.float32)] + [dma((seq_count - 1,))] * 4


def forward_kernel(plane, seq_count, count, *refs):
    layers = seq_count // 2
    bound_ref, qkv_ref, shards = refs[0], refs[1], refs[2:2 + count]
    refs = refs[2 + count:]
    pieces, refs = refs[0], refs[1:]
    kept_ref, mixture_ref, log_ref, fulls = refs[0], refs[1], refs[2], refs[3:3 + count]
    (
        key_scr, query_scr, value_t_scr, score_scr, mix_t_scr, mix_scr,
        send_sem, recv_sem, back_send_sem, back_recv_sem, local_sem,
    ) = refs[3 + count:14 + count]
    own_sem, first_send, first_recv, second_send, second_recv, core_send, core_recv = refs[14 + count:]
    group_count, local_rows, local_width = qkv_ref.shape[1], qkv_ref.shape[3], qkv_ref.shape[4]
    total_rows = seq_count * local_rows
    heads = local_width // HEAD_DIM
    me = lax.axis_index("seq")
    grp = lax.axis_index("grp")
    others = [lax.rem(me + step, seq_count) for step in range(1, seq_count)]
    origins = [lax.rem(me + seq_count - step, seq_count) for step in range(1, seq_count)]
    block = min(256, total_rows // 3)
    place = Place(plane, seq_count)
    enter([(grp, other) for other in others] + [(other, me) for other in place.beside + place.along])
    copies = []

    def begin_group(group):
        own = pltpu.make_async_copy(qkv_ref.at[me, group], kept_ref.at[me, group], local_sem.at[group])
        own.start()
        row = [own]
        for step, other in enumerate(others):
            copy = pltpu.make_async_remote_copy(
                qkv_ref.at[other, group], kept_ref.at[me, group],
                send_sem.at[group, step], recv_sem.at[group, step],
                device_id=(grp, other), device_id_type=MESH,
            )
            copy.start()
            row.append(copy)
        copies.append(row)

    begin_group(0)
    side = place.cols_x
    segments, _ = piece_segments(
        [shard.shape for shard in shards], side, min(shard.shape[1] for shard in shards) // side
    )
    spread = PlaneGather(
        place, shards, pieces, segments, fulls,
        own_sem, first_send, first_recv, second_send, second_recv, core_send, core_recv,
    )
    spread.begin()
    back = []
    for group in range(group_count):
        for copy in copies[group]:
            copy.wait()
        if group + 1 < group_count:
            begin_group(group + 1)
        if group == 0:
            spread.middle()
            hooks = spread.late()
            held = len(hooks) // 3
        boundary = bound_ref[group]
        keys = kept_ref[:, group, 1].reshape(total_rows, local_width)
        values = kept_ref[:, group, 2].reshape(total_rows, local_width)
        key_scr[:, :local_width] = keys
        key_scr[:, local_width:] = utter_features(boundary, total_rows, True)
        query_scr[:, local_width:] = utter_features(boundary, total_rows, False)
        value_t_scr[...] = values.astype(jnp.float32).T.astype(jnp.bfloat16)

        for head in range(heads):
            queries = kept_ref[:, group, 0].reshape(total_rows, local_width)
            query_scr[:, :local_width] = head_lanes(queries, head) * jnp.bfloat16(HEAD_DIM ** (-0.5))
            for third in range(3):
                first_key, last_key = key_span(third, total_rows)
                chunks = range(first_key, last_key, block)

                def one_block(index, carry):
                    first_row = pl.multiple_of(third * (total_rows // 3) + index * block, block)
                    query_block = query_scr[pl.ds(first_row, block), :]
                    peak = jnp.full((8, block), -jnp.inf, jnp.float32)
                    for first in chunks:
                        scores = dot_nt(key_scr[first:first + block, :], query_block)
                        score_scr[first:first + block, :] = scores
                        peak = jnp.maximum(peak, fold_rows(scores, jnp.max))
                    peak = jnp.max(peak, axis=0, keepdims=True)
                    total = jnp.zeros((8, block), jnp.float32)
                    for first in chunks:
                        lifted = jnp.exp(score_scr[first:first + block, :] - peak)
                        score_scr[first:first + block, :] = lifted
                        total = total + fold_rows(lifted, jnp.sum)
                    total = jnp.sum(total, axis=0, keepdims=True)
                    inverse = 1.0 / total
                    mixed = jnp.zeros((HEAD_DIM, block), jnp.float32)
                    rows = slice(head * HEAD_DIM, (head + 1) * HEAD_DIM)
                    for first in chunks:
                        weight = (score_scr[first:first + block, :] * inverse).astype(jnp.bfloat16)
                        mixed = mixed + dot_nn(value_t_scr[rows, first:first + block], weight)
                    mix_t_scr[rows, pl.ds(first_row, block)] = mixed
                    log_ref[group, head, :, pl.ds(first_row, block)] = peak + jnp.log(total)
                    return carry

                lax.fori_loop(0, total_rows // 3 // block, one_block, 0)
                if group > 0 and len(hooks) > held:
                    hooks.pop(0)()
        mix_scr[group] = mix_t_scr[...].T.astype(jnp.bfloat16).reshape(seq_count, local_rows, local_width)
        own = pltpu.make_async_copy(
            mix_scr.at[group, me], mixture_ref.at[me, group], local_sem.at[group_count + group]
        )
        own.start()
        back.append(own)
        for step, other in enumerate(others):
            copy = pltpu.make_async_remote_copy(
                mix_scr.at[group, other], mixture_ref.at[me, group],
                back_send_sem.at[group, step], back_recv_sem.at[group, step],
                device_id=(grp, other), device_id_type=MESH,
            )
            copy.start()
            back.append(copy)
    for hook in hooks:
        hook()
    for copy in back:
        copy.wait()
    for index in range(count):
        spread.arrive(index)
    spread.finish()


def attend_forward(bounds, qkv, shards, pieces):
    side = math.isqrt(lax.axis_size("grp"))
    hops = max(side - 1, 1)
    count = len(shards)
    dma = pltpu.SemaphoreType.DMA
    anywhere = pl.BlockSpec(memory_space=pl.ANY)
    layers = qkv.shape[0] // 2
    seq_count, group_count, _, local_rows, local_width = qkv.shape
    total_rows = seq_count * local_rows
    heads = local_width // HEAD_DIM
    block = min(256, total_rows // 3)
    vmem = pl.BlockSpec(memory_space=pltpu.VMEM)
    return pl.pallas_call(
        functools.partial(forward_kernel, (side, side), seq_count, count),
        out_shape=(
            jax.ShapeDtypeStruct(qkv.shape, jnp.bfloat16),
            jax.ShapeDtypeStruct((seq_count, group_count, local_rows, local_width), jnp.bfloat16),
            jax.ShapeDtypeStruct((group_count, heads, 1, total_rows), jnp.float32),
        ) + tuple(jax.ShapeDtypeStruct((seq_count,) + part.shape, part.dtype) for part in shards),
        in_specs=[pl.BlockSpec(memory_space=pltpu.SMEM)] + [anywhere] * (2 + count),
        out_specs=(vmem, vmem, vmem) + (anywhere,) * count,
        scratch_shapes=[
            pltpu.VMEM((total_rows, local_width + 128), jnp.bfloat16),
            pltpu.VMEM((total_rows, local_width + 128), jnp.bfloat16),
            pltpu.VMEM((local_width, total_rows), jnp.bfloat16),
            pltpu.VMEM((total_rows, block), jnp.float32),
            pltpu.VMEM((local_width, total_rows), jnp.float32),
            pltpu.VMEM((group_count, seq_count, local_rows, local_width), jnp.bfloat16),
            pltpu.SemaphoreType.DMA((group_count, seq_count - 1)),
            pltpu.SemaphoreType.DMA((group_count, seq_count - 1)),
            pltpu.SemaphoreType.DMA((group_count, seq_count - 1)),
            pltpu.SemaphoreType.DMA((group_count, seq_count - 1)),
            pltpu.SemaphoreType.DMA((2 * group_count,)),
            dma((count, layers, 2, 2)),
            dma((count, layers - 1, 2, hops, 2)), dma((count, layers - 1, 2, hops, 2)),
            dma((count, layers - 1, 2, hops, side)), dma((count, layers - 1, 2, hops, side)),
            dma((count, layers)), dma((count, layers)),
        ],
        compiler_params=pltpu.CompilerParams(
            collective_id=1, has_side_effects=True, vmem_limit_bytes=48 * 1024 * 1024
        ),
        name="attend_forward",
    )(bounds, qkv, *shards, pieces)


def backward_kernel(plane, seq_count, count, *refs):
    layers = seq_count // 2
    bound_ref, kept_ref, grad_ref, log_ref = refs[:4]
    parts, given, refs = refs[4:4 + count], refs[4 + count:4 + 2 * count], refs[4 + 2 * count:]
    out_ref, refs = refs[0], refs[1:]
    pieces, refs = refs[0], refs[1:]
    (
        taken_scr, key_scr, query_scr, key_t_scr, head_query_scr, head_grad_scr, prob_scr, weight_scr,
        query_t_scr, key_sum_scr, value_sum_scr, back_scr,
        send_sem, recv_sem, back_send_sem, back_recv_sem, local_sem,
    ) = refs[:17]
    buffers, semaphores = refs[17:17 + 6 * count], refs[17 + 6 * count:]
    group_count, local_rows, local_width = grad_ref.shape[1], grad_ref.shape[2], grad_ref.shape[3]
    total_rows = seq_count * local_rows
    heads = local_width // HEAD_DIM
    me = lax.axis_index("seq")
    grp = lax.axis_index("grp")
    others = [lax.rem(me + step, seq_count) for step in range(1, seq_count)]
    block = min(256, total_rows // 3)
    place = Place(plane, seq_count)
    enter([(grp, other) for other in others] + [(other, me) for other in place.beside + place.along])
    copies = []

    def begin_group(group):
        own = pltpu.make_async_copy(grad_ref.at[me, group], taken_scr.at[me, group], local_sem.at[group])
        own.start()
        row = [own]
        for step, other in enumerate(others):
            copy = pltpu.make_async_remote_copy(
                grad_ref.at[other, group], taken_scr.at[me, group],
                send_sem.at[group, step], recv_sem.at[group, step],
                device_id=(grp, other), device_id_type=MESH,
            )
            copy.start()
            row.append(copy)
        copies.append(row)

    begin_group(0)
    side = place.cols_x
    segments, _ = piece_segments(
        [part.shape[1:] for part in parts], side, min(part.shape[2] for part in parts) // side
    )
    plane_sum = PlaneSum(
        place, parts, [[pieces.at[step] for step in range(layers)]] * count, segments, buffers, semaphores,
        given=given,
    )
    plane_sum.begin()
    firsts = plane_sum.steps(plane_sum.first)
    seconds = plane_sum.steps(plane_sum.second)
    units = 3 * heads * group_count
    plan = [[] for _ in range(units + 1)]
    for spot, hook in enumerate(seconds):
        plan[min(PLAN_FIRST + spot * PLAN_RATE // 4, units)].append(hook)
    for hook in firsts:
        hook()
    back = []
    for group in range(group_count):
        for copy in copies[group]:
            copy.wait()
        if group + 1 < group_count:
            begin_group(group + 1)
        boundary = bound_ref[group]
        keys = kept_ref[:, group, 1].reshape(total_rows, local_width)
        key_scr[:, :local_width] = keys
        key_scr[:, local_width:] = utter_features(boundary, total_rows, True)
        query_scr[:, local_width:] = utter_features(boundary, total_rows, False)
        key_t_scr[...] = keys.astype(jnp.float32).T.astype(jnp.bfloat16)
        key_sum_scr[...] = jnp.zeros_like(key_sum_scr)
        value_sum_scr[...] = jnp.zeros_like(value_sum_scr)

        for head in range(heads):
            queries = head_lanes(kept_ref[:, group, 0].reshape(total_rows, local_width), head)
            head_query_scr[...] = queries
            query_scr[:, :local_width] = queries * jnp.bfloat16(HEAD_DIM ** (-0.5))
            head_grad_scr[...] = head_lanes(taken_scr[:, group].reshape(total_rows, local_width), head)
            for third in range(3):
                first_key, last_key = key_span(third, total_rows)
                chunks = range(first_key, last_key, block)

                def one_block(index, carry):
                    first_row = pl.multiple_of(third * (total_rows // 3) + index * block, block)
                    own_rows = pl.ds(first_row, block)
                    query_block = query_scr[own_rows, :]
                    grad_block = head_grad_scr[own_rows, :]
                    plain_block = head_query_scr[own_rows, :]
                    log_block = log_ref[group, head, :, own_rows]
                    row_dot = jnp.zeros((8, block), jnp.float32)
                    for first in chunks:
                        scores = dot_nt(key_scr[first:first + block, :], query_block)
                        prob = jnp.exp(scores - log_block)
                        values = kept_ref[
                            first // local_rows:(first + block - 1) // local_rows + 1, group, 2
                        ].reshape(-1, local_width)
                        skip = first % local_rows
                        weight_grad = dot_nt(values[skip:skip + block], grad_block)
                        prob_scr[first:first + block, :] = prob
                        weight_scr[first:first + block, :] = weight_grad
                        row_dot = row_dot + fold_rows(prob * weight_grad, jnp.sum)
                    row_dot = jnp.sum(row_dot, axis=0, keepdims=True)
                    rows = slice(head * HEAD_DIM, (head + 1) * HEAD_DIM)
                    turned = jnp.zeros((HEAD_DIM, block), jnp.float32)
                    for first in chunks:
                        prob = prob_scr[first:first + block, :]
                        score_grad = (
                            HEAD_DIM ** (-0.5) * (prob * (weight_scr[first:first + block, :] - row_dot))
                        ).astype(jnp.bfloat16)
                        key_sum_scr[first:first + block, :] += dot_nn(score_grad, plain_block)
                        value_sum_scr[first:first + block, :] += dot_nn(
                            prob.astype(jnp.bfloat16), grad_block
                        )
                        turned = turned + dot_nn(key_t_scr[rows, first:first + block], score_grad)
                    query_t_scr[rows, own_rows] = turned
                    return carry

                lax.fori_loop(0, total_rows // 3 // block, one_block, 0)
                for hook in plan.pop(0):
                    hook()
        shape = (seq_count, local_rows, local_width)
        back_scr[:, group, 0] = query_t_scr[...].T.astype(jnp.bfloat16).reshape(shape)
        back_scr[:, group, 1] = key_sum_scr[...].astype(jnp.bfloat16).reshape(shape)
        back_scr[:, group, 2] = value_sum_scr[...].astype(jnp.bfloat16).reshape(shape)
        own = pltpu.make_async_copy(
            back_scr.at[me, group], out_ref.at[me, group], local_sem.at[group_count + group]
        )
        own.start()
        back.append(own)
        for step, other in enumerate(others):
            copy = pltpu.make_async_remote_copy(
                back_scr.at[other, group], out_ref.at[me, group],
                back_send_sem.at[group, step], back_recv_sem.at[group, step],
                device_id=(grp, other), device_id_type=MESH,
            )
            copy.start()
            back.append(copy)
    for hook in plan[0] + plane_sum.steps(plane_sum.third):
        hook()
    for copy in back:
        copy.wait()
    plane_sum.finish()


def attend_backward(bounds, kept, grad, log_total, parts, given):
    side = math.isqrt(lax.axis_size("grp"))
    count = len(parts)
    layers = kept.shape[0] // 2
    anywhere = pl.BlockSpec(memory_space=pl.ANY)
    width = min(part.shape[2] for part in parts) // side
    _, piece_rows = piece_segments([part.shape[1:] for part in parts], side, width)
    seq_count, group_count, _, local_rows, local_width = kept.shape
    total_rows = seq_count * local_rows
    block = min(256, total_rows // 3)
    vmem = pl.BlockSpec(memory_space=pltpu.VMEM)
    return pl.pallas_call(
        functools.partial(backward_kernel, (side, side), seq_count, count),
        out_shape=(jax.ShapeDtypeStruct(kept.shape, jnp.bfloat16),) + tuple(
            jax.ShapeDtypeStruct((layers, piece_rows, width), jnp.bfloat16) for _ in range(1)
        ),
        in_specs=[pl.BlockSpec(memory_space=pltpu.SMEM), vmem, anywhere, vmem] + [anywhere] * (2 * count),
        out_specs=(vmem,) * 2,
        scratch_shapes=[
            pltpu.VMEM(grad.shape, jnp.bfloat16),
            pltpu.VMEM((total_rows, local_width + 128), jnp.bfloat16),
            pltpu.VMEM((total_rows, local_width + 128), jnp.bfloat16),
            pltpu.VMEM((local_width, total_rows), jnp.bfloat16),
            pltpu.VMEM((total_rows, local_width), jnp.bfloat16),
            pltpu.VMEM((total_rows, local_width), jnp.bfloat16),
            pltpu.VMEM((total_rows, block), jnp.float32),
            pltpu.VMEM((total_rows, block), jnp.float32),
            pltpu.VMEM((local_width, total_rows), jnp.float32),
            pltpu.VMEM((total_rows, local_width), jnp.float32),
            pltpu.VMEM((total_rows, local_width), jnp.float32),
            pltpu.VMEM(kept.shape, jnp.bfloat16),
            pltpu.SemaphoreType.DMA((group_count, seq_count - 1)),
            pltpu.SemaphoreType.DMA((group_count, seq_count - 1)),
            pltpu.SemaphoreType.DMA((group_count, seq_count - 1)),
            pltpu.SemaphoreType.DMA((group_count, seq_count - 1)),
            pltpu.SemaphoreType.DMA((2 * group_count,)),
        ] + plane_sum_scratch(parts, side),
        compiler_params=pltpu.CompilerParams(
            collective_id=2, has_side_effects=True, vmem_limit_bytes=62 * 1024 * 1024
        ),
        name="attend_backward",
    )(bounds, kept, grad, log_total, *parts, *given)


class LineChain:
    def __init__(self, place, sources, slots, sends, recvs):
        self.place, self.sources, self.slots = place, sources, slots
        self.sends, self.recvs = sends, recvs
        self.pushed = []
        middle = []
        low, high = 0, place.layers - 2
        while low <= high:
            middle += [low] if low == high else [low, high]
            low, high = low + 1, high - 1
        first, last = place.layer == 0, place.layer == place.layers - 1
        self.ranks = [
            jnp.where(first, place.layers - 2 - rank, jnp.where(last, rank, step)).astype(jnp.int32)
            for rank, step in enumerate(middle)
        ]

    def owner(self, step):
        place = self.place
        return lax.rem(place.layer + place.layers - 1 - step, place.layers) * 2 + place.core

    def copy(self, index, source, owner, slot, target, send_slot):
        return pltpu.make_async_remote_copy(
            source, self.slots(index, owner, slot),
            self.sends.at[index, send_slot], self.recvs.at[index, slot],
            device_id=(self.place.grp, target * 2 + self.place.core), device_id_type=MESH,
        )

    def push(self, when, *given):
        self.pushed.append((when, given))

        @pl.when(when)
        def _():
            self.copy(*given).start()

    def begin(self, index):
        place = self.place
        source = self.sources[index]
        self.push(place.layer < place.layers - 1, index, source, place.me, 0, place.layer + 1, 0)
        self.push(place.layer > 0, index, source, place.me, place.layers - 2, place.layer - 1, 1)

    def forward(self, index, rank):
        place = self.place
        step = self.ranks[rank]
        owner = self.owner(step)
        held = self.slots(index, owner, step)
        self.copy(index, held, owner, step, place.layer, 0).wait_recv()
        below = step < place.layer
        going = (below & (place.layer < place.layers - 1)) | ((step >= place.layer) & (place.layer > 0))
        slot = jnp.where(below, step + 1, step - 1)
        target = jnp.where(below, place.layer + 1, place.layer - 1)
        self.push(going, index, held, owner, slot, target, rank + 2)
        return owner

    def sent(self):
        for when, given in self.pushed:

            @pl.when(when)
            def _(given=given):
                self.copy(*given).wait_send()


class WholeGather(PlaneGather):
    def __init__(self, place, shards, fulls, line_send, line_recv, *semaphores):
        super().__init__(place, shards, None, None, fulls, *semaphores)

        def piece(ref, index):
            rows, height, width = self.sizes(index)
            return window(ref, place.gy * height, height, 2 * place.gx * width, 2 * width)

        self.chain = LineChain(
            place, [piece(shard, index) for index, shard in enumerate(shards)],
            lambda index, owner, slot: piece(fulls[index].at[owner], index), line_send, line_recv,
        )
        self.jobs = [(index, rank) for index in range(len(shards)) for rank in range(place.layers - 1)]

    def owner(self, step):
        return self.chain.owner(self.chain.ranks[step])

    def begin(self):
        place = self.place
        for index in range(len(self.shards)):
            self.chain.begin(index)
        for index, shard in enumerate(self.shards):
            copy = pltpu.make_async_copy(shard, self.fulls[index].at[place.me], self.own_sem.at[index, place.layers - 1, 0, 0])
            copy.start()
            push = place.push(shard, self.fulls[index].at[place.me], *self.core, (index, 0), (place.grp, place.partner))
            self.own.append((copy, push))

    def spread_first(self, index, step):
        place = self.place
        rows, height, width = self.sizes(index)
        full = self.fulls[index].at[self.chain.forward(index, step)]
        row, col = place.gy * height, 2 * place.gx * width
        self.waiting[index, step] = []
        for half, partners in enumerate((place.beside, place.along)):
            part = window(full, row, height, col + half * width, width)
            for hop, other in enumerate(partners):
                self.waiting[index, step].append(
                    place.push(part, part, *self.first, (index, step, half, hop, 0), (other, place.me))
                )

    def finish(self):
        super().finish()
        self.chain.sent()


def turn_lanes(values, cos, sin):
    lane = lax.broadcasted_iota(jnp.int32, values.shape, 1)
    ahead = pltpu.roll(values, values.shape[1] - HEAD_DIM // 2, 1)
    behind = pltpu.roll(values, HEAD_DIM // 2, 1)
    other = jnp.where(lax.rem(lane, HEAD_DIM) < HEAD_DIM // 2, ahead, behind)
    return values * cos + other * sin


def second_mask(bound_ref, group, me, local_rows, first, rows):
    row = lax.broadcasted_iota(jnp.int32, (rows, 1), 0) + (me * local_rows + first)
    return row >= bound_ref[group]


def centered(values):
    center = values - jnp.mean(values, axis=-1, keepdims=True)
    scale = lax.rsqrt(jnp.mean(center * center, axis=-1, keepdims=True) + epsilon)
    return center * scale, scale


def front_kernel(plane, seq_count, late_count, *refs):
    layers = seq_count // 2
    bound_ref, frames_ref, shortcut_ref, ladder_ref, kept_ref, token_ref, modulation_ref = refs[:7]
    shards, late_shards, refs = refs[7:9], refs[9:9 + late_count], refs[9 + late_count:]
    fulls_out, late_out, refs = refs[:2], refs[2], refs[3:]
    hidden_ref, normed_ref, qkv_ref, cos_ref, sin_ref, mods_ref, scale_ref, tokens_ref = refs[:8]
    partial_ref, total_ref, refs = refs[8], refs[9], refs[10:]
    fulls, refs = refs[:2], refs[2:]
    token_scr, token_send, token_recv, out_sem = refs[:4]
    small_refs, (late_scr, late_send, late_recv, late_sem), refs = refs[4:9], refs[9:13], refs[13:]
    group_count, local_rows, local_width = qkv_ref.shape[1], qkv_ref.shape[3], qkv_ref.shape[4]
    row_count, width = hidden_ref.shape
    rows_all = plane[0] * plane[1]
    place = Place(plane, seq_count)
    me = place.me
    enter([(place.grp, other) for other in place.others] + [(other, me) for other in place.groups])
    whole = WholeGather(place, shards, fulls, *refs)
    whole.begin()
    block = partial_ref.shape[1]
    partial_ref[...] = jnp.zeros_like(partial_ref)
    shard_rows = modulation_ref.shape[0]
    factor = token_ref[:, :shard_rows].astype(jnp.bfloat16)
    for part in range(6):
        found = dot_nn(factor, modulation_ref[:, part * width:(part + 1) * width])
        for utter in range(2 * group_count):
            spot = utter * 6 + part
            partial_ref[spot // block, spot % block:spot % block + 1, :] = found[utter:utter + 1, :]
    kept = jnp.sum(jnp.sum(kept_ref[...], axis=1, keepdims=True), axis=0, keepdims=True)
    partial_ref[seq_count - 1, block - 1:block, :] = jnp.broadcast_to(kept, (1, width))
    small = SmallSum(place, partial_ref, total_ref, *small_refs)
    small.begin()
    for group in range(group_count):
        rows = slice(group * local_rows, (group + 1) * local_rows)
        frame = lax.broadcasted_iota(jnp.int32, (local_rows, 1), 0) + me * local_rows
        place_in = frame - jnp.where(frame >= bound_ref[group], bound_ref[group], 0)
        angles = place_in.astype(jnp.float32) * ladder_ref[0:1, :]
        cos_ref[rows, :] = jnp.cos(angles)
        sin_ref[rows, :] = jnp.sin(angles) * ladder_ref[1:2, :]
    side = place.cols_x
    cut = late_scr.shape[1]
    late_own, base = [], 0
    for index, shard in enumerate(late_shards):
        height, cols = shard.shape[0] // side, shard.shape[1] // side
        for spot in range(cols // cut):
            late_own.append(pltpu.make_async_copy(
                window(shard, place.gy * height, height, place.gx * cols + spot * cut, cut),
                late_scr.at[pl.ds(base, height), :],
                late_sem.at[len(late_own)],
            ))
            late_own[-1].start()
            base += height
    late_chain = LineChain(place, [late_scr], lambda index, owner, slot: late_out.at[slot], late_send, late_recv)
    combine_jobs = [job for job in whole.jobs if job[0] == 0]
    projection_jobs = [job for job in whole.jobs if job[0] == 1]
    for job in combine_jobs:
        whole.spread_first(*job)
    for job, late in zip(combine_jobs, projection_jobs):
        whole.spread_second(*job)
        whole.spread_first(*late)
    for copy in late_own:
        copy.wait()
    late_chain.begin(0)
    small.middle()
    for job, late in zip(combine_jobs, projection_jobs):
        whole.over_core(*job)
        whole.spread_second(*late)
    whole.arrive(0)
    outs = [pltpu.make_async_copy(fulls[0], fulls_out[0], out_sem.at[0])]
    outs[0].start()
    late_chain.forward(0, 0)
    half = seq_count // 2

    def hidden_tile(index, carry):
        at = pl.ds(pl.multiple_of(index * 256, 256), 256)
        upper = fulls[0][0:half, :, at].reshape(width, 256)
        lower = fulls[0][half:seq_count, :, at].reshape(width, 256)
        hidden_ref[:, at] = dot_nn(frames_ref[...], upper) + dot_nn(shortcut_ref[...], lower)
        return carry

    lax.fori_loop(0, width // 256, hidden_tile, 0)
    small.finish()
    last = total_ref.shape[1] - 1
    token_scr[...] = token_ref[...]
    token_scr[4:5, :] = total_ref[seq_count - 1, last:last + 1, :128]
    tokens_ref[place.grp] = token_scr[...]
    tokens = [
        place.push(token_scr, tokens_ref.at[place.grp], token_send, token_recv, step, (other, me))
        for step, other in enumerate(place.groups)
    ]
    for spot in range(seq_count):
        mods_ref[spot * block:(spot + 1) * block, :] = total_ref[spot]

    def vector(group, part, second):
        def row(utter):
            at = (group * 2 + utter) * 6 + part
            return mods_ref[at:at + 1, :]

        return jnp.where(second, row(1), row(0))

    chunk = 32
    for group in range(group_count):

        def norm_rows(index, carry):
            first = pl.multiple_of(index * chunk, chunk)
            at = pl.ds(pl.multiple_of(group * local_rows + first, chunk), chunk)
            second = second_mask(bound_ref, group, me, local_rows, first, chunk)
            normal, _ = centered(hidden_ref[at, :])
            normed_ref[at, :] = (
                normal * (1.0 + vector(group, 1, second)) + vector(group, 0, second)
            ).astype(jnp.bfloat16)
            return carry

        lax.fori_loop(0, local_rows // chunk, norm_rows, 0)
    for job in projection_jobs:
        whole.over_core(*job)
    whole.arrive(1)
    late_chain.forward(0, 1)
    outs.append(pltpu.make_async_copy(fulls[1], fulls_out[1], out_sem.at[1]))
    outs[1].start()
    each = 256 // local_width

    def head_tile(index, carry):
        for kind in range(3):
            at = pl.ds(pl.multiple_of(kind * width + index * 256, 256), 256)
            packed = dot_nn(normed_ref[...], fulls[1][:, :, at].reshape(width, 256))
            for half in range(2):
                lanes = packed[:, half * 128:(half + 1) * 128]
                if kind < 2:
                    lanes = turn_lanes(lanes, cos_ref[...], sin_ref[...])
                lanes = lanes.astype(jnp.bfloat16)
                for spot in range(each // 2):
                    cut = lanes[:, spot * local_width:(spot + 1) * local_width]
                    for group in range(group_count):
                        qkv_ref[index * each + half * (each // 2) + spot, group, kind] = cut[
                            group * local_rows:(group + 1) * local_rows
                        ]
        return carry

    lax.fori_loop(0, width // 256, head_tile, 0)
    for rank in range(2, layers - 1):
        late_chain.forward(0, rank)
    whole.finish()
    late_chain.sent()
    for copy in tokens:
        copy.wait_recv()
    kept = tokens_ref[0, 4:5, :]
    for group in range(1, rows_all):
        kept = kept + tokens_ref[group, 4:5, :]
    frames_all = float(rows_all * group_count * local_rows * seq_count)
    scale_ref[...] = jnp.broadcast_to(frames_all / kept, scale_ref.shape)
    for copy in outs:
        copy.wait()


def front(bounds, frames, shortcut, ladder, kept, token, modulation, combine, projection, late_shards):
    grp_count = lax.axis_size("grp")
    seq_count = lax.axis_size("seq")
    side = math.isqrt(grp_count)
    layers = seq_count // 2
    anywhere = pl.BlockSpec(memory_space=pl.ANY)
    vmem = pl.BlockSpec(memory_space=pltpu.VMEM)
    dma = pltpu.SemaphoreType.DMA
    hops = max(side - 1, 1)
    shards = (combine, projection)
    group_count = bounds.shape[0]
    row_count, width = frames.shape
    low, full = jnp.bfloat16, jnp.float32
    cut = min(shard.shape[1] for shard in late_shards) // side
    late_rows = sum(shard.shape[0] // side * (shard.shape[1] // side // cut) for shard in late_shards)
    most = max(shard.shape[1] // side // cut for shard in late_shards)
    small = jax.ShapeDtypeStruct((seq_count, 32 // seq_count, width), full)
    wholes = [(seq_count,) + part.shape for part in shards]
    return pl.pallas_call(
        functools.partial(front_kernel, (side, side), seq_count, len(late_shards)),
        out_shape=tuple(jax.ShapeDtypeStruct(shape, low) for shape in wholes) + (
            jax.ShapeDtypeStruct((layers - 1, late_rows, cut), low),
            jax.ShapeDtypeStruct((row_count, width), full),
            jax.ShapeDtypeStruct((row_count, width), low),
            jax.ShapeDtypeStruct(
                (seq_count, group_count, 3, row_count // group_count, width // seq_count), low
            ),
            jax.ShapeDtypeStruct((row_count, 128), full),
            jax.ShapeDtypeStruct((row_count, 128), full),
            jax.ShapeDtypeStruct((32, width), full),
            jax.ShapeDtypeStruct(token.shape, full),
            jax.ShapeDtypeStruct((grp_count,) + token.shape, full),
        ),
        in_specs=[pl.BlockSpec(memory_space=pltpu.SMEM)] + [vmem] * 6 + [anywhere] * (2 + len(late_shards)),
        out_specs=(anywhere,) * 3 + (vmem,) * 8,
        scratch_shapes=[pltpu.VMEM(small.shape, full)] * 2 + [pltpu.VMEM(shape, low) for shape in wholes] + [
            pltpu.VMEM(token.shape, full), dma((grp_count - 1,)), dma((grp_count - 1,)), dma((2,)),
        ] + small_scratch(small) + [
            pltpu.VMEM((late_rows, cut), low),
            dma((1, layers + 1)), dma((1, layers - 1)), dma((len(late_shards) * most,)),
            dma((2, layers + 1)), dma((2, layers - 1)),
            dma((2, layers, 1, 1)),
            dma((2, layers - 1, 2, hops, 1)), dma((2, layers - 1, 2, hops, 1)),
            dma((2, layers - 1, 2, hops, side)), dma((2, layers - 1, 2, hops, side)),
            dma((2, layers)), dma((2, layers)),
        ],
        compiler_params=pltpu.CompilerParams(
            collective_id=3, has_side_effects=True, vmem_limit_bytes=62 * 1024 * 1024
        ),
        name="front",
    )(bounds, frames, shortcut, ladder, kept, token, modulation, *shards, *late_shards)


def middle_kernel(plane, seq_count, *refs):
    (
        bound_ref, mixture_ref, hidden_ref, target_ref, kept_ref, mods_ref, scale_ref,
        readout_ref, expand_ref, contract_ref,
    ) = refs[:10]
    result_ref, middle_grad_ref, mixture_grad_ref, late_ref = refs[10:14]
    own_parts, swapped_parts, refs = refs[14:17], refs[17:20], refs[20:]
    (
        readout_scr, expand_scr, contract_scr, mixture_scr, branch_scr, middle_scr, normed_scr, slope_scr, active_scr,
        active_t_scr, wide_scr, grad_scr, low_scr, left_t_scr, stage_scr, value_scr, weight_sem, stage_sem,
        swap_send, swap_recv,
    ) = refs
    row_count, width = hidden_ref.shape
    wide = expand_ref.shape[1]
    group_count = mixture_ref.shape[1]
    local_rows = row_count // group_count
    local_width = width // seq_count
    place = Place(plane, seq_count)
    me = place.me
    enter([(place.grp, place.partner)])
    weights = [
        pltpu.make_async_copy(source, scratch, weight_sem.at[index])
        for index, (source, scratch) in enumerate(
            ((readout_ref, readout_scr), (expand_ref, expand_scr), (contract_ref, contract_scr))
        )
    ]
    weights[0].start()
    for source in range(seq_count):
        for group in range(group_count):
            mixture_scr[
                group * local_rows:(group + 1) * local_rows, source * local_width:(source + 1) * local_width
            ] = mixture_ref[source, group]
    chunk = 32
    tile = 256

    def tiles(count, body):
        def one(index, carry):
            body(pl.ds(pl.multiple_of(index * tile, tile), tile))
            return carry

        lax.fori_loop(0, count // tile, one, 0)

    def chunks(body, many):
        sums = []
        for group in range(group_count):

            def one(index, carry, group=group):
                first = pl.multiple_of(index * chunk, chunk)
                at = pl.ds(pl.multiple_of(group * local_rows + first, chunk), chunk)
                second = second_mask(bound_ref, group, me, local_rows, first, chunk)

                def vector(part):
                    row = group * 12 + part
                    return jnp.where(second, mods_ref[row + 6:row + 7, :], mods_ref[row:row + 1, :])

                later = second.astype(jnp.float32)
                found = body(at, vector)
                out = []
                for spot, value in enumerate(found):
                    late = value * later
                    out.append(carry[2 * spot] + fold_rows(value - late, jnp.sum))
                    out.append(carry[2 * spot + 1] + fold_rows(late, jnp.sum))
                return tuple(out)

            zero = jnp.zeros((8, width), jnp.float32)
            sums.append(lax.fori_loop(0, local_rows // chunk, one, (zero,) * (2 * many)))
        return sums

    def put(part, spot, sums):
        for group in range(group_count):
            for utter in range(2):
                row = part * 2 * group_count + group * 2 + utter
                late_ref[row:row + 1, :] = jnp.sum(sums[group][2 * spot + utter], axis=0, keepdims=True)

    weights[0].wait()
    weights[1].start()
    weights[2].start()
    tiles(width, lambda at: branch_scr.__setitem__((slice(None), at), dot_nn(mixture_scr[...], readout_scr[:, at])))

    def second_norm(at, vector):
        middle = hidden_ref[at, :] + vector(2) * branch_scr[at, :]
        middle_scr[at, :] = middle
        normal, _ = centered(middle)
        normed_scr[at, :] = (normal * (1.0 + vector(4)) + vector(3)).astype(jnp.bfloat16)
        return ()

    chunks(second_norm, 0)
    weights[1].wait()

    def expand_dot(index, slot):
        at = pl.ds(pl.multiple_of(jnp.minimum(index, wide // tile - 1) * tile, tile), tile)
        value_scr[slot] = dot_nn(normed_scr[...], expand_scr[:, at])

    def bend(index, slot):
        at = pl.ds(pl.multiple_of(index * tile, tile), tile)
        value = value_scr[slot]
        square = value * value
        factor = (2.0 / math.pi) ** 0.5
        bent = jnp.tanh(value * (factor + (factor * 0.044715) * square))
        half = 0.5 + 0.5 * bent
        active_scr[:, at] = (value * half).astype(jnp.bfloat16)
        slope_scr[:, at] = half + (0.5 * value * (1.0 - bent * bent)) * (factor + (factor * 3 * 0.044715) * square)

    def expand_pair(index, carry):
        expand_dot(2 * index + 1, 1)
        bend(2 * index, 0)
        expand_dot(2 * index + 2, 0)
        bend(2 * index + 1, 1)
        return carry

    expand_dot(0, 0)
    lax.fori_loop(0, wide // tile // 2, expand_pair, 0)
    weights[2].wait()
    tiles(width, lambda at: grad_scr.__setitem__((slice(None), at), dot_nn(active_scr[...], contract_scr[:, at])))
    loss_scale = scale_ref[0:1, 0:1]

    def close(at, vector):
        contracted = grad_scr[at, :]
        gate = vector(5)
        output = middle_scr[at, :] + gate * contracted
        result_ref[at, :] = output.astype(jnp.bfloat16)
        output_grad = loss_scale * kept_ref[at, :] * (output - target_ref[at, :].astype(jnp.float32))
        middle_grad_ref[at, :] = output_grad
        low_scr[at, :] = (gate * output_grad).astype(jnp.bfloat16)
        return (output_grad * contracted,)

    put(3, 0, chunks(close, 1))
    pushed = []

    def share_out(number, left, right, across):
        own, swapped = own_parts[number], swapped_parts[number]
        layers, rows, columns = own.shape
        many = columns // width if across else layers * 2 * rows // width
        each = width // (2 * rows)
        out = {}
        for block in range(many):
            slot = block % 2
            if block >= 2:
                for copy, push in out[block - 2]:
                    copy.wait()
                    push.wait_send()

            def one(index, carry, block=block, slot=slot):
                at = pl.ds(pl.multiple_of(index * tile, tile), tile)
                first = left[...] if across else left[block * width:(block + 1) * width, :]
                lanes = pl.ds(pl.multiple_of(index * tile + (block * width if across else 0), tile), tile)
                stage_scr[slot, :, at] = dot_nn(first, right[:, lanes]).astype(jnp.bfloat16)
                return carry

            lax.fori_loop(0, width // tile, one, 0)
            out[block] = []
            for spot in range(each):
                layer = spot if across else block * each + spot
                lanes = pl.ds(block * width if across else 0, width)
                mine = stage_scr.at[slot, pl.ds(pl.multiple_of((2 * spot + place.core) * rows, rows), rows), :]
                other = stage_scr.at[slot, pl.ds(pl.multiple_of((2 * spot + 1 - place.core) * rows, rows), rows), :]
                copy = pltpu.make_async_copy(mine, own.at[layer, :, lanes], stage_sem.at[slot, spot])
                copy.start()
                push = pltpu.make_async_remote_copy(
                    other, swapped.at[layer, :, lanes],
                    swap_send.at[number, block, spot], swap_recv.at[number, block, spot],
                    device_id=(place.grp, place.partner), device_id_type=MESH,
                )
                push.start()
                pushed.append(push)
                out[block].append((copy, push))
        return [pair for block in range(max(many - 2, 0), many) for pair in out[block]]

    def drain(pairs):
        for copy, push in pairs:
            copy.wait()
            push.wait_send()

    def active_dot(index, slot):
        at = pl.ds(pl.multiple_of(jnp.minimum(index, wide // tile - 1) * tile, tile), tile)
        value_scr[slot] = dot_nt(low_scr[...], contract_scr[at, :])

    def unbend(index, slot):
        at = pl.ds(pl.multiple_of(index * tile, tile), tile)
        active_t_scr[at, :] = active_scr[:, at].T
        wide_scr[:, at] = (value_scr[slot] * slope_scr[:, at]).astype(jnp.bfloat16)

    def active_pair(index, carry):
        active_dot(2 * index + 1, 1)
        unbend(2 * index, 0)
        active_dot(2 * index + 2, 0)
        unbend(2 * index + 1, 1)
        return carry

    active_dot(0, 0)
    lax.fori_loop(0, wide // tile // 2, active_pair, 0)

    out = share_out(0, active_t_scr, low_scr, False)
    tiles(width, lambda at: grad_scr.__setitem__((slice(None), at), dot_nt(wide_scr[...], expand_scr[at, :])))
    tiles(width, lambda at: left_t_scr.__setitem__(
        (at, slice(None)), normed_scr[:, at].astype(jnp.float32).T.astype(jnp.bfloat16)
    ))

    drain(out)
    out = share_out(1, left_t_scr, wide_scr, True)

    def norm_back(at, vector):
        grad = grad_scr[at, :]
        normal, scale = centered(middle_scr[at, :])
        inner = grad * (1.0 + vector(4))
        turned = scale * (
            inner
            - jnp.mean(inner, axis=-1, keepdims=True)
            - normal * jnp.mean(inner * normal, axis=-1, keepdims=True)
        )
        middle_grad = middle_grad_ref[at, :] + turned
        middle_grad_ref[at, :] = middle_grad
        low_scr[at, :] = (vector(2) * middle_grad).astype(jnp.bfloat16)
        return middle_grad * branch_scr[at, :], grad, grad * normal

    sums = chunks(norm_back, 3)
    for spot in range(3):
        put(spot, spot, sums)

    def mixture_tile(at):
        left_t_scr[at, :] = mixture_scr[:, at].astype(jnp.float32).T.astype(jnp.bfloat16)
        grad_scr[:, at] = dot_nt(low_scr[...], readout_scr[at, :])

    tiles(width, mixture_tile)
    for source in range(seq_count):
        for group in range(group_count):
            mixture_grad_ref[source, group] = grad_scr[
                group * local_rows:(group + 1) * local_rows, source * local_width:(source + 1) * local_width
            ].astype(jnp.bfloat16)

    drain(out)
    drain(share_out(2, left_t_scr, low_scr, True))
    for push in pushed:
        push.wait_recv()


def middle(bounds, mixture, hidden, target, kept, mods, loss_scale, readout, expand, contract):
    seq_count, group_count, local_rows, local_width = mixture.shape
    row_count, width = hidden.shape
    wide = expand.shape[1]
    layers = seq_count // 2
    side = math.isqrt(lax.axis_size("grp"))
    anywhere = pl.BlockSpec(memory_space=pl.ANY)
    vmem = pl.BlockSpec(memory_space=pltpu.VMEM)
    smem = pl.BlockSpec(memory_space=pltpu.SMEM)
    low, full = jnp.bfloat16, jnp.float32
    dma = pltpu.SemaphoreType.DMA
    return pl.pallas_call(
        functools.partial(middle_kernel, (side, side), seq_count),
        out_shape=(
            jax.ShapeDtypeStruct((row_count, width), low),
            jax.ShapeDtypeStruct((row_count, width), full),
            jax.ShapeDtypeStruct(mixture.shape, low),
            jax.ShapeDtypeStruct((8 * group_count, width), full),
        ) + tuple(
            jax.ShapeDtypeStruct((layers, weight.shape[0] // seq_count, weight.shape[1]), low)
            for _ in range(2) for weight in (contract, expand, readout)
        ),
        in_specs=[smem] + [vmem] * 6 + [anywhere] * 3,
        out_specs=(vmem,) * 4 + (anywhere,) * 6,
        scratch_shapes=[
            pltpu.VMEM(readout.shape, low),
            pltpu.VMEM(expand.shape, low),
            pltpu.VMEM(contract.shape, low),
            pltpu.VMEM((row_count, width), low),
            pltpu.VMEM((row_count, width), full),
            pltpu.VMEM((row_count, width), full),
            pltpu.VMEM((row_count, width), low),
            pltpu.VMEM((row_count, wide), full),
            pltpu.VMEM((row_count, wide), low),
            pltpu.VMEM((wide, row_count), low),
            pltpu.VMEM((row_count, wide), low),
            pltpu.VMEM((row_count, width), full),
            pltpu.VMEM((row_count, width), low),
            pltpu.VMEM((width, row_count), low),
            pltpu.VMEM((2, width, width), low),
            pltpu.VMEM((2, row_count, 256), full),
            dma((3,)),
            dma((2, layers)),
            dma((3, wide // width, layers)), dma((3, wide // width, layers)),
        ],
        compiler_params=pltpu.CompilerParams(
            collective_id=5, has_side_effects=True, vmem_limit_bytes=62 * 1024 * 1024
        ),
        name="feed_forward",
    )(bounds, mixture, hidden, target, kept, mods, loss_scale, readout, expand, contract)


def back_kernel(plane, seq_count, *refs):
    layers = seq_count // 2
    (
        bound_ref, back_ref, cos_ref, sin_ref, normed_ref, hidden_ref, middle_ref, frames_ref, shortcut_ref,
        combine_ref, projection_ref, mods_ref, late_ref, modulation_ref,
    ) = refs[:14]
    finished, refs = refs[14], refs[15:]
    frames_out, shortcut_out, outs, refs = refs[0], refs[1], refs[2:7], refs[7:]
    utters_ref, conditions_ref, refs = refs[0], refs[1], refs[2:]
    (
        packed_scr, combine_scr, projection_scr, normed_t_scr, joined_t_scr, grad_scr, low_scr,
        shortcut_scr, total_ref, utter_scr, flat_scr, condition_scr,
    ) = refs[:12]
    frames_scr = grad_scr
    parts, line_refs, refs = refs[12:14], refs[14:20], refs[20:]
    buffers, semaphores, refs = refs[:10], refs[10:17], refs[17:]
    small_refs, spread_sems, refs = refs[:5], refs[5:9], refs[9:]
    weight_sem, out_sem, token_send, token_recv, last_send, last_recv, *line_sems = refs
    group_count, local_rows, local_width = back_ref.shape[1], back_ref.shape[3], back_ref.shape[4]
    row_count, width = normed_ref.shape
    place = Place(plane, seq_count)
    me = place.me
    side = place.cols_x
    enter([(place.grp, other) for other in place.others] + [(other, me) for other in place.groups])
    chains = [
        LineSum(place, *line_refs[2 * index:2 * index + 2], *line_sems[2 * index:2 * index + 2])
        for index in range(3)
    ]
    held = pltpu.make_async_copy(finished, line_refs[4], weight_sem.at[2])
    held.start()
    weights = [
        pltpu.make_async_copy(projection_ref, projection_scr, weight_sem.at[0]),
        pltpu.make_async_copy(combine_ref, combine_scr, weight_sem.at[1]),
    ]
    for copy in weights:
        copy.start()
    held.wait()
    chains[2].begin()
    for source in range(seq_count):
        for kind in range(3):
            for group in range(group_count):
                packed_scr[
                    group * local_rows:(group + 1) * local_rows,
                    kind * width + source * local_width:kind * width + (source + 1) * local_width,
                ] = back_ref[source, group, kind]

    def turn(index, carry):
        lanes = pl.ds(pl.multiple_of(index * 128, 128), 128)
        packed_scr[:, lanes] = turn_lanes(
            packed_scr[:, lanes].astype(jnp.float32), cos_ref[...], -sin_ref[...]
        ).astype(jnp.bfloat16)
        return carry

    lax.fori_loop(0, 2 * width // 128, turn, 0)
    normed_t_scr[...] = normed_ref[...].T
    joined_t_scr[:width, :] = frames_ref[...].T
    joined_t_scr[width:, :] = shortcut_ref[...].T
    segments = [
        piece_segments([part.shape[1:]], side, part.shape[2] // side)[0][0] for part in parts
    ]
    done_segments, _ = piece_segments(
        [out.shape for out in outs[2:]], side, min(out.shape[1] for out in outs[2:]) // side
    )
    pieces = [[line_refs[2 * index].at[step] for step in range(layers)] for index in range(2)]
    plane_sum = PlaneSum(place, parts, pieces, segments, buffers, semaphores, True)
    late_rounds = chains[2].rounds()
    spread = PlaneSpread(place, outs, *spread_sems)

    def share(index, left, right, tile):
        rows, columns = parts[index].shape[1:]

        def one(turn, carry):
            lanes = pl.ds(pl.multiple_of(turn * tile, tile), tile)
            parts[index][:, :, lanes] = dot_nn(left[...], right[:, lanes]).astype(jnp.bfloat16).reshape(
                seq_count, rows, tile
            )
            return carry

        lax.fori_loop(0, columns // tile, one, 0)
        for step in range(layers):
            plane_sum.swap(index, step)

    share(0, normed_t_scr, packed_scr, 256)
    weights[0].wait()

    def grad_tile(index, carry):
        at = pl.ds(pl.multiple_of(index * 256, 256), 256)
        grad_scr[:, at] = dot_nt(packed_scr[...], projection_scr[at, :])
        return carry

    lax.fori_loop(0, width // 256, grad_tile, 0)
    for hook in plane_sum.steps(plane_sum.first, 0):
        hook()
    block, utter_rows = utter_scr.shape[1], 2 * group_count
    utter_scr[...] = jnp.zeros_like(utter_scr)

    def put(part, utter, value):
        row = part * utter_rows + utter
        utter_scr[row // block, row % block:row % block + 1, :] = value

    for part in range(4):
        for utter in range(utter_rows):
            put(part + 2, utter, late_ref[part * utter_rows + utter:part * utter_rows + utter + 1, :])
    chunk = 32
    for group in range(group_count):

        def norm_back(index, sums):
            first = pl.multiple_of(index * chunk, chunk)
            at = pl.ds(pl.multiple_of(group * local_rows + first, chunk), chunk)
            second = second_mask(bound_ref, group, me, local_rows, first, chunk)
            row = group * 2 * 6
            scale_part = jnp.where(second, mods_ref[row + 7:row + 8, :], mods_ref[row + 1:row + 2, :])
            grad = grad_scr[at, :]
            normal, scale = centered(hidden_ref[at, :])
            inner = grad * (1.0 + scale_part)
            turned = scale * (
                inner
                - jnp.mean(inner, axis=-1, keepdims=True)
                - normal * jnp.mean(inner * normal, axis=-1, keepdims=True)
            )
            low_scr[at, :] = (middle_ref[at, :] + turned).astype(jnp.bfloat16)
            scaled = grad * normal
            later = second.astype(jnp.float32)
            shift_later, scale_later = grad * later, scaled * later
            return (
                sums[0] + fold_rows(grad - shift_later, jnp.sum),
                sums[1] + fold_rows(shift_later, jnp.sum),
                sums[2] + fold_rows(scaled - scale_later, jnp.sum),
                sums[3] + fold_rows(scale_later, jnp.sum),
            )

        zero = jnp.zeros((8, width), jnp.float32)
        sums = lax.fori_loop(0, local_rows // chunk, norm_back, (zero, zero, zero, zero))
        for spot, value in enumerate(sums):
            put(spot // 2, group * 2 + spot % 2, jnp.sum(value, axis=0, keepdims=True))
    small = SmallSum(place, utter_scr, total_ref, *small_refs)
    small.begin()
    share(1, joined_t_scr, low_scr, 256)
    late_rounds[0]()
    for hook in plane_sum.steps(plane_sum.first, 1) + plane_sum.steps(plane_sum.second, 0):
        hook()
    weights[1].wait()

    def joined_tile(index, carry):
        at = pl.ds(pl.multiple_of(index * 256, 256), 256)
        late = pl.ds(pl.multiple_of(width + index * 256, 256), 256)
        frames_scr[:, at] = dot_nt(low_scr[...], combine_scr[at, :])
        shortcut_scr[:, at] = dot_nt(low_scr[...], combine_scr[late, :])
        return carry

    lax.fori_loop(0, width // 256, joined_tile, 0)
    grads = [
        pltpu.make_async_copy(frames_scr, frames_out, out_sem.at[0]),
        pltpu.make_async_copy(shortcut_scr, shortcut_out, out_sem.at[1]),
    ]
    for copy in grads:
        copy.start()
    for hook in late_rounds[1:]:
        hook()
    small.middle()
    for hook in plane_sum.steps(plane_sum.second, 1) + plane_sum.steps(plane_sum.third, 0):
        hook()
    chains[0].begin()
    small.finish()
    for spot in range(seq_count):
        flat_scr[spot * block:(spot + 1) * block, :] = total_ref[spot]
    utters_ref[place.grp] = flat_scr[...].astype(jnp.bfloat16)
    tokens = [
        place.push(utters_ref.at[place.grp], utters_ref.at[place.grp], token_send, token_recv, step, (other, me))
        for step, other in enumerate(place.groups)
    ]
    condition_scr[...] = jnp.zeros_like(condition_scr)
    shard_rows = modulation_ref.shape[0]
    for spot in range(6 * utter_rows // block):
        part, row = spot * block // utter_rows, spot * block % utter_rows
        condition_scr[row:row + block, :shard_rows] += dot_nt(
            total_ref[spot].astype(jnp.bfloat16), modulation_ref[:, part * width:(part + 1) * width]
        )
    conditions_ref[me] = condition_scr[...]
    tokens += [
        place.push(condition_scr, conditions_ref.at[me], last_send, last_recv, step, (place.grp, other))
        for step, other in enumerate(place.others)
    ]
    rounds = [chains[0].rounds(), chains[1].rounds()]
    piece, others = chains[2].close()
    for index in range(2, 5):
        spread.total(index, piece, others, done_segments[index - 2])
    rounds[0][0]()
    for hook in plane_sum.steps(plane_sum.third, 1):
        hook()
    chains[1].begin()
    for hook in rounds[0][1:]:
        hook()
    for index in range(2, 5):
        spread.second(index)
    piece, others = chains[0].close()
    spread.total(0, piece, others, segments[0])
    for hook in rounds[1]:
        hook()
    piece, others = chains[1].close()
    spread.total(1, piece, others, segments[1])
    spread.second(0)
    spread.second(1)
    for chain in chains:
        chain.sent()
    place.sent()
    for copy in tokens:
        copy.wait_recv()
    for copy in grads:
        copy.wait()
    for index in range(5):
        spread.finish(index)


def finish_backward(bounds, back, cos, sin, normed, hidden, middle_grad, frames, shortcut, combine, projection, mods, late, modulation, finished, done_shapes):
    grp_count = lax.axis_size("grp")
    seq_count = lax.axis_size("seq")
    side = math.isqrt(grp_count)
    layers = seq_count // 2
    hops = max(side - 1, 1)
    anywhere = pl.BlockSpec(memory_space=pl.ANY)
    vmem = pl.BlockSpec(memory_space=pltpu.VMEM)
    dma = pltpu.SemaphoreType.DMA
    row_count, width = normed.shape
    low, full = jnp.bfloat16, jnp.float32
    parts = [
        jax.ShapeDtypeStruct((seq_count, weight.shape[0] // seq_count, weight.shape[1]), low)
        for weight in (projection, combine)
    ]
    out_shapes = [part.shape[1:] for part in parts] + list(done_shapes)
    small = jax.ShapeDtypeStruct((seq_count, 32 // seq_count, width), full)
    return pl.pallas_call(
        functools.partial(back_kernel, (side, side), seq_count),
        out_shape=(
            jax.ShapeDtypeStruct((row_count, width), full),
            jax.ShapeDtypeStruct((row_count, width), full),
        ) + tuple(jax.ShapeDtypeStruct(shape, low) for shape in out_shapes) + (
            jax.ShapeDtypeStruct((grp_count, 32, width), low),
            jax.ShapeDtypeStruct((seq_count, 8, 128), full),
        ),
        in_specs=[pl.BlockSpec(memory_space=pltpu.SMEM)] + [vmem] * 8 + [anywhere] * 2 + [vmem] * 3 + [anywhere],
        out_specs=(anywhere,) * 2 + (vmem,) * 7,
        scratch_shapes=[
            pltpu.VMEM((row_count, 3 * width), low),
            pltpu.VMEM(combine.shape, low),
            pltpu.VMEM(projection.shape, low),
            pltpu.VMEM((width, row_count), low),
            pltpu.VMEM((2 * width, row_count), low),
            pltpu.VMEM((row_count, width), full),
            pltpu.VMEM((row_count, width), low),
            pltpu.VMEM((row_count, width), full),
            pltpu.VMEM(small.shape, full),
            pltpu.VMEM(small.shape, full),
            pltpu.VMEM((32, width), full),
            pltpu.VMEM((8, 128), full),
        ] + [pltpu.VMEM(part.shape, low) for part in parts] + [
            pltpu.VMEM((layers + more,) + shape, low)
            for shape in [
                (part.shape[1] // side, part.shape[2] // side) for part in parts
            ] + [finished.shape[1:]] for more in range(2)
        ] + plane_sum_scratch(parts, side, True) + small_scratch(small) + [
            dma((5, 2, hops)), dma((5, 2, hops)),
            dma((5, 2, hops, side)), dma((5, 2, hops, side)),
            dma((3,)), dma((2,)),
            dma((grp_count - 1,)), dma((grp_count - 1,)),
            dma((seq_count - 1,)), dma((seq_count - 1,)),
        ] + [dma((2, layers))] * 6 + [
        ],
        compiler_params=pltpu.CompilerParams(
            collective_id=4, has_side_effects=True, vmem_limit_bytes=62 * 1024 * 1024
        ),
        name="finish_backward",
    )(bounds, back, cos, sin, normed, hidden, middle_grad, frames, shortcut, combine, projection, mods, late, modulation, finished)


def shards(
    frames,
    shortcut,
    time_embed,
    lengths,
    kept_mask,
    target,
    combine,
    modulation,
    projection,
    readout,
    expand,
    contract,
):
    group_count = frames.shape[0]
    local_rows = frames.shape[1]
    width = HEADS * HEAD_DIM
    row_count = group_count * local_rows
    seq_count = lax.axis_size("seq")
    utter_count = time_embed.shape[1]
    kept_float = kept_mask.astype(jnp.float32)
    half_dim = HEAD_DIM // 2
    inverse = jnp.exp(-jnp.log(rope_base) * (jnp.arange(half_dim, dtype=jnp.float32) / half_dim))
    signs = jnp.where(jnp.arange(128) % HEAD_DIM < half_dim, -1.0, 1.0).astype(jnp.float32)
    ladder = jnp.zeros((8, 128), jnp.float32).at[0].set(jnp.tile(inverse, 128 // half_dim)).at[1].set(signs)
    silu_value, silu_pull = jax.vjp(jax.nn.silu, time_embed)
    condition = silu_value.astype(jnp.bfloat16)
    shard_rows = modulation.shape[0]
    utter_rows = group_count * utter_count
    condition_part = lax.dynamic_slice_in_dim(
        condition, lax.axis_index("seq") * shard_rows, shard_rows, 2
    ).reshape(utter_rows, shard_rows)
    token = jnp.zeros((8, 128), jnp.float32)
    token = token.at[:utter_rows, :shard_rows].set(condition_part.astype(jnp.float32))
    late_shards = (readout, expand, contract)
    bounds = lengths[:, 0]
    combine_full, projection_full, *rest = front(
        bounds,
        frames.reshape(row_count, width),
        shortcut.reshape(row_count, width),
        ladder,
        kept_float,
        token,
        modulation,
        combine,
        projection,
        late_shards,
    )
    late_pieces, hidden, normed, qkv, cos_lanes, sin_lanes, mods, loss_scale, tokens = rest
    combine_full = combine_full.reshape(2 * width, width)
    projection_full = projection_full.reshape(width, 3 * width)
    condition_all = tokens[:, :utter_rows, :shard_rows].reshape(-1, shard_rows).astype(jnp.bfloat16)
    split_shape = (group_count, local_rows, width)
    kept_heads, mixture_blocks, log_total, *late_full = attend_forward(
        bounds, qkv, late_shards, late_pieces
    )
    readout_full = late_full[0].reshape(width, width)
    expand_full = late_full[1].reshape(width, -1)
    contract_full = late_full[2].reshape(-1, width)
    result, middle_grad, mixture_grad, late_rows, *late_parts = middle(
        bounds,
        mixture_blocks,
        hidden,
        target.reshape(row_count, width),
        kept_float.reshape(row_count, 1),
        mods,
        loss_scale,
        late_full[0].reshape(width, width),
        late_full[1].reshape(width, -1),
        late_full[2].reshape(-1, width),
    )
    back_blocks, plane_pieces = attend_backward(
        bounds,
        kept_heads,
        mixture_grad,
        log_total,
        late_parts[:3],
        late_parts[3:],
    )
    frames_grad, shortcut_grad, *shares, utters, condition_back = finish_backward(
        bounds,
        back_blocks,
        cos_lanes,
        sin_lanes,
        normed,
        hidden,
        middle_grad,
        frames.reshape(row_count, width),
        shortcut.reshape(row_count, width),
        combine_full,
        projection_full,
        mods,
        late_rows,
        modulation,
        plane_pieces,
        [contract.shape, expand.shape, readout.shape],
    )
    frames_grad = frames_grad.reshape(split_shape)
    shortcut_grad = shortcut_grad.reshape(split_shape)
    projection_grad, combine_grad, contract_grad, expand_grad, readout_grad = [
        share.astype(jnp.float32) for share in shares
    ]
    utter_all = jnp.transpose(
        utters[:, :6 * utter_rows].reshape(-1, 6, utter_rows, width), (0, 2, 1, 3)
    ).reshape(-1, 6 * width)
    modulation_grad = product_left(condition_all, utter_all)
    condition_grad = jnp.transpose(
        condition_back[:, :utter_rows, :shard_rows], (1, 0, 2)
    ).reshape(group_count, utter_count, width)
    time_grad = silu_pull(condition_grad)[0]
    summed = (combine_grad, modulation_grad, projection_grad, readout_grad, expand_grad, contract_grad)
    return (
        result.reshape(split_shape),
        frames_grad,
        shortcut_grad,
        time_grad,
        summed[0],
        summed[1],
        summed[2],
        summed[3],
        summed[4],
        summed[5],
    )


def solution(mesh):
    return jax.shard_map(
        shards,
        mesh=mesh,
        in_specs=(
            P("grp", "seq", None),
            P("grp", "seq", None),
            P("grp", None, None),
            P("grp", None),
            P("grp", "seq"),
            P("grp", "seq", None),
            P("seq", None),
            P("seq", None),
            P("seq", None),
            P("seq", None),
            P("seq", None),
            P("seq", None),
        ),
        out_specs=(
            P("grp", "seq", None),
            P("grp", "seq", None),
            P("grp", "seq", None),
            P("grp", None, None),
            P("seq", None),
            P("seq", None),
            P("seq", None),
            P("seq", None),
            P("seq", None),
            P("seq", None),
        ),
        check_vma=False,
    )
```

```python
import functools
import math

import jax
import jax.numpy as jnp
from jax import lax
from jax.experimental import pallas as pl
from jax.experimental.pallas import tpu as pltpu
from jax.sharding import PartitionSpec as P

HEADS = 16
HEAD_DIM = 64


precise = lax.Precision.HIGHEST
epsilon = 1e-06
rope_base = 10000.0


def product(first_op, second_op):
    return jnp.dot(first_op, second_op, preferred_element_type=jnp.float32)


def product_left(first_op, second_op):
    return lax.dot_general(
        first_op, second_op, (((0,), (0,)), ((), ())), preferred_element_type=jnp.float32
    )


def product_right(first_op, second_op):
    return lax.dot_general(
        first_op, second_op, (((1,), (1,)), ((), ())), preferred_element_type=jnp.float32
    )


def gelu_tanh(values):
    return jax.nn.gelu(values, approximate=True)


def modulate(hidden, shift_part, scale_part):
    center = hidden - jnp.mean(hidden, axis=-1, keepdims=True)
    variance = jnp.mean(center * center, axis=-1, keepdims=True)
    return center * lax.rsqrt(variance + epsilon) * (1.0 + scale_part) + shift_part


def segment_info(lengths, frame_index):
    utter_count = lengths.shape[0]
    utter_ends = jnp.cumsum(lengths)
    starts = utter_ends - lengths
    segment = jnp.sum((frame_index[:, None] >= utter_ends[None, :]).astype(jnp.int32), axis=1)
    member = segment[:, None] == jnp.arange(utter_count, dtype=jnp.int32)[None, :]
    offset = jnp.sum(jnp.where(member, starts[None, :], 0), axis=1)
    return (segment, member, frame_index - offset)


def rotary_tables(position):
    half_dim = HEAD_DIM // 2
    ladder = jnp.arange(half_dim, dtype=jnp.float32) / half_dim
    inverse = jnp.exp(-jnp.log(rope_base) * ladder)
    angles = position.astype(jnp.float32)[:, None] * inverse[None, :]
    return (jnp.cos(angles)[:, None, :], jnp.sin(angles)[:, None, :])


def rotate(vectors, cos_table, sin_table):
    half_dim = vectors.shape[-1] // 2
    front_half = vectors[..., :half_dim]
    back_half = vectors[..., half_dim:]
    return jnp.concatenate(
        [
            front_half * cos_table - back_half * sin_table,
            back_half * cos_table + front_half * sin_table,
        ],
        axis=-1,
    )


MESH = pl.DeviceIdType.MESH
PLAN_FIRST, PLAN_RATE = 2, 4
NEG = -1e30


def utter_features(boundary, total_rows, for_keys):
    row = lax.broadcasted_iota(jnp.int32, (total_rows, 128), 0)
    lane = lax.broadcasted_iota(jnp.int32, (total_rows, 128), 1)
    second = (row >= boundary).astype(jnp.float32)
    ahead = (lane == 0).astype(jnp.float32)
    after = (lane == 1).astype(jnp.float32)
    if for_keys:
        return (NEG * (second * ahead + (1.0 - second) * after)).astype(jnp.bfloat16)
    return (second * after + (1.0 - second) * ahead).astype(jnp.bfloat16)


def head_lanes(values, head):
    lane = lax.broadcasted_iota(jnp.int32, values.shape, 1)
    own = (lane >= head * HEAD_DIM) & (lane < (head + 1) * HEAD_DIM)
    return jnp.where(own, values.astype(jnp.float32), 0.0).astype(jnp.bfloat16)


def dot_nn(first_op, second_op):
    return jnp.dot(first_op, second_op, preferred_element_type=jnp.float32)


def dot_nt(first_op, second_op):
    return lax.dot_general(
        first_op, second_op, (((1,), (1,)), ((), ())), preferred_element_type=jnp.float32
    )


def fold_rows(values, combine):
    return combine(values.reshape(values.shape[0] // 8, 8, values.shape[1]), axis=0)


def enter(partners):
    barrier = pltpu.get_barrier_semaphore()
    for partner in partners:
        pl.semaphore_signal(barrier, inc=1, device_id=partner, device_id_type=MESH)
    pl.semaphore_wait(barrier, len(partners))


def key_span(third, total_rows):
    size = total_rows // 3
    return (max(third - 1, 0) * size, min(third + 2, 3) * size)


class Place:
    def __init__(self, plane, seq_count):
        self.rows_y, self.cols_x = rows_y, cols_x = plane
        self.grp, self.me = grp, me = lax.axis_index("grp"), lax.axis_index("seq")
        self.gy, self.gx = gy, gx = grp // cols_x, lax.rem(grp, cols_x)
        self.layers = layers = seq_count // 2
        self.layer, self.core = layer, core = me // 2, lax.rem(me, 2)
        self.xs = [lax.rem(gx + step, cols_x) for step in range(1, cols_x)]
        self.ys = [lax.rem(gy + step, rows_y) for step in range(1, rows_y)]
        self.beside = [gy * cols_x + x for x in self.xs]
        self.along = [y * cols_x + gx for y in self.ys]
        self.beside_from = [lax.rem(gx + cols_x - step, cols_x) for step in range(1, cols_x)]
        self.far = [lax.rem(layer + step, layers) for step in range(1, layers)]
        self.line_from = [lax.rem(layer + layers - step, layers) * 2 + core for step in range(1, layers)]
        self.lines = [target * 2 + core for target in self.far]
        self.partner = layer * 2 + 1 - core
        self.others = [lax.rem(me + step, seq_count) for step in range(1, seq_count)]
        self.groups = [lax.rem(grp + step, rows_y * cols_x) for step in range(1, rows_y * cols_x)]
        self.started = []

    def push(self, src, dst, sends, recvs, slot, device):
        copy = pltpu.make_async_remote_copy(
            src, dst, sends.at[slot], recvs.at[slot], device_id=device, device_id_type=MESH
        )
        copy.start()
        self.started.append(copy)
        return copy

    def sent(self):
        for copy in self.started:
            copy.wait_send()
        self.started = []


def window(ref, row, rows, col, cols):
    return ref.at[pl.ds(pl.multiple_of(row, 16), rows), pl.ds(pl.multiple_of(col, 128), cols)]


def piece_segments(shapes, side, width):
    base, found = 0, []
    for rows, cols in shapes:
        height, many = rows // side, cols // side // width
        if many == 1:
            half = width // 2
            found.append([[(base, 0, height, half, 0)], [(base, half, height, half, half)]])
        else:
            blocks = [(base + spot * height, 0, height, width, spot * width) for spot in range(many)]
            found.append([blocks[:many // 2], blocks[many // 2:]])
        base += height * many
    return found, base


class PlaneGather:
    def __init__(self, place, shards, pieces, segments, fulls, own_sem, first_send, first_recv, second_send, second_recv, core_send, core_recv):
        self.place, self.shards, self.pieces, self.fulls = place, shards, pieces, fulls
        self.segments = segments
        self.own_sem = own_sem
        self.first = (first_send, first_recv)
        self.second = (second_send, second_recv)
        self.core = (core_send, core_recv)
        self.jobs = [(index, step) for step in range(place.layers - 1) for index in range(len(shards))]
        self.waiting, self.local, self.own = {}, {}, []

    def sizes(self, index):
        _, rows, cols = self.fulls[index].shape
        return rows, rows // self.place.rows_y, cols // (2 * self.place.cols_x)

    def owner(self, step):
        return self.place.line_from[step]

    def begin(self):
        place = self.place
        for index, step in self.jobs:
            self.spread_first(index, step)
        for index, shard in enumerate(self.shards):
            copy = pltpu.make_async_copy(shard, self.fulls[index].at[place.me], self.own_sem.at[index, place.layers - 1, 0, 0])
            copy.start()
            push = place.push(shard, self.fulls[index].at[place.me], *self.core, (index, 0), (place.grp, place.partner))
            self.own.append((copy, push))

    def spread_first(self, index, step):
        place = self.place
        rows, height, width = self.sizes(index)
        full = self.fulls[index].at[self.owner(step)]
        piece = self.pieces.at[step]
        first_row, first_col = place.gy * height, 2 * place.gx * width
        self.local[index, step] = []
        self.waiting[index, step] = []
        for half, partners in enumerate((place.beside, place.along)):
            for spot, (row, col, rows, cols, off) in enumerate(self.segments[index][half]):
                source = piece.at[pl.ds(row, rows), pl.ds(col, cols)]
                part = window(full, first_row, rows, first_col + off, cols)
                copy = pltpu.make_async_copy(source, part, self.own_sem.at[index, step, half, spot])
                copy.start()
                self.local[index, step].append(copy)
                for hop, other in enumerate(partners):
                    self.waiting[index, step].append(place.push(
                        source, part, *self.first, (index, step, half, hop, spot), (other, place.me)
                    ))

    def spread_second(self, index, step):
        place = self.place
        rows, height, width = self.sizes(index)
        for copy in self.local.get((index, step), []):
            copy.wait()
        for copy in self.waiting[index, step]:
            copy.wait_recv()
        full = self.fulls[index].at[self.owner(step)]
        copies = []
        for hop, other in enumerate(place.along):
            for spot, column in enumerate([place.gx] + place.beside_from):
                part = window(full, place.gy * height, height, 2 * column * width, width)
                copies.append(place.push(part, part, *self.second, (index, step, 0, hop, spot), (other, place.me)))
        for hop, other in enumerate(place.beside):
            part = window(full, 0, rows, (2 * place.gx + 1) * width, width)
            copies.append(place.push(part, part, *self.second, (index, step, 1, hop, 0), (other, place.me)))
        self.waiting[index, step] = copies

    def over_core(self, index, step):
        place = self.place
        for copy in self.waiting[index, step]:
            copy.wait_recv()
        full = self.fulls[index].at[self.owner(step)]
        self.waiting[index, step] = [
            place.push(full, full, *self.core, (index, step + 1), (place.grp, place.partner))
        ]

    def middle(self):
        for job in self.jobs:
            self.spread_second(*job)

    def late(self):
        return [functools.partial(self.over_core, *job) for job in self.jobs]

    def arrive(self, index):
        for job in self.jobs:
            if job[0] == index:
                for copy in self.waiting[job]:
                    copy.wait_recv()
        copy, push = self.own[index]
        copy.wait()
        push.wait_recv()

    def finish(self):
        self.place.sent()


def add_rows(target, source, first_row, rows, first_col, cols, out=None):
    step = next(size for size in (64, 32, 16) if rows % size == 0)
    col = pl.multiple_of(first_col, 128)

    def one(index, carry):
        at = pl.ds(pl.multiple_of(first_row + index * step, 16), step)
        off = pl.ds(pl.multiple_of(index * step, step), step)
        value = target[at, pl.ds(col, cols)] + source[off, :]
        if out is None:
            target[at, pl.ds(col, cols)] = value
        else:
            out[off, :] = value
        return carry

    lax.fori_loop(0, rows // step, one, 0)


def add_segments(target, source, first_row, first_col, segments, out):
    for row, col, rows, cols, off in segments:
        begin = off - segments[0][4]
        add_rows(
            target, source.at[:, pl.ds(begin, cols)], first_row, rows, first_col + off, cols,
            out.at[pl.ds(row, rows), pl.ds(col, cols)],
        )


def plane_sum_scratch(parts, side, in_place=False):
    layers = parts[0].shape[0] // 2 if in_place else parts[0].shape[0]
    hops = max(side - 1, 1)
    count = len(parts)
    dma = pltpu.SemaphoreType.DMA

    def buffers(lead, row_cut, col_cut):
        return [
            pltpu.VMEM(lead + (part.shape[1] // row_cut, part.shape[2] // col_cut), jnp.bfloat16)
            for part in parts
        ]

    return (
        ([] if in_place else buffers((layers,), 1, 1))
        + buffers((layers,), 1, 1)
        + buffers((layers, hops, side), side, 2 * side)
        + buffers((layers, hops), side, 2 * side)
        + buffers((layers, hops), 1, 2 * side)
        + buffers((layers, hops), side, 2 * side)
        + [
            dma((count, layers)), dma((count, layers)), dma((count, layers)),
            dma((count, layers, 2, hops, side)), dma((count, layers, 2, hops, side)),
            dma((count, layers, 2, hops)), dma((count, layers, 2, hops)),
        ]
    )


class PlaneSum:
    def __init__(self, place, parts, pieces, segments, buffers, semaphores, in_place=False, given=None):
        self.given = given
        self.place, self.parts, self.pieces, self.segments = place, parts, pieces, segments
        count = len(parts)
        buffers = (() if in_place else buffers[:count], *[
            buffers[index * count:(index + 1) * count] for index in range(0 if in_place else 1, 5 if in_place else 6)
        ])
        self.in_place = in_place
        self.sums, self.swapped, self.y_first, self.x_second, self.x_first, self.y_second = buffers
        self.load_sem = semaphores[0]
        self.core, self.first_sem, self.second_sem = semaphores[1:3], semaphores[3:5], semaphores[5:7]
        self.order = place.far + [place.layer]
        self.jobs = [(index, step) for index in range(count) for step in range(place.layers)]
        self.loads, self.swaps, self.waiting = {}, {}, {}

    def sizes(self, index):
        _, rows, cols = self.parts[index].shape
        return rows, cols, rows // self.place.rows_y, cols // (2 * self.place.cols_x)

    def begin(self):
        place = self.place
        for index, step in self.jobs:
            target = self.order[step]
            for source, kept, sem in (
                (self.parts, self.sums, self.load_sem), (self.given, self.swapped, self.core[0]),
            ):
                copy = pltpu.make_async_copy(source[index].at[target], kept[index].at[step], sem.at[index, step])
                copy.start()
                self.loads.setdefault((index, step), []).append(copy)

    def swap(self, index, step):
        place = self.place
        self.swaps[index, step] = place.push(
            self.parts[index].at[self.order[step] * 2 + 1 - place.core], self.swapped[index].at[step],
            *self.core, (index, step), (place.grp, place.partner),
        )

    def running(self, index, step):
        if self.in_place:
            return self.parts[index].at[self.order[step] * 2 + self.place.core]
        return self.sums[index].at[step]

    def first(self, index, step):
        place = self.place
        rows, cols, height, width = self.sizes(index)
        for copy in self.loads.get((index, step), []):
            copy.wait()
        if self.given is None:
            self.swaps[index, step].wait_recv()
        total = self.running(index, step)
        add_rows(total, self.swapped[index].at[step], 0, rows, 0, cols)
        copies = []
        for hop, other in enumerate(place.along):
            for column in range(place.cols_x):
                copies.append(place.push(
                    window(total, place.ys[hop] * height, height, 2 * column * width, width),
                    self.y_first[index].at[step, hop, column],
                    *self.first_sem, (index, step, 0, hop, column), (other, place.me),
                ))
        for hop, other in enumerate(place.beside):
            copies.append(place.push(
                window(total, 0, rows, (2 * place.xs[hop] + 1) * width, width),
                self.x_first[index].at[step, hop],
                *self.first_sem, (index, step, 1, hop, 0), (other, place.me),
            ))
        self.waiting[index, step] = copies

    def second(self, index, step):
        place = self.place
        rows, cols, height, width = self.sizes(index)
        for copy in self.waiting[index, step]:
            copy.wait_recv()
        total = self.running(index, step)
        for hop in range(place.rows_y - 1):
            for column in range(place.cols_x):
                add_rows(
                    total, self.y_first[index].at[step, hop, column],
                    place.gy * height, height, 2 * column * width, width,
                )
        for hop in range(place.cols_x - 1):
            add_rows(total, self.x_first[index].at[step, hop], 0, rows, (2 * place.gx + 1) * width, width)
        copies = []
        for hop, other in enumerate(place.beside):
            copies.append(place.push(
                window(total, place.gy * height, height, 2 * place.xs[hop] * width, width),
                self.x_second[index].at[step, hop],
                *self.second_sem, (index, step, 0, hop), (other, place.me),
            ))
        for hop, other in enumerate(place.along):
            copies.append(place.push(
                window(total, place.ys[hop] * height, height, (2 * place.gx + 1) * width, width),
                self.y_second[index].at[step, hop],
                *self.second_sem, (index, step, 1, hop), (other, place.me),
            ))
        self.waiting[index, step] = copies

    def third(self, index, step):
        place = self.place
        rows, cols, height, width = self.sizes(index)
        for copy in self.waiting[index, step]:
            copy.wait_recv()
        self.waiting[index, step] = []
        total = self.running(index, step)
        out = self.pieces[index][step]
        row, col = place.gy * height, 2 * place.gx * width
        for hop in range(place.cols_x - 1):
            source = self.x_second[index].at[step, hop]
            if hop == place.cols_x - 2:
                add_segments(total, source, row, col, self.segments[index][0], out)
            else:
                add_rows(total, source, row, height, col, width)
        for hop in range(place.rows_y - 1):
            source = self.y_second[index].at[step, hop]
            if hop == place.rows_y - 2:
                add_segments(total, source, row, col, self.segments[index][1], out)
            else:
                add_rows(total, source, row, height, col + width, width)

    def steps(self, stage, only=None):
        return [functools.partial(stage, *job) for job in self.jobs if only is None or job[0] == only]

    def finish(self):
        self.place.sent()


class LineSum:
    def __init__(self, place, pieces, sums, sends, recvs):
        self.place, self.pieces, self.sums = place, pieces, sums
        self.sends, self.recvs = sends, recvs
        self.pushed = []

    def mine(self, owner):
        place = self.place
        return self.pieces.at[lax.rem(place.layers + owner - place.layer - 1, place.layers)]

    def slot(self, way, owner, layer):
        return owner if way == 0 else jnp.where(layer == owner, self.place.layers, owner)

    def copy(self, way, owner):
        place = self.place
        target = place.layer + (1 if way == 0 else -1)
        return pltpu.make_async_remote_copy(
            self.mine(owner), self.sums.at[self.slot(way, owner, target)],
            self.sends.at[way, owner], self.recvs.at[way, owner],
            device_id=(place.grp, target * 2 + place.core), device_id_type=MESH,
        )

    def push(self, when, way, owner, add):
        self.pushed.append((when, way, owner))

        @pl.when(when)
        def _():
            if add:
                self.arrived(way, owner)
                mine, other = self.mine(owner), self.sums.at[self.slot(way, owner, self.place.layer)]
                rows = mine.shape[0]
                step = next(size for size in (64, 32, 16) if rows % size == 0)

                def one(index, carry):
                    at = pl.ds(pl.multiple_of(index * step, 16), step)
                    mine[at, :] = mine[at, :] + other[at, :]
                    return carry

                lax.fori_loop(0, rows // step, one, 0)
            self.copy(way, owner).start()

    def arrived(self, way, owner):
        place = self.place
        part = self.sums.at[self.slot(way, owner, place.layer)]
        pltpu.make_async_remote_copy(
            part, part, self.sends.at[way, owner], self.recvs.at[way, owner],
            device_id=(place.grp, place.me), device_id_type=MESH,
        ).wait_recv()

    def begin(self):
        place, last = self.place, self.place.layers - 1
        for hop in range(last):
            self.push(place.layer == 0, 0, last - hop, False)
            self.push(place.layer == last, 1, hop, False)

    def round(self, turn):
        place, last = self.place, self.place.layers - 1
        for owner in range(place.layers):
            up = turn + 1 - (last - owner)
            if 1 <= up < owner:
                self.push(place.layer == up, 0, owner, True)
            down = turn + 1 - owner
            if 1 <= down < last - owner:
                self.push(place.layer == last - down, 1, owner, True)

    def rounds(self):
        return [functools.partial(self.round, turn) for turn in range(2 * self.place.layers - 5)]

    def close(self):
        place, last = self.place, self.place.layers - 1
        for owner in range(place.layers):
            for way, ends in ((0, owner == 0), (1, owner == last)):

                @pl.when(place.layer == owner)
                def _(way=way, ends=ends, owner=owner):
                    if ends:
                        spot = owner if way == 0 else place.layers
                        self.sums[spot] = jnp.zeros(self.sums.shape[1:], jnp.bfloat16)
                    else:
                        self.arrived(way, owner)

        return self.pieces.at[last], [self.sums.at[place.layer], self.sums.at[place.layers]]

    def sent(self):
        for when, way, owner in self.pushed:

            @pl.when(when)
            def _(way=way, owner=owner):
                self.copy(way, owner).wait_send()


class PlaneSpread:
    def __init__(self, place, outs, first_send, first_recv, second_send, second_recv):
        self.place, self.outs = place, outs
        self.first_sem, self.second_sem = (first_send, first_recv), (second_send, second_recv)
        self.waiting = {}

    def sizes(self, index):
        rows, cols = self.outs[index].shape
        return rows, rows // self.place.rows_y, cols // (2 * self.place.cols_x)

    def total(self, index, piece, others, segments):
        place = self.place
        rows, height, width = self.sizes(index)
        row = place.gy * height
        col = pl.multiple_of(2 * place.gx * width, 128)
        for first, left, _, cols, off in segments[0] + segments[1]:

            def one(turn, carry):
                at = pl.ds(pl.multiple_of(first + turn * 16, 16), 16)
                value = piece[at, pl.ds(left, cols)].astype(jnp.float32)
                for other in others:
                    value = value + other[at, pl.ds(left, cols)].astype(jnp.float32)
                self.outs[index][
                    pl.ds(pl.multiple_of(row + turn * 16, 16), 16), pl.ds(pl.multiple_of(col + off, 128), cols)
                ] = value.astype(jnp.bfloat16)
                return carry

            lax.fori_loop(0, height // 16, one, 0)
        copies = []
        for hop, other in enumerate(place.beside):
            part = window(self.outs[index], row, height, 2 * place.gx * width, width)
            copies.append(place.push(part, part, *self.first_sem, (index, 0, hop), (other, place.me)))
        for hop, other in enumerate(place.along):
            part = window(self.outs[index], row, height, (2 * place.gx + 1) * width, width)
            copies.append(place.push(part, part, *self.first_sem, (index, 1, hop), (other, place.me)))
        self.waiting[index] = copies

    def second(self, index):
        place = self.place
        rows, height, width = self.sizes(index)
        for copy in self.waiting[index]:
            copy.wait_recv()
        copies = []
        for hop, other in enumerate(place.along):
            for spot, column in enumerate([place.gx] + place.beside_from):
                part = window(self.outs[index], place.gy * height, height, 2 * column * width, width)
                copies.append(place.push(part, part, *self.second_sem, (index, 0, hop, spot), (other, place.me)))
        for hop, other in enumerate(place.beside):
            part = window(self.outs[index], 0, rows, (2 * place.gx + 1) * width, width)
            copies.append(place.push(part, part, *self.second_sem, (index, 1, hop, 0), (other, place.me)))
        self.waiting[index] = copies

    def finish(self, index):
        for copy in self.waiting[index]:
            copy.wait_recv()


class SmallSum:
    def __init__(self, place, source, total, scratch, first_send, first_recv, second_send, second_recv):
        self.place, self.source, self.total_ref, self.scratch = place, source, total, scratch
        self.first_sem, self.second_sem = (first_send, first_recv), (second_send, second_recv)

    def begin(self):
        place = self.place
        self.waiting = [
            place.push(self.source.at[other], self.scratch.at[step], *self.first_sem, step, (place.grp, other))
            for step, other in enumerate(place.others)
        ]

    def middle(self):
        place = self.place
        value = self.source[place.me]
        for step, copy in enumerate(self.waiting):
            copy.wait_recv()
            value = value + self.scratch[step]
        self.total_ref[place.me] = value
        part = self.total_ref.at[place.me]
        self.waiting = [
            place.push(part, part, *self.second_sem, step, (place.grp, other))
            for step, other in enumerate(place.others)
        ]

    def finish(self):
        for copy in self.waiting:
            copy.wait_recv()


def small_scratch(source):
    seq_count = source.shape[0]
    dma = pltpu.SemaphoreType.DMA
    return [pltpu.VMEM((seq_count - 1,) + source.shape[1:], jnp.float32)] + [dma((seq_count - 1,))] * 4


def forward_kernel(plane, seq_count, count, *refs):
    layers = seq_count // 2
    bound_ref, qkv_ref, shards = refs[0], refs[1], refs[2:2 + count]
    refs = refs[2 + count:]
    pieces, refs = refs[0], refs[1:]
    kept_ref, mixture_ref, log_ref, fulls = refs[0], refs[1], refs[2], refs[3:3 + count]
    (
        key_scr, query_scr, value_t_scr, score_scr, mix_t_scr, mix_scr,
        send_sem, recv_sem, back_send_sem, back_recv_sem, local_sem,
    ) = refs[3 + count:14 + count]
    own_sem, first_send, first_recv, second_send, second_recv, core_send, core_recv = refs[14 + count:]
    group_count, local_rows, local_width = qkv_ref.shape[1], qkv_ref.shape[3], qkv_ref.shape[4]
    total_rows = seq_count * local_rows
    heads = local_width // HEAD_DIM
    me = lax.axis_index("seq")
    grp = lax.axis_index("grp")
    others = [lax.rem(me + step, seq_count) for step in range(1, seq_count)]
    origins = [lax.rem(me + seq_count - step, seq_count) for step in range(1, seq_count)]
    block = min(256, total_rows // 3)
    place = Place(plane, seq_count)
    enter([(grp, other) for other in others] + [(other, me) for other in place.beside + place.along])
    copies = []

    def begin_group(group):
        own = pltpu.make_async_copy(qkv_ref.at[me, group], kept_ref.at[me, group], local_sem.at[group])
        own.start()
        row = [own]
        for step, other in enumerate(others):
            copy = pltpu.make_async_remote_copy(
                qkv_ref.at[other, group], kept_ref.at[me, group],
                send_sem.at[group, step], recv_sem.at[group, step],
                device_id=(grp, other), device_id_type=MESH,
            )
            copy.start()
            row.append(copy)
        copies.append(row)

    begin_group(0)
    side = place.cols_x
    segments, _ = piece_segments(
        [shard.shape for shard in shards], side, min(shard.shape[1] for shard in shards) // side
    )
    spread = PlaneGather(
        place, shards, pieces, segments, fulls,
        own_sem, first_send, first_recv, second_send, second_recv, core_send, core_recv,
    )
    spread.begin()
    back = []
    for group in range(group_count):
        for copy in copies[group]:
            copy.wait()
        if group + 1 < group_count:
            begin_group(group + 1)
        if group == 0:
            spread.middle()
            hooks = spread.late()
            held = len(hooks) // 3
        boundary = bound_ref[group]
        keys = kept_ref[:, group, 1].reshape(total_rows, local_width)
        values = kept_ref[:, group, 2].reshape(total_rows, local_width)
        key_scr[:, :local_width] = keys
        key_scr[:, local_width:] = utter_features(boundary, total_rows, True)
        query_scr[:, local_width:] = utter_features(boundary, total_rows, False)
        value_t_scr[...] = values.astype(jnp.float32).T.astype(jnp.bfloat16)

        for head in range(heads):
            queries = kept_ref[:, group, 0].reshape(total_rows, local_width)
            query_scr[:, :local_width] = head_lanes(queries, head) * jnp.bfloat16(HEAD_DIM ** (-0.5))
            for third in range(3):
                first_key, last_key = key_span(third, total_rows)
                chunks = range(first_key, last_key, block)

                def one_block(index, carry):
                    first_row = pl.multiple_of(third * (total_rows // 3) + index * block, block)
                    query_block = query_scr[pl.ds(first_row, block), :]
                    peak = jnp.full((8, block), -jnp.inf, jnp.float32)
                    for first in chunks:
                        scores = dot_nt(key_scr[first:first + block, :], query_block)
                        score_scr[first:first + block, :] = scores
                        peak = jnp.maximum(peak, fold_rows(scores, jnp.max))
                    peak = jnp.max(peak, axis=0, keepdims=True)
                    total = jnp.zeros((8, block), jnp.float32)
                    for first in chunks:
                        lifted = jnp.exp(score_scr[first:first + block, :] - peak)
                        score_scr[first:first + block, :] = lifted
                        total = total + fold_rows(lifted, jnp.sum)
                    total = jnp.sum(total, axis=0, keepdims=True)
                    inverse = 1.0 / total
                    mixed = jnp.zeros((HEAD_DIM, block), jnp.float32)
                    rows = slice(head * HEAD_DIM, (head + 1) * HEAD_DIM)
                    for first in chunks:
                        weight = (score_scr[first:first + block, :] * inverse).astype(jnp.bfloat16)
                        mixed = mixed + dot_nn(value_t_scr[rows, first:first + block], weight)
                    mix_t_scr[rows, pl.ds(first_row, block)] = mixed
                    log_ref[group, head, :, pl.ds(first_row, block)] = peak + jnp.log(total)
                    return carry

                lax.fori_loop(0, total_rows // 3 // block, one_block, 0)
                if group > 0 and len(hooks) > held:
                    hooks.pop(0)()
        mix_scr[group] = mix_t_scr[...].T.astype(jnp.bfloat16).reshape(seq_count, local_rows, local_width)
        own = pltpu.make_async_copy(
            mix_scr.at[group, me], mixture_ref.at[me, group], local_sem.at[group_count + group]
        )
        own.start()
        back.append(own)
        for step, other in enumerate(others):
            copy = pltpu.make_async_remote_copy(
                mix_scr.at[group, other], mixture_ref.at[me, group],
                back_send_sem.at[group, step], back_recv_sem.at[group, step],
                device_id=(grp, other), device_id_type=MESH,
            )
            copy.start()
            back.append(copy)
    for hook in hooks:
        hook()
    for copy in back:
        copy.wait()
    for index in range(count):
        spread.arrive(index)
    spread.finish()


def attend_forward(bounds, qkv, shards, pieces):
    side = math.isqrt(lax.axis_size("grp"))
    hops = max(side - 1, 1)
    count = len(shards)
    dma = pltpu.SemaphoreType.DMA
    anywhere = pl.BlockSpec(memory_space=pl.ANY)
    layers = qkv.shape[0] // 2
    seq_count, group_count, _, local_rows, local_width = qkv.shape
    total_rows = seq_count * local_rows
    heads = local_width // HEAD_DIM
    block = min(256, total_rows // 3)
    vmem = pl.BlockSpec(memory_space=pltpu.VMEM)
    return pl.pallas_call(
        functools.partial(forward_kernel, (side, side), seq_count, count),
        out_shape=(
            jax.ShapeDtypeStruct(qkv.shape, jnp.bfloat16),
            jax.ShapeDtypeStruct((seq_count, group_count, local_rows, local_width), jnp.bfloat16),
            jax.ShapeDtypeStruct((group_count, heads, 1, total_rows), jnp.float32),
        ) + tuple(jax.ShapeDtypeStruct((seq_count,) + part.shape, part.dtype) for part in shards),
        in_specs=[pl.BlockSpec(memory_space=pltpu.SMEM)] + [anywhere] * (2 + count),
        out_specs=(vmem, vmem, vmem) + (anywhere,) * count,
        scratch_shapes=[
            pltpu.VMEM((total_rows, local_width + 128), jnp.bfloat16),
            pltpu.VMEM((total_rows, local_width + 128), jnp.bfloat16),
            pltpu.VMEM((local_width, total_rows), jnp.bfloat16),
            pltpu.VMEM((total_rows, block), jnp.float32),
            pltpu.VMEM((local_width, total_rows), jnp.float32),
            pltpu.VMEM((group_count, seq_count, local_rows, local_width), jnp.bfloat16),
            pltpu.SemaphoreType.DMA((group_count, seq_count - 1)),
            pltpu.SemaphoreType.DMA((group_count, seq_count - 1)),
            pltpu.SemaphoreType.DMA((group_count, seq_count - 1)),
            pltpu.SemaphoreType.DMA((group_count, seq_count - 1)),
            pltpu.SemaphoreType.DMA((2 * group_count,)),
            dma((count, layers, 2, 2)),
            dma((count, layers - 1, 2, hops, 2)), dma((count, layers - 1, 2, hops, 2)),
            dma((count, layers - 1, 2, hops, side)), dma((count, layers - 1, 2, hops, side)),
            dma((count, layers)), dma((count, layers)),
        ],
        compiler_params=pltpu.CompilerParams(
            collective_id=1, has_side_effects=True, vmem_limit_bytes=48 * 1024 * 1024
        ),
        name="attend_forward",
    )(bounds, qkv, *shards, pieces)


def backward_kernel(plane, seq_count, count, *refs):
    layers = seq_count // 2
    bound_ref, kept_ref, grad_ref, log_ref = refs[:4]
    parts, given, refs = refs[4:4 + count], refs[4 + count:4 + 2 * count], refs[4 + 2 * count:]
    out_ref, refs = refs[0], refs[1:]
    pieces, refs = refs[0], refs[1:]
    (
        taken_scr, key_scr, query_scr, key_t_scr, head_query_scr, head_grad_scr, prob_scr, weight_scr,
        query_t_scr, key_sum_scr, value_sum_scr, back_scr,
        send_sem, recv_sem, back_send_sem, back_recv_sem, local_sem,
    ) = refs[:17]
    buffers, semaphores = refs[17:17 + 6 * count], refs[17 + 6 * count:]
    group_count, local_rows, local_width = grad_ref.shape[1], grad_ref.shape[2], grad_ref.shape[3]
    total_rows = seq_count * local_rows
    heads = local_width // HEAD_DIM
    me = lax.axis_index("seq")
    grp = lax.axis_index("grp")
    others = [lax.rem(me + step, seq_count) for step in range(1, seq_count)]
    block = min(256, total_rows // 3)
    place = Place(plane, seq_count)
    enter([(grp, other) for other in others] + [(other, me) for other in place.beside + place.along])
    copies = []

    def begin_group(group):
        own = pltpu.make_async_copy(grad_ref.at[me, group], taken_scr.at[me, group], local_sem.at[group])
        own.start()
        row = [own]
        for step, other in enumerate(others):
            copy = pltpu.make_async_remote_copy(
                grad_ref.at[other, group], taken_scr.at[me, group],
                send_sem.at[group, step], recv_sem.at[group, step],
                device_id=(grp, other), device_id_type=MESH,
            )
            copy.start()
            row.append(copy)
        copies.append(row)

    begin_group(0)
    side = place.cols_x
    segments, _ = piece_segments(
        [part.shape[1:] for part in parts], side, min(part.shape[2] for part in parts) // side
    )
    plane_sum = PlaneSum(
        place, parts, [[pieces.at[step] for step in range(layers)]] * count, segments, buffers, semaphores,
        given=given,
    )
    plane_sum.begin()
    firsts = plane_sum.steps(plane_sum.first)
    seconds = plane_sum.steps(plane_sum.second)
    units = 3 * heads * group_count
    plan = [[] for _ in range(units + 1)]
    for spot, hook in enumerate(seconds):
        plan[min(PLAN_FIRST + spot * PLAN_RATE // 4, units)].append(hook)
    for hook in firsts:
        hook()
    back = []
    for group in range(group_count):
        for copy in copies[group]:
            copy.wait()
        if group + 1 < group_count:
            begin_group(group + 1)
        boundary = bound_ref[group]
        keys = kept_ref[:, group, 1].reshape(total_rows, local_width)
        key_scr[:, :local_width] = keys
        key_scr[:, local_width:] = utter_features(boundary, total_rows, True)
        query_scr[:, local_width:] = utter_features(boundary, total_rows, False)
        key_t_scr[...] = keys.astype(jnp.float32).T.astype(jnp.bfloat16)
        key_sum_scr[...] = jnp.zeros_like(key_sum_scr)
        value_sum_scr[...] = jnp.zeros_like(value_sum_scr)

        for head in range(heads):
            queries = head_lanes(kept_ref[:, group, 0].reshape(total_rows, local_width), head)
            head_query_scr[...] = queries
            query_scr[:, :local_width] = queries * jnp.bfloat16(HEAD_DIM ** (-0.5))
            head_grad_scr[...] = head_lanes(taken_scr[:, group].reshape(total_rows, local_width), head)
            for third in range(3):
                first_key, last_key = key_span(third, total_rows)
                chunks = range(first_key, last_key, block)

                def one_block(index, carry):
                    first_row = pl.multiple_of(third * (total_rows // 3) + index * block, block)
                    own_rows = pl.ds(first_row, block)
                    query_block = query_scr[own_rows, :]
                    grad_block = head_grad_scr[own_rows, :]
                    plain_block = head_query_scr[own_rows, :]
                    log_block = log_ref[group, head, :, own_rows]
                    row_dot = jnp.zeros((8, block), jnp.float32)
                    for first in chunks:
                        scores = dot_nt(key_scr[first:first + block, :], query_block)
                        prob = jnp.exp(scores - log_block)
                        values = kept_ref[
                            first // local_rows:(first + block - 1) // local_rows + 1, group, 2
                        ].reshape(-1, local_width)
                        skip = first % local_rows
                        weight_grad = dot_nt(values[skip:skip + block], grad_block)
                        prob_scr[first:first + block, :] = prob
                        weight_scr[first:first + block, :] = weight_grad
                        row_dot = row_dot + fold_rows(prob * weight_grad, jnp.sum)
                    row_dot = jnp.sum(row_dot, axis=0, keepdims=True)
                    rows = slice(head * HEAD_DIM, (head + 1) * HEAD_DIM)
                    turned = jnp.zeros((HEAD_DIM, block), jnp.float32)
                    for first in chunks:
                        prob = prob_scr[first:first + block, :]
                        score_grad = (
                            HEAD_DIM ** (-0.5) * (prob * (weight_scr[first:first + block, :] - row_dot))
                        ).astype(jnp.bfloat16)
                        key_sum_scr[first:first + block, :] += dot_nn(score_grad, plain_block)
                        value_sum_scr[first:first + block, :] += dot_nn(
                            prob.astype(jnp.bfloat16), grad_block
                        )
                        turned = turned + dot_nn(key_t_scr[rows, first:first + block], score_grad)
                    query_t_scr[rows, own_rows] = turned
                    return carry

                lax.fori_loop(0, total_rows // 3 // block, one_block, 0)
                for hook in plan.pop(0):
                    hook()
        shape = (seq_count, local_rows, local_width)
        back_scr[:, group, 0] = query_t_scr[...].T.astype(jnp.bfloat16).reshape(shape)
        back_scr[:, group, 1] = key_sum_scr[...].astype(jnp.bfloat16).reshape(shape)
        back_scr[:, group, 2] = value_sum_scr[...].astype(jnp.bfloat16).reshape(shape)
        own = pltpu.make_async_copy(
            back_scr.at[me, group], out_ref.at[me, group], local_sem.at[group_count + group]
        )
        own.start()
        back.append(own)
        for step, other in enumerate(others):
            copy = pltpu.make_async_remote_copy(
                back_scr.at[other, group], out_ref.at[me, group],
                back_send_sem.at[group, step], back_recv_sem.at[group, step],
                device_id=(grp, other), device_id_type=MESH,
            )
            copy.start()
            back.append(copy)
    for hook in plan[0] + plane_sum.steps(plane_sum.third):
        hook()
    for copy in back:
        copy.wait()
    plane_sum.finish()


def attend_backward(bounds, kept, grad, log_total, parts, given):
    side = math.isqrt(lax.axis_size("grp"))
    count = len(parts)
    layers = kept.shape[0] // 2
    anywhere = pl.BlockSpec(memory_space=pl.ANY)
    width = min(part.shape[2] for part in parts) // side
    _, piece_rows = piece_segments([part.shape[1:] for part in parts], side, width)
    seq_count, group_count, _, local_rows, local_width = kept.shape
    total_rows = seq_count * local_rows
    block = min(256, total_rows // 3)
    vmem = pl.BlockSpec(memory_space=pltpu.VMEM)
    return pl.pallas_call(
        functools.partial(backward_kernel, (side, side), seq_count, count),
        out_shape=(jax.ShapeDtypeStruct(kept.shape, jnp.bfloat16),) + tuple(
            jax.ShapeDtypeStruct((layers, piece_rows, width), jnp.bfloat16) for _ in range(1)
        ),
        in_specs=[pl.BlockSpec(memory_space=pltpu.SMEM), vmem, anywhere, vmem] + [anywhere] * (2 * count),
        out_specs=(vmem,) * 2,
        scratch_shapes=[
            pltpu.VMEM(grad.shape, jnp.bfloat16),
            pltpu.VMEM((total_rows, local_width + 128), jnp.bfloat16),
            pltpu.VMEM((total_rows, local_width + 128), jnp.bfloat16),
            pltpu.VMEM((local_width, total_rows), jnp.bfloat16),
            pltpu.VMEM((total_rows, local_width), jnp.bfloat16),
            pltpu.VMEM((total_rows, local_width), jnp.bfloat16),
            pltpu.VMEM((total_rows, block), jnp.float32),
            pltpu.VMEM((total_rows, block), jnp.float32),
            pltpu.VMEM((local_width, total_rows), jnp.float32),
            pltpu.VMEM((total_rows, local_width), jnp.float32),
            pltpu.VMEM((total_rows, local_width), jnp.float32),
            pltpu.VMEM(kept.shape, jnp.bfloat16),
            pltpu.SemaphoreType.DMA((group_count, seq_count - 1)),
            pltpu.SemaphoreType.DMA((group_count, seq_count - 1)),
            pltpu.SemaphoreType.DMA((group_count, seq_count - 1)),
            pltpu.SemaphoreType.DMA((group_count, seq_count - 1)),
            pltpu.SemaphoreType.DMA((2 * group_count,)),
        ] + plane_sum_scratch(parts, side),
        compiler_params=pltpu.CompilerParams(
            collective_id=2, has_side_effects=True, vmem_limit_bytes=62 * 1024 * 1024
        ),
        name="attend_backward",
    )(bounds, kept, grad, log_total, *parts, *given)


class LineChain:
    def __init__(self, place, sources, slots, sends, recvs):
        self.place, self.sources, self.slots = place, sources, slots
        self.sends, self.recvs = sends, recvs
        self.pushed = []
        middle = []
        low, high = 0, place.layers - 2
        while low <= high:
            middle += [low] if low == high else [low, high]
            low, high = low + 1, high - 1
        first, last = place.layer == 0, place.layer == place.layers - 1
        self.ranks = [
            jnp.where(first, place.layers - 2 - rank, jnp.where(last, rank, step)).astype(jnp.int32)
            for rank, step in enumerate(middle)
        ]

    def owner(self, step):
        place = self.place
        return lax.rem(place.layer + place.layers - 1 - step, place.layers) * 2 + place.core

    def copy(self, index, source, owner, slot, target, send_slot):
        return pltpu.make_async_remote_copy(
            source, self.slots(index, owner, slot),
            self.sends.at[index, send_slot], self.recvs.at[index, slot],
            device_id=(self.place.grp, target * 2 + self.place.core), device_id_type=MESH,
        )

    def push(self, when, *given):
        self.pushed.append((when, given))

        @pl.when(when)
        def _():
            self.copy(*given).start()

    def begin(self, index):
        place = self.place
        source = self.sources[index]
        self.push(place.layer < place.layers - 1, index, source, place.me, 0, place.layer + 1, 0)
        self.push(place.layer > 0, index, source, place.me, place.layers - 2, place.layer - 1, 1)

    def forward(self, index, rank):
        place = self.place
        step = self.ranks[rank]
        owner = self.owner(step)
        held = self.slots(index, owner, step)
        self.copy(index, held, owner, step, place.layer, 0).wait_recv()
        below = step < place.layer
        going = (below & (place.layer < place.layers - 1)) | ((step >= place.layer) & (place.layer > 0))
        slot = jnp.where(below, step + 1, step - 1)
        target = jnp.where(below, place.layer + 1, place.layer - 1)
        self.push(going, index, held, owner, slot, target, rank + 2)
        return owner

    def sent(self):
        for when, given in self.pushed:

            @pl.when(when)
            def _(given=given):
                self.copy(*given).wait_send()


class WholeGather(PlaneGather):
    def __init__(self, place, shards, fulls, line_send, line_recv, *semaphores):
        super().__init__(place, shards, None, None, fulls, *semaphores)

        def piece(ref, index):
            rows, height, width = self.sizes(index)
            return window(ref, place.gy * height, height, 2 * place.gx * width, 2 * width)

        self.chain = LineChain(
            place, [piece(shard, index) for index, shard in enumerate(shards)],
            lambda index, owner, slot: piece(fulls[index].at[owner], index), line_send, line_recv,
        )
        self.jobs = [(index, rank) for index in range(len(shards)) for rank in range(place.layers - 1)]

    def owner(self, step):
        return self.chain.owner(self.chain.ranks[step])

    def begin(self):
        place = self.place
        for index in range(len(self.shards)):
            self.chain.begin(index)
        for index, shard in enumerate(self.shards):
            copy = pltpu.make_async_copy(shard, self.fulls[index].at[place.me], self.own_sem.at[index, place.layers - 1, 0, 0])
            copy.start()
            push = place.push(shard, self.fulls[index].at[place.me], *self.core, (index, 0), (place.grp, place.partner))
            self.own.append((copy, push))

    def spread_first(self, index, step):
        place = self.place
        rows, height, width = self.sizes(index)
        full = self.fulls[index].at[self.chain.forward(index, step)]
        row, col = place.gy * height, 2 * place.gx * width
        self.waiting[index, step] = []
        for half, partners in enumerate((place.beside, place.along)):
            part = window(full, row, height, col + half * width, width)
            for hop, other in enumerate(partners):
                self.waiting[index, step].append(
                    place.push(part, part, *self.first, (index, step, half, hop, 0), (other, place.me))
                )

    def finish(self):
        super().finish()
        self.chain.sent()


def turn_lanes(values, cos, sin):
    lane = lax.broadcasted_iota(jnp.int32, values.shape, 1)
    ahead = pltpu.roll(values, values.shape[1] - HEAD_DIM // 2, 1)
    behind = pltpu.roll(values, HEAD_DIM // 2, 1)
    other = jnp.where(lax.rem(lane, HEAD_DIM) < HEAD_DIM // 2, ahead, behind)
    return values * cos + other * sin


def second_mask(bound_ref, group, me, local_rows, first, rows):
    row = lax.broadcasted_iota(jnp.int32, (rows, 1), 0) + (me * local_rows + first)
    return row >= bound_ref[group]


def centered(values):
    center = values - jnp.mean(values, axis=-1, keepdims=True)
    scale = lax.rsqrt(jnp.mean(center * center, axis=-1, keepdims=True) + epsilon)
    return center * scale, scale


def front_kernel(plane, seq_count, late_count, *refs):
    layers = seq_count // 2
    bound_ref, frames_ref, shortcut_ref, ladder_ref, kept_ref, token_ref, modulation_ref = refs[:7]
    shards, late_shards, refs = refs[7:9], refs[9:9 + late_count], refs[9 + late_count:]
    fulls_out, late_out, refs = refs[:2], refs[2], refs[3:]
    hidden_ref, normed_ref, qkv_ref, cos_ref, sin_ref, mods_ref, scale_ref, tokens_ref = refs[:8]
    partial_ref, total_ref, refs = refs[8], refs[9], refs[10:]
    fulls, refs = refs[:2], refs[2:]
    token_scr, token_send, token_recv, out_sem = refs[:4]
    small_refs, (late_scr, late_send, late_recv, late_sem), refs = refs[4:9], refs[9:13], refs[13:]
    group_count, local_rows, local_width = qkv_ref.shape[1], qkv_ref.shape[3], qkv_ref.shape[4]
    row_count, width = hidden_ref.shape
    rows_all = plane[0] * plane[1]
    place = Place(plane, seq_count)
    me = place.me
    enter([(place.grp, other) for other in place.others] + [(other, me) for other in place.groups])
    whole = WholeGather(place, shards, fulls, *refs)
    whole.begin()
    block = partial_ref.shape[1]
    partial_ref[...] = jnp.zeros_like(partial_ref)
    shard_rows = modulation_ref.shape[0]
    factor = token_ref[:, :shard_rows].astype(jnp.bfloat16)
    for part in range(6):
        found = dot_nn(factor, modulation_ref[:, part * width:(part + 1) * width])
        for utter in range(2 * group_count):
            spot = utter * 6 + part
            partial_ref[spot // block, spot % block:spot % block + 1, :] = found[utter:utter + 1, :]
    kept = jnp.sum(jnp.sum(kept_ref[...], axis=1, keepdims=True), axis=0, keepdims=True)
    partial_ref[seq_count - 1, block - 1:block, :] = jnp.broadcast_to(kept, (1, width))
    small = SmallSum(place, partial_ref, total_ref, *small_refs)
    small.begin()
    for group in range(group_count):
        rows = slice(group * local_rows, (group + 1) * local_rows)
        frame = lax.broadcasted_iota(jnp.int32, (local_rows, 1), 0) + me * local_rows
        place_in = frame - jnp.where(frame >= bound_ref[group], bound_ref[group], 0)
        angles = place_in.astype(jnp.float32) * ladder_ref[0:1, :]
        cos_ref[rows, :] = jnp.cos(angles)
        sin_ref[rows, :] = jnp.sin(angles) * ladder_ref[1:2, :]
    side = place.cols_x
    cut = late_scr.shape[1]
    late_own, base = [], 0
    for index, shard in enumerate(late_shards):
        height, cols = shard.shape[0] // side, shard.shape[1] // side
        for spot in range(cols // cut):
            late_own.append(pltpu.make_async_copy(
                window(shard, place.gy * height, height, place.gx * cols + spot * cut, cut),
                late_scr.at[pl.ds(base, height), :],
                late_sem.at[len(late_own)],
            ))
            late_own[-1].start()
            base += height
    late_chain = LineChain(place, [late_scr], lambda index, owner, slot: late_out.at[slot], late_send, late_recv)
    combine_jobs = [job for job in whole.jobs if job[0] == 0]
    projection_jobs = [job for job in whole.jobs if job[0] == 1]
    for job in combine_jobs + projection_jobs:
        whole.spread_first(*job)
    for copy in late_own:
        copy.wait()
    late_chain.begin(0)
    small.middle()
    for job in combine_jobs:
        whole.spread_second(*job)
    for job, late in zip(combine_jobs, projection_jobs):
        whole.over_core(*job)
        whole.spread_second(*late)
    whole.arrive(0)
    outs = [pltpu.make_async_copy(fulls[0], fulls_out[0], out_sem.at[0])]
    outs[0].start()
    late_chain.forward(0, 0)
    half = seq_count // 2

    def hidden_tile(index, carry):
        at = pl.ds(pl.multiple_of(index * 512, 512), 512)
        upper = fulls[0][0:half, :, at].reshape(width, 512)
        lower = fulls[0][half:seq_count, :, at].reshape(width, 512)
        hidden_ref[:, at] = dot_nn(frames_ref[...], upper) + dot_nn(shortcut_ref[...], lower)
        return carry

    lax.fori_loop(0, width // 512, hidden_tile, 0)
    late_chain.forward(0, 1)
    small.finish()
    last = total_ref.shape[1] - 1
    token_scr[...] = token_ref[...]
    token_scr[4:5, :] = total_ref[seq_count - 1, last:last + 1, :128]
    tokens_ref[place.grp] = token_scr[...]
    tokens = [
        place.push(token_scr, tokens_ref.at[place.grp], token_send, token_recv, step, (other, me))
        for step, other in enumerate(place.groups)
    ]
    for spot in range(seq_count):
        mods_ref[spot * block:(spot + 1) * block, :] = total_ref[spot]

    def vector(group, part, second):
        def row(utter):
            at = (group * 2 + utter) * 6 + part
            return mods_ref[at:at + 1, :]

        return jnp.where(second, row(1), row(0))

    chunk = 32
    for group in range(group_count):

        def norm_rows(index, carry):
            first = pl.multiple_of(index * chunk, chunk)
            at = pl.ds(pl.multiple_of(group * local_rows + first, chunk), chunk)
            second = second_mask(bound_ref, group, me, local_rows, first, chunk)
            normal, _ = centered(hidden_ref[at, :])
            normed_ref[at, :] = (
                normal * (1.0 + vector(group, 1, second)) + vector(group, 0, second)
            ).astype(jnp.bfloat16)
            return carry

        lax.fori_loop(0, local_rows // chunk, norm_rows, 0)
    for job in projection_jobs:
        whole.over_core(*job)
    whole.arrive(1)
    outs.append(pltpu.make_async_copy(fulls[1], fulls_out[1], out_sem.at[1]))
    outs[1].start()
    each = 512 // local_width

    def head_tile(index, carry):
        for kind in range(3):
            at = pl.ds(pl.multiple_of(kind * width + index * 512, 512), 512)
            packed = dot_nn(normed_ref[...], fulls[1][:, :, at].reshape(width, 512))
            for half in range(4):
                lanes = packed[:, half * 128:(half + 1) * 128]
                if kind < 2:
                    lanes = turn_lanes(lanes, cos_ref[...], sin_ref[...])
                lanes = lanes.astype(jnp.bfloat16)
                for spot in range(each // 4):
                    cut = lanes[:, spot * local_width:(spot + 1) * local_width]
                    for group in range(group_count):
                        qkv_ref[index * each + half * (each // 4) + spot, group, kind] = cut[
                            group * local_rows:(group + 1) * local_rows
                        ]
        return carry

    lax.fori_loop(0, width // 512, head_tile, 0)
    for rank in range(2, layers - 1):
        late_chain.forward(0, rank)
    whole.finish()
    late_chain.sent()
    for copy in tokens:
        copy.wait_recv()
    kept = tokens_ref[0, 4:5, :]
    for group in range(1, rows_all):
        kept = kept + tokens_ref[group, 4:5, :]
    frames_all = float(rows_all * group_count * local_rows * seq_count)
    scale_ref[...] = jnp.broadcast_to(frames_all / kept, scale_ref.shape)
    for copy in outs:
        copy.wait()


def front(bounds, frames, shortcut, ladder, kept, token, modulation, combine, projection, late_shards):
    grp_count = lax.axis_size("grp")
    seq_count = lax.axis_size("seq")
    side = math.isqrt(grp_count)
    layers = seq_count // 2
    anywhere = pl.BlockSpec(memory_space=pl.ANY)
    vmem = pl.BlockSpec(memory_space=pltpu.VMEM)
    dma = pltpu.SemaphoreType.DMA
    hops = max(side - 1, 1)
    shards = (combine, projection)
    group_count = bounds.shape[0]
    row_count, width = frames.shape
    low, full = jnp.bfloat16, jnp.float32
    cut = min(shard.shape[1] for shard in late_shards) // side
    late_rows = sum(shard.shape[0] // side * (shard.shape[1] // side // cut) for shard in late_shards)
    most = max(shard.shape[1] // side // cut for shard in late_shards)
    small = jax.ShapeDtypeStruct((seq_count, 32 // seq_count, width), full)
    wholes = [(seq_count,) + part.shape for part in shards]
    return pl.pallas_call(
        functools.partial(front_kernel, (side, side), seq_count, len(late_shards)),
        out_shape=tuple(jax.ShapeDtypeStruct(shape, low) for shape in wholes) + (
            jax.ShapeDtypeStruct((layers - 1, late_rows, cut), low),
            jax.ShapeDtypeStruct((row_count, width), full),
            jax.ShapeDtypeStruct((row_count, width), low),
            jax.ShapeDtypeStruct(
                (seq_count, group_count, 3, row_count // group_count, width // seq_count), low
            ),
            jax.ShapeDtypeStruct((row_count, 128), full),
            jax.ShapeDtypeStruct((row_count, 128), full),
            jax.ShapeDtypeStruct((32, width), full),
            jax.ShapeDtypeStruct(token.shape, full),
            jax.ShapeDtypeStruct((grp_count,) + token.shape, full),
        ),
        in_specs=[pl.BlockSpec(memory_space=pltpu.SMEM)] + [vmem] * 6 + [anywhere] * (2 + len(late_shards)),
        out_specs=(anywhere,) * 3 + (vmem,) * 8,
        scratch_shapes=[pltpu.VMEM(small.shape, full)] * 2 + [pltpu.VMEM(shape, low) for shape in wholes] + [
            pltpu.VMEM(token.shape, full), dma((grp_count - 1,)), dma((grp_count - 1,)), dma((2,)),
        ] + small_scratch(small) + [
            pltpu.VMEM((late_rows, cut), low),
            dma((1, layers + 1)), dma((1, layers - 1)), dma((len(late_shards) * most,)),
            dma((2, layers + 1)), dma((2, layers - 1)),
            dma((2, layers, 1, 1)),
            dma((2, layers - 1, 2, hops, 1)), dma((2, layers - 1, 2, hops, 1)),
            dma((2, layers - 1, 2, hops, side)), dma((2, layers - 1, 2, hops, side)),
            dma((2, layers)), dma((2, layers)),
        ],
        compiler_params=pltpu.CompilerParams(
            collective_id=3, has_side_effects=True, vmem_limit_bytes=62 * 1024 * 1024
        ),
        name="front",
    )(bounds, frames, shortcut, ladder, kept, token, modulation, *shards, *late_shards)


def middle_kernel(plane, seq_count, *refs):
    (
        bound_ref, mixture_ref, hidden_ref, target_ref, kept_ref, mods_ref, scale_ref,
        readout_ref, expand_ref, contract_ref,
    ) = refs[:10]
    result_ref, middle_grad_ref, mixture_grad_ref, late_ref = refs[10:14]
    own_parts, swapped_parts, refs = refs[14:17], refs[17:20], refs[20:]
    (
        readout_scr, expand_scr, contract_scr, mixture_scr, branch_scr, middle_scr, normed_scr, slope_scr, active_scr,
        active_t_scr, wide_scr, grad_scr, low_scr, left_t_scr, stage_scr, value_scr, weight_sem, stage_sem,
        swap_send, swap_recv,
    ) = refs
    row_count, width = hidden_ref.shape
    wide = expand_ref.shape[1]
    group_count = mixture_ref.shape[1]
    local_rows = row_count // group_count
    local_width = width // seq_count
    place = Place(plane, seq_count)
    me = place.me
    enter([(place.grp, place.partner)])
    weights = [
        pltpu.make_async_copy(source, scratch, weight_sem.at[index])
        for index, (source, scratch) in enumerate(
            ((readout_ref, readout_scr), (expand_ref, expand_scr), (contract_ref, contract_scr))
        )
    ]
    weights[0].start()
    for source in range(seq_count):
        for group in range(group_count):
            mixture_scr[
                group * local_rows:(group + 1) * local_rows, source * local_width:(source + 1) * local_width
            ] = mixture_ref[source, group]
    chunk = 32
    tile = 1024

    def tiles(count, body):
        def one(index, carry):
            body(pl.ds(pl.multiple_of(index * tile, tile), tile))
            return carry

        lax.fori_loop(0, count // tile, one, 0)

    def chunks(body, many):
        sums = []
        for group in range(group_count):

            def one(index, carry, group=group):
                first = pl.multiple_of(index * chunk, chunk)
                at = pl.ds(pl.multiple_of(group * local_rows + first, chunk), chunk)
                second = second_mask(bound_ref, group, me, local_rows, first, chunk)

                def vector(part):
                    row = group * 12 + part
                    return jnp.where(second, mods_ref[row + 6:row + 7, :], mods_ref[row:row + 1, :])

                later = second.astype(jnp.float32)
                found = body(at, vector)
                out = []
                for spot, value in enumerate(found):
                    late = value * later
                    out.append(carry[2 * spot] + fold_rows(value - late, jnp.sum))
                    out.append(carry[2 * spot + 1] + fold_rows(late, jnp.sum))
                return tuple(out)

            zero = jnp.zeros((8, width), jnp.float32)
            sums.append(lax.fori_loop(0, local_rows // chunk, one, (zero,) * (2 * many)))
        return sums

    def put(part, spot, sums):
        for group in range(group_count):
            for utter in range(2):
                row = part * 2 * group_count + group * 2 + utter
                late_ref[row:row + 1, :] = jnp.sum(sums[group][2 * spot + utter], axis=0, keepdims=True)

    weights[0].wait()
    weights[1].start()
    weights[2].start()
    tiles(width, lambda at: branch_scr.__setitem__((slice(None), at), dot_nn(mixture_scr[...], readout_scr[:, at])))

    def second_norm(at, vector):
        middle = hidden_ref[at, :] + vector(2) * branch_scr[at, :]
        middle_scr[at, :] = middle
        normal, _ = centered(middle)
        normed_scr[at, :] = (normal * (1.0 + vector(4)) + vector(3)).astype(jnp.bfloat16)
        return ()

    chunks(second_norm, 0)
    weights[1].wait()

    def expand_dot(index, slot):
        at = pl.ds(pl.multiple_of(jnp.minimum(index, wide // tile - 1) * tile, tile), tile)
        value_scr[slot] = dot_nn(normed_scr[...], expand_scr[:, at])

    def bend(index, slot):
        at = pl.ds(pl.multiple_of(index * tile, tile), tile)
        value = value_scr[slot]
        square = value * value
        factor = (2.0 / math.pi) ** 0.5
        bent = jnp.tanh(value * (factor + (factor * 0.044715) * square))
        half = 0.5 + 0.5 * bent
        active_scr[:, at] = (value * half).astype(jnp.bfloat16)
        slope_scr[:, at] = half + (0.5 * value * (1.0 - bent * bent)) * (factor + (factor * 3 * 0.044715) * square)

    def expand_pair(index, carry):
        expand_dot(2 * index + 1, 1)
        bend(2 * index, 0)
        expand_dot(2 * index + 2, 0)
        bend(2 * index + 1, 1)
        return carry

    expand_dot(0, 0)
    lax.fori_loop(0, wide // tile // 2, expand_pair, 0)
    weights[2].wait()
    tiles(width, lambda at: grad_scr.__setitem__((slice(None), at), dot_nn(active_scr[...], contract_scr[:, at])))
    loss_scale = scale_ref[0:1, 0:1]

    def close(at, vector):
        contracted = grad_scr[at, :]
        gate = vector(5)
        output = middle_scr[at, :] + gate * contracted
        result_ref[at, :] = output.astype(jnp.bfloat16)
        output_grad = loss_scale * kept_ref[at, :] * (output - target_ref[at, :].astype(jnp.float32))
        middle_grad_ref[at, :] = output_grad
        low_scr[at, :] = (gate * output_grad).astype(jnp.bfloat16)
        return (output_grad * contracted,)

    put(3, 0, chunks(close, 1))
    pushed = []

    def share_out(number, left, right, across):
        own, swapped = own_parts[number], swapped_parts[number]
        layers, rows, columns = own.shape
        many = columns // width if across else layers * 2 * rows // width
        each = width // (2 * rows)
        out = {}
        for block in range(many):
            slot = block % 2
            if block >= 2:
                for copy, push in out[block - 2]:
                    copy.wait()
                    push.wait_send()

            def one(index, carry, block=block, slot=slot):
                at = pl.ds(pl.multiple_of(index * tile, tile), tile)
                first = left[...] if across else left[block * width:(block + 1) * width, :]
                lanes = pl.ds(pl.multiple_of(index * tile + (block * width if across else 0), tile), tile)
                stage_scr[slot, :, at] = dot_nn(first, right[:, lanes]).astype(jnp.bfloat16)
                return carry

            lax.fori_loop(0, width // tile, one, 0)
            out[block] = []
            for spot in range(each):
                layer = spot if across else block * each + spot
                lanes = pl.ds(block * width if across else 0, width)
                mine = stage_scr.at[slot, pl.ds(pl.multiple_of((2 * spot + place.core) * rows, rows), rows), :]
                other = stage_scr.at[slot, pl.ds(pl.multiple_of((2 * spot + 1 - place.core) * rows, rows), rows), :]
                copy = pltpu.make_async_copy(mine, own.at[layer, :, lanes], stage_sem.at[slot, spot])
                copy.start()
                push = pltpu.make_async_remote_copy(
                    other, swapped.at[layer, :, lanes],
                    swap_send.at[number, block, spot], swap_recv.at[number, block, spot],
                    device_id=(place.grp, place.partner), device_id_type=MESH,
                )
                push.start()
                pushed.append(push)
                out[block].append((copy, push))
        return [pair for block in range(max(many - 2, 0), many) for pair in out[block]]

    def drain(pairs):
        for copy, push in pairs:
            copy.wait()
            push.wait_send()

    def active_dot(index, slot):
        at = pl.ds(pl.multiple_of(jnp.minimum(index, wide // tile - 1) * tile, tile), tile)
        value_scr[slot] = dot_nt(low_scr[...], contract_scr[at, :])

    def unbend(index, slot):
        at = pl.ds(pl.multiple_of(index * tile, tile), tile)
        active_t_scr[at, :] = active_scr[:, at].T
        wide_scr[:, at] = (value_scr[slot] * slope_scr[:, at]).astype(jnp.bfloat16)

    def active_pair(index, carry):
        active_dot(2 * index + 1, 1)
        unbend(2 * index, 0)
        active_dot(2 * index + 2, 0)
        unbend(2 * index + 1, 1)
        return carry

    active_dot(0, 0)
    lax.fori_loop(0, wide // tile // 2, active_pair, 0)

    out = share_out(0, active_t_scr, low_scr, False)
    tiles(width, lambda at: grad_scr.__setitem__((slice(None), at), dot_nt(wide_scr[...], expand_scr[at, :])))
    tiles(width, lambda at: left_t_scr.__setitem__(
        (at, slice(None)), normed_scr[:, at].astype(jnp.float32).T.astype(jnp.bfloat16)
    ))

    drain(out)
    out = share_out(1, left_t_scr, wide_scr, True)

    def norm_back(at, vector):
        grad = grad_scr[at, :]
        normal, scale = centered(middle_scr[at, :])
        inner = grad * (1.0 + vector(4))
        turned = scale * (
            inner
            - jnp.mean(inner, axis=-1, keepdims=True)
            - normal * jnp.mean(inner * normal, axis=-1, keepdims=True)
        )
        middle_grad = middle_grad_ref[at, :] + turned
        middle_grad_ref[at, :] = middle_grad
        low_scr[at, :] = (vector(2) * middle_grad).astype(jnp.bfloat16)
        return middle_grad * branch_scr[at, :], grad, grad * normal

    sums = chunks(norm_back, 3)
    for spot in range(3):
        put(spot, spot, sums)

    def mixture_tile(at):
        left_t_scr[at, :] = mixture_scr[:, at].astype(jnp.float32).T.astype(jnp.bfloat16)
        grad_scr[:, at] = dot_nt(low_scr[...], readout_scr[at, :])

    tiles(width, mixture_tile)
    for source in range(seq_count):
        for group in range(group_count):
            mixture_grad_ref[source, group] = grad_scr[
                group * local_rows:(group + 1) * local_rows, source * local_width:(source + 1) * local_width
            ].astype(jnp.bfloat16)

    drain(out)
    drain(share_out(2, left_t_scr, low_scr, True))
    for push in pushed:
        push.wait_recv()


def middle(bounds, mixture, hidden, target, kept, mods, loss_scale, readout, expand, contract):
    seq_count, group_count, local_rows, local_width = mixture.shape
    row_count, width = hidden.shape
    wide = expand.shape[1]
    layers = seq_count // 2
    side = math.isqrt(lax.axis_size("grp"))
    anywhere = pl.BlockSpec(memory_space=pl.ANY)
    vmem = pl.BlockSpec(memory_space=pltpu.VMEM)
    smem = pl.BlockSpec(memory_space=pltpu.SMEM)
    low, full = jnp.bfloat16, jnp.float32
    dma = pltpu.SemaphoreType.DMA
    return pl.pallas_call(
        functools.partial(middle_kernel, (side, side), seq_count),
        out_shape=(
            jax.ShapeDtypeStruct((row_count, width), low),
            jax.ShapeDtypeStruct((row_count, width), full),
            jax.ShapeDtypeStruct(mixture.shape, low),
            jax.ShapeDtypeStruct((8 * group_count, width), full),
        ) + tuple(
            jax.ShapeDtypeStruct((layers, weight.shape[0] // seq_count, weight.shape[1]), low)
            for _ in range(2) for weight in (contract, expand, readout)
        ),
        in_specs=[smem] + [vmem] * 6 + [anywhere] * 3,
        out_specs=(vmem,) * 4 + (anywhere,) * 6,
        scratch_shapes=[
            pltpu.VMEM(readout.shape, low),
            pltpu.VMEM(expand.shape, low),
            pltpu.VMEM(contract.shape, low),
            pltpu.VMEM((row_count, width), low),
            pltpu.VMEM((row_count, width), full),
            pltpu.VMEM((row_count, width), full),
            pltpu.VMEM((row_count, width), low),
            pltpu.VMEM((row_count, wide), full),
            pltpu.VMEM((row_count, wide), low),
            pltpu.VMEM((wide, row_count), low),
            pltpu.VMEM((row_count, wide), low),
            pltpu.VMEM((row_count, width), full),
            pltpu.VMEM((row_count, width), low),
            pltpu.VMEM((width, row_count), low),
            pltpu.VMEM((2, width, width), low),
            pltpu.VMEM((2, row_count, 1024), full),
            dma((3,)),
            dma((2, layers)),
            dma((3, wide // width, layers)), dma((3, wide // width, layers)),
        ],
        compiler_params=pltpu.CompilerParams(
            collective_id=5, has_side_effects=True, vmem_limit_bytes=62 * 1024 * 1024
        ),
        name="feed_forward",
    )(bounds, mixture, hidden, target, kept, mods, loss_scale, readout, expand, contract)


def back_kernel(plane, seq_count, *refs):
    layers = seq_count // 2
    (
        bound_ref, back_ref, cos_ref, sin_ref, normed_ref, hidden_in, middle_in, frames_in, shortcut_in,
        combine_ref, projection_ref, mods_ref, late_ref, modulation_in,
    ) = refs[:14]
    finished, refs = refs[14], refs[15:]
    frames_out, shortcut_out, outs, refs = refs[0], refs[1], refs[2:7], refs[7:]
    utters_ref, conditions_ref, refs = refs[0], refs[1], refs[2:]
    (
        packed_scr, combine_scr, projection_scr, normed_t_scr, joined_t_scr, grad_scr, low_scr,
        shortcut_scr, total_ref, utter_scr, flat_scr, condition_scr,
    ) = refs[:12]
    frames_scr = grad_scr
    parts, line_refs, refs = refs[12:14], refs[14:20], refs[20:]
    buffers, semaphores, refs = refs[:10], refs[10:17], refs[17:]
    small_refs, spread_sems, refs = refs[:5], refs[5:9], refs[9:]
    weight_sem, out_sem, token_send, token_recv, last_send, last_recv, *line_sems = refs
    group_count, local_rows, local_width = back_ref.shape[1], back_ref.shape[3], back_ref.shape[4]
    row_count, width = normed_ref.shape
    later, later_sem, line_sems = line_sems[:5], line_sems[5], line_sems[6:]
    hidden_ref, middle_ref, frames_ref, shortcut_ref, modulation_ref = later
    place = Place(plane, seq_count)
    me = place.me
    side = place.cols_x
    enter([(place.grp, other) for other in place.others] + [(other, me) for other in place.groups])
    chains = [
        LineSum(place, *line_refs[2 * index:2 * index + 2], *line_sems[2 * index:2 * index + 2])
        for index in range(3)
    ]
    held = pltpu.make_async_copy(finished, line_refs[4], weight_sem.at[2])
    held.start()
    weights = [
        pltpu.make_async_copy(projection_ref, projection_scr, weight_sem.at[0]),
        pltpu.make_async_copy(combine_ref, combine_scr, weight_sem.at[1]),
    ]
    for copy in weights:
        copy.start()
    loads = [
        pltpu.make_async_copy(source, scratch, later_sem.at[index])
        for index, (source, scratch) in enumerate(
            zip((hidden_in, middle_in, frames_in, shortcut_in, modulation_in), later)
        )
    ]
    for copy in loads:
        copy.start()
    held.wait()
    chains[2].begin()
    for source in range(seq_count):
        for kind in range(3):
            for group in range(group_count):
                packed_scr[
                    group * local_rows:(group + 1) * local_rows,
                    kind * width + source * local_width:kind * width + (source + 1) * local_width,
                ] = back_ref[source, group, kind]

    def turn(index, carry):
        lanes = pl.ds(pl.multiple_of(index * 128, 128), 128)
        packed_scr[:, lanes] = turn_lanes(
            packed_scr[:, lanes].astype(jnp.float32), cos_ref[...], -sin_ref[...]
        ).astype(jnp.bfloat16)
        return carry

    lax.fori_loop(0, 2 * width // 128, turn, 0)
    normed_t_scr[...] = normed_ref[...].T
    segments = [
        piece_segments([part.shape[1:]], side, part.shape[2] // side)[0][0] for part in parts
    ]
    done_segments, _ = piece_segments(
        [out.shape for out in outs[2:]], side, min(out.shape[1] for out in outs[2:]) // side
    )
    pieces = [[line_refs[2 * index].at[step] for step in range(layers)] for index in range(2)]
    plane_sum = PlaneSum(place, parts, pieces, segments, buffers, semaphores, True)
    late_rounds = chains[2].rounds()
    spread = PlaneSpread(place, outs, *spread_sems)

    def share(index, left, right, tile):
        rows, columns = parts[index].shape[1:]

        def one(turn, carry):
            lanes = pl.ds(pl.multiple_of(turn * tile, tile), tile)
            parts[index][:, :, lanes] = dot_nn(left[...], right[:, lanes]).astype(jnp.bfloat16).reshape(
                seq_count, rows, tile
            )
            return carry

        lax.fori_loop(0, columns // tile, one, 0)
        for step in range(layers):
            plane_sum.swap(index, step)

    share(0, normed_t_scr, packed_scr, 512)
    for copy in loads:
        copy.wait()
    joined_t_scr[:width, :] = frames_ref[...].T
    joined_t_scr[width:, :] = shortcut_ref[...].T
    weights[0].wait()

    def grad_tile(index, carry):
        at = pl.ds(pl.multiple_of(index * 512, 512), 512)
        grad_scr[:, at] = dot_nt(packed_scr[...], projection_scr[at, :])
        return carry

    lax.fori_loop(0, width // 512, grad_tile, 0)
    for hook in plane_sum.steps(plane_sum.first, 0):
        hook()
    block, utter_rows = utter_scr.shape[1], 2 * group_count
    utter_scr[...] = jnp.zeros_like(utter_scr)

    def put(part, utter, value):
        row = part * utter_rows + utter
        utter_scr[row // block, row % block:row % block + 1, :] = value

    for part in range(4):
        for utter in range(utter_rows):
            put(part + 2, utter, late_ref[part * utter_rows + utter:part * utter_rows + utter + 1, :])
    chunk = 32
    for group in range(group_count):

        def norm_back(index, sums):
            first = pl.multiple_of(index * chunk, chunk)
            at = pl.ds(pl.multiple_of(group * local_rows + first, chunk), chunk)
            second = second_mask(bound_ref, group, me, local_rows, first, chunk)
            row = group * 2 * 6
            scale_part = jnp.where(second, mods_ref[row + 7:row + 8, :], mods_ref[row + 1:row + 2, :])
            grad = grad_scr[at, :]
            normal, scale = centered(hidden_ref[at, :])
            inner = grad * (1.0 + scale_part)
            turned = scale * (
                inner
                - jnp.mean(inner, axis=-1, keepdims=True)
                - normal * jnp.mean(inner * normal, axis=-1, keepdims=True)
            )
            low_scr[at, :] = (middle_ref[at, :] + turned).astype(jnp.bfloat16)
            scaled = grad * normal
            later = second.astype(jnp.float32)
            shift_later, scale_later = grad * later, scaled * later
            return (
                sums[0] + fold_rows(grad - shift_later, jnp.sum),
                sums[1] + fold_rows(shift_later, jnp.sum),
                sums[2] + fold_rows(scaled - scale_later, jnp.sum),
                sums[3] + fold_rows(scale_later, jnp.sum),
            )

        zero = jnp.zeros((8, width), jnp.float32)
        sums = lax.fori_loop(0, local_rows // chunk, norm_back, (zero, zero, zero, zero))
        for spot, value in enumerate(sums):
            put(spot // 2, group * 2 + spot % 2, jnp.sum(value, axis=0, keepdims=True))
    small = SmallSum(place, utter_scr, total_ref, *small_refs)
    small.begin()
    share(1, joined_t_scr, low_scr, 512)
    late_rounds[0]()
    for hook in plane_sum.steps(plane_sum.first, 1) + plane_sum.steps(plane_sum.second, 0):
        hook()
    weights[1].wait()

    def joined_tile(index, carry):
        at = pl.ds(pl.multiple_of(index * 512, 512), 512)
        late = pl.ds(pl.multiple_of(width + index * 512, 512), 512)
        frames_scr[:, at] = dot_nt(low_scr[...], combine_scr[at, :])
        shortcut_scr[:, at] = dot_nt(low_scr[...], combine_scr[late, :])
        return carry

    lax.fori_loop(0, width // 512, joined_tile, 0)
    grads = [
        pltpu.make_async_copy(frames_scr, frames_out, out_sem.at[0]),
        pltpu.make_async_copy(shortcut_scr, shortcut_out, out_sem.at[1]),
    ]
    for copy in grads:
        copy.start()
    for hook in late_rounds[1:]:
        hook()
    small.middle()
    for hook in plane_sum.steps(plane_sum.second, 1) + plane_sum.steps(plane_sum.third, 0):
        hook()
    chains[0].begin()
    small.finish()
    for spot in range(seq_count):
        flat_scr[spot * block:(spot + 1) * block, :] = total_ref[spot]
    utters_ref[place.grp] = flat_scr[...].astype(jnp.bfloat16)
    tokens = [
        place.push(utters_ref.at[place.grp], utters_ref.at[place.grp], token_send, token_recv, step, (other, me))
        for step, other in enumerate(place.groups)
    ]
    condition_scr[...] = jnp.zeros_like(condition_scr)
    shard_rows = modulation_ref.shape[0]
    for spot in range(6 * utter_rows // block):
        part, row = spot * block // utter_rows, spot * block % utter_rows
        condition_scr[row:row + block, :shard_rows] += dot_nt(
            total_ref[spot].astype(jnp.bfloat16), modulation_ref[:, part * width:(part + 1) * width]
        )
    conditions_ref[me] = condition_scr[...]
    tokens += [
        place.push(condition_scr, conditions_ref.at[me], last_send, last_recv, step, (place.grp, other))
        for step, other in enumerate(place.others)
    ]
    rounds = [chains[0].rounds(), chains[1].rounds()]
    piece, others = chains[2].close()
    for index in range(2, 5):
        spread.total(index, piece, others, done_segments[index - 2])
    rounds[0][0]()
    for hook in plane_sum.steps(plane_sum.third, 1):
        hook()
    chains[1].begin()
    for hook in rounds[0][1:]:
        hook()
    for index in range(2, 5):
        spread.second(index)
    piece, others = chains[0].close()
    spread.total(0, piece, others, segments[0])
    for hook in rounds[1]:
        hook()
    piece, others = chains[1].close()
    spread.total(1, piece, others, segments[1])
    spread.second(0)
    spread.second(1)
    for chain in chains:
        chain.sent()
    place.sent()
    for copy in tokens:
        copy.wait_recv()
    for copy in grads:
        copy.wait()
    for index in range(5):
        spread.finish(index)


def finish_backward(bounds, back, cos, sin, normed, hidden, middle_grad, frames, shortcut, combine, projection, mods, late, modulation, finished, done_shapes):
    grp_count = lax.axis_size("grp")
    seq_count = lax.axis_size("seq")
    side = math.isqrt(grp_count)
    layers = seq_count // 2
    hops = max(side - 1, 1)
    anywhere = pl.BlockSpec(memory_space=pl.ANY)
    vmem = pl.BlockSpec(memory_space=pltpu.VMEM)
    dma = pltpu.SemaphoreType.DMA
    row_count, width = normed.shape
    low, full = jnp.bfloat16, jnp.float32
    parts = [
        jax.ShapeDtypeStruct((seq_count, weight.shape[0] // seq_count, weight.shape[1]), low)
        for weight in (projection, combine)
    ]
    out_shapes = [part.shape[1:] for part in parts] + list(done_shapes)
    small = jax.ShapeDtypeStruct((seq_count, 32 // seq_count, width), full)
    return pl.pallas_call(
        functools.partial(back_kernel, (side, side), seq_count),
        out_shape=(
            jax.ShapeDtypeStruct((row_count, width), full),
            jax.ShapeDtypeStruct((row_count, width), full),
        ) + tuple(jax.ShapeDtypeStruct(shape, low) for shape in out_shapes) + (
            jax.ShapeDtypeStruct((grp_count, 32, width), low),
            jax.ShapeDtypeStruct((seq_count, 8, 128), full),
        ),
        in_specs=[pl.BlockSpec(memory_space=pltpu.SMEM)] + [vmem] * 4 + [anywhere] * 6 + [vmem] * 2 + [anywhere] * 2,
        out_specs=(anywhere,) * 2 + (vmem,) * 7,
        scratch_shapes=[
            pltpu.VMEM((row_count, 3 * width), low),
            pltpu.VMEM(combine.shape, low),
            pltpu.VMEM(projection.shape, low),
            pltpu.VMEM((width, row_count), low),
            pltpu.VMEM((2 * width, row_count), low),
            pltpu.VMEM((row_count, width), full),
            pltpu.VMEM((row_count, width), low),
            pltpu.VMEM((row_count, width), full),
            pltpu.VMEM(small.shape, full),
            pltpu.VMEM(small.shape, full),
            pltpu.VMEM((32, width), full),
            pltpu.VMEM((8, 128), full),
        ] + [pltpu.VMEM(part.shape, low) for part in parts] + [
            pltpu.VMEM((layers + more,) + shape, low)
            for shape in [
                (part.shape[1] // side, part.shape[2] // side) for part in parts
            ] + [finished.shape[1:]] for more in range(2)
        ] + plane_sum_scratch(parts, side, True) + small_scratch(small) + [
            dma((5, 2, hops)), dma((5, 2, hops)),
            dma((5, 2, hops, side)), dma((5, 2, hops, side)),
            dma((3,)), dma((2,)),
            dma((grp_count - 1,)), dma((grp_count - 1,)),
            dma((seq_count - 1,)), dma((seq_count - 1,)),
        ] + [
            pltpu.VMEM((row_count, width), full), pltpu.VMEM((row_count, width), full),
            pltpu.VMEM((row_count, width), low), pltpu.VMEM((row_count, width), low),
            pltpu.VMEM(modulation.shape, low), dma((5,)),
        ] + [dma((2, layers))] * 6 + [
        ],
        compiler_params=pltpu.CompilerParams(
            collective_id=4, has_side_effects=True, vmem_limit_bytes=62 * 1024 * 1024
        ),
        name="finish_backward",
    )(bounds, back, cos, sin, normed, hidden, middle_grad, frames, shortcut, combine, projection, mods, late, modulation, finished)


def shards(
    frames,
    shortcut,
    time_embed,
    lengths,
    kept_mask,
    target,
    combine,
    modulation,
    projection,
    readout,
    expand,
    contract,
):
    group_count = frames.shape[0]
    local_rows = frames.shape[1]
    width = HEADS * HEAD_DIM
    row_count = group_count * local_rows
    seq_count = lax.axis_size("seq")
    utter_count = time_embed.shape[1]
    kept_float = kept_mask.astype(jnp.float32)
    half_dim = HEAD_DIM // 2
    inverse = jnp.exp(-jnp.log(rope_base) * (jnp.arange(half_dim, dtype=jnp.float32) / half_dim))
    signs = jnp.where(jnp.arange(128) % HEAD_DIM < half_dim, -1.0, 1.0).astype(jnp.float32)
    ladder = jnp.zeros((8, 128), jnp.float32).at[0].set(jnp.tile(inverse, 128 // half_dim)).at[1].set(signs)
    silu_value, silu_pull = jax.vjp(jax.nn.silu, time_embed)
    condition = silu_value.astype(jnp.bfloat16)
    shard_rows = modulation.shape[0]
    utter_rows = group_count * utter_count
    condition_part = lax.dynamic_slice_in_dim(
        condition, lax.axis_index("seq") * shard_rows, shard_rows, 2
    ).reshape(utter_rows, shard_rows)
    token = jnp.zeros((8, 128), jnp.float32)
    token = token.at[:utter_rows, :shard_rows].set(condition_part.astype(jnp.float32))
    late_shards = (readout, expand, contract)
    bounds = lengths[:, 0]
    combine_full, projection_full, *rest = front(
        bounds,
        frames.reshape(row_count, width),
        shortcut.reshape(row_count, width),
        ladder,
        kept_float,
        token,
        modulation,
        combine,
        projection,
        late_shards,
    )
    late_pieces, hidden, normed, qkv, cos_lanes, sin_lanes, mods, loss_scale, tokens = rest
    combine_full = combine_full.reshape(2 * width, width)
    projection_full = projection_full.reshape(width, 3 * width)
    condition_all = tokens[:, :utter_rows, :shard_rows].reshape(-1, shard_rows).astype(jnp.bfloat16)
    split_shape = (group_count, local_rows, width)
    kept_heads, mixture_blocks, log_total, *late_full = attend_forward(
        bounds, qkv, late_shards, late_pieces
    )
    readout_full = late_full[0].reshape(width, width)
    expand_full = late_full[1].reshape(width, -1)
    contract_full = late_full[2].reshape(-1, width)
    result, middle_grad, mixture_grad, late_rows, *late_parts = middle(
        bounds,
        mixture_blocks,
        hidden,
        target.reshape(row_count, width),
        kept_float.reshape(row_count, 1),
        mods,
        loss_scale,
        late_full[0].reshape(width, width),
        late_full[1].reshape(width, -1),
        late_full[2].reshape(-1, width),
    )
    back_blocks, plane_pieces = attend_backward(
        bounds,
        kept_heads,
        mixture_grad,
        log_total,
        late_parts[:3],
        late_parts[3:],
    )
    frames_grad, shortcut_grad, *shares, utters, condition_back = finish_backward(
        bounds,
        back_blocks,
        cos_lanes,
        sin_lanes,
        normed,
        hidden,
        middle_grad,
        frames.reshape(row_count, width),
        shortcut.reshape(row_count, width),
        combine_full,
        projection_full,
        mods,
        late_rows,
        modulation,
        plane_pieces,
        [contract.shape, expand.shape, readout.shape],
    )
    frames_grad = frames_grad.reshape(split_shape)
    shortcut_grad = shortcut_grad.reshape(split_shape)
    projection_grad, combine_grad, contract_grad, expand_grad, readout_grad = [
        share.astype(jnp.float32) for share in shares
    ]
    utter_all = jnp.transpose(
        utters[:, :6 * utter_rows].reshape(-1, 6, utter_rows, width), (0, 2, 1, 3)
    ).reshape(-1, 6 * width)
    modulation_grad = product_left(condition_all, utter_all)
    condition_grad = jnp.transpose(
        condition_back[:, :utter_rows, :shard_rows], (1, 0, 2)
    ).reshape(group_count, utter_count, width)
    time_grad = silu_pull(condition_grad)[0]
    summed = (combine_grad, modulation_grad, projection_grad, readout_grad, expand_grad, contract_grad)
    return (
        result.reshape(split_shape),
        frames_grad,
        shortcut_grad,
        time_grad,
        summed[0],
        summed[1],
        summed[2],
        summed[3],
        summed[4],
        summed[5],
    )


def solution(mesh):
    return jax.shard_map(
        shards,
        mesh=mesh,
        in_specs=(
            P("grp", "seq", None),
            P("grp", "seq", None),
            P("grp", None, None),
            P("grp", None),
            P("grp", "seq"),
            P("grp", "seq", None),
            P("seq", None),
            P("seq", None),
            P("seq", None),
            P("seq", None),
            P("seq", None),
            P("seq", None),
        ),
        out_specs=(
            P("grp", "seq", None),
            P("grp", "seq", None),
            P("grp", "seq", None),
            P("grp", None, None),
            P("seq", None),
            P("seq", None),
            P("seq", None),
            P("seq", None),
            P("seq", None),
            P("seq", None),
        ),
        check_vma=False,
    )
```
